32 devices in a mesh: dp: 8 (over y, x, core), fsdp: 4 (over z).
Axes of the slice: x: 2, y: 2, z: 4, core: 2. Of those that a mesh axis runs over, the one named last changes fastest.
Arguments:
- owner_ids: int32 [16384, 8], P(('dp', 'fsdp')), may hold values from 0 to 31, all different within a row; in each aligned block of 512 rows (0 to 511, 512 to 1023, ...) at most 256 rows name the same one
- row_ids: int32 [16384, 8], P(('dp', 'fsdp')), may hold values from 0 to 4095
- embed_table: bfloat16 [131072, 64], P(('dp', 'fsdp')), may hold values from -6 to 6
- expandone: bfloat16 [3072, 256], P(('dp', 'fsdp')), may hold values from -0.25 to 0.25
- expbiasone: bfloat16 [1536], P(('dp', 'fsdp')), may hold values from -4 to 4
- reduceone: bfloat16 [1536, 256], P(('dp', 'fsdp')), may hold values from -0.375 to 0.375
- redbiasone: bfloat16 [1536], P(('dp', 'fsdp')), may hold values from -6 to 6
- normgainone: bfloat16 [1536], P(('dp', 'fsdp')), may hold values from 0.25 to 1.75
- taskgateone: bfloat16 [1024, 4], P(('dp', 'fsdp')), may hold values from -0.4375 to 0.4375
- sharegateone: bfloat16 [512, 6], P(('dp', 'fsdp')), may hold values from -0.4375 to 0.4375
- expandtwo: bfloat16 [1536, 256], P(('dp', 'fsdp')), may hold values from -0.375 to 0.375
- expbiastwo: bfloat16 [1536], P(('dp', 'fsdp')), may hold values from -4 to 4
- reducetwo: bfloat16 [1536, 256], P(('dp', 'fsdp')), may hold values from -0.375 to 0.375
- redbiastwo: bfloat16 [1536], P(('dp', 'fsdp')), may hold values from -6 to 6
- normgaintwo: bfloat16 [1536], P(('dp', 'fsdp')), may hold values from 0.25 to 1.75
- taskgatetwo: bfloat16 [512, 4], P(('dp', 'fsdp')), may hold values from -1 to 1
- towerinner: bfloat16 [512, 128], P(('dp', 'fsdp')), may hold values from -0.375 to 0.375
- towerbias: bfloat16 [256], P(('dp', 'fsdp')), may hold values from -4 to 4
- towermiddle: bfloat16 [256, 64], P(('dp', 'fsdp')), may hold values from -0.5 to 0.5
- towertail: bfloat16 [256], P(('dp', 'fsdp')), may hold values from -4 to 4
- logit_cot: float32 [2, 16384], P(None, ('dp', 'fsdp')), may hold values from -6 to 6
Outputs:
- logits: float32 [2, 16384], P(None, ('dp', 'fsdp'))
- x_grad: float32 [16384, 512], P(('dp', 'fsdp'))
- embed_table_grad: float32 [131072, 64], P(('dp', 'fsdp'))
- expandone_grad: float32 [3072, 256], replicated
- expbiasone_grad: float32 [1536], replicated
- reduceone_grad: float32 [1536, 256], replicated
- redbiasone_grad: float32 [1536], replicated
- normgainone_grad: float32 [1536], replicated
- taskgateone_grad: float32 [1024, 4], replicated
- sharegateone_grad: float32 [512, 6], replicated
- expandtwo_grad: float32 [1536, 256], replicated
- expbiastwo_grad: float32 [1536], replicated
- reducetwo_grad: float32 [1536, 256], replicated
- redbiastwo_grad: float32 [1536], replicated
- normgaintwo_grad: float32 [1536], replicated
- taskgatetwo_grad: float32 [512, 4], replicated
- towerinner_grad: float32 [512, 128], replicated
- towerbias_grad: float32 [256], replicated
- towermiddle_grad: float32 [256, 64], replicated
- towertail_grad: float32 [256], replicated
The draws below stay inside these ranges and needn't reach their ends.
Inputs may be any that keep to these rules, and one draw needn't show every extreme that they name: `owner_ids`: an event's 8 owners are different. Among the lookups of one device's events, no owner is named more than 256 times, a bound that some block reaches.
All inputs are finite; a program needn't handle non-finite values.
Results may differ from the reference program's by a relative error of at most 0.017.
Values may be sent and summed in bfloat16 or wider, within the bound.
No kernel may reach another device: no remote copies, remote signals or barrier semaphores. Data moves between devices by JAX's collectives and lax.ppermute only.
A program may use at most 128 MiB of HBM per device.

```python
import math
import jax
import jax.numpy as jnp
import numpy as np
from jax import lax

EV_DEV = 512
ROWS_DEV = 4096
EMB = 64
D_IN = 512
HID = 256
TOWER_ONE = 128
TOWER_TWO = 64
FIELDS = 8
TOKENS = 16384
ROWS = 131072
CAP = 256
DEVICES = 32


def with_ends(drawn, rng, low, high):
    shape = drawn.shape
    place = [jax.random.randint(jax.random.fold_in(rng, axis), (), 0, shape[axis]) for axis in range(len(shape))]
    drawn = drawn.at[tuple(place)].set(low)
    longest = shape.index(max(shape))
    place[longest] = (place[longest] + 1) % shape[longest]
    return drawn.at[tuple(place)].set(high)


def shard_levels(rng, extent, cuts, smallest, high):
    def one(position, shards_of):
        draws = jax.random.uniform(jax.random.fold_in(jax.random.fold_in(rng, 6), position), (shards_of,), jnp.float32, smallest / len(cuts), high / len(cuts))
        return jnp.repeat(jnp.exp(draws), extent[position] // shards_of).reshape((-1,) + (1,) * (len(extent) - position - 1))

    gain = one(*cuts[0])
    for cut in cuts[1:]:
        gain = gain * one(*cut)
    return gain


def cumulative_ranks(number_of, skew):
    loads = [(1 << 20) // math.isqrt(rank ** skew) + 1 for rank in range(1, number_of + 1)]
    deviation = 1 + sum(loads) // (1 << 30)
    return np.cumsum(np.array([max(1, weight // deviation) for weight in loads]))


def skewed_ids(key, dims, count, slope):
    listing = cumulative_ranks(count, slope)
    lot = jax.random.randint(jax.random.fold_in(key, 1), dims, 0, int(listing[count - 1]))
    standing = jnp.searchsorted(jnp.asarray(listing, jnp.int32), lot, side="right")
    return jax.random.permutation(jax.random.fold_in(key, 2), count)[standing].astype(jnp.int32)


def shared_out(own_key, own, number, rows, amount, top, bound, skew):
    sequence = jax.random.permutation(own_key, amount)
    packed, usual = shares(amount, rows * top, bound, skew, True), shares(amount, rows * top, bound, skew, False)
    places = jnp.arange(amount)

    def named(lengths, rotation):
        used = int((lengths > 0).sum())
        fixed = max(1, used // 4)
        shifted = fixed + (places - fixed + rotation * (used - fixed)) % max(1, amount - fixed)
        return jnp.zeros((amount,), jnp.int32).at[sequence[jnp.where(places < fixed, places, shifted)]].set(jnp.asarray(lengths, jnp.int32))

    lengths = jnp.where(number % 4 == 0, named(packed, number // 4), named(usual, number - number // 4 - 1))
    mixed = jax.random.permutation(jax.random.fold_in(own, 3), amount)
    giver, receiver = mixed[0:amount // 2 * 2:2], mixed[1:amount // 2 * 2:2]
    room = jnp.minimum(lengths[giver] - 1, bound - lengths[receiver]) // 2
    room = jnp.where((giver == sequence[0]) | (receiver == sequence[0]) | (lengths[receiver] == 0), 0, jnp.maximum(room, 0))
    shifted = jax.random.randint(jax.random.fold_in(own, 4), (amount // 2,), 0, 1 << 20) % (room + 1)
    lengths = lengths.at[giver].add(-shifted).at[receiver].add(shifted)
    members = jnp.searchsorted(jnp.cumsum(lengths), jnp.arange(rows * top), side="right").astype(jnp.int32)
    listing = members.reshape(top, rows).T
    listing = listing[jax.random.permutation(jax.random.fold_in(own, 1), rows)]
    rotation = jax.random.randint(jax.random.fold_in(own, 2), (rows, 1), 0, top)
    return jnp.take_along_axis(listing, (jnp.arange(top)[None, :] + rotation) % top, axis=1)


def shares(count, total, most, slope, full):
    portions = [(1 << 20) // math.isqrt(rank ** slope) + 1 for rank in range(1, count + 1)]
    largest = most if full else min(most, max(-(-total // count), total * portions[0] // sum(portions)))
    least = 1 if total - largest >= count - 1 else 0
    counts, rest = [largest] + [least] * (count - 1), total - largest - least * (count - 1)
    while rest > 0:
        movable = [i for i in range(1, count) if counts[i] < largest] or [i for i in range(1, count) if counts[i] < most]
        pool, budget = sum([portions[i] for i in movable]), rest
        for i in movable:
            extra = min(most - counts[i], max(1, budget * portions[i] // pool), rest)
            counts[i] = counts[i] + extra
            rest = rest - extra
    return np.array(counts)


def bell_draw(key, dims, scale, reach, cuts=(), dtype=jnp.bfloat16):
    array = scale * jax.random.normal(key, dims, jnp.float32)
    if cuts:
        array = array * shard_levels(key, dims, cuts, -0.22, 0.18)
    return jnp.clip(array, -reach, reach).astype(dtype)


def setup_inputs(seed: int = 0) -> dict:
    streams_of = jax.random.split(jax.random.key(seed), 22)
    owner_ids_keys = jax.random.split(jax.random.fold_in(streams_of[0], 1), TOKENS // EV_DEV)
    owner_ids_turns = jax.random.permutation(jax.random.fold_in(streams_of[0], 3), TOKENS // EV_DEV)
    owner_ids = jax.vmap(lambda own, number: shared_out(jax.random.fold_in(streams_of[0], 2), own, number, EV_DEV, DEVICES, FIELDS, CAP, 2))(owner_ids_keys, owner_ids_turns).reshape((TOKENS, FIELDS))
    row_ids = with_ends(skewed_ids(streams_of[1], (TOKENS, FIELDS), ROWS_DEV, 2), jax.random.fold_in(streams_of[1], 3), 0, ROWS_DEV - 1).astype(jnp.int32)
    embed_table = bell_draw(streams_of[2], (ROWS, EMB), 1.0, 6.0, ((0, 32),))
    expandone = bell_draw(streams_of[3], (6 * D_IN, HID), D_IN ** -0.5, 0.25, ((0, 32),))
    expbiasone = bell_draw(streams_of[4], (6 * HID,), 0.3, 4.0, ((0, 32),))
    reduceone = bell_draw(streams_of[5], (6 * HID, HID), HID ** -0.5, 0.375, ((0, 32),))
    redbiasone = bell_draw(streams_of[6], (6 * HID,), 0.5, 6.0, ((0, 32),))
    normgainone = jnp.clip(1.0 + 0.15 * jax.random.normal(streams_of[7], (6 * HID,), jnp.float32), 0.25, 1.75).astype(jnp.bfloat16)
    taskgateone = bell_draw(streams_of[8], (2 * D_IN, 4), (0.7 / D_IN ** 0.5), 0.4375, ((0, 32),))
    sharegateone = bell_draw(streams_of[9], (D_IN, 6), (0.7 / D_IN ** 0.5), 0.4375, ((0, 32),))
    expandtwo = bell_draw(streams_of[10], (6 * HID, HID), HID ** -0.5, 0.375, ((0, 32),))
    expbiastwo = bell_draw(streams_of[11], (6 * HID,), 0.3, 4.0, ((0, 32),))
    reducetwo = bell_draw(streams_of[12], (6 * HID, HID), HID ** -0.5, 0.375, ((0, 32),))
    redbiastwo = bell_draw(streams_of[13], (6 * HID,), 0.5, 6.0, ((0, 32),))
    normgaintwo = jnp.clip(1.0 + 0.15 * jax.random.normal(streams_of[14], (6 * HID,), jnp.float32), 0.25, 1.75).astype(jnp.bfloat16)
    taskgatetwo = bell_draw(streams_of[15], (2 * HID, 4), (1.0 / HID ** 0.5), 1.0, ((0, 32),))
    towerinner = bell_draw(streams_of[16], (2 * HID, TOWER_ONE), HID ** -0.5, 0.375, ((0, 32),))
    towerbias = bell_draw(streams_of[17], (2 * TOWER_ONE,), 0.3, 4.0, ((0, 32),))
    towermiddle = bell_draw(streams_of[18], (2 * TOWER_ONE, TOWER_TWO), TOWER_ONE ** -0.5, 0.5, ((0, 32),))
    towertail = bell_draw(streams_of[19], (4 * TOWER_TWO,), 0.25, 4.0, ((0, 32),))
    logit_cot = bell_draw(streams_of[20], (2, TOKENS), 1.0, 6.0, ((1, 32),), jnp.float32)
    return {"owner_ids": owner_ids, "row_ids": row_ids, "embed_table": embed_table, "expandone": expandone, "expbiasone": expbiasone, "reduceone": reduceone, "redbiasone": redbiasone, "normgainone": normgainone, "taskgateone": taskgateone, "sharegateone": sharegateone, "expandtwo": expandtwo, "expbiastwo": expbiastwo, "reducetwo": reducetwo, "redbiastwo": redbiastwo, "normgaintwo": normgaintwo, "taskgatetwo": taskgatetwo, "towerinner": towerinner, "towerbias": towerbias, "towermiddle": towermiddle, "towertail": towertail, "logit_cot": logit_cot}


EPS = 1e-05
HIGH = lax.Precision.HIGHEST

@jax.custom_vjp
def low(v):
    return lax.optimization_barrier(v.astype(jnp.bfloat16)).astype(jnp.float32)

@jax.custom_vjp
def low_back(v):
    return v

def low_keep(v):
    return (low(v), None)

def low_pass(kept, grad):
    return (grad,)

def back_keep(v):
    return (v, None)

def back_low(kept, grad):
    return (low(grad),)
low.defvjp(low_keep, low_pass)
low_back.defvjp(back_keep, back_low)

def layer_norm(values, gain_w):
    centered = values - lax.optimization_barrier(jnp.mean(values, axis=-1, keepdims=True))
    spread = lax.optimization_barrier(jnp.mean(centered * centered, axis=-1, keepdims=True))
    return centered * lax.rsqrt(spread + EPS) * gain_w

def experts(inputs, expand, expbias, shrink, shrinkbias, gain_w):
    in_width = inputs.shape[2]
    hidden = shrink.shape[1]
    expand_w = expand.reshape(3, 2, in_width, hidden)
    preact = low_back(jnp.einsum('gnd,gkdh->gknh', inputs, expand_w, precision=HIGH) + expbias.reshape(3, 2, 1, hidden))
    active = low(jax.nn.silu(preact))
    output = low_back(jnp.einsum('gknh,gkho->gkno', active, shrink.reshape(3, 2, hidden, hidden), precision=HIGH) + shrinkbias.reshape(3, 2, 1, hidden))
    return layer_norm(output, gain_w.reshape(3, 2, 1, hidden))

def gate_probs(inputs, weights):
    scores = low_back(jnp.dot(inputs, weights, precision=HIGH))
    return jax.nn.softmax(scores, axis=-1)

def task_mix(weights, outputs, task_index):
    pieces = jnp.concatenate([outputs[task_index], outputs[2]], axis=0)
    return jnp.einsum('nk,knh->nh', weights, pieces, precision=HIGH)

def dense_net(params, features):
    expandone, expbiasone, reduceone, redbiasone, normgainone, taskgateone, sharegateone, expandtwo, expbiastwo, reducetwo, redbiastwo, normgaintwo, taskgatetwo, towerinner, towerbias, towermiddle, towertail = params
    in_width = features.shape[1]
    hidden = reduceone.shape[1]
    level_one = experts(jnp.broadcast_to(features, (3,) + features.shape), expandone, expbiasone, reduceone, redbiasone, normgainone)
    lower_gates = taskgateone.reshape(2, in_width, 4)
    mixture = [task_mix(gate_probs(features, lower_gates[task_index]), level_one, task_index) for task_index in range(2)]
    shared = jnp.einsum('nk,knh->nh', gate_probs(features, sharegateone), level_one.reshape(6, -1, hidden), precision=HIGH)
    carried = low(jnp.stack(mixture + [shared]))
    level_two = experts(carried, expandtwo, expbiastwo, reducetwo, redbiastwo, normgaintwo)
    upper_gates = taskgatetwo.reshape(2, hidden, 4)
    tower_input = low(jnp.stack([task_mix(gate_probs(carried[task_index], upper_gates[task_index]), level_two, task_index) for task_index in range(2)]))
    inner_w = towerinner.reshape(2, hidden, -1)
    first_tower = low_back(jnp.einsum('tnd,tdh->tnh', tower_input, inner_w, precision=HIGH) + towerbias.reshape(2, 1, -1))
    tower_act = low(jax.nn.silu(first_tower))
    middle_w = towermiddle.reshape(2, inner_w.shape[2], -1)
    narrow = middle_w.shape[2]
    tail_parts = towertail.reshape(2, 2, narrow)
    second_tower = low_back(jnp.einsum('tnh,thk->tkn', tower_act, middle_w, precision=HIGH) + tail_parts[:, 0, :, None])
    return lax.optimization_barrier(jnp.sum(jax.nn.silu(second_tower) * tail_parts[:, 1, :, None], axis=1))

def reference(owner_ids, row_ids, embed_table, expandone, expbiasone, reduceone, redbiasone, normgainone, taskgateone, sharegateone, expandtwo, expbiastwo, reducetwo, redbiastwo, normgaintwo, taskgatetwo, towerinner, towerbias, towermiddle, towertail, logit_cot):
    params = tuple((weight.astype(jnp.float32) for weight in (expandone, expbiasone, reduceone, redbiasone, normgainone, taskgateone, sharegateone, expandtwo, expbiastwo, reducetwo, redbiastwo, normgaintwo, taskgatetwo, towerinner, towerbias, towermiddle, towertail)))
    table_full = embed_table.astype(jnp.float32)
    tokens, fields = owner_ids.shape
    emb_width = table_full.shape[1]
    block_rows = math.gcd(tokens, 4096)
    nblocks = tokens // block_rows
    lookup = (owner_ids * ROWS_DEV + row_ids).astype(jnp.int32).reshape(nblocks, block_rows, fields)
    cot_blocks = logit_cot.astype(jnp.float32).reshape(2, nblocks, block_rows).transpose(1, 0, 2)

    def block_step(running, inputs):
        param_sums, table_sum = running
        indices, cot_part = inputs

        def gather_rows(whole):
            return whole[indices].reshape(block_rows, fields * emb_width)
        features, pull_rows = jax.vjp(gather_rows, table_full)
        block_logits, pull_dense = jax.vjp(dense_net, params, features)
        param_part, row_grad = pull_dense(cot_part)
        table_part, = pull_rows(row_grad)
        return ((jax.tree.map(jnp.add, param_sums, param_part), table_sum + table_part), (block_logits, row_grad))
    initial = (jax.tree.map(jnp.zeros_like, params), jnp.zeros_like(table_full))
    (param_sums, table_sum), (logit_blocks, grad_blocks) = lax.scan(block_step, initial, (lookup, cot_blocks))
    logits = logit_blocks.transpose(1, 0, 2).reshape(2, tokens)
    x_grad = grad_blocks.reshape(tokens, fields * emb_width)
    g_expandone, g_expbiasone, g_reduceone, g_redbiasone, g_normgainone, g_taskgateone, g_sharegateone, g_expandtwo, g_expbiastwo, g_reducetwo, g_redbiastwo, g_normgaintwo, g_taskgatetwo, g_towerinner, g_towerbias, g_towermiddle, g_towertail = param_sums
    return (logits, x_grad, table_sum, g_expandone, g_expbiasone, g_reduceone, g_redbiasone, g_normgainone, g_taskgateone, g_sharegateone, g_expandtwo, g_expbiastwo, g_reducetwo, g_redbiastwo, g_normgaintwo, g_taskgatetwo, g_towerinner, g_towerbias, g_towermiddle, g_towertail)
```

```python
import jax
import jax.numpy as jnp
from jax import lax
from jax.sharding import PartitionSpec as P

EPS = 1e-05


def silu_slope(values):
    sigmoid_v = jax.nn.sigmoid(values)
    return sigmoid_v * (1.0 + values * (1.0 - sigmoid_v))


def expert_forward(inputs, pattern, expand, expbias, shrink, shrinkbias, gain_w):
    hidden = shrink.shape[1]
    in_width = expand.shape[0] // 6
    expand_w = expand.reshape(3, 2, in_width, hidden)
    preact = jnp.einsum(
        pattern, inputs, expand_w, preferred_element_type=jnp.float32
    ) + expbias.astype(jnp.float32).reshape(3, 2, 1, hidden)
    active = jax.nn.silu(preact).astype(jnp.bfloat16)
    output = jnp.einsum(
        "gknh,gkho->gkno",
        active,
        shrink.reshape(3, 2, hidden, hidden),
        preferred_element_type=jnp.float32,
    ) + shrinkbias.astype(jnp.float32).reshape(3, 2, 1, hidden)
    centered = output - jnp.mean(output, axis=-1, keepdims=True)
    inverse = lax.rsqrt(jnp.mean(centered * centered, axis=-1, keepdims=True) + EPS)
    normed = centered * inverse
    result = normed * gain_w.astype(jnp.float32).reshape(3, 2, 1, hidden)
    return (result, (preact, active, normed, inverse))


def expert_backward(inputs, level_first, expand, shrink, gain_w, saved_parts, upstream):
    preact, active, normed, inverse = saved_parts
    hidden = shrink.shape[1]
    in_width = expand.shape[0] // 6
    scaled = upstream * gain_w.astype(jnp.float32).reshape(3, 2, 1, hidden)
    gain_grad = jnp.sum(upstream * normed, axis=2)
    out_grad = inverse * (
        scaled
        - jnp.mean(scaled, axis=-1, keepdims=True)
        - normed * jnp.mean(scaled * normed, axis=-1, keepdims=True)
    )
    out_low = out_grad.astype(jnp.bfloat16)
    shrinkbias_grad = jnp.sum(out_low.astype(jnp.float32), axis=2)
    shrink_grad = jnp.einsum("gknh,gkno->gkho", active, out_low, preferred_element_type=jnp.float32)
    act_grad = jnp.einsum(
        "gkno,gkho->gknh",
        out_low,
        shrink.reshape(3, 2, hidden, hidden),
        preferred_element_type=jnp.float32,
    )
    pre_low = (act_grad * silu_slope(preact)).astype(jnp.bfloat16)
    expbias_grad = jnp.sum(pre_low.astype(jnp.float32), axis=2)
    expand_w = expand.reshape(3, 2, in_width, hidden)
    if level_first:
        expand_grad = jnp.einsum(
            "nd,gknh->gkdh", inputs, pre_low, preferred_element_type=jnp.float32
        )
        input_grad = jnp.einsum(
            "gknh,gkdh->nd", pre_low, expand_w, preferred_element_type=jnp.float32
        )
    else:
        expand_grad = jnp.einsum(
            "gnd,gknh->gkdh", inputs, pre_low, preferred_element_type=jnp.float32
        )
        input_grad = jnp.einsum(
            "gknh,gkdh->gnd", pre_low, expand_w, preferred_element_type=jnp.float32
        )
    weight_grads = (
        expand_grad.reshape(6 * in_width, hidden),
        expbias_grad.reshape(-1),
        shrink_grad.reshape(6 * hidden, hidden),
        shrinkbias_grad.reshape(-1),
        gain_grad.reshape(-1),
    )
    return (weight_grads, input_grad)


def gate_forward(inputs, gate_w):
    scores = jnp.einsum("nd,dk->kn", inputs, gate_w, preferred_element_type=jnp.float32)
    return jax.nn.softmax(scores, axis=0)


def mix_forward(task_probs, pieces):
    return jnp.sum(task_probs[:, :, None] * pieces, axis=0)


def mix_backward(task_probs, pieces, upstream):
    piece_grad = task_probs[:, :, None] * upstream[None]
    prob_grad = jnp.sum(pieces * upstream[None], axis=-1)
    score_grad = task_probs * (prob_grad - jnp.sum(task_probs * prob_grad, axis=0, keepdims=True))
    return (piece_grad, score_grad.astype(jnp.bfloat16))


def pack_rows(parts, row_tile):
    width = 256
    wide = [part for part in parts if part.ndim == 2 and part.shape[1] == width]
    thin = [part.reshape(-1) for part in parts if part.ndim != 2 or part.shape[1] != width]
    rest = jnp.concatenate(thin)
    rest = jnp.pad(rest, (0, -rest.size % (row_tile * width))).reshape(-1, width)
    return jnp.concatenate(wide + [rest], axis=0)


def unpack_rows(whole, parts):
    devices, rows, width = whole.shape
    wide_rows = sum(part.shape[0] for part in parts if part.ndim == 2 and part.shape[1] == width)
    rest = whole[:, wide_rows:].reshape(devices, -1)
    out = []
    row = 0
    place = 0
    for part in parts:
        if part.ndim == 2 and part.shape[1] == width:
            piece = whole[:, row : row + part.shape[0]]
            row += part.shape[0]
        else:
            piece = rest[:, place : place + part.size]
            place += part.size
        out.append(piece.reshape((devices * part.shape[0],) + part.shape[1:]))
    return out


def on_device(
    owner_ids,
    row_ids,
    embed_table,
    expandone,
    expbiasone,
    reduceone,
    redbiasone,
    normgainone,
    taskgateone,
    sharegateone,
    expandtwo,
    expbiastwo,
    reducetwo,
    redbiastwo,
    normgaintwo,
    taskgatetwo,
    towerinner,
    towerbias,
    towermiddle,
    towertail,
    logit_cot,
):
    devices = lax.axis_size(("dp", "fsdp"))
    events, fields = owner_ids.shape
    emb_width = embed_table.shape[1]
    capacity = 2 * events * fields // devices
    owner_flat = owner_ids.reshape(-1)
    owner_hits = (owner_flat[:, None] == jnp.arange(devices, dtype=jnp.int32)[None, :]).astype(
        jnp.int32
    )
    slot_rank = jnp.sum((jnp.cumsum(owner_hits, axis=0) - 1) * owner_hits, axis=1)
    position = owner_flat * capacity + slot_rank
    request = (
        jnp.zeros((devices * capacity,), jnp.int32)
        .at[position]
        .set(row_ids.reshape(-1))
        .reshape(devices, capacity)
    )
    asked_rows = lax.all_to_all(request, ("dp", "fsdp"), split_axis=0, concat_axis=0, tiled=True)
    found_rows = jnp.take(embed_table, asked_rows.reshape(-1), axis=0).reshape(
        devices, capacity, emb_width
    )
    returned = lax.all_to_all(found_rows, ("dp", "fsdp"), split_axis=0, concat_axis=0, tiled=True)
    features = jnp.take(returned.reshape(-1, emb_width), position, axis=0).reshape(
        events, fields * emb_width
    )
    packed = pack_rows(
        (
            expandone,
            reduceone,
            expandtwo,
            reducetwo,
            expbiasone,
            redbiasone,
            normgainone,
            expbiastwo,
            redbiastwo,
            normgaintwo,
            taskgateone,
            sharegateone,
            taskgatetwo,
            towerinner,
            towerbias,
            towermiddle,
            towertail,
        ),
        16,
    )
    whole = lax.all_gather(packed, "fsdp", axis=0, tiled=False)
    whole = lax.all_gather(whole, "dp", axis=0, tiled=False)
    whole = whole.reshape((devices,) + packed.shape)
    (
        one_expand,
        one_shrink,
        two_expand,
        two_shrink,
        one_inbias,
        one_outbias,
        one_gain,
        two_inbias,
        two_outbias,
        two_gain,
        one_taskgate,
        one_sharegate,
        two_taskgate,
        inner_full,
        tbias_full,
        middle_full,
        tail_full,
    ) = unpack_rows(
        whole,
        (
            expandone,
            reduceone,
            expandtwo,
            reducetwo,
            expbiasone,
            redbiasone,
            normgainone,
            expbiastwo,
            redbiastwo,
            normgaintwo,
            taskgateone,
            sharegateone,
            taskgatetwo,
            towerinner,
            towerbias,
            towermiddle,
            towertail,
        ),
    )
    in_width = features.shape[1]
    hidden = one_shrink.shape[1]
    first_out, first_saved = expert_forward(
        features, "nd,gkdh->gknh", one_expand, one_inbias, one_shrink, one_outbias, one_gain
    )
    lower_gates = one_taskgate.reshape(2, in_width, 4)
    first_probs = [gate_forward(features, lower_gates[task_index]) for task_index in range(2)]
    shared_probs = gate_forward(features, one_sharegate)
    first_pieces = [
        jnp.concatenate([first_out[task_index], first_out[2]], axis=0) for task_index in range(2)
    ]
    first_flat = first_out.reshape(6, events, hidden)
    carried = jnp.stack(
        [
            mix_forward(first_probs[0], first_pieces[0]),
            mix_forward(first_probs[1], first_pieces[1]),
            mix_forward(shared_probs, first_flat),
        ]
    ).astype(jnp.bfloat16)
    second_out, second_saved = expert_forward(
        carried, "gnd,gkdh->gknh", two_expand, two_inbias, two_shrink, two_outbias, two_gain
    )
    upper_gates = two_taskgate.reshape(2, hidden, 4)
    second_probs = [
        gate_forward(carried[task_index], upper_gates[task_index]) for task_index in range(2)
    ]
    second_pieces = [
        jnp.concatenate([second_out[task_index], second_out[2]], axis=0) for task_index in range(2)
    ]
    tower_input = jnp.stack(
        [
            mix_forward(second_probs[task_index], second_pieces[task_index])
            for task_index in range(2)
        ]
    ).astype(jnp.bfloat16)
    inner_w = inner_full.reshape(2, hidden, -1)
    first_tower = jnp.einsum(
        "tnd,tdh->tnh", tower_input, inner_w, preferred_element_type=jnp.float32
    ) + tbias_full.astype(jnp.float32).reshape(2, 1, -1)
    tower_act = jax.nn.silu(first_tower).astype(jnp.bfloat16)
    middle_w = middle_full.reshape(2, inner_w.shape[2], -1)
    narrow = middle_w.shape[2]
    tail_parts = tail_full.astype(jnp.float32).reshape(2, 2, narrow)
    second_tower = (
        jnp.einsum("tnh,thk->tkn", tower_act, middle_w, preferred_element_type=jnp.float32)
        + tail_parts[:, 0, :, None]
    )
    tower_top = jax.nn.silu(second_tower)
    logits = jnp.sum(tower_top * tail_parts[:, 1, :, None], axis=1)
    top_grad = (
        logit_cot[:, None, :] * tail_parts[:, 1, :, None] * silu_slope(second_tower)
    ).astype(jnp.bfloat16)
    tail_grad = jnp.stack(
        [
            jnp.sum(top_grad.astype(jnp.float32), axis=2),
            jnp.sum(tower_top * logit_cot[:, None, :], axis=2),
        ],
        axis=1,
    ).reshape(-1)
    middle_grad = jnp.einsum(
        "tnh,tkn->thk", tower_act, top_grad, preferred_element_type=jnp.float32
    ).reshape(-1, narrow)
    tower_act_grad = jnp.einsum(
        "tkn,thk->tnh", top_grad, middle_w, preferred_element_type=jnp.float32
    )
    first_grad = (tower_act_grad * silu_slope(first_tower)).astype(jnp.bfloat16)
    tbias_grad = jnp.sum(first_grad.astype(jnp.float32), axis=1).reshape(-1)
    inner_grad = jnp.einsum(
        "tnd,tnh->tdh", tower_input, first_grad, preferred_element_type=jnp.float32
    ).reshape(-1, inner_w.shape[2])
    tower_in_grad = jnp.einsum(
        "tnh,tdh->tnd", first_grad, inner_w, preferred_element_type=jnp.float32
    )
    second_piece_grads = []
    two_gate_grads = []
    gate_side_grads = []
    for task_index in range(2):
        piece_grad, score_low = mix_backward(
            second_probs[task_index], second_pieces[task_index], tower_in_grad[task_index]
        )
        second_piece_grads.append(piece_grad)
        two_gate_grads.append(
            jnp.einsum(
                "nd,kn->dk", carried[task_index], score_low, preferred_element_type=jnp.float32
            )
        )
        gate_side_grads.append(
            jnp.einsum(
                "kn,dk->nd", score_low, upper_gates[task_index], preferred_element_type=jnp.float32
            )
        )
    second_upstream = jnp.stack(
        [
            second_piece_grads[0][:2],
            second_piece_grads[1][:2],
            second_piece_grads[0][2:] + second_piece_grads[1][2:],
        ]
    )
    second_grads, second_in_grad = expert_backward(
        carried, False, two_expand, two_shrink, two_gain, second_saved, second_upstream
    )
    carried_total = second_in_grad + jnp.stack(
        [gate_side_grads[0], gate_side_grads[1], jnp.zeros_like(gate_side_grads[0])]
    )
    up_expand, up_inbias, up_shrink, up_outbias, up_gain = second_grads
    up_taskgate = jnp.concatenate(two_gate_grads, axis=0)
    first_piece_grads = []
    one_gate_grads = []
    feature_grad = jnp.zeros((events, in_width), jnp.float32)
    for task_index in range(2):
        piece_grad, score_low = mix_backward(
            first_probs[task_index], first_pieces[task_index], carried_total[task_index]
        )
        first_piece_grads.append(piece_grad)
        one_gate_grads.append(
            jnp.einsum("nd,kn->dk", features, score_low, preferred_element_type=jnp.float32)
        )
        feature_grad = feature_grad + jnp.einsum(
            "kn,dk->nd", score_low, lower_gates[task_index], preferred_element_type=jnp.float32
        )
    shared_piece_grad, shared_low = mix_backward(shared_probs, first_flat, carried_total[2])
    low_sharegate = jnp.einsum(
        "nd,kn->dk", features, shared_low, preferred_element_type=jnp.float32
    )
    feature_grad = feature_grad + jnp.einsum(
        "kn,dk->nd", shared_low, one_sharegate, preferred_element_type=jnp.float32
    )
    first_upstream = shared_piece_grad.reshape(3, 2, events, hidden) + jnp.stack(
        [
            first_piece_grads[0][:2],
            first_piece_grads[1][:2],
            first_piece_grads[0][2:] + first_piece_grads[1][2:],
        ]
    )
    first_grads, expert_feature_grad = expert_backward(
        features, True, one_expand, one_shrink, one_gain, first_saved, first_upstream
    )
    x_grad = expert_feature_grad + feature_grad
    low_expand, low_inbias, low_shrink, low_outbias, low_gain = first_grads
    low_taskgate = jnp.concatenate(one_gate_grads, axis=0)
    outgoing = (
        jnp.zeros((devices * capacity, emb_width), jnp.float32)
        .at[position]
        .set(x_grad.reshape(-1, emb_width))
        .reshape(devices, capacity, emb_width)
    )
    incoming = lax.all_to_all(
        outgoing.astype(jnp.bfloat16), ("dp", "fsdp"), split_axis=0, concat_axis=0, tiled=True
    ).astype(outgoing.dtype)
    table_grad = (
        jnp.zeros((embed_table.shape[0], emb_width), jnp.float32)
        .at[asked_rows.reshape(-1)]
        .add(incoming.reshape(-1, emb_width))
    )
    grads = (
        low_expand,
        low_inbias,
        low_shrink,
        low_outbias,
        low_gain,
        low_taskgate,
        low_sharegate,
        up_expand,
        up_inbias,
        up_shrink,
        up_outbias,
        up_gain,
        up_taskgate,
        inner_grad,
        tbias_grad,
        middle_grad,
        tail_grad,
    )
    sizes = [grad.size for grad in grads]
    width = one_shrink.shape[1]
    chunk = 16 * devices * width
    flat = jnp.concatenate([grad.astype(jnp.bfloat16).reshape(-1) for grad in grads])
    flat = jnp.pad(flat, (0, -flat.size % chunk)).reshape(-1, width)
    part = lax.psum_scatter(flat, "dp", scatter_dimension=0, tiled=True)
    part = lax.psum_scatter(part, "fsdp", scatter_dimension=0, tiled=True)
    total = lax.all_gather(part, "fsdp", axis=0, tiled=True)
    total = lax.all_gather(total, "dp", axis=0, tiled=True).reshape(-1)
    done = []
    start = 0
    for grad, size in zip(grads, sizes):
        done.append(total[start : start + size].reshape(grad.shape).astype(jnp.float32))
        start += size
    return (logits, x_grad, table_grad, *done)


def solution(mesh):
    return jax.shard_map(
        on_device,
        mesh=mesh,
        in_specs=(
            P(("dp", "fsdp"), None),
            P(("dp", "fsdp"), None),
            P(("dp", "fsdp"), None),
            P(("dp", "fsdp"), None),
            P(("dp", "fsdp")),
            P(("dp", "fsdp"), None),
            P(("dp", "fsdp")),
            P(("dp", "fsdp")),
            P(("dp", "fsdp"), None),
            P(("dp", "fsdp"), None),
            P(("dp", "fsdp"), None),
            P(("dp", "fsdp")),
            P(("dp", "fsdp"), None),
            P(("dp", "fsdp")),
            P(("dp", "fsdp")),
            P(("dp", "fsdp"), None),
            P(("dp", "fsdp"), None),
            P(("dp", "fsdp")),
            P(("dp", "fsdp"), None),
            P(("dp", "fsdp")),
            P(None, ("dp", "fsdp")),
        ),
        out_specs=(
            P(None, ("dp", "fsdp")),
            P(("dp", "fsdp"), None),
            P(("dp", "fsdp"), None),
            P(),
            P(),
            P(),
            P(),
            P(),
            P(),
            P(),
            P(),
            P(),
            P(),
            P(),
            P(),
            P(),
            P(),
            P(),
            P(),
            P(),
        ),
        check_vma=False,
    )
```

```python
import jax
import jax.numpy as jnp
from jax import lax
from jax.experimental import pallas as pl
from jax.experimental.pallas import tpu as pltpu
from jax.sharding import PartitionSpec as P

EPS = 1e-05
VMEM_LIMIT = 56 * 1024 * 1024
ROW_BLOCKS = 8


def silu_slope(values):
    sigmoid_v = jax.nn.sigmoid(values)
    return sigmoid_v * (1.0 + values * (1.0 - sigmoid_v))


def expert_forward(inputs, pattern, expand, expbias, shrink, shrinkbias, gain_w):
    hidden = shrink.shape[1]
    in_width = expand.shape[0] // 6
    expand_w = expand.reshape(3, 2, in_width, hidden)
    preact = jnp.einsum(
        pattern, inputs, expand_w, preferred_element_type=jnp.float32
    ) + expbias.astype(jnp.float32).reshape(3, 2, 1, hidden)
    active = jax.nn.silu(preact).astype(jnp.bfloat16)
    output = jnp.einsum(
        "gknh,gkho->gkno",
        active,
        shrink.reshape(3, 2, hidden, hidden),
        preferred_element_type=jnp.float32,
    ) + shrinkbias.astype(jnp.float32).reshape(3, 2, 1, hidden)
    centered = output - jnp.mean(output, axis=-1, keepdims=True)
    inverse = lax.rsqrt(jnp.mean(centered * centered, axis=-1, keepdims=True) + EPS)
    normed = centered * inverse
    result = normed * gain_w.astype(jnp.float32).reshape(3, 2, 1, hidden)
    return (result, (preact, active, normed, inverse))


def expert_backward(inputs, level_first, expand, shrink, gain_w, saved_parts, upstream):
    preact, active, normed, inverse = saved_parts
    hidden = shrink.shape[1]
    in_width = expand.shape[0] // 6
    scaled = upstream * gain_w.astype(jnp.float32).reshape(3, 2, 1, hidden)
    gain_grad = jnp.sum(upstream * normed, axis=2)
    out_grad = inverse * (
        scaled
        - jnp.mean(scaled, axis=-1, keepdims=True)
        - normed * jnp.mean(scaled * normed, axis=-1, keepdims=True)
    )
    out_low = out_grad.astype(jnp.bfloat16)
    shrinkbias_grad = jnp.sum(out_low.astype(jnp.float32), axis=2)
    shrink_grad = jnp.einsum("gknh,gkno->gkho", active, out_low, preferred_element_type=jnp.float32)
    act_grad = jnp.einsum(
        "gkno,gkho->gknh",
        out_low,
        shrink.reshape(3, 2, hidden, hidden),
        preferred_element_type=jnp.float32,
    )
    pre_low = (act_grad * silu_slope(preact)).astype(jnp.bfloat16)
    expbias_grad = jnp.sum(pre_low.astype(jnp.float32), axis=2)
    expand_w = expand.reshape(3, 2, in_width, hidden)
    if level_first:
        expand_grad = jnp.einsum(
            "nd,gknh->gkdh", inputs, pre_low, preferred_element_type=jnp.float32
        )
        input_grad = jnp.einsum(
            "gknh,gkdh->nd", pre_low, expand_w, preferred_element_type=jnp.float32
        )
    else:
        expand_grad = jnp.einsum(
            "gnd,gknh->gkdh", inputs, pre_low, preferred_element_type=jnp.float32
        )
        input_grad = jnp.einsum(
            "gknh,gkdh->gnd", pre_low, expand_w, preferred_element_type=jnp.float32
        )
    weight_grads = (
        expand_grad.reshape(6 * in_width, hidden),
        expbias_grad.reshape(-1),
        shrink_grad.reshape(6 * hidden, hidden),
        shrinkbias_grad.reshape(-1),
        gain_grad.reshape(-1),
    )
    return (weight_grads, input_grad)


def gate_forward(inputs, gate_w):
    scores = jnp.einsum("nd,dk->kn", inputs, gate_w, preferred_element_type=jnp.float32)
    return jax.nn.softmax(scores, axis=0)


def mix_forward(task_probs, pieces):
    return jnp.sum(task_probs[:, :, None] * pieces, axis=0)


def mix_backward(task_probs, pieces, upstream):
    piece_grad = task_probs[:, :, None] * upstream[None]
    prob_grad = jnp.sum(pieces * upstream[None], axis=-1)
    score_grad = task_probs * (prob_grad - jnp.sum(task_probs * prob_grad, axis=0, keepdims=True))
    return (piece_grad, score_grad.astype(jnp.bfloat16))


def local_kernel(body, out_shape, flops, moved, scratch=()):
    return pl.pallas_call(
        body,
        out_shape=out_shape,
        scratch_shapes=list(scratch),
        compiler_params=pltpu.CompilerParams(vmem_limit_bytes=VMEM_LIMIT),
        cost_estimate=pl.CostEstimate(flops=flops, bytes_accessed=moved, transcendentals=0),
    )


def one_hot(hit):
    return jnp.where(hit, 1.0, 0.0).astype(jnp.bfloat16)


def iota(shape, axis):
    return lax.broadcasted_iota(jnp.int32, shape, axis)


def slot_body(owner_ref, row_ref, request_ref, rank_ref):
    fields, events = owner_ref.shape
    devices, capacity = request_ref.shape
    place = iota((devices, events), 0)
    asked = jnp.zeros((devices, events), jnp.float32)
    for field in range(fields):
        asked = asked + jnp.where(owner_ref[field : field + 1, :] == place, 1.0, 0.0)
    earlier = one_hot(iota((events, events), 0) < iota((events, events), 1))
    rank = jnp.dot(asked.astype(jnp.bfloat16), earlier, preferred_element_type=jnp.float32)
    rank = jnp.where(asked > 0.5, rank.astype(jnp.int32), -1)
    rank_ref[...] = rank
    slots = iota((capacity, events), 0)
    total = jnp.zeros((2 * devices, capacity), jnp.float32)
    for field in range(fields):
        mine = owner_ref[field : field + 1, :] == place
        field_rank = jnp.max(jnp.where(mine, rank, -1).astype(jnp.float32), axis=0, keepdims=True)
        rows = row_ref[field : field + 1, :]
        high = jnp.where(mine, (rows >> 6).astype(jnp.float32), 0.0)
        low = jnp.where(mine, (rows & 63).astype(jnp.float32), 0.0)
        value = jnp.concatenate([high, low], axis=0).astype(jnp.bfloat16)
        total = total + lax.dot_general(
            value,
            one_hot(field_rank.astype(jnp.int32) == slots),
            (((1,), (1,)), ((), ())),
            preferred_element_type=jnp.float32,
        )
    request_ref[...] = (total[:devices] * 64.0 + total[devices:]).astype(jnp.int32)


def assign_slots(owner_rows, row_rows, devices, capacity):
    fields, events = owner_rows.shape
    return local_kernel(
        slot_body,
        (
            jax.ShapeDtypeStruct((devices, capacity), jnp.int32),
            jax.ShapeDtypeStruct((devices, events), jnp.int32),
        ),
        2 * devices * events * (events + 2 * fields * capacity),
        4 * events * (2 * fields + devices),
    )(owner_rows, row_rows)


def find_body(request_ref, table_ref, found_ref):
    devices, capacity = request_ref.shape
    depth, span = table_ref.shape
    width = depth // ROW_BLOCKS
    places = iota((span, capacity), 0)

    def step(source, carry):
        rows = request_ref[pl.ds(source, 1), :]
        block = rows // span
        hits = one_hot(rows - block * span == places)
        rows_all = jnp.dot(table_ref[...], hits, preferred_element_type=jnp.float32)
        picked = jnp.zeros((width, capacity), jnp.float32)
        for index in range(ROW_BLOCKS):
            picked = jnp.where(
                block == index, rows_all[index * width : (index + 1) * width, :], picked
            )
        found_ref[source] = picked.astype(jnp.bfloat16)
        return carry

    lax.fori_loop(0, devices, step, 0, unroll=2)


def find_rows(request, table_wide):
    devices, capacity = request.shape
    depth, span = table_wide.shape
    return local_kernel(
        find_body,
        jax.ShapeDtypeStruct((devices, depth // ROW_BLOCKS, capacity), jnp.bfloat16),
        2 * devices * capacity * depth * span,
        2 * (depth * span + devices * capacity * depth // ROW_BLOCKS),
    )(request, table_wide)


def place_body(found_ref, rank_ref, owner_ref, flipped_ref, total_ref):
    devices, width, capacity = found_ref.shape
    fields, events = owner_ref.shape
    slots = iota((capacity, events), 0)
    group = 4
    total_ref[...] = jnp.zeros_like(total_ref)

    def step(start, carry):
        pieces = []
        for index in range(group):
            owner = start * group + index
            hits = one_hot(rank_ref[pl.ds(owner, 1), :] == slots)
            pieces.append(jnp.dot(found_ref[owner], hits, preferred_element_type=jnp.float32))
        for field in range(fields):
            rows = slice(field * width, (field + 1) * width)
            owners = owner_ref[field : field + 1, :]
            value = total_ref[rows, :]
            for index in range(group):
                value = jnp.where(owners == start * group + index, pieces[index], value)
            total_ref[rows, :] = value
        return carry

    lax.fori_loop(0, devices // group, step, 0)
    flipped_ref[...] = total_ref[...].astype(jnp.bfloat16)


def place_rows(found, rank, owner_rows):
    devices, width, capacity = found.shape
    fields, events = owner_rows.shape
    return local_kernel(
        place_body,
        jax.ShapeDtypeStruct((fields * width, events), jnp.bfloat16),
        2 * devices * width * capacity * events,
        2 * (devices * width * capacity + fields * width * events),
        [pltpu.VMEM((fields * width, events), jnp.float32)],
    )(found, rank, owner_rows)


def send_body(grad_ref, rank_ref, owner_ref, sent_ref, low_ref):
    devices, width, capacity = sent_ref.shape
    fields, events = owner_ref.shape
    slots = iota((capacity, events), 0)
    low_ref[...] = grad_ref[...].astype(jnp.bfloat16).astype(jnp.float32).T

    def step(owner, carry):
        chosen = jnp.zeros((width, events), jnp.float32)
        for field in range(fields):
            rows = slice(field * width, (field + 1) * width)
            chosen = jnp.where(owner_ref[field : field + 1, :] == owner, low_ref[rows, :], chosen)
        hits = one_hot(rank_ref[pl.ds(owner, 1), :] == slots)
        sent_ref[owner] = lax.dot_general(
            chosen.astype(jnp.bfloat16),
            hits,
            (((1,), (1,)), ((), ())),
            preferred_element_type=jnp.float32,
        ).astype(jnp.bfloat16)
        return carry

    lax.fori_loop(0, devices, step, 0, unroll=2)


def send_rows(grad, rank, owner_rows, capacity):
    devices = rank.shape[0]
    fields, events = owner_rows.shape
    width = grad.shape[1] // fields
    return local_kernel(
        send_body,
        jax.ShapeDtypeStruct((devices, width, capacity), jnp.bfloat16),
        2 * devices * width * capacity * events,
        2 * (devices * width * capacity + 2 * fields * width * events),
        [pltpu.VMEM((fields * width, events), jnp.float32)],
    )(grad, rank, owner_rows)


def add_body(came_ref, request_ref, out_ref, total_ref):
    devices, width, capacity = came_ref.shape
    span = total_ref.shape[0]
    group = 4
    places = iota((span, capacity), 0)
    total_ref[...] = jnp.zeros_like(total_ref)

    def step(start, carry):
        hits = []
        spread = []
        for index in range(group):
            source = start * group + index
            rows = request_ref[pl.ds(source, 1), :]
            block = rows // span
            hits.append(one_hot(rows - block * span == places))
            came = came_ref[source].astype(jnp.float32)
            spread.append(
                jnp.concatenate(
                    [jnp.where(block == place, came, 0.0) for place in range(ROW_BLOCKS)], axis=0
                ).astype(jnp.bfloat16)
            )
        total_ref[...] += lax.dot_general(
            jnp.concatenate(hits, axis=1),
            jnp.concatenate(spread, axis=1),
            (((1,), (1,)), ((), ())),
            preferred_element_type=jnp.float32,
        )
        return carry

    lax.fori_loop(0, devices // group, step, 0)
    for index in range(ROW_BLOCKS):
        out_ref[index * span : (index + 1) * span, :] = total_ref[
            :, index * width : (index + 1) * width
        ]


def add_rows(came, request, rows):
    devices, width, capacity = came.shape
    span = rows // ROW_BLOCKS
    return local_kernel(
        add_body,
        jax.ShapeDtypeStruct((rows, width), jnp.float32),
        2 * devices * capacity * rows * width,
        2 * devices * width * capacity + 4 * rows * width,
        [pltpu.VMEM((span, ROW_BLOCKS * width), jnp.float32)],
    )(came, request)


def pack_rows(parts, row_tile):
    width = 256
    wide = [part for part in parts if part.ndim == 2 and part.shape[1] == width]
    thin = [part.reshape(-1) for part in parts if part.ndim != 2 or part.shape[1] != width]
    rest = jnp.concatenate(thin)
    rest = jnp.pad(rest, (0, -rest.size % (row_tile * width))).reshape(-1, width)
    return jnp.concatenate(wide + [rest], axis=0)


def unpack_rows(whole, parts):
    devices, rows, width = whole.shape
    wide_rows = sum(part.shape[0] for part in parts if part.ndim == 2 and part.shape[1] == width)
    rest = whole[:, wide_rows:].reshape(devices, -1)
    out = []
    row = 0
    place = 0
    for part in parts:
        if part.ndim == 2 and part.shape[1] == width:
            piece = whole[:, row : row + part.shape[0]]
            row += part.shape[0]
        else:
            piece = rest[:, place : place + part.size]
            place += part.size
        out.append(piece.reshape((devices * part.shape[0],) + part.shape[1:]))
    return out


def on_device(
    owner_ids,
    row_ids,
    embed_table,
    expandone,
    expbiasone,
    reduceone,
    redbiasone,
    normgainone,
    taskgateone,
    sharegateone,
    expandtwo,
    expbiastwo,
    reducetwo,
    redbiastwo,
    normgaintwo,
    taskgatetwo,
    towerinner,
    towerbias,
    towermiddle,
    towertail,
    logit_cot,
):
    devices = lax.axis_size(("dp", "fsdp"))
    events, fields = owner_ids.shape
    emb_width = embed_table.shape[1]
    capacity = 2 * events * fields // devices
    owner_rows = owner_ids.T
    request, rank = assign_slots(owner_rows, row_ids.T, devices, capacity)
    asked_rows = lax.all_to_all(request, ("dp", "fsdp"), split_axis=0, concat_axis=0, tiled=True)
    table_wide = (
        embed_table.reshape(ROW_BLOCKS, -1, emb_width).transpose(0, 2, 1).reshape(ROW_BLOCKS * emb_width, -1)
    )
    found = find_rows(asked_rows, table_wide)
    returned = lax.all_to_all(found, ("dp", "fsdp"), split_axis=0, concat_axis=0, tiled=True)
    features = place_rows(returned, rank, owner_rows).T
    packed = pack_rows(
        (
            expandone,
            reduceone,
            expandtwo,
            reducetwo,
            expbiasone,
            redbiasone,
            normgainone,
            expbiastwo,
            redbiastwo,
            normgaintwo,
            taskgateone,
            sharegateone,
            taskgatetwo,
            towerinner,
            towerbias,
            towermiddle,
            towertail,
        ),
        16,
    )
    whole = lax.all_gather(packed, "fsdp", axis=0, tiled=False)
    whole = lax.all_gather(whole, "dp", axis=0, tiled=False)
    whole = whole.reshape((devices,) + packed.shape)
    (
        one_expand,
        one_shrink,
        two_expand,
        two_shrink,
        one_inbias,
        one_outbias,
        one_gain,
        two_inbias,
        two_outbias,
        two_gain,
        one_taskgate,
        one_sharegate,
        two_taskgate,
        inner_full,
        tbias_full,
        middle_full,
        tail_full,
    ) = unpack_rows(
        whole,
        (
            expandone,
            reduceone,
            expandtwo,
            reducetwo,
            expbiasone,
            redbiasone,
            normgainone,
            expbiastwo,
            redbiastwo,
            normgaintwo,
            taskgateone,
            sharegateone,
            taskgatetwo,
            towerinner,
            towerbias,
            towermiddle,
            towertail,
        ),
    )
    in_width = features.shape[1]
    hidden = one_shrink.shape[1]
    first_out, first_saved = expert_forward(
        features, "nd,gkdh->gknh", one_expand, one_inbias, one_shrink, one_outbias, one_gain
    )
    lower_gates = one_taskgate.reshape(2, in_width, 4)
    first_probs = [gate_forward(features, lower_gates[task_index]) for task_index in range(2)]
    shared_probs = gate_forward(features, one_sharegate)
    first_pieces = [
        jnp.concatenate([first_out[task_index], first_out[2]], axis=0) for task_index in range(2)
    ]
    first_flat = first_out.reshape(6, events, hidden)
    carried = jnp.stack(
        [
            mix_forward(first_probs[0], first_pieces[0]),
            mix_forward(first_probs[1], first_pieces[1]),
            mix_forward(shared_probs, first_flat),
        ]
    ).astype(jnp.bfloat16)
    second_out, second_saved = expert_forward(
        carried, "gnd,gkdh->gknh", two_expand, two_inbias, two_shrink, two_outbias, two_gain
    )
    upper_gates = two_taskgate.reshape(2, hidden, 4)
    second_probs = [
        gate_forward(carried[task_index], upper_gates[task_index]) for task_index in range(2)
    ]
    second_pieces = [
        jnp.concatenate([second_out[task_index], second_out[2]], axis=0) for task_index in range(2)
    ]
    tower_input = jnp.stack(
        [
            mix_forward(second_probs[task_index], second_pieces[task_index])
            for task_index in range(2)
        ]
    ).astype(jnp.bfloat16)
    inner_w = inner_full.reshape(2, hidden, -1)
    first_tower = jnp.einsum(
        "tnd,tdh->tnh", tower_input, inner_w, preferred_element_type=jnp.float32
    ) + tbias_full.astype(jnp.float32).reshape(2, 1, -1)
    tower_act = jax.nn.silu(first_tower).astype(jnp.bfloat16)
    middle_w = middle_full.reshape(2, inner_w.shape[2], -1)
    narrow = middle_w.shape[2]
    tail_parts = tail_full.astype(jnp.float32).reshape(2, 2, narrow)
    second_tower = (
        jnp.einsum("tnh,thk->tkn", tower_act, middle_w, preferred_element_type=jnp.float32)
        + tail_parts[:, 0, :, None]
    )
    tower_top = jax.nn.silu(second_tower)
    logits = jnp.sum(tower_top * tail_parts[:, 1, :, None], axis=1)
    top_grad = (
        logit_cot[:, None, :] * tail_parts[:, 1, :, None] * silu_slope(second_tower)
    ).astype(jnp.bfloat16)
    tail_grad = jnp.stack(
        [
            jnp.sum(top_grad.astype(jnp.float32), axis=2),
            jnp.sum(tower_top * logit_cot[:, None, :], axis=2),
        ],
        axis=1,
    ).reshape(-1)
    middle_grad = jnp.einsum(
        "tnh,tkn->thk", tower_act, top_grad, preferred_element_type=jnp.float32
    ).reshape(-1, narrow)
    tower_act_grad = jnp.einsum(
        "tkn,thk->tnh", top_grad, middle_w, preferred_element_type=jnp.float32
    )
    first_grad = (tower_act_grad * silu_slope(first_tower)).astype(jnp.bfloat16)
    tbias_grad = jnp.sum(first_grad.astype(jnp.float32), axis=1).reshape(-1)
    inner_grad = jnp.einsum(
        "tnd,tnh->tdh", tower_input, first_grad, preferred_element_type=jnp.float32
    ).reshape(-1, inner_w.shape[2])
    tower_in_grad = jnp.einsum(
        "tnh,tdh->tnd", first_grad, inner_w, preferred_element_type=jnp.float32
    )
    second_piece_grads = []
    two_gate_grads = []
    gate_side_grads = []
    for task_index in range(2):
        piece_grad, score_low = mix_backward(
            second_probs[task_index], second_pieces[task_index], tower_in_grad[task_index]
        )
        second_piece_grads.append(piece_grad)
        two_gate_grads.append(
            jnp.einsum(
                "nd,kn->dk", carried[task_index], score_low, preferred_element_type=jnp.float32
            )
        )
        gate_side_grads.append(
            jnp.einsum(
                "kn,dk->nd", score_low, upper_gates[task_index], preferred_element_type=jnp.float32
            )
        )
    second_upstream = jnp.stack(
        [
            second_piece_grads[0][:2],
            second_piece_grads[1][:2],
            second_piece_grads[0][2:] + second_piece_grads[1][2:],
        ]
    )
    second_grads, second_in_grad = expert_backward(
        carried, False, two_expand, two_shrink, two_gain, second_saved, second_upstream
    )
    carried_total = second_in_grad + jnp.stack(
        [gate_side_grads[0], gate_side_grads[1], jnp.zeros_like(gate_side_grads[0])]
    )
    up_expand, up_inbias, up_shrink, up_outbias, up_gain = second_grads
    up_taskgate = jnp.concatenate(two_gate_grads, axis=0)
    first_piece_grads = []
    one_gate_grads = []
    feature_grad = jnp.zeros((events, in_width), jnp.float32)
    for task_index in range(2):
        piece_grad, score_low = mix_backward(
            first_probs[task_index], first_pieces[task_index], carried_total[task_index]
        )
        first_piece_grads.append(piece_grad)
        one_gate_grads.append(
            jnp.einsum("nd,kn->dk", features, score_low, preferred_element_type=jnp.float32)
        )
        feature_grad = feature_grad + jnp.einsum(
            "kn,dk->nd", score_low, lower_gates[task_index], preferred_element_type=jnp.float32
        )
    shared_piece_grad, shared_low = mix_backward(shared_probs, first_flat, carried_total[2])
    low_sharegate = jnp.einsum(
        "nd,kn->dk", features, shared_low, preferred_element_type=jnp.float32
    )
    feature_grad = feature_grad + jnp.einsum(
        "kn,dk->nd", shared_low, one_sharegate, preferred_element_type=jnp.float32
    )
    first_upstream = shared_piece_grad.reshape(3, 2, events, hidden) + jnp.stack(
        [
            first_piece_grads[0][:2],
            first_piece_grads[1][:2],
            first_piece_grads[0][2:] + first_piece_grads[1][2:],
        ]
    )
    first_grads, expert_feature_grad = expert_backward(
        features, True, one_expand, one_shrink, one_gain, first_saved, first_upstream
    )
    x_grad = expert_feature_grad + feature_grad
    low_expand, low_inbias, low_shrink, low_outbias, low_gain = first_grads
    low_taskgate = jnp.concatenate(one_gate_grads, axis=0)
    outgoing = send_rows(x_grad, rank, owner_rows, capacity)
    incoming = lax.all_to_all(
        outgoing, ("dp", "fsdp"), split_axis=0, concat_axis=0, tiled=True
    )
    table_grad = add_rows(incoming, asked_rows, embed_table.shape[0])
    grads = (
        low_expand,
        low_inbias,
        low_shrink,
        low_outbias,
        low_gain,
        low_taskgate,
        low_sharegate,
        up_expand,
        up_inbias,
        up_shrink,
        up_outbias,
        up_gain,
        up_taskgate,
        inner_grad,
        tbias_grad,
        middle_grad,
        tail_grad,
    )
    sizes = [grad.size for grad in grads]
    width = one_shrink.shape[1]
    chunk = 16 * devices * width
    flat = jnp.concatenate([grad.astype(jnp.bfloat16).reshape(-1) for grad in grads])
    flat = jnp.pad(flat, (0, -flat.size % chunk)).reshape(-1, width)
    part = lax.psum_scatter(flat, "dp", scatter_dimension=0, tiled=True)
    part = lax.psum_scatter(part, "fsdp", scatter_dimension=0, tiled=True)
    total = lax.all_gather(part, "fsdp", axis=0, tiled=True)
    total = lax.all_gather(total, "dp", axis=0, tiled=True).reshape(-1)
    done = []
    start = 0
    for grad, size in zip(grads, sizes):
        done.append(total[start : start + size].reshape(grad.shape).astype(jnp.float32))
        start += size
    return (logits, x_grad, table_grad, *done)


def solution(mesh):
    return jax.shard_map(
        on_device,
        mesh=mesh,
        in_specs=(
            P(("dp", "fsdp"), None),
            P(("dp", "fsdp"), None),
            P(("dp", "fsdp"), None),
            P(("dp", "fsdp"), None),
            P(("dp", "fsdp")),
            P(("dp", "fsdp"), None),
            P(("dp", "fsdp")),
            P(("dp", "fsdp")),
            P(("dp", "fsdp"), None),
            P(("dp", "fsdp"), None),
            P(("dp", "fsdp"), None),
            P(("dp", "fsdp")),
            P(("dp", "fsdp"), None),
            P(("dp", "fsdp")),
            P(("dp", "fsdp")),
            P(("dp", "fsdp"), None),
            P(("dp", "fsdp"), None),
            P(("dp", "fsdp")),
            P(("dp", "fsdp"), None),
            P(("dp", "fsdp")),
            P(None, ("dp", "fsdp")),
        ),
        out_specs=(
            P(None, ("dp", "fsdp")),
            P(("dp", "fsdp"), None),
            P(("dp", "fsdp"), None),
            P(),
            P(),
            P(),
            P(),
            P(),
            P(),
            P(),
            P(),
            P(),
            P(),
            P(),
            P(),
            P(),
            P(),
            P(),
            P(),
            P(),
        ),
        check_vma=False,
    )
```

```python
import jax
import jax.numpy as jnp
from jax import lax
from jax.experimental import pallas as pl
from jax.experimental.pallas import tpu as pltpu
from jax.sharding import PartitionSpec as P

EPS = 1e-05
VMEM_LIMIT = 56 * 1024 * 1024
ROW_BLOCKS = 8


def local_kernel(body, out_shape, flops, moved, scratch=()):
    return pl.pallas_call(
        body,
        out_shape=out_shape,
        scratch_shapes=list(scratch),
        compiler_params=pltpu.CompilerParams(vmem_limit_bytes=VMEM_LIMIT),
        cost_estimate=pl.CostEstimate(flops=flops, bytes_accessed=moved, transcendentals=0),
    )


def one_hot(hit):
    return jnp.where(hit, 1.0, 0.0).astype(jnp.bfloat16)


def iota(shape, axis):
    return lax.broadcasted_iota(jnp.int32, shape, axis)


def slot_body(owner_ref, row_ref, request_ref, rank_ref):
    fields, events = owner_ref.shape
    devices, capacity = request_ref.shape
    place = iota((devices, events), 0)
    asked = jnp.zeros((devices, events), jnp.float32)
    for field in range(fields):
        asked = asked + jnp.where(owner_ref[field : field + 1, :] == place, 1.0, 0.0)
    earlier = one_hot(iota((events, events), 0) < iota((events, events), 1))
    rank = jnp.dot(asked.astype(jnp.bfloat16), earlier, preferred_element_type=jnp.float32)
    rank = jnp.where(asked > 0.5, rank.astype(jnp.int32), -1)
    rank_ref[...] = rank
    slots = iota((capacity, events), 0)
    total = jnp.zeros((2 * devices, capacity), jnp.float32)
    for field in range(fields):
        mine = owner_ref[field : field + 1, :] == place
        field_rank = jnp.max(jnp.where(mine, rank, -1).astype(jnp.float32), axis=0, keepdims=True)
        rows = row_ref[field : field + 1, :]
        high = jnp.where(mine, (rows >> 6).astype(jnp.float32), 0.0)
        low = jnp.where(mine, (rows & 63).astype(jnp.float32), 0.0)
        value = jnp.concatenate([high, low], axis=0).astype(jnp.bfloat16)
        total = total + lax.dot_general(
            value,
            one_hot(field_rank.astype(jnp.int32) == slots),
            (((1,), (1,)), ((), ())),
            preferred_element_type=jnp.float32,
        )
    request_ref[...] = (total[:devices] * 64.0 + total[devices:]).astype(jnp.int32)


def assign_slots(owner_rows, row_rows, devices, capacity):
    fields, events = owner_rows.shape
    return local_kernel(
        slot_body,
        (
            jax.ShapeDtypeStruct((devices, capacity), jnp.int32),
            jax.ShapeDtypeStruct((devices, events), jnp.int32),
        ),
        2 * devices * events * (events + 2 * fields * capacity),
        4 * events * (2 * fields + devices),
    )(owner_rows, row_rows)


def find_body(request_ref, table_ref, found_ref):
    devices, capacity = request_ref.shape
    depth, span = table_ref.shape
    width = depth // ROW_BLOCKS
    places = iota((span, capacity), 0)

    def step(source, carry):
        rows = request_ref[pl.ds(source, 1), :]
        block = rows // span
        hits = one_hot(rows - block * span == places)
        rows_all = jnp.dot(table_ref[...], hits, preferred_element_type=jnp.float32)
        picked = jnp.zeros((width, capacity), jnp.float32)
        for index in range(ROW_BLOCKS):
            picked = jnp.where(
                block == index, rows_all[index * width : (index + 1) * width, :], picked
            )
        found_ref[source] = picked.astype(jnp.bfloat16)
        return carry

    lax.fori_loop(0, devices, step, 0, unroll=2)


def find_rows(request, table_wide):
    devices, capacity = request.shape
    depth, span = table_wide.shape
    return local_kernel(
        find_body,
        jax.ShapeDtypeStruct((devices, depth // ROW_BLOCKS, capacity), jnp.bfloat16),
        2 * devices * capacity * depth * span,
        2 * (depth * span + devices * capacity * depth // ROW_BLOCKS),
    )(request, table_wide)


def place_body(found_ref, rank_ref, owner_ref, flipped_ref, total_ref):
    devices, width, capacity = found_ref.shape
    fields, events = owner_ref.shape
    slots = iota((capacity, events), 0)
    group = 4
    total_ref[...] = jnp.zeros_like(total_ref)

    def step(start, carry):
        pieces = []
        for index in range(group):
            owner = start * group + index
            hits = one_hot(rank_ref[pl.ds(owner, 1), :] == slots)
            pieces.append(jnp.dot(found_ref[owner], hits, preferred_element_type=jnp.float32))
        for field in range(fields):
            rows = slice(field * width, (field + 1) * width)
            owners = owner_ref[field : field + 1, :]
            value = total_ref[rows, :]
            for index in range(group):
                value = jnp.where(owners == start * group + index, pieces[index], value)
            total_ref[rows, :] = value
        return carry

    lax.fori_loop(0, devices // group, step, 0)
    flipped_ref[...] = total_ref[...].astype(jnp.bfloat16)


def place_rows(found, rank, owner_rows):
    devices, width, capacity = found.shape
    fields, events = owner_rows.shape
    return local_kernel(
        place_body,
        jax.ShapeDtypeStruct((fields * width, events), jnp.bfloat16),
        2 * devices * width * capacity * events,
        2 * (devices * width * capacity + fields * width * events),
        [pltpu.VMEM((fields * width, events), jnp.float32)],
    )(found, rank, owner_rows)


def send_body(grad_ref, rank_ref, owner_ref, sent_ref, low_ref):
    devices, width, capacity = sent_ref.shape
    fields, events = owner_ref.shape
    slots = iota((capacity, events), 0)
    low_ref[...] = grad_ref[...].astype(jnp.bfloat16).astype(jnp.float32)

    def step(owner, carry):
        chosen = jnp.zeros((width, events), jnp.float32)
        for field in range(fields):
            rows = slice(field * width, (field + 1) * width)
            chosen = jnp.where(owner_ref[field : field + 1, :] == owner, low_ref[rows, :], chosen)
        hits = one_hot(rank_ref[pl.ds(owner, 1), :] == slots)
        sent_ref[owner] = lax.dot_general(
            chosen.astype(jnp.bfloat16),
            hits,
            (((1,), (1,)), ((), ())),
            preferred_element_type=jnp.float32,
        ).astype(jnp.bfloat16)
        return carry

    lax.fori_loop(0, devices, step, 0, unroll=2)


def send_rows(grad, rank, owner_rows, capacity):
    devices = rank.shape[0]
    fields, events = owner_rows.shape
    width = grad.shape[0] // fields
    return local_kernel(
        send_body,
        jax.ShapeDtypeStruct((devices, width, capacity), jnp.bfloat16),
        2 * devices * width * capacity * events,
        2 * (devices * width * capacity + 2 * fields * width * events),
        [pltpu.VMEM((fields * width, events), jnp.float32)],
    )(grad, rank, owner_rows)


def add_body(came_ref, request_ref, out_ref, total_ref):
    devices, width, capacity = came_ref.shape
    span = total_ref.shape[0]
    group = 4
    places = iota((span, capacity), 0)
    total_ref[...] = jnp.zeros_like(total_ref)

    def step(start, carry):
        hits = []
        spread = []
        for index in range(group):
            source = start * group + index
            rows = request_ref[pl.ds(source, 1), :]
            block = rows // span
            hits.append(one_hot(rows - block * span == places))
            came = came_ref[source].astype(jnp.float32)
            spread.append(
                jnp.concatenate(
                    [jnp.where(block == place, came, 0.0) for place in range(ROW_BLOCKS)], axis=0
                ).astype(jnp.bfloat16)
            )
        total_ref[...] += lax.dot_general(
            jnp.concatenate(hits, axis=1),
            jnp.concatenate(spread, axis=1),
            (((1,), (1,)), ((), ())),
            preferred_element_type=jnp.float32,
        )
        return carry

    lax.fori_loop(0, devices // group, step, 0)
    for index in range(ROW_BLOCKS):
        out_ref[index * span : (index + 1) * span, :] = total_ref[
            :, index * width : (index + 1) * width
        ]


def add_rows(came, request, rows):
    devices, width, capacity = came.shape
    span = rows // ROW_BLOCKS
    return local_kernel(
        add_body,
        jax.ShapeDtypeStruct((rows, width), jnp.float32),
        2 * devices * capacity * rows * width,
        2 * devices * width * capacity + 4 * rows * width,
        [pltpu.VMEM((span, ROW_BLOCKS * width), jnp.float32)],
    )(came, request)


SPAN = 256
ONES = 16


def over_events(left, right):
    return lax.dot_general(left, right, (((1,), (1,)), ((), ())), preferred_element_type=jnp.float32)


def times(left, right):
    return jnp.dot(left, right, preferred_element_type=jnp.float32)


def sum_rows(values):
    return jnp.sum(values, axis=0, keepdims=True)


def sigmoid_of(values):
    return 0.5 * jnp.tanh(0.5 * values) + 0.5


def silu_parts(values):
    sig = sigmoid_of(values)
    active = values * sig
    return active, sig + active * (1.0 - sig)


def expert_up(inputs, expand, expbias, shrink, shrinkbias):
    active, slope = silu_parts(times(expand, inputs) + expbias)
    active = active.astype(jnp.bfloat16)
    output = times(shrink, active) + shrinkbias
    scale = 1.0 / output.shape[0]
    centered = output - sum_rows(output) * scale
    inverse = lax.rsqrt(sum_rows(centered * centered) * scale + EPS)
    return active, slope, centered * inverse, inverse


def soft(scores, count):
    valid = iota(scores.shape, 0) < count
    scores = jnp.where(valid, scores, -1e30)
    shifted = jnp.exp(scores - jnp.max(scores, axis=0, keepdims=True))
    shifted = jnp.where(valid, shifted, 0.0)
    return shifted / sum_rows(shifted)


def soft_back(probs, rows):
    tall = jnp.concatenate(rows + [jnp.zeros_like(rows[0])] * (probs.shape[0] - len(rows)), axis=0)
    return probs * (tall - sum_rows(probs * tall))


def dense_body(
    flipped_ref,
    expand_one_ref,
    expand_one_back_ref,
    shrink_one_ref,
    shrink_one_back_ref,
    expand_two_ref,
    expand_two_back_ref,
    shrink_two_ref,
    shrink_two_back_ref,
    gate_one_ref,
    gate_one_back_ref,
    gate_two_ref,
    gate_two_back_ref,
    inner_ref,
    inner_back_ref,
    middle_ref,
    middle_back_ref,
    columns_ref,
    cot_ref,
    logits_ref,
    flipped_grad_ref,
    grads_ref,
    input_keep,
    active_one,
    out_one,
    pre_one,
    score_one,
    carried_keep,
    active_two,
    out_two,
    pre_two,
    score_two,
    tower_keep,
    tower_act_keep,
    first_keep,
    top_keep,
    tail_keep,
    gain_keep,
):
    width, events = flipped_ref.shape
    hidden = shrink_one_ref.shape[1]
    inner = inner_ref.shape[0] // 2
    narrow = middle_ref.shape[0] // 2
    tall = hidden + ONES
    span = min(SPAN, events)
    unit = jnp.ones((ONES, events), jnp.bfloat16)

    input_keep[:width, :] = flipped_ref[...]
    input_keep[width:, :] = unit
    for expert in range(6):
        active_one[expert * tall + hidden : (expert + 1) * tall, :] = unit
        active_two[expert * tall + hidden : (expert + 1) * tall, :] = unit
    for group in range(3):
        carried_keep[group * tall + hidden : (group + 1) * tall, :] = unit
    for task in range(2):
        tower_keep[task * tall + hidden : (task + 1) * tall, :] = unit
    gain_keep[...] = jnp.zeros_like(gain_keep)

    def column(index, rows=hidden, start=0):
        return columns_ref[start : start + rows, index : index + 1]

    def experts_rows(expert):
        return slice(expert * hidden, (expert + 1) * hidden)

    def span_step(step, carry):
        lanes = pl.ds(pl.multiple_of(step * span, span), span)
        inputs = flipped_ref[:, lanes]

        def up(level, inputs_of, expand_ref, shrink_ref, active_keep):
            kept = []
            for expert in range(6):
                active, slope, normed, inverse = expert_up(
                    inputs_of(expert),
                    expand_ref[experts_rows(expert), :],
                    column(level + expert),
                    shrink_ref[experts_rows(expert), :],
                    column(level + 6 + expert),
                )
                active_keep[expert * tall : expert * tall + hidden, lanes] = active
                kept.append((slope, normed, inverse, normed * column(level + 12 + expert)))
            return kept

        kept_one = up(0, lambda expert: inputs, expand_one_ref, shrink_one_ref, active_one)
        scores = times(gate_one_ref[...], inputs)
        probs_one = [soft(scores[0:8], 4), soft(scores[8:16], 4), soft(scores[16:24], 6)]
        carried = []
        for group in range(3):
            members = [2 * group, 2 * group + 1, 4, 5] if group < 2 else range(6)
            mixed = 0.0
            for place, expert in enumerate(members):
                mixed = mixed + probs_one[group][place : place + 1, :] * kept_one[expert][3]
            carried.append(mixed.astype(jnp.bfloat16))
            carried_keep[group * tall : group * tall + hidden, lanes] = carried[group]

        kept_two = up(
            18, lambda expert: carried[expert // 2], expand_two_ref, shrink_two_ref, active_two
        )
        probs_two = []
        tower_grads = []
        dq_two = []
        for task in range(2):
            probs = soft(times(gate_two_ref[task * 8 : task * 8 + 8, :], carried[task]), 4)
            probs_two.append(probs)
            members = [2 * task, 2 * task + 1, 4, 5]
            mixed = 0.0
            for place, expert in enumerate(members):
                mixed = mixed + probs[place : place + 1, :] * kept_two[expert][3]
            mixed = mixed.astype(jnp.bfloat16)
            tower_keep[task * tall : task * tall + hidden, lanes] = mixed
            first, first_slope = silu_parts(
                times(inner_ref[task * inner : (task + 1) * inner, :], mixed)
                + column(36, inner, task * inner)
            )
            first = first.astype(jnp.bfloat16)
            tower_act_keep[task * inner : (task + 1) * inner, lanes] = first
            top, top_slope = silu_parts(
                times(middle_ref[task * narrow : (task + 1) * narrow, :], first)
                + column(37, narrow, 2 * task * narrow)
            )
            weight = column(37, narrow, (2 * task + 1) * narrow)
            logits_ref[task : task + 1, lanes] = sum_rows(top * weight)
            cot = cot_ref[task : task + 1, lanes]
            top_grad = (cot * weight * top_slope).astype(jnp.bfloat16)
            top_keep[task * narrow : (task + 1) * narrow, lanes] = top_grad
            seen = cot * top
            high = seen.astype(jnp.bfloat16)
            tail_keep[2 * task * narrow : (2 * task + 1) * narrow, lanes] = high
            tail_keep[(2 * task + 1) * narrow : (2 * task + 2) * narrow, lanes] = (
                seen - high.astype(jnp.float32)
            ).astype(jnp.bfloat16)
            first_grad = (
                times(middle_back_ref[task * inner : (task + 1) * inner, :], top_grad) * first_slope
            ).astype(jnp.bfloat16)
            first_keep[task * inner : (task + 1) * inner, lanes] = first_grad
            grad = times(inner_back_ref[task * hidden : (task + 1) * hidden, :], first_grad)
            tower_grads.append(grad)
            dq_two.append([sum_rows(kept_two[expert][3] * grad) for expert in members])

        def expert_down(level, expert, kept, upstream, slant, shrink_back_ref, out_keep, pre_keep):
            slope, normed, inverse, _ = kept
            gained = upstream * normed
            part = gained[:, :128]
            for start in range(128, span, 128):
                part = part + gained[:, start : start + 128]
            gain_rows = slice((level + expert) * hidden, (level + expert + 1) * hidden)
            gain_keep[gain_rows, :] += part
            scaled = upstream * column(3 * level + 12 + expert)
            scale = 1.0 / hidden
            out_low = (
                inverse * (scaled - sum_rows(scaled) * scale - normed * (slant * scale))
            ).astype(jnp.bfloat16)
            out_keep[experts_rows(expert), lanes] = out_low
            pre_low = (times(shrink_back_ref[experts_rows(expert), :], out_low) * slope).astype(
                jnp.bfloat16
            )
            pre_keep[experts_rows(expert), lanes] = pre_low
            return pre_low

        pre_lows = []
        for expert in range(6):
            if expert < 4:
                task, place = expert // 2, expert % 2
                prob = probs_two[task][place : place + 1, :]
                upstream = prob * tower_grads[task]
                slant = prob * dq_two[task][place]
            else:
                place = expert - 2
                prob = [probs_two[task][place : place + 1, :] for task in range(2)]
                upstream = prob[0] * tower_grads[0] + prob[1] * tower_grads[1]
                slant = prob[0] * dq_two[0][place] + prob[1] * dq_two[1][place]
            pre_lows.append(
                expert_down(
                    6, expert, kept_two[expert], upstream, slant, shrink_two_back_ref, out_two, pre_two
                )
            )
        carried_grads = []
        for group in range(3):
            grad = 0.0
            for expert in (2 * group, 2 * group + 1):
                grad = grad + times(expand_two_back_ref[experts_rows(expert), :], pre_lows[expert])
            if group < 2:
                score = soft_back(probs_two[group], dq_two[group])
                score = jnp.concatenate([score, jnp.zeros_like(score)], axis=0).astype(jnp.bfloat16)
                score_two[group * 16 : group * 16 + 16, lanes] = score
                grad = grad + times(gate_two_back_ref[experts_rows(group), :], score)
            carried_grads.append(grad)

        dq_one = []
        for group in range(3):
            members = [2 * group, 2 * group + 1, 4, 5] if group < 2 else range(6)
            dq_one.append([sum_rows(kept_one[expert][3] * carried_grads[group]) for expert in members])
        pre_lows = []
        for expert in range(6):
            prob = probs_one[2][expert : expert + 1, :]
            upstream = prob * carried_grads[2]
            slant = prob * dq_one[2][expert]
            for task in range(2):
                if expert // 2 in (task, 2):
                    place = expert % 2 if expert < 4 else expert - 2
                    prob = probs_one[task][place : place + 1, :]
                    upstream = upstream + prob * carried_grads[task]
                    slant = slant + prob * dq_one[task][place]
            pre_lows.append(
                expert_down(
                    0, expert, kept_one[expert], upstream, slant, shrink_one_back_ref, out_one, pre_one
                )
            )
        scores_low = [soft_back(probs_one[group], dq_one[group]) for group in range(3)]
        score = jnp.concatenate(scores_low + [jnp.zeros_like(scores_low[0])], axis=0).astype(
            jnp.bfloat16
        )
        score_one[:, lanes] = score
        grad = times(gate_one_back_ref[...], score)
        for expert in range(6):
            grad = grad + times(
                expand_one_back_ref[expert * width : (expert + 1) * width, :], pre_lows[expert]
            )
        flipped_grad_ref[:, lanes] = grad
        return carry

    lax.fori_loop(0, events // span, span_step, 0)

    def put(row, value):
        grads_ref[row : row + value.shape[0], :] = value.astype(jnp.bfloat16)

    rows = 0
    biases = []
    for expert in range(6):
        both = over_events(input_keep[...], pre_one[experts_rows(expert), :])
        put(rows + expert * width, both[:width])
        biases.append(both[width : width + 1])
    rows += 6 * width
    for expert in range(6):
        both = over_events(active_one[expert * tall : (expert + 1) * tall, :], out_one[experts_rows(expert), :])
        put(rows + expert * hidden, both[:hidden])
        biases.append(both[hidden : hidden + 1])
    rows += 6 * hidden
    for expert in range(6):
        group = expert // 2
        both = over_events(carried_keep[group * tall : (group + 1) * tall, :], pre_two[experts_rows(expert), :])
        put(rows + expert * hidden, both[:hidden])
        biases.append(both[hidden : hidden + 1])
    rows += 6 * hidden
    for expert in range(6):
        both = over_events(active_two[expert * tall : (expert + 1) * tall, :], out_two[experts_rows(expert), :])
        put(rows + expert * hidden, both[:hidden])
        biases.append(both[hidden : hidden + 1])
    rows += 6 * hidden
    tower = []
    for task in range(2):
        tower.append(
            over_events(tower_keep[task * tall : (task + 1) * tall, :], first_keep[task * inner : (task + 1) * inner, :])
        )
    tower = jnp.concatenate(tower, axis=1)
    put(rows, tower[:hidden])
    biases.append(tower[hidden : hidden + 1])
    rows += hidden
    put(
        rows,
        jnp.concatenate(
            [
                over_events(
                    top_keep[task * narrow : (task + 1) * narrow, :],
                    tower_act_keep[task * inner : (task + 1) * inner, :],
                )
                for task in range(2)
            ],
            axis=1,
        ),
    )
    rows += narrow
    gates = over_events(score_one[...], flipped_ref[...])
    for start in range(0, width, hidden):
        put(rows, gates[:, start : start + hidden])
        rows += gates.shape[0]
    for task in range(2):
        put(
            rows,
            over_events(
                score_two[task * 16 : task * 16 + 16, :],
                carried_keep[task * tall : task * tall + hidden, :],
            ),
        )
        rows += 16
    tops = over_events(unit, top_keep[...])[:1]
    seen = over_events(unit, tail_keep[...])[:1]
    pieces = []
    for task in range(2):
        pieces.append(tops[:, task * narrow : (task + 1) * narrow])
        pieces.append(
            seen[:, 2 * task * narrow : (2 * task + 1) * narrow]
            + seen[:, (2 * task + 1) * narrow : (2 * task + 2) * narrow]
        )
    biases.append(jnp.concatenate(pieces, axis=1))
    gains = gain_keep[...]
    high = gains.astype(jnp.bfloat16)
    low = (gains - high.astype(jnp.float32)).astype(jnp.bfloat16)
    gains = (over_events(unit[:, :128], high) + over_events(unit[:, :128], low))[:1]
    for expert in range(12):
        biases.append(gains[:, experts_rows(expert)])
    biases = jnp.concatenate(biases, axis=0)
    extra = grads_ref.shape[0] - rows - biases.shape[0]
    put(rows, jnp.concatenate([biases, jnp.zeros((extra, hidden), jnp.float32)], axis=0))


def dense(flipped, weights, columns, cot, grad_rows):
    width, events = flipped.shape
    hidden = columns.shape[0]
    inner, narrow = 128, 64
    tall = hidden + ONES
    return pl.pallas_call(
        dense_body,
        out_shape=(
            jax.ShapeDtypeStruct((2, events), jnp.float32),
            jax.ShapeDtypeStruct((width, events), jnp.float32),
            jax.ShapeDtypeStruct((grad_rows, hidden), jnp.bfloat16),
        ),
        scratch_shapes=[
            pltpu.VMEM((rows, events), jnp.bfloat16)
            for rows in (
                width + ONES,
                6 * tall,
                6 * hidden,
                6 * hidden,
                32,
                3 * tall,
                6 * tall,
                6 * hidden,
                6 * hidden,
                32,
                2 * tall,
                2 * inner,
                2 * inner,
                2 * narrow,
                4 * narrow,
            )
        ]
        + [pltpu.VMEM((12 * hidden, 128), jnp.float32)],
        compiler_params=pltpu.CompilerParams(vmem_limit_bytes=VMEM_LIMIT),
        cost_estimate=pl.CostEstimate(
            flops=6 * events * hidden * (6 * (width + 3 * hidden) + 2 * inner),
            bytes_accessed=24 * 1024 * 1024,
            transcendentals=12 * events * hidden,
        ),
    )(flipped, *weights, columns, cot)


def pack_rows(parts, row_tile):
    width = 256
    wide = [part for part in parts if part.ndim == 2 and part.shape[1] == width]
    thin = [part.reshape(-1) for part in parts if part.ndim != 2 or part.shape[1] != width]
    rest = jnp.concatenate(thin)
    rest = jnp.pad(rest, (0, -rest.size % (row_tile * width))).reshape(-1, width)
    return jnp.concatenate(wide + [rest], axis=0)


def unpack_rows(whole, parts):
    devices, rows, width = whole.shape
    wide_rows = sum(part.shape[0] for part in parts if part.ndim == 2 and part.shape[1] == width)
    rest = whole[:, wide_rows:].reshape(devices, -1)
    out = []
    row = 0
    place = 0
    for part in parts:
        if part.ndim == 2 and part.shape[1] == width:
            piece = whole[:, row : row + part.shape[0]]
            row += part.shape[0]
        else:
            piece = rest[:, place : place + part.size]
            place += part.size
        out.append(piece.reshape((devices * part.shape[0],) + part.shape[1:]))
    return out


def split_grads(total, width, hidden):
    place = 0

    def take(rows):
        nonlocal place
        place += rows
        return total[place - rows : place].astype(jnp.float32)

    low_expand = take(6 * width)
    low_shrink = take(6 * hidden)
    up_expand = take(6 * hidden)
    up_shrink = take(6 * hidden)
    inner = take(hidden).reshape(hidden, 2, -1).transpose(1, 0, 2).reshape(2 * hidden, -1)
    middle = take(64).reshape(64, 2, -1).transpose(1, 2, 0).reshape(-1, 64)
    gates = take(32 * (width // hidden)).reshape(-1, 32, hidden).transpose(0, 2, 1).reshape(width, 32)
    taskgate = jnp.concatenate([gates[:, 0:4], gates[:, 8:12]], axis=0)
    sharegate = gates[:, 16:22]
    upper = take(32).reshape(2, 16, hidden)[:, :4].transpose(0, 2, 1).reshape(2 * hidden, 4)
    rows = take(48)
    low_inbias, low_outbias, up_inbias, up_outbias = (
        rows[6 * index : 6 * index + 6].reshape(-1) for index in range(4)
    )
    low_gain, up_gain = (rows[26 + 6 * index : 32 + 6 * index].reshape(-1) for index in range(2))
    return (
        low_expand,
        low_inbias,
        low_shrink,
        low_outbias,
        low_gain,
        taskgate,
        sharegate,
        up_expand,
        up_inbias,
        up_shrink,
        up_outbias,
        up_gain,
        upper,
        inner,
        rows[24],
        middle,
        rows[25],
    )


def on_device(
    owner_ids,
    row_ids,
    embed_table,
    expandone,
    expbiasone,
    reduceone,
    redbiasone,
    normgainone,
    taskgateone,
    sharegateone,
    expandtwo,
    expbiastwo,
    reducetwo,
    redbiastwo,
    normgaintwo,
    taskgatetwo,
    towerinner,
    towerbias,
    towermiddle,
    towertail,
    logit_cot,
):
    devices = lax.axis_size(("dp", "fsdp"))
    events, fields = owner_ids.shape
    emb_width = embed_table.shape[1]
    capacity = 2 * events * fields // devices
    owner_rows = owner_ids.T
    request, rank = assign_slots(owner_rows, row_ids.T, devices, capacity)
    asked_rows = lax.all_to_all(request, ("dp", "fsdp"), split_axis=0, concat_axis=0, tiled=True)
    table_wide = (
        embed_table.reshape(ROW_BLOCKS, -1, emb_width).transpose(0, 2, 1).reshape(ROW_BLOCKS * emb_width, -1)
    )
    found = find_rows(asked_rows, table_wide)
    returned = lax.all_to_all(found, ("dp", "fsdp"), split_axis=0, concat_axis=0, tiled=True)
    flipped = place_rows(returned, rank, owner_rows)
    packed = pack_rows(
        (
            expandone,
            reduceone,
            expandtwo,
            reducetwo,
            expbiasone,
            redbiasone,
            normgainone,
            expbiastwo,
            redbiastwo,
            normgaintwo,
            taskgateone,
            sharegateone,
            taskgatetwo,
            towerinner,
            towerbias,
            towermiddle,
            towertail,
        ),
        16,
    )
    whole = lax.all_gather(packed, "fsdp", axis=0, tiled=False)
    whole = lax.all_gather(whole, "dp", axis=0, tiled=False)
    whole = whole.reshape((devices,) + packed.shape)
    (
        one_expand,
        one_shrink,
        two_expand,
        two_shrink,
        one_inbias,
        one_outbias,
        one_gain,
        two_inbias,
        two_outbias,
        two_gain,
        one_taskgate,
        one_sharegate,
        two_taskgate,
        inner_full,
        tbias_full,
        middle_full,
        tail_full,
    ) = unpack_rows(
        whole,
        (
            expandone,
            reduceone,
            expandtwo,
            reducetwo,
            expbiasone,
            redbiasone,
            normgainone,
            expbiastwo,
            redbiastwo,
            normgaintwo,
            taskgateone,
            sharegateone,
            taskgatetwo,
            towerinner,
            towerbias,
            towermiddle,
            towertail,
        ),
    )
    hidden = expandone.shape[1]
    width = fields * emb_width
    gates = jnp.concatenate(
        [
            jnp.pad(one_taskgate.reshape(2, width, 4), ((0, 0), (0, 0), (0, 4)))[0],
            jnp.pad(one_taskgate.reshape(2, width, 4), ((0, 0), (0, 0), (0, 4)))[1],
            jnp.pad(one_sharegate, ((0, 0), (0, 10))),
        ],
        axis=1,
    )
    upper = jnp.pad(two_taskgate.reshape(2, hidden, 4), ((0, 0), (0, 0), (0, 12)))

    def swap(weight, blocks):
        return weight.reshape(blocks, -1, weight.shape[1]).transpose(0, 2, 1).reshape(
            blocks * weight.shape[1], -1
        )

    weights = (
        swap(one_expand, 6),
        one_expand,
        swap(one_shrink, 6),
        one_shrink,
        swap(two_expand, 6),
        two_expand,
        swap(two_shrink, 6),
        two_shrink,
        gates[:, :24].T,
        gates,
        upper[:, :, :8].transpose(0, 2, 1).reshape(16, hidden),
        upper.reshape(2 * hidden, 16),
        swap(inner_full, 2),
        inner_full,
        swap(middle_full, 2),
        middle_full,
    )
    columns = (
        jnp.concatenate(
            [
                one_inbias,
                one_outbias,
                one_gain,
                two_inbias,
                two_outbias,
                two_gain,
                tbias_full,
                tail_full,
            ]
        )
        .reshape(-1, hidden)
        .astype(jnp.float32)
        .T
    )
    chunk = 16 * devices
    grad_rows = -(-(12 * (width + 3 * hidden) // 2 + 2 * hidden) // chunk) * chunk
    logits, flipped_grad, grads = dense(flipped, weights, columns, logit_cot, grad_rows)
    x_grad = flipped_grad.T
    outgoing = send_rows(flipped_grad, rank, owner_rows, capacity)
    incoming = lax.all_to_all(
        outgoing, ("dp", "fsdp"), split_axis=0, concat_axis=0, tiled=True
    )
    table_grad = add_rows(incoming, asked_rows, embed_table.shape[0])
    part = lax.psum_scatter(grads, "dp", scatter_dimension=0, tiled=True)
    part = lax.psum_scatter(part, "fsdp", scatter_dimension=0, tiled=True)
    total = lax.all_gather(part, "fsdp", axis=0, tiled=True)
    total = lax.all_gather(total, "dp", axis=0, tiled=True)
    return (logits, x_grad, table_grad, *split_grads(total, width, hidden))


def solution(mesh):
    return jax.shard_map(
        on_device,
        mesh=mesh,
        in_specs=(
            P(("dp", "fsdp"), None),
            P(("dp", "fsdp"), None),
            P(("dp", "fsdp"), None),
            P(("dp", "fsdp"), None),
            P(("dp", "fsdp")),
            P(("dp", "fsdp"), None),
            P(("dp", "fsdp")),
            P(("dp", "fsdp")),
            P(("dp", "fsdp"), None),
            P(("dp", "fsdp"), None),
            P(("dp", "fsdp"), None),
            P(("dp", "fsdp")),
            P(("dp", "fsdp"), None),
            P(("dp", "fsdp")),
            P(("dp", "fsdp")),
            P(("dp", "fsdp"), None),
            P(("dp", "fsdp"), None),
            P(("dp", "fsdp")),
            P(("dp", "fsdp"), None),
            P(("dp", "fsdp")),
            P(None, ("dp", "fsdp")),
        ),
        out_specs=(
            P(None, ("dp", "fsdp")),
            P(("dp", "fsdp"), None),
            P(("dp", "fsdp"), None),
            P(),
            P(),
            P(),
            P(),
            P(),
            P(),
            P(),
            P(),
            P(),
            P(),
            P(),
            P(),
            P(),
            P(),
            P(),
            P(),
            P(),
        ),
        check_vma=False,
    )
```

```python
import functools

import jax
import jax.numpy as jnp
from jax import lax
from jax.experimental import pallas as pl
from jax.experimental.pallas import tpu as pltpu
from jax.sharding import PartitionSpec as P

EPS = 1e-05
VMEM_LIMIT = 56 * 1024 * 1024
ROW_BLOCKS = 8


def local_kernel(body, out_shape, flops, moved, scratch=()):
    return pl.pallas_call(
        body,
        out_shape=out_shape,
        scratch_shapes=list(scratch),
        compiler_params=pltpu.CompilerParams(vmem_limit_bytes=VMEM_LIMIT),
        cost_estimate=pl.CostEstimate(flops=flops, bytes_accessed=moved, transcendentals=0),
    )


def one_hot(hit):
    return jnp.where(hit, 1.0, 0.0).astype(jnp.bfloat16)


def iota(shape, axis):
    return lax.broadcasted_iota(jnp.int32, shape, axis)


def slot_body(owner_ref, row_ref, request_ref, rank_ref):
    fields, events = owner_ref.shape
    devices, _, capacity = request_ref.shape
    place = iota((devices, events), 0)
    asked = jnp.zeros((devices, events), jnp.float32)
    for field in range(fields):
        asked = asked + jnp.where(owner_ref[field : field + 1, :] == place, 1.0, 0.0)
    earlier = one_hot(iota((events, events), 0) < iota((events, events), 1))
    rank = jnp.dot(asked.astype(jnp.bfloat16), earlier, preferred_element_type=jnp.float32)
    rank = jnp.where(asked > 0.5, rank.astype(jnp.int32), -1)
    rank_ref[...] = rank
    slots = iota((capacity, events), 0)
    total = jnp.zeros((2 * devices, capacity), jnp.float32)
    for field in range(fields):
        mine = owner_ref[field : field + 1, :] == place
        field_rank = jnp.max(jnp.where(mine, rank, -1).astype(jnp.float32), axis=0, keepdims=True)
        rows = row_ref[field : field + 1, :]
        high = jnp.where(mine, (rows >> 6).astype(jnp.float32), 0.0)
        low = jnp.where(mine, (rows & 63).astype(jnp.float32), 0.0)
        value = jnp.concatenate([high, low], axis=0).astype(jnp.bfloat16)
        total = total + lax.dot_general(
            value,
            one_hot(field_rank.astype(jnp.int32) == slots),
            (((1,), (1,)), ((), ())),
            preferred_element_type=jnp.float32,
        )
    request = (total[:devices] * 64.0 + total[devices:]).astype(jnp.int32)
    for owner in range(devices):
        request_ref[owner] = request[owner : owner + 1]


def assign_slots(owner_rows, row_rows, devices, capacity):
    fields, events = owner_rows.shape
    return local_kernel(
        slot_body,
        (
            jax.ShapeDtypeStruct((devices, 1, capacity), jnp.int32),
            jax.ShapeDtypeStruct((devices, events), jnp.int32),
        ),
        2 * devices * events * (events + 2 * fields * capacity),
        4 * events * (2 * fields + devices),
    )(owner_rows, row_rows)


def find_body(request_ref, table_ref, found_ref, wide_ref):
    devices, _, capacity = request_ref.shape
    width = table_ref.shape[0]
    span = wide_ref.shape[1]
    places = iota((span, capacity), 0)
    for index in range(ROW_BLOCKS):
        wide_ref[index * width : (index + 1) * width, :] = table_ref[
            :, index * span : (index + 1) * span
        ]

    def step(source, carry):
        rows = request_ref[source]
        block = rows // span
        hits = one_hot(rows - block * span == places)
        rows_all = jnp.dot(wide_ref[...], hits, preferred_element_type=jnp.float32)
        picked = jnp.zeros((width, capacity), jnp.float32)
        for index in range(ROW_BLOCKS):
            picked = jnp.where(
                block == index, rows_all[index * width : (index + 1) * width, :], picked
            )
        found_ref[source] = picked.astype(jnp.bfloat16)
        return carry

    lax.fori_loop(0, devices, step, 0, unroll=2)


def find_rows(request, table):
    devices, _, capacity = request.shape
    width, rows = table.shape
    return local_kernel(
        find_body,
        jax.ShapeDtypeStruct((devices, width, capacity), jnp.bfloat16),
        2 * devices * capacity * rows * width,
        2 * (rows * width + devices * capacity * width),
        [pltpu.VMEM((ROW_BLOCKS * width, rows // ROW_BLOCKS), jnp.bfloat16)],
    )(request, table)


def place_body(found_ref, rank_ref, owner_ref, flipped_ref, total_ref):
    devices, width, capacity = found_ref.shape
    fields, events = owner_ref.shape
    slots = iota((capacity, events), 0)
    group = 4
    total_ref[...] = jnp.zeros_like(total_ref)

    def step(start, carry):
        pieces = []
        for index in range(group):
            owner = start * group + index
            hits = one_hot(rank_ref[pl.ds(owner, 1), :] == slots)
            pieces.append(jnp.dot(found_ref[owner], hits, preferred_element_type=jnp.float32))
        for field in range(fields):
            rows = slice(field * width, (field + 1) * width)
            owners = owner_ref[field : field + 1, :]
            value = total_ref[rows, :]
            for index in range(group):
                value = jnp.where(owners == start * group + index, pieces[index], value)
            total_ref[rows, :] = value
        return carry

    lax.fori_loop(0, devices // group, step, 0)
    flipped_ref[...] = total_ref[...].astype(jnp.bfloat16)


def place_rows(found, rank, owner_rows):
    devices, width, capacity = found.shape
    fields, events = owner_rows.shape
    return local_kernel(
        place_body,
        jax.ShapeDtypeStruct((fields * width, events), jnp.bfloat16),
        2 * devices * width * capacity * events,
        2 * (devices * width * capacity + fields * width * events),
        [pltpu.VMEM((fields * width, events), jnp.float32)],
    )(found, rank, owner_rows)


def send_body(grad_ref, rank_ref, owner_ref, sent_ref, low_ref):
    devices, width, capacity = sent_ref.shape
    fields, events = owner_ref.shape
    slots = iota((capacity, events), 0)
    low_ref[...] = grad_ref[...].astype(jnp.bfloat16).astype(jnp.float32)

    def step(owner, carry):
        chosen = jnp.zeros((width, events), jnp.float32)
        for field in range(fields):
            rows = slice(field * width, (field + 1) * width)
            chosen = jnp.where(owner_ref[field : field + 1, :] == owner, low_ref[rows, :], chosen)
        hits = one_hot(rank_ref[pl.ds(owner, 1), :] == slots)
        sent_ref[owner] = lax.dot_general(
            chosen.astype(jnp.bfloat16),
            hits,
            (((1,), (1,)), ((), ())),
            preferred_element_type=jnp.float32,
        ).astype(jnp.bfloat16)
        return carry

    lax.fori_loop(0, devices, step, 0, unroll=2)


def send_rows(grad, rank, owner_rows, capacity):
    devices = rank.shape[0]
    fields, events = owner_rows.shape
    width = grad.shape[0] // fields
    return local_kernel(
        send_body,
        jax.ShapeDtypeStruct((devices, width, capacity), jnp.bfloat16),
        2 * devices * width * capacity * events,
        2 * (devices * width * capacity + 2 * fields * width * events),
        [pltpu.VMEM((fields * width, events), jnp.float32)],
    )(grad, rank, owner_rows)


def add_body(came_ref, request_ref, out_ref, total_ref):
    devices, width, capacity = came_ref.shape
    span = total_ref.shape[1]
    group = 4
    places = iota((span, capacity), 0)
    total_ref[...] = jnp.zeros_like(total_ref)

    def step(start, carry):
        hits = []
        spread = []
        for index in range(group):
            source = start * group + index
            rows = request_ref[source]
            block = rows // span
            hits.append(one_hot(rows - block * span == places))
            came = came_ref[source].astype(jnp.float32)
            spread.append(
                jnp.concatenate(
                    [jnp.where(block == part, came, 0.0) for part in range(ROW_BLOCKS)], axis=0
                ).astype(jnp.bfloat16)
            )
        total_ref[...] += lax.dot_general(
            jnp.concatenate(spread, axis=1),
            jnp.concatenate(hits, axis=1),
            (((1,), (1,)), ((), ())),
            preferred_element_type=jnp.float32,
        )
        return carry

    lax.fori_loop(0, devices // group, step, 0)
    for index in range(ROW_BLOCKS):
        out_ref[:, index * span : (index + 1) * span] = total_ref[
            index * width : (index + 1) * width, :
        ]


def add_rows(came, request, rows):
    devices, width, capacity = came.shape
    span = rows // ROW_BLOCKS
    return local_kernel(
        add_body,
        jax.ShapeDtypeStruct((width, rows), jnp.float32),
        2 * devices * capacity * rows * width,
        2 * devices * width * capacity + 4 * rows * width,
        [pltpu.VMEM((ROW_BLOCKS * width, span), jnp.float32)],
    )(came, request)


THIN_ROWS = 48


def pack_thin_body(*refs):
    *biases, tbias, tail, taskgate, sharegate, upgate, inner, middle, thin_ref, hold = refs
    hold[...] = jnp.zeros_like(hold)
    for row, piece in enumerate(biases + [tbias, tail]):
        hold[row : row + 1, : piece.shape[0]] = piece[...].astype(jnp.float32).reshape(1, -1)
    for row, piece in ((8, taskgate), (16, sharegate), (24, upgate), (32, inner)):
        hold[row : row + piece.shape[0], : piece.shape[1]] = piece[...].astype(jnp.float32)
    hold[32 : 32 + middle.shape[0], 128 : 128 + middle.shape[1]] = middle[...].astype(jnp.float32)
    thin_ref[...] = hold[...].astype(jnp.bfloat16)


def pack_thin(biases, tbias, tail, taskgate, sharegate, upgate, inner, middle):
    return local_kernel(
        pack_thin_body,
        jax.ShapeDtypeStruct((THIN_ROWS, 256), jnp.bfloat16),
        0,
        THIN_ROWS * 1024,
        [pltpu.VMEM((THIN_ROWS, 256), jnp.float32)],
    )(*biases, tbias, tail, taskgate, sharegate, upgate, inner, middle)


def prep_thin_body(
    thin_ref,
    columns_ref,
    gate_one_ref,
    gate_one_back_ref,
    gate_two_ref,
    gate_two_back_ref,
    inner_ref,
    inner_back_ref,
    middle_ref,
    middle_back_ref,
    rows,
    task_rows,
    share_rows,
    up_rows,
    inner_rows,
    middle_rows,
):
    devices = thin_ref.shape[0]
    hidden = columns_ref.shape[0]
    width = gate_one_ref.shape[1]

    def lay(target, source, index, count):
        target[:, index * count : (index + 1) * count] = source[:, :count]

    rows[...] = jnp.zeros_like(rows)
    task_rows[...] = jnp.zeros_like(task_rows)
    share_rows[...] = jnp.zeros_like(share_rows)
    up_rows[...] = jnp.zeros_like(up_rows)
    bias = 6 * hidden // devices
    flat = hidden // devices
    for index in range(devices):
        thin = thin_ref[index].astype(jnp.float32)
        rows[0:6, index * bias : (index + 1) * bias] = thin[0:6, :bias]
        rows[6:8, index * flat : (index + 1) * flat] = thin[6:8, :flat]
        lay(task_rows, thin[8:16], index, 2 * width // devices)
        lay(share_rows, thin[16:24], index, width // devices)
        lay(up_rows, thin[24:32], index, 2 * hidden // devices)
        count = 2 * hidden // devices
        inner_rows[index * count : (index + 1) * count, :] = thin[32 : 32 + count, :128]
        count = hidden // devices
        middle_rows[index * count : (index + 1) * count, :] = thin[32 : 32 + count, 128:192]
    columns_ref[...] = jnp.zeros_like(columns_ref)
    for expert in range(6):
        columns_ref[:, expert * 8 : expert * 8 + 8] = rows[:, expert * hidden : (expert + 1) * hidden].T
    gates = jnp.concatenate(
        [
            task_rows[:, :width],
            task_rows[:, width:],
            share_rows[...],
            jnp.zeros((8, width), jnp.float32),
        ],
        axis=0,
    )
    gate_one_ref[...] = gates.astype(jnp.bfloat16)
    gate_one_back_ref[...] = gates.T.astype(jnp.bfloat16)
    gate_two_ref[...] = jnp.concatenate([up_rows[:, :hidden], up_rows[:, hidden:]], axis=0).astype(
        jnp.bfloat16
    )
    for task in range(2):
        span = slice(task * hidden, (task + 1) * hidden)
        wide = jnp.concatenate([up_rows[:, span], jnp.zeros((8, hidden), jnp.float32)], axis=0)
        gate_two_back_ref[span, :] = wide.T.astype(jnp.bfloat16)
        inner_ref[task * 128 : (task + 1) * 128, :] = inner_rows[span, :].T.astype(jnp.bfloat16)
        span = slice(task * 128, (task + 1) * 128)
        middle_ref[task * 64 : (task + 1) * 64, :] = middle_rows[span, :].T.astype(jnp.bfloat16)
    inner_back_ref[...] = inner_rows[...].astype(jnp.bfloat16)
    middle_back_ref[...] = middle_rows[...].astype(jnp.bfloat16)


def prep_thin(thin, width, hidden):
    low = functools.partial(jax.ShapeDtypeStruct, dtype=jnp.bfloat16)
    return local_kernel(
        prep_thin_body,
        (
            jax.ShapeDtypeStruct((hidden, 64), jnp.float32),
            low((32, width)),
            low((width, 32)),
            low((16, hidden)),
            low((2 * hidden, 16)),
            low((hidden, hidden)),
            low((2 * hidden, 128)),
            low((128, 128)),
            low((hidden, 64)),
        ),
        0,
        2 * thin.size,
        [
            pltpu.VMEM((8, 6 * hidden), jnp.float32),
            pltpu.VMEM((8, 2 * width), jnp.float32),
            pltpu.VMEM((8, width), jnp.float32),
            pltpu.VMEM((8, 2 * hidden), jnp.float32),
            pltpu.VMEM((2 * hidden, 128), jnp.float32),
            pltpu.VMEM((hidden, 64), jnp.float32),
        ],
    )(thin)


SPAN = 256
ONES = 16


def over_events(left, right):
    return lax.dot_general(left, right, (((1,), (1,)), ((), ())), preferred_element_type=jnp.float32)


def times(left, right):
    return jnp.dot(left, right, preferred_element_type=jnp.float32)


def sum_rows(values):
    return jnp.sum(values, axis=0, keepdims=True)


def sigmoid_of(values):
    return 0.5 * jnp.tanh(0.5 * values) + 0.5


def silu_parts(values):
    sig = sigmoid_of(values)
    active = values * sig
    return active, sig + active * (1.0 - sig)


def expert_up(inputs, expand, expbias, shrink, shrinkbias):
    active, slope = silu_parts(times(expand, inputs) + expbias)
    active = active.astype(jnp.bfloat16)
    output = times(shrink, active) + shrinkbias
    scale = 1.0 / output.shape[0]
    centered = output - sum_rows(output) * scale
    inverse = lax.rsqrt(sum_rows(centered * centered) * scale + EPS)
    return active, slope, centered * inverse, inverse


def soft(scores, count):
    valid = iota(scores.shape, 0) < count
    scores = jnp.where(valid, scores, -1e30)
    shifted = jnp.exp(scores - jnp.max(scores, axis=0, keepdims=True))
    shifted = jnp.where(valid, shifted, 0.0)
    return shifted / sum_rows(shifted)


def soft_back(probs, rows):
    tall = jnp.concatenate(rows + [jnp.zeros_like(rows[0])] * (probs.shape[0] - len(rows)), axis=0)
    return probs * (tall - sum_rows(probs * tall))


def assemble(bit, own_ref, came_ref, homes, places, blocks):
    rows = own_ref.shape[0] // blocks
    sizes = [home.shape[0] // (2 * blocks) for home in homes]

    def lay(pieces):
        for half, source in enumerate(pieces):
            for block in range(blocks):
                start = block * rows
                for home, size in zip(homes, sizes):
                    target = places[half][block] * size
                    home[target : target + size, :] = source[start : start + size, :]
                    start += size

    @pl.when(bit == 0)
    def _():
        lay((own_ref, came_ref))

    @pl.when(bit != 0)
    def _():
        lay((came_ref, own_ref))


def dense_body(places, *refs):
    if places is None:
        *naturals, refs = *refs[:4], refs[4:]
    else:
        bit_ref, own_a, own_b, came_a, came_b, *refs = refs
        naturals, refs = refs[-4:], refs[:-4]
    expand_one_back_ref, shrink_one_back_ref, expand_two_back_ref, shrink_two_back_ref = naturals
    (
        flipped_ref,
        columns_ref,
        gate_one_ref,
        gate_one_back_ref,
        gate_two_ref,
        gate_two_back_ref,
        inner_ref,
        inner_back_ref,
        middle_ref,
        middle_back_ref,
        cot_ref,
        logits_ref,
        flipped_grad_ref,
        grads_ref,
        input_keep,
        active_one,
        out_one,
        pre_one,
        score_one,
        carried_keep,
        active_two,
        out_two,
        pre_two,
        score_two,
        tower_keep,
        tower_act_keep,
        first_keep,
        top_keep,
        tail_keep,
        gain_keep,
        expand_one_ref,
        shrink_one_ref,
        expand_two_ref,
        shrink_two_ref,
    ) = refs
    if places is not None:
        bit = bit_ref[0]
        blocks = len(places[0][0])
        assemble(bit, own_a, came_a, [expand_one_back_ref], places[0], blocks)
        assemble(
            bit,
            own_b,
            came_b,
            [shrink_one_back_ref, expand_two_back_ref, shrink_two_back_ref],
            places[1],
            blocks,
        )
    for natural, turned in (
        (expand_one_back_ref, expand_one_ref),
        (shrink_one_back_ref, shrink_one_ref),
        (expand_two_back_ref, expand_two_ref),
        (shrink_two_back_ref, shrink_two_ref),
    ):
        depth = natural.shape[0] // 6
        across = natural.shape[1]
        for expert in range(6):
            turned[expert * across : (expert + 1) * across, :] = natural[
                expert * depth : (expert + 1) * depth, :
            ].T

    width, events = flipped_ref.shape
    hidden = shrink_one_back_ref.shape[1]
    inner = inner_ref.shape[0] // 2
    narrow = middle_ref.shape[0] // 2
    tall = hidden + ONES
    span = min(SPAN, events)
    unit = jnp.ones((ONES, events), jnp.bfloat16)

    input_keep[:width, :] = flipped_ref[...]
    input_keep[width:, :] = unit
    for expert in range(6):
        active_one[expert * tall + hidden : (expert + 1) * tall, :] = unit
        active_two[expert * tall + hidden : (expert + 1) * tall, :] = unit
    for group in range(3):
        carried_keep[group * tall + hidden : (group + 1) * tall, :] = unit
    for task in range(2):
        tower_keep[task * tall + hidden : (task + 1) * tall, :] = unit
    gain_keep[...] = jnp.zeros_like(gain_keep)

    def column(index, rows=hidden, start=0):
        return columns_ref[start : start + rows, index : index + 1]

    def experts_rows(expert):
        return slice(expert * hidden, (expert + 1) * hidden)

    def span_step(step, carry):
        lanes = pl.ds(pl.multiple_of(step * span, span), span)
        inputs = flipped_ref[:, lanes]

        def up(level, inputs_of, expand_ref, shrink_ref, active_keep):
            kept = []
            for expert in range(6):
                active, slope, normed, inverse = expert_up(
                    inputs_of(expert),
                    expand_ref[experts_rows(expert), :],
                    column(expert * 8 + level),
                    shrink_ref[experts_rows(expert), :],
                    column(expert * 8 + level + 1),
                )
                active_keep[expert * tall : expert * tall + hidden, lanes] = active
                kept.append((slope, normed, inverse, normed * column(expert * 8 + level + 2)))
            return kept

        kept_one = up(0, lambda expert: inputs, expand_one_ref, shrink_one_ref, active_one)
        scores = times(gate_one_ref[...], inputs)
        probs_one = [soft(scores[0:8], 4), soft(scores[8:16], 4), soft(scores[16:24], 6)]
        carried = []
        for group in range(3):
            members = [2 * group, 2 * group + 1, 4, 5] if group < 2 else range(6)
            mixed = 0.0
            for place, expert in enumerate(members):
                mixed = mixed + probs_one[group][place : place + 1, :] * kept_one[expert][3]
            carried.append(mixed.astype(jnp.bfloat16))
            carried_keep[group * tall : group * tall + hidden, lanes] = carried[group]

        kept_two = up(
            3, lambda expert: carried[expert // 2], expand_two_ref, shrink_two_ref, active_two
        )
        probs_two = []
        tower_grads = []
        dq_two = []
        for task in range(2):
            probs = soft(times(gate_two_ref[task * 8 : task * 8 + 8, :], carried[task]), 4)
            probs_two.append(probs)
            members = [2 * task, 2 * task + 1, 4, 5]
            mixed = 0.0
            for place, expert in enumerate(members):
                mixed = mixed + probs[place : place + 1, :] * kept_two[expert][3]
            mixed = mixed.astype(jnp.bfloat16)
            tower_keep[task * tall : task * tall + hidden, lanes] = mixed
            first, first_slope = silu_parts(
                times(inner_ref[task * inner : (task + 1) * inner, :], mixed)
                + column(6, inner, task * inner)
            )
            first = first.astype(jnp.bfloat16)
            tower_act_keep[task * inner : (task + 1) * inner, lanes] = first
            top, top_slope = silu_parts(
                times(middle_ref[task * narrow : (task + 1) * narrow, :], first)
                + column(7, narrow, 2 * task * narrow)
            )
            weight = column(7, narrow, (2 * task + 1) * narrow)
            logits_ref[task : task + 1, lanes] = sum_rows(top * weight)
            cot = cot_ref[task : task + 1, lanes]
            top_grad = (cot * weight * top_slope).astype(jnp.bfloat16)
            top_keep[task * narrow : (task + 1) * narrow, lanes] = top_grad
            seen = cot * top
            high = seen.astype(jnp.bfloat16)
            tail_keep[2 * task * narrow : (2 * task + 1) * narrow, lanes] = high
            tail_keep[(2 * task + 1) * narrow : (2 * task + 2) * narrow, lanes] = (
                seen - high.astype(jnp.float32)
            ).astype(jnp.bfloat16)
            first_grad = (
                times(middle_back_ref[task * inner : (task + 1) * inner, :], top_grad) * first_slope
            ).astype(jnp.bfloat16)
            first_keep[task * inner : (task + 1) * inner, lanes] = first_grad
            grad = times(inner_back_ref[task * hidden : (task + 1) * hidden, :], first_grad)
            tower_grads.append(grad)
            dq_two.append([sum_rows(kept_two[expert][3] * grad) for expert in members])

        def expert_down(level, expert, kept, upstream, slant, shrink_back_ref, out_keep, pre_keep):
            slope, normed, inverse, _ = kept
            gained = upstream * normed
            part = gained[:, :128]
            for start in range(128, span, 128):
                part = part + gained[:, start : start + 128]
            gain_rows = slice((level + expert) * hidden, (level + expert + 1) * hidden)
            gain_keep[gain_rows, :] += part
            scaled = upstream * column(expert * 8 + level // 2 + 2)
            scale = 1.0 / hidden
            out_low = (
                inverse * (scaled - sum_rows(scaled) * scale - normed * (slant * scale))
            ).astype(jnp.bfloat16)
            out_keep[experts_rows(expert), lanes] = out_low
            pre_low = (times(shrink_back_ref[experts_rows(expert), :], out_low) * slope).astype(
                jnp.bfloat16
            )
            pre_keep[experts_rows(expert), lanes] = pre_low
            return pre_low

        pre_lows = []
        for expert in range(6):
            if expert < 4:
                task, place = expert // 2, expert % 2
                prob = probs_two[task][place : place + 1, :]
                upstream = prob * tower_grads[task]
                slant = prob * dq_two[task][place]
            else:
                place = expert - 2
                prob = [probs_two[task][place : place + 1, :] for task in range(2)]
                upstream = prob[0] * tower_grads[0] + prob[1] * tower_grads[1]
                slant = prob[0] * dq_two[0][place] + prob[1] * dq_two[1][place]
            pre_lows.append(
                expert_down(
                    6, expert, kept_two[expert], upstream, slant, shrink_two_back_ref, out_two, pre_two
                )
            )
        carried_grads = []
        for group in range(3):
            grad = 0.0
            for expert in (2 * group, 2 * group + 1):
                grad = grad + times(expand_two_back_ref[experts_rows(expert), :], pre_lows[expert])
            if group < 2:
                score = soft_back(probs_two[group], dq_two[group])
                score = jnp.concatenate([score, jnp.zeros_like(score)], axis=0).astype(jnp.bfloat16)
                score_two[group * 16 : group * 16 + 16, lanes] = score
                grad = grad + times(gate_two_back_ref[experts_rows(group), :], score)
            carried_grads.append(grad)

        dq_one = []
        for group in range(3):
            members = [2 * group, 2 * group + 1, 4, 5] if group < 2 else range(6)
            dq_one.append([sum_rows(kept_one[expert][3] * carried_grads[group]) for expert in members])
        pre_lows = []
        for expert in range(6):
            prob = probs_one[2][expert : expert + 1, :]
            upstream = prob * carried_grads[2]
            slant = prob * dq_one[2][expert]
            for task in range(2):
                if expert // 2 in (task, 2):
                    place = expert % 2 if expert < 4 else expert - 2
                    prob = probs_one[task][place : place + 1, :]
                    upstream = upstream + prob * carried_grads[task]
                    slant = slant + prob * dq_one[task][place]
            pre_lows.append(
                expert_down(
                    0, expert, kept_one[expert], upstream, slant, shrink_one_back_ref, out_one, pre_one
                )
            )
        scores_low = [soft_back(probs_one[group], dq_one[group]) for group in range(3)]
        score = jnp.concatenate(scores_low + [jnp.zeros_like(scores_low[0])], axis=0).astype(
            jnp.bfloat16
        )
        score_one[:, lanes] = score
        grad = times(gate_one_back_ref[...], score)
        for expert in range(6):
            grad = grad + times(
                expand_one_back_ref[expert * width : (expert + 1) * width, :], pre_lows[expert]
            )
        flipped_grad_ref[:, lanes] = grad
        return carry

    lax.fori_loop(0, events // span, span_step, 0)

    def put(row, value):
        grads_ref[row : row + value.shape[0], :] = value.astype(jnp.bfloat16)

    rows = 0
    biases = []
    for expert in range(6):
        both = over_events(input_keep[...], pre_one[experts_rows(expert), :])
        put(rows + expert * width, both[:width])
        biases.append(both[width : width + 1])
    rows += 6 * width
    for expert in range(6):
        both = over_events(active_one[expert * tall : (expert + 1) * tall, :], out_one[experts_rows(expert), :])
        put(rows + expert * hidden, both[:hidden])
        biases.append(both[hidden : hidden + 1])
    rows += 6 * hidden
    for expert in range(6):
        group = expert // 2
        both = over_events(carried_keep[group * tall : (group + 1) * tall, :], pre_two[experts_rows(expert), :])
        put(rows + expert * hidden, both[:hidden])
        biases.append(both[hidden : hidden + 1])
    rows += 6 * hidden
    for expert in range(6):
        both = over_events(active_two[expert * tall : (expert + 1) * tall, :], out_two[experts_rows(expert), :])
        put(rows + expert * hidden, both[:hidden])
        biases.append(both[hidden : hidden + 1])
    rows += 6 * hidden
    tower = []
    for task in range(2):
        tower.append(
            over_events(tower_keep[task * tall : (task + 1) * tall, :], first_keep[task * inner : (task + 1) * inner, :])
        )
    tower = jnp.concatenate(tower, axis=1)
    put(rows, tower[:hidden])
    biases.append(tower[hidden : hidden + 1])
    rows += hidden
    put(
        rows,
        jnp.concatenate(
            [
                over_events(
                    top_keep[task * narrow : (task + 1) * narrow, :],
                    tower_act_keep[task * inner : (task + 1) * inner, :],
                )
                for task in range(2)
            ],
            axis=1,
        ),
    )
    rows += narrow
    gates = over_events(score_one[...], flipped_ref[...])
    for start in range(0, width, hidden):
        put(rows, gates[:, start : start + hidden])
        rows += gates.shape[0]
    for task in range(2):
        put(
            rows,
            over_events(
                score_two[task * 16 : task * 16 + 16, :],
                carried_keep[task * tall : task * tall + hidden, :],
            ),
        )
        rows += 16
    tops = over_events(unit, top_keep[...])[:1]
    seen = over_events(unit, tail_keep[...])[:1]
    pieces = []
    for task in range(2):
        pieces.append(tops[:, task * narrow : (task + 1) * narrow])
        pieces.append(
            seen[:, 2 * task * narrow : (2 * task + 1) * narrow]
            + seen[:, (2 * task + 1) * narrow : (2 * task + 2) * narrow]
        )
    biases.append(jnp.concatenate(pieces, axis=1))
    gains = gain_keep[...]
    high = gains.astype(jnp.bfloat16)
    low = (gains - high.astype(jnp.float32)).astype(jnp.bfloat16)
    gains = (over_events(unit[:, :128], high) + over_events(unit[:, :128], low))[:1]
    for expert in range(12):
        biases.append(gains[:, experts_rows(expert)])
    biases = jnp.concatenate(biases, axis=0)
    extra = grads_ref.shape[0] - rows - biases.shape[0]
    put(rows, jnp.concatenate([biases, jnp.zeros((extra, hidden), jnp.float32)], axis=0))


def dense(flipped, weights, places, thin, cot, grad_rows):
    width, events = flipped.shape
    hidden = thin[0].shape[0]
    inner, narrow = 128, 64
    tall = hidden + ONES
    low = functools.partial(pltpu.VMEM, dtype=jnp.bfloat16)
    kept = (
        width + ONES,
        6 * tall,
        6 * hidden,
        6 * hidden,
        32,
        3 * tall,
        6 * tall,
        6 * hidden,
        6 * hidden,
        32,
        2 * tall,
        2 * inner,
        2 * inner,
        2 * narrow,
        4 * narrow,
    )
    scratch = [low((rows, events)) for rows in kept]
    scratch.append(pltpu.VMEM((12 * hidden, 128), jnp.float32))
    scratch += [low((6 * hidden, depth)) for depth in (width, hidden, hidden, hidden)]
    specs = [pl.BlockSpec(memory_space=pltpu.VMEM)] * (len(weights) + len(thin) + 2)
    if places is not None:
        scratch += [low((6 * depth, hidden)) for depth in (width, hidden, hidden, hidden)]
        specs[0] = pl.BlockSpec(memory_space=pltpu.SMEM)
    return pl.pallas_call(
        functools.partial(dense_body, places),
        out_shape=(
            jax.ShapeDtypeStruct((2, events), jnp.float32),
            jax.ShapeDtypeStruct((width, events), jnp.float32),
            jax.ShapeDtypeStruct((grad_rows, hidden), jnp.bfloat16),
        ),
        in_specs=specs,
        scratch_shapes=scratch,
        compiler_params=pltpu.CompilerParams(vmem_limit_bytes=VMEM_LIMIT),
        cost_estimate=pl.CostEstimate(
            flops=6 * events * hidden * (6 * (width + 3 * hidden) + 2 * inner),
            bytes_accessed=24 * 1024 * 1024,
            transcendentals=12 * events * hidden,
        ),
    )(*weights, flipped, *thin, cot)


def grad_layout(width, hidden):
    sizes = [6 * width, 6 * hidden, 6 * hidden, 6 * hidden]
    starts = [sum(sizes[:index]) for index in range(5)]
    return sizes, starts


def finish_body(
    bit_ref,
    own_a_ref,
    own_b_ref,
    came_a_ref,
    came_b_ref,
    low_expand_ref,
    low_inbias_ref,
    low_shrink_ref,
    low_outbias_ref,
    low_gain_ref,
    low_taskgate_ref,
    low_sharegate_ref,
    up_expand_ref,
    up_inbias_ref,
    up_shrink_ref,
    up_outbias_ref,
    up_gain_ref,
    up_taskgate_ref,
    inner_ref,
    tbias_ref,
    middle_ref,
    tail_ref,
):
    part = own_a_ref.shape[0]
    hidden = up_expand_ref.shape[1]
    width = low_expand_ref.shape[0] // 6
    inner = inner_ref.shape[1]
    narrow = middle_ref.shape[0]
    wide = (low_expand_ref, low_shrink_ref, up_expand_ref, up_shrink_ref)
    sizes, starts = grad_layout(width, hidden)
    block = 128

    def move(source, start, target, place, rows):
        def step(index, carry):
            target[pl.ds(pl.multiple_of(place + index * block, block), block), :] = source[
                pl.ds(pl.multiple_of(start + index * block, block), block), :
            ].astype(jnp.float32)
            return carry

        lax.fori_loop(0, rows // block, step, 0)

    def rest(source, start):
        def take(rows):
            nonlocal start
            start += rows
            return source[start - rows : start, :].astype(jnp.float32)

        both = take(hidden)
        inner_ref[:hidden, :] = both[:, :inner]
        inner_ref[hidden:, :] = both[:, inner:]
        both = take(narrow)
        middle_ref[...] = both
        for index in range(width // hidden):
            gates = take(32)
            span = slice(index * hidden, (index + 1) * hidden)
            low_taskgate_ref[:, span] = gates[0:4]
            low_taskgate_ref[:, width + index * hidden : width + (index + 1) * hidden] = gates[8:12]
            low_sharegate_ref[:, span] = gates[16:22]
        for task in range(2):
            up_taskgate_ref[:, task * hidden : (task + 1) * hidden] = take(16)[0:4]
        rows = take(48)
        flat = (low_inbias_ref, low_outbias_ref, up_inbias_ref, up_outbias_ref, tbias_ref, tail_ref)
        place = 0
        for target in flat + (low_gain_ref, up_gain_ref):
            for index in range(target.shape[0] // hidden):
                target[index * hidden : (index + 1) * hidden] = rows[place]
                place += 1

    def all_parts(pieces):
        for index, source in enumerate(pieces):
            first, last = index * part, (index + 1) * part
            for target, start, size in zip(wide, starts, sizes):
                low, high = max(first, start), min(last, start + size)
                if low < high:
                    move(source, low - first, target, low - start, high - low)
        rest(pieces[-1], starts[4] - (len(pieces) - 1) * part)

    @pl.when(bit_ref[0] == 0)
    def _():
        all_parts((own_a_ref, own_b_ref, came_a_ref, came_b_ref))

    @pl.when(bit_ref[0] != 0)
    def _():
        all_parts((came_a_ref, came_b_ref, own_a_ref, own_b_ref))


def finish(bit, own, came, width, hidden):
    shapes = (
        (6 * width, hidden),
        (6 * hidden,),
        (6 * hidden, hidden),
        (6 * hidden,),
        (6 * hidden,),
        (4, 2 * width),
        (6, width),
        (6 * hidden, hidden),
        (6 * hidden,),
        (6 * hidden, hidden),
        (6 * hidden,),
        (6 * hidden,),
        (4, 2 * hidden),
        (2 * hidden, 128),
        (256,),
        (64, 256),
        (256,),
    )
    done = pl.pallas_call(
        finish_body,
        out_shape=tuple(jax.ShapeDtypeStruct(shape, jnp.float32) for shape in shapes),
        in_specs=[pl.BlockSpec(memory_space=pltpu.SMEM)] + [pl.BlockSpec(memory_space=pltpu.VMEM)] * 4,
        compiler_params=pltpu.CompilerParams(vmem_limit_bytes=VMEM_LIMIT),
        cost_estimate=pl.CostEstimate(
            flops=0, bytes_accessed=12 * width * hidden * 16, transcendentals=0
        ),
    )(bit, *own, *came)
    return tuple(value.T if value.shape[0] in (4, 6, 64) else value for value in done)


def partners(mask, size):
    return [(index, index ^ mask) for index in range(size)]


def swap_with(values, mask, size):
    return lax.ppermute(values, "dp", partners(mask, size))


def halve(values, mask, place, size):
    rows = values.shape[0] // 2
    bit = jnp.where((place & mask) != 0, 1, 0)
    sent = lax.dynamic_slice_in_dim(values, (1 - bit) * rows, rows, 0)
    kept = lax.dynamic_slice_in_dim(values, bit * rows, rows, 0)
    came = swap_with(sent, mask, size)
    return (kept.astype(jnp.float32) + came.astype(jnp.float32)).astype(values.dtype)


def double(values, mask, place, size):
    came = swap_with(values, mask, size)
    upper = (place & mask) != 0
    return jnp.concatenate(
        [jnp.where(upper, came, values), jnp.where(upper, values, came)], axis=0
    )


def swap_groups(values, mask):
    return lax.ppermute(values, "fsdp", partners(mask, lax.axis_size("fsdp")))


def share(values):
    group = lax.axis_size("fsdp")
    place = lax.axis_index("fsdp")
    pieces = [values] + [swap_groups(values, mask) for mask in range(1, group)]
    return jnp.stack([pick(place ^ index, pieces) for index in range(group)])


def pick(index, pieces):
    chosen = pieces[0]
    for place in range(1, len(pieces)):
        chosen = jnp.where(index == place, pieces[place], chosen)
    return chosen


def scatter_sum(values):
    group = lax.axis_size("fsdp")
    place = lax.axis_index("fsdp")
    rows = values.shape[0] // group
    pieces = [
        lax.dynamic_slice_in_dim(values, (place ^ mask) * rows, rows, 0) for mask in range(group)
    ]
    pieces = pieces[:1] + [swap_groups(pieces[mask], mask) for mask in range(1, group)]
    total = pieces[0].astype(jnp.float32)
    for piece in pieces[1:]:
        total = total + piece.astype(jnp.float32)
    return total.astype(values.dtype)


def dp_masks(size):
    return [1 << index for index in range(size.bit_length() - 1)]


def dp_orders():
    first, *others = dp_masks(lax.axis_size("dp"))
    return first, [others, others[::-1]]


def spread(parts):
    size = lax.axis_size("dp")
    place = lax.axis_index("dp")
    first, orders = dp_orders()
    for step in reversed(range(len(orders[0]))):
        parts = [double(part, order[step], place, size) for part, order in zip(parts, orders)]
    return parts, [swap_with(part, first, size) for part in parts]


def arrival(order, first, group):
    devices = []
    for half in range(2):
        places = []
        for block in range(1 << len(order)):
            dp = half * first
            for index, mask in enumerate(order):
                if block >> (len(order) - 1 - index) & 1:
                    dp |= mask
            places += [dp * group + index for index in range(group)]
        devices.append(places)
    return devices


def in_order(own, came, bit, places, rows):
    whole = jnp.concatenate([jnp.where(bit == 0, own, came), jnp.where(bit == 0, came, own)], axis=0)
    whole = whole.reshape((-1, rows) + own.shape[1:])
    flat = places[0] + places[1]
    return jnp.stack([whole[flat.index(device)] for device in range(len(flat))])


def sum_grads(grads, flipped_grad, send, width, hidden):
    size = lax.axis_size("dp")
    place = lax.axis_index("dp")
    first, orders = dp_orders()
    mine = halve(grads, first, place, size)
    rows = mine.shape[0] // 2
    parts = [mine[:rows], mine[rows:]]
    parts, flipped_grad = lax.optimization_barrier((parts, flipped_grad))
    outgoing = send(flipped_grad)
    for step in range(len(orders[0])):
        parts = [halve(part, order[step], place, size) for part, order in zip(parts, orders)]
        if step == 0:
            parts, outgoing = lax.optimization_barrier((parts, outgoing))
    rows = parts[0].shape[0]
    summed = scatter_sum(jnp.concatenate([part.reshape((lax.axis_size("fsdp"), -1) + part.shape[1:]) for part in parts], axis=1).reshape((-1,) + grads.shape[1:]))
    shared = share(summed)
    parts = [
        piece.reshape((-1,) + grads.shape[1:]) for piece in jnp.split(shared, 2, axis=1)
    ]
    own, came = spread(parts)
    return finish((place & first).reshape(1), own, came, width, hidden), outgoing


def on_device(
    owner_ids,
    row_ids,
    embed_table,
    expandone,
    expbiasone,
    reduceone,
    redbiasone,
    normgainone,
    taskgateone,
    sharegateone,
    expandtwo,
    expbiastwo,
    reducetwo,
    redbiastwo,
    normgaintwo,
    taskgatetwo,
    towerinner,
    towerbias,
    towermiddle,
    towertail,
    logit_cot,
):
    devices = lax.axis_size(("dp", "fsdp"))
    events, fields = owner_ids.shape
    emb_width = embed_table.shape[1]
    capacity = 2 * events * fields // devices
    hidden = expandone.shape[1]
    width = fields * emb_width
    group = lax.axis_size("fsdp")
    owner_rows = owner_ids.T
    request, rank = assign_slots(owner_rows, row_ids.T, devices, capacity)
    asked_rows = lax.all_to_all(request, ("dp", "fsdp"), split_axis=0, concat_axis=0, tiled=True)

    thin = pack_thin(
        (expbiasone, redbiasone, normgainone, expbiastwo, redbiastwo, normgaintwo),
        towerbias,
        towertail,
        taskgateone.T,
        sharegateone.T,
        taskgatetwo.T,
        towerinner,
        towermiddle,
    )
    packed = jnp.concatenate([expandone, reduceone, expandtwo, reducetwo, thin], axis=0)
    packed = share(packed)
    shards = (expandone, reduceone, expandtwo, reducetwo)
    sizes = [shard.shape[0] for shard in shards]
    wide_rows = sum(sizes)
    thin = lax.all_gather(packed[:, wide_rows:], "dp", axis=0, tiled=True)
    thin = prep_thin(thin, width, hidden)
    first, orders = dp_orders()
    parts = [packed[:, : sizes[0]], packed[:, sizes[0] : wide_rows]]
    own, came = spread([part.reshape(-1, hidden) for part in parts])
    bit = (lax.axis_index("dp") & first).reshape(1)
    places = [arrival(order, first, group) for order in orders]
    if all(size % 16 == 0 for size in sizes):
        weights = (bit, *own, *came)
    else:
        whole = [
            in_order(mine, other, bit[0], place, part.shape[1])
            for mine, other, place, part in zip(own, came, places, parts)
        ]
        whole = jnp.concatenate(whole, axis=1)
        starts = [sum(sizes[:index]) for index in range(4)]
        weights = tuple(
            whole[:, start : start + size].reshape(-1, hidden) for start, size in zip(starts, sizes)
        )
        places = None

    found = find_rows(asked_rows, embed_table.T)
    returned = lax.all_to_all(found, ("dp", "fsdp"), split_axis=0, concat_axis=0, tiled=True)
    flipped = place_rows(returned, rank, owner_rows)
    chunk = 16 * devices
    grad_rows = -(-(6 * (width + 3 * hidden) + 2 * hidden) // chunk) * chunk
    logits, flipped_grad, grads = dense(flipped, weights, places, thin, logit_cot, grad_rows)

    def send(flipped_grad):
        return send_rows(flipped_grad, rank, owner_rows, capacity)

    done, outgoing = sum_grads(grads, flipped_grad, send, width, hidden)
    incoming = lax.all_to_all(outgoing, ("dp", "fsdp"), split_axis=0, concat_axis=0, tiled=True)
    table_grad = add_rows(incoming, asked_rows, embed_table.shape[0])
    return (logits, flipped_grad.T, table_grad.T, *done)


def solution(mesh):
    return jax.shard_map(
        on_device,
        mesh=mesh,
        in_specs=(
            P(("dp", "fsdp"), None),
            P(("dp", "fsdp"), None),
            P(("dp", "fsdp"), None),
            P(("dp", "fsdp"), None),
            P(("dp", "fsdp")),
            P(("dp", "fsdp"), None),
            P(("dp", "fsdp")),
            P(("dp", "fsdp")),
            P(("dp", "fsdp"), None),
            P(("dp", "fsdp"), None),
            P(("dp", "fsdp"), None),
            P(("dp", "fsdp")),
            P(("dp", "fsdp"), None),
            P(("dp", "fsdp")),
            P(("dp", "fsdp")),
            P(("dp", "fsdp"), None),
            P(("dp", "fsdp"), None),
            P(("dp", "fsdp")),
            P(("dp", "fsdp"), None),
            P(("dp", "fsdp")),
            P(None, ("dp", "fsdp")),
        ),
        out_specs=(
            P(None, ("dp", "fsdp")),
            P(("dp", "fsdp"), None),
            P(("dp", "fsdp"), None),
            P(),
            P(),
            P(),
            P(),
            P(),
            P(),
            P(),
            P(),
            P(),
            P(),
            P(),
            P(),
            P(),
            P(),
            P(),
            P(),
            P(),
        ),
        check_vma=False,
    )
```

```python
import functools

import jax
import jax.numpy as jnp
from jax import lax
from jax.experimental import pallas as pl
from jax.experimental.pallas import tpu as pltpu
from jax.sharding import PartitionSpec as P

EPS = 1e-05
VMEM_LIMIT = 56 * 1024 * 1024
ROW_BLOCKS = 8


def local_kernel(body, out_shape, flops, moved, scratch=()):
    return pl.pallas_call(
        body,
        out_shape=out_shape,
        scratch_shapes=list(scratch),
        compiler_params=pltpu.CompilerParams(vmem_limit_bytes=VMEM_LIMIT),
        cost_estimate=pl.CostEstimate(flops=flops, bytes_accessed=moved, transcendentals=0),
    )


def one_hot(hit):
    return jnp.where(hit, 1.0, 0.0).astype(jnp.bfloat16)


def iota(shape, axis):
    return lax.broadcasted_iota(jnp.int32, shape, axis)


def slot_body(owner_ref, row_ref, request_ref, rank_ref):
    fields, events = owner_ref.shape
    devices, _, capacity = request_ref.shape
    place = iota((devices, events), 0)
    asked = jnp.zeros((devices, events), jnp.float32)
    for field in range(fields):
        asked = asked + jnp.where(owner_ref[field : field + 1, :] == place, 1.0, 0.0)
    earlier = one_hot(iota((events, events), 0) < iota((events, events), 1))
    rank = jnp.dot(asked.astype(jnp.bfloat16), earlier, preferred_element_type=jnp.float32)
    rank = jnp.where(asked > 0.5, rank.astype(jnp.int32), -1)
    rank_ref[...] = rank
    slots = iota((capacity, events), 0)
    total = jnp.zeros((2 * devices, capacity), jnp.float32)
    for field in range(fields):
        mine = owner_ref[field : field + 1, :] == place
        field_rank = jnp.max(jnp.where(mine, rank, -1).astype(jnp.float32), axis=0, keepdims=True)
        rows = row_ref[field : field + 1, :]
        high = jnp.where(mine, (rows >> 6).astype(jnp.float32), 0.0)
        low = jnp.where(mine, (rows & 63).astype(jnp.float32), 0.0)
        value = jnp.concatenate([high, low], axis=0).astype(jnp.bfloat16)
        total = total + lax.dot_general(
            value,
            one_hot(field_rank.astype(jnp.int32) == slots),
            (((1,), (1,)), ((), ())),
            preferred_element_type=jnp.float32,
        )
    request = (total[:devices] * 64.0 + total[devices:]).astype(jnp.int32)
    for owner in range(devices):
        request_ref[owner] = request[owner : owner + 1]


def assign_slots(owner_rows, row_rows, devices, capacity):
    fields, events = owner_rows.shape
    return local_kernel(
        slot_body,
        (
            jax.ShapeDtypeStruct((devices, 1, capacity), jnp.int32),
            jax.ShapeDtypeStruct((devices, events), jnp.int32),
        ),
        2 * devices * events * (events + 2 * fields * capacity),
        4 * events * (2 * fields + devices),
    )(owner_rows, row_rows)


def find_body(request_ref, table_ref, found_ref, wide_ref):
    devices, _, capacity = request_ref.shape
    width = table_ref.shape[0]
    span = wide_ref.shape[1]
    places = iota((span, capacity), 0)
    for index in range(ROW_BLOCKS):
        wide_ref[index * width : (index + 1) * width, :] = table_ref[
            :, index * span : (index + 1) * span
        ]

    def step(source, carry):
        rows = request_ref[source]
        block = rows // span
        hits = one_hot(rows - block * span == places)
        rows_all = jnp.dot(wide_ref[...], hits, preferred_element_type=jnp.float32)
        picked = jnp.zeros((width, capacity), jnp.float32)
        for index in range(ROW_BLOCKS):
            picked = jnp.where(
                block == index, rows_all[index * width : (index + 1) * width, :], picked
            )
        found_ref[source] = picked.astype(jnp.bfloat16)
        return carry

    lax.fori_loop(0, devices, step, 0, unroll=2)


def find_rows(request, table):
    devices, _, capacity = request.shape
    width, rows = table.shape
    return local_kernel(
        find_body,
        jax.ShapeDtypeStruct((devices, width, capacity), jnp.bfloat16),
        2 * devices * capacity * rows * width,
        2 * (rows * width + devices * capacity * width),
        [pltpu.VMEM((ROW_BLOCKS * width, rows // ROW_BLOCKS), jnp.bfloat16)],
    )(request, table)


def place_body(found_ref, rank_ref, owner_ref, flipped_ref, total_ref):
    devices, width, capacity = found_ref.shape
    fields, events = owner_ref.shape
    slots = iota((capacity, events), 0)
    group = 4
    total_ref[...] = jnp.zeros_like(total_ref)

    def step(start, carry):
        pieces = []
        for index in range(group):
            owner = start * group + index
            hits = one_hot(rank_ref[pl.ds(owner, 1), :] == slots)
            pieces.append(jnp.dot(found_ref[owner], hits, preferred_element_type=jnp.float32))
        for field in range(fields):
            rows = slice(field * width, (field + 1) * width)
            owners = owner_ref[field : field + 1, :]
            value = total_ref[rows, :]
            for index in range(group):
                value = jnp.where(owners == start * group + index, pieces[index], value)
            total_ref[rows, :] = value
        return carry

    lax.fori_loop(0, devices // group, step, 0)
    flipped_ref[...] = total_ref[...].astype(jnp.bfloat16)


def place_rows(found, rank, owner_rows):
    devices, width, capacity = found.shape
    fields, events = owner_rows.shape
    return local_kernel(
        place_body,
        jax.ShapeDtypeStruct((fields * width, events), jnp.bfloat16),
        2 * devices * width * capacity * events,
        2 * (devices * width * capacity + fields * width * events),
        [pltpu.VMEM((fields * width, events), jnp.float32)],
    )(found, rank, owner_rows)


def send_body(grad_ref, rank_ref, owner_ref, sent_ref, low_ref):
    devices, width, capacity = sent_ref.shape
    fields, events = owner_ref.shape
    slots = iota((capacity, events), 0)
    low_ref[...] = grad_ref[...].astype(jnp.bfloat16).astype(jnp.float32)

    def step(owner, carry):
        chosen = jnp.zeros((width, events), jnp.float32)
        for field in range(fields):
            rows = slice(field * width, (field + 1) * width)
            chosen = jnp.where(owner_ref[field : field + 1, :] == owner, low_ref[rows, :], chosen)
        hits = one_hot(rank_ref[pl.ds(owner, 1), :] == slots)
        sent_ref[owner] = lax.dot_general(
            chosen.astype(jnp.bfloat16),
            hits,
            (((1,), (1,)), ((), ())),
            preferred_element_type=jnp.float32,
        ).astype(jnp.bfloat16)
        return carry

    lax.fori_loop(0, devices, step, 0, unroll=2)


def send_rows(grad, rank, owner_rows, capacity):
    devices = rank.shape[0]
    fields, events = owner_rows.shape
    width = grad.shape[0] // fields
    return local_kernel(
        send_body,
        jax.ShapeDtypeStruct((devices, width, capacity), jnp.bfloat16),
        2 * devices * width * capacity * events,
        2 * (devices * width * capacity + 2 * fields * width * events),
        [pltpu.VMEM((fields * width, events), jnp.float32)],
    )(grad, rank, owner_rows)


def add_body(came_ref, request_ref, out_ref, total_ref):
    devices, width, capacity = came_ref.shape
    span = total_ref.shape[1]
    group = 4
    places = iota((span, capacity), 0)
    total_ref[...] = jnp.zeros_like(total_ref)

    def step(start, carry):
        hits = []
        spread = []
        for index in range(group):
            source = start * group + index
            rows = request_ref[source]
            block = rows // span
            hits.append(one_hot(rows - block * span == places))
            came = came_ref[source].astype(jnp.float32)
            spread.append(
                jnp.concatenate(
                    [jnp.where(block == part, came, 0.0) for part in range(ROW_BLOCKS)], axis=0
                ).astype(jnp.bfloat16)
            )
        total_ref[...] += lax.dot_general(
            jnp.concatenate(spread, axis=1),
            jnp.concatenate(hits, axis=1),
            (((1,), (1,)), ((), ())),
            preferred_element_type=jnp.float32,
        )
        return carry

    lax.fori_loop(0, devices // group, step, 0)
    for index in range(ROW_BLOCKS):
        out_ref[:, index * span : (index + 1) * span] = total_ref[
            index * width : (index + 1) * width, :
        ]


def add_rows(came, request, rows):
    devices, width, capacity = came.shape
    span = rows // ROW_BLOCKS
    return local_kernel(
        add_body,
        jax.ShapeDtypeStruct((width, rows), jnp.float32),
        2 * devices * capacity * rows * width,
        2 * devices * width * capacity + 4 * rows * width,
        [pltpu.VMEM((ROW_BLOCKS * width, span), jnp.float32)],
    )(came, request)


THIN_ROWS = 48


def pack_thin_body(*refs):
    *biases, tbias, tail, taskgate, sharegate, upgate, inner, middle = refs[:13]
    *wide, out_ref, hold = refs[13:]
    hold[...] = jnp.zeros_like(hold)
    for row, piece in enumerate(biases + [tbias, tail]):
        hold[row : row + 1, : piece.shape[0]] = piece[...].astype(jnp.float32).reshape(1, -1)
    for row, piece in ((8, taskgate), (16, sharegate), (24, upgate), (32, inner)):
        hold[row : row + piece.shape[0], : piece.shape[1]] = piece[...].astype(jnp.float32)
    hold[32 : 32 + middle.shape[0], 128 : 128 + middle.shape[1]] = middle[...].astype(jnp.float32)
    thin = hold[...].astype(jnp.bfloat16)
    if not wide:
        out_ref[...] = thin
    start = 0
    for index, piece in enumerate(wide):
        out_ref[start : start + piece.shape[0], :] = piece[...]
        start += piece.shape[0]
        if index == 0:
            out_ref[start : start + THIN_ROWS, :] = thin
            start += THIN_ROWS


def pack(biases, others, wide):
    aligned = all(piece.shape[0] % 16 == 0 for piece in wide)
    rows = THIN_ROWS + (sum(piece.shape[0] for piece in wide) if aligned else 0)
    packed = local_kernel(
        pack_thin_body,
        jax.ShapeDtypeStruct((rows, 256), jnp.bfloat16),
        0,
        rows * 1024,
        [pltpu.VMEM((THIN_ROWS, 256), jnp.float32)],
    )(*biases, *others, *(wide if aligned else ()))
    if aligned:
        return packed
    return jnp.concatenate([wide[0], packed, *wide[1:]], axis=0)


def prep_thin_body(
    places,
    bit_ref,
    own_ref,
    came_ref,
    columns_ref,
    gate_one_ref,
    gate_one_back_ref,
    gate_two_ref,
    gate_two_back_ref,
    inner_ref,
    inner_back_ref,
    middle_ref,
    middle_back_ref,
    rows,
    task_rows,
    share_rows,
    up_rows,
    inner_rows,
    middle_rows,
):
    devices = 2 * len(places[0])
    shard = own_ref.shape[0] // len(places[0])
    hidden = columns_ref.shape[0]
    width = gate_one_ref.shape[1]

    def lay(target, source, index, count):
        target[:, index * count : (index + 1) * count] = source[:, :count]

    rows[...] = jnp.zeros_like(rows)
    task_rows[...] = jnp.zeros_like(task_rows)
    share_rows[...] = jnp.zeros_like(share_rows)
    up_rows[...] = jnp.zeros_like(up_rows)
    bias = 6 * hidden // devices
    flat = hidden // devices

    def unpack(pieces):
        for half, source in enumerate(pieces):
            for block, index in enumerate(places[half]):
                end = (block + 1) * shard
                thin = source[end - THIN_ROWS : end, :].astype(jnp.float32)
                rows[0:6, index * bias : (index + 1) * bias] = thin[0:6, :bias]
                rows[6:8, index * flat : (index + 1) * flat] = thin[6:8, :flat]
                lay(task_rows, thin[8:16], index, 2 * width // devices)
                lay(share_rows, thin[16:24], index, width // devices)
                lay(up_rows, thin[24:32], index, 2 * hidden // devices)
                count = 2 * hidden // devices
                inner_rows[index * count : (index + 1) * count, :] = thin[32 : 32 + count, :128]
                count = hidden // devices
                middle_rows[index * count : (index + 1) * count, :] = thin[32 : 32 + count, 128:192]

    @pl.when(bit_ref[0] == 0)
    def _():
        unpack((own_ref, came_ref))

    @pl.when(bit_ref[0] != 0)
    def _():
        unpack((came_ref, own_ref))

    columns_ref[...] = jnp.zeros_like(columns_ref)
    for expert in range(6):
        columns_ref[:, expert * 8 : expert * 8 + 8] = rows[:, expert * hidden : (expert + 1) * hidden].T
    gates = jnp.concatenate(
        [
            task_rows[:, :width],
            task_rows[:, width:],
            share_rows[...],
            jnp.zeros((8, width), jnp.float32),
        ],
        axis=0,
    )
    gate_one_ref[...] = gates.astype(jnp.bfloat16)
    gate_one_back_ref[...] = gates.T.astype(jnp.bfloat16)
    gate_two_ref[...] = jnp.concatenate([up_rows[:, :hidden], up_rows[:, hidden:]], axis=0).astype(
        jnp.bfloat16
    )
    for task in range(2):
        span = slice(task * hidden, (task + 1) * hidden)
        wide = jnp.concatenate([up_rows[:, span], jnp.zeros((8, hidden), jnp.float32)], axis=0)
        gate_two_back_ref[span, :] = wide.T.astype(jnp.bfloat16)
        inner_ref[task * 128 : (task + 1) * 128, :] = inner_rows[span, :].T.astype(jnp.bfloat16)
        span = slice(task * 128, (task + 1) * 128)
        middle_ref[task * 64 : (task + 1) * 64, :] = middle_rows[span, :].T.astype(jnp.bfloat16)
    inner_back_ref[...] = inner_rows[...].astype(jnp.bfloat16)
    middle_back_ref[...] = middle_rows[...].astype(jnp.bfloat16)


def prep_thin(bit, own, came, places, width, hidden):
    low = functools.partial(jax.ShapeDtypeStruct, dtype=jnp.bfloat16)
    return pl.pallas_call(
        functools.partial(prep_thin_body, places),
        out_shape=(
            jax.ShapeDtypeStruct((hidden, 64), jnp.float32),
            low((32, width)),
            low((width, 32)),
            low((16, hidden)),
            low((2 * hidden, 16)),
            low((hidden, hidden)),
            low((2 * hidden, 128)),
            low((128, 128)),
            low((hidden, 64)),
        ),
        in_specs=[pl.BlockSpec(memory_space=pltpu.SMEM)] + [pl.BlockSpec(memory_space=pltpu.VMEM)] * 2,
        scratch_shapes=[
            pltpu.VMEM((8, 6 * hidden), jnp.float32),
            pltpu.VMEM((8, 2 * width), jnp.float32),
            pltpu.VMEM((8, width), jnp.float32),
            pltpu.VMEM((8, 2 * hidden), jnp.float32),
            pltpu.VMEM((2 * hidden, 128), jnp.float32),
            pltpu.VMEM((hidden, 64), jnp.float32),
        ],
        compiler_params=pltpu.CompilerParams(vmem_limit_bytes=VMEM_LIMIT),
        cost_estimate=pl.CostEstimate(flops=0, bytes_accessed=4 * own.size, transcendentals=0),
    )(bit, own, came)


SPAN = 256
ONES = 16


def over_events(left, right):
    return lax.dot_general(left, right, (((1,), (1,)), ((), ())), preferred_element_type=jnp.float32)


def times(left, right):
    return jnp.dot(left, right, preferred_element_type=jnp.float32)


def sum_rows(values):
    return jnp.sum(values, axis=0, keepdims=True)


def sigmoid_of(values):
    return 0.5 * jnp.tanh(0.5 * values) + 0.5


def silu_parts(values):
    sig = sigmoid_of(values)
    active = values * sig
    return active, sig + active * (1.0 - sig)


def expert_up(inputs, expand, expbias, shrink, shrinkbias):
    active, slope = silu_parts(times(expand, inputs) + expbias)
    active = active.astype(jnp.bfloat16)
    output = times(shrink, active) + shrinkbias
    scale = 1.0 / output.shape[0]
    centered = output - sum_rows(output) * scale
    inverse = lax.rsqrt(sum_rows(centered * centered) * scale + EPS)
    return active, slope, centered * inverse, inverse


def soft(scores, count):
    valid = iota(scores.shape, 0) < count
    scores = jnp.where(valid, scores, -1e30)
    shifted = jnp.exp(scores - jnp.max(scores, axis=0, keepdims=True))
    shifted = jnp.where(valid, shifted, 0.0)
    return shifted / sum_rows(shifted)


def soft_back(probs, rows):
    tall = jnp.concatenate(rows + [jnp.zeros_like(rows[0])] * (probs.shape[0] - len(rows)), axis=0)
    return probs * (tall - sum_rows(probs * tall))


def assemble(bit, own_ref, came_ref, homes, places, blocks):
    rows = own_ref.shape[0] // blocks
    sizes = [home.shape[0] // (2 * blocks) for home in homes]

    def lay(pieces):
        for half, source in enumerate(pieces):
            for block in range(blocks):
                start = block * rows
                for home, size in zip(homes, sizes):
                    target = places[half][block] * size
                    home[target : target + size, :] = source[start : start + size, :]
                    start += size

    @pl.when(bit == 0)
    def _():
        lay((own_ref, came_ref))

    @pl.when(bit != 0)
    def _():
        lay((came_ref, own_ref))


def dense_body(places, *refs):
    bit_ref, *refs = refs
    if places is None:
        *naturals, refs = *refs[:4], refs[4:]
    else:
        own_a, own_b, came_a, came_b, *refs = refs
        naturals, refs = refs[-4:], refs[:-4]
    expand_one_back_ref, shrink_one_back_ref, expand_two_back_ref, shrink_two_back_ref = naturals
    (
        flipped_ref,
        columns_ref,
        gate_one_ref,
        gate_one_back_ref,
        gate_two_ref,
        gate_two_back_ref,
        inner_ref,
        inner_back_ref,
        middle_ref,
        middle_back_ref,
        cot_ref,
        logits_ref,
        flipped_grad_ref,
        kept_ref,
        sent_ref,
        sems,
        grads_ref,
        input_keep,
        active_one,
        out_one,
        pre_one,
        score_one,
        carried_keep,
        active_two,
        out_two,
        pre_two,
        score_two,
        tower_keep,
        tower_act_keep,
        first_keep,
        top_keep,
        tail_keep,
        gain_keep,
        expand_one_ref,
        shrink_one_ref,
        expand_two_ref,
        shrink_two_ref,
    ) = refs
    bit = jnp.minimum(bit_ref[0], 1)
    if places is not None:
        blocks = len(places[0][0])
        assemble(bit, own_a, came_a, [expand_one_back_ref], places[0], blocks)
        assemble(
            bit,
            own_b,
            came_b,
            [shrink_one_back_ref, expand_two_back_ref, shrink_two_back_ref],
            places[1],
            blocks,
        )
    for natural, turned in (
        (expand_one_back_ref, expand_one_ref),
        (shrink_one_back_ref, shrink_one_ref),
        (expand_two_back_ref, expand_two_ref),
        (shrink_two_back_ref, shrink_two_ref),
    ):
        depth = natural.shape[0] // 6
        across = natural.shape[1]
        for expert in range(6):
            turned[expert * across : (expert + 1) * across, :] = natural[
                expert * depth : (expert + 1) * depth, :
            ].T

    width, events = flipped_ref.shape
    hidden = shrink_one_back_ref.shape[1]
    inner = inner_ref.shape[0] // 2
    narrow = middle_ref.shape[0] // 2
    tall = hidden + ONES
    span = min(SPAN, events)
    unit = jnp.ones((ONES, events), jnp.bfloat16)

    input_keep[:width, :] = flipped_ref[...]
    input_keep[width:, :] = unit
    for expert in range(6):
        active_one[expert * tall + hidden : (expert + 1) * tall, :] = unit
        active_two[expert * tall + hidden : (expert + 1) * tall, :] = unit
    for group in range(3):
        carried_keep[group * tall + hidden : (group + 1) * tall, :] = unit
    for task in range(2):
        tower_keep[task * tall + hidden : (task + 1) * tall, :] = unit
    gain_keep[...] = jnp.zeros_like(gain_keep)

    def column(index, rows=hidden, start=0):
        return columns_ref[start : start + rows, index : index + 1]

    def experts_rows(expert):
        return slice(expert * hidden, (expert + 1) * hidden)

    def span_step(step, carry):
        lanes = pl.ds(pl.multiple_of(step * span, span), span)
        inputs = flipped_ref[:, lanes]

        def up(level, inputs_of, expand_ref, shrink_ref, active_keep):
            kept = []
            for expert in range(6):
                active, slope, normed, inverse = expert_up(
                    inputs_of(expert),
                    expand_ref[experts_rows(expert), :],
                    column(expert * 8 + level),
                    shrink_ref[experts_rows(expert), :],
                    column(expert * 8 + level + 1),
                )
                active_keep[expert * tall : expert * tall + hidden, lanes] = active
                kept.append((slope, normed, inverse, normed * column(expert * 8 + level + 2)))
            return kept

        kept_one = up(0, lambda expert: inputs, expand_one_ref, shrink_one_ref, active_one)
        scores = times(gate_one_ref[...], inputs)
        probs_one = [soft(scores[0:8], 4), soft(scores[8:16], 4), soft(scores[16:24], 6)]
        carried = []
        for group in range(3):
            members = [2 * group, 2 * group + 1, 4, 5] if group < 2 else range(6)
            mixed = 0.0
            for place, expert in enumerate(members):
                mixed = mixed + probs_one[group][place : place + 1, :] * kept_one[expert][3]
            carried.append(mixed.astype(jnp.bfloat16))
            carried_keep[group * tall : group * tall + hidden, lanes] = carried[group]

        kept_two = up(
            3, lambda expert: carried[expert // 2], expand_two_ref, shrink_two_ref, active_two
        )
        probs_two = []
        tower_grads = []
        dq_two = []
        for task in range(2):
            probs = soft(times(gate_two_ref[task * 8 : task * 8 + 8, :], carried[task]), 4)
            probs_two.append(probs)
            members = [2 * task, 2 * task + 1, 4, 5]
            mixed = 0.0
            for place, expert in enumerate(members):
                mixed = mixed + probs[place : place + 1, :] * kept_two[expert][3]
            mixed = mixed.astype(jnp.bfloat16)
            tower_keep[task * tall : task * tall + hidden, lanes] = mixed
            first, first_slope = silu_parts(
                times(inner_ref[task * inner : (task + 1) * inner, :], mixed)
                + column(6, inner, task * inner)
            )
            first = first.astype(jnp.bfloat16)
            tower_act_keep[task * inner : (task + 1) * inner, lanes] = first
            top, top_slope = silu_parts(
                times(middle_ref[task * narrow : (task + 1) * narrow, :], first)
                + column(7, narrow, 2 * task * narrow)
            )
            weight = column(7, narrow, (2 * task + 1) * narrow)
            logits_ref[task : task + 1, lanes] = sum_rows(top * weight)
            cot = cot_ref[task : task + 1, lanes]
            top_grad = (cot * weight * top_slope).astype(jnp.bfloat16)
            top_keep[task * narrow : (task + 1) * narrow, lanes] = top_grad
            seen = cot * top
            high = seen.astype(jnp.bfloat16)
            tail_keep[2 * task * narrow : (2 * task + 1) * narrow, lanes] = high
            tail_keep[(2 * task + 1) * narrow : (2 * task + 2) * narrow, lanes] = (
                seen - high.astype(jnp.float32)
            ).astype(jnp.bfloat16)
            first_grad = (
                times(middle_back_ref[task * inner : (task + 1) * inner, :], top_grad) * first_slope
            ).astype(jnp.bfloat16)
            first_keep[task * inner : (task + 1) * inner, lanes] = first_grad
            grad = times(inner_back_ref[task * hidden : (task + 1) * hidden, :], first_grad)
            tower_grads.append(grad)
            dq_two.append([sum_rows(kept_two[expert][3] * grad) for expert in members])

        def expert_down(level, expert, kept, upstream, slant, shrink_back_ref, out_keep, pre_keep):
            slope, normed, inverse, _ = kept
            gained = upstream * normed
            part = gained[:, :128]
            for start in range(128, span, 128):
                part = part + gained[:, start : start + 128]
            gain_rows = slice((level + expert) * hidden, (level + expert + 1) * hidden)
            gain_keep[gain_rows, :] += part
            scaled = upstream * column(expert * 8 + level // 2 + 2)
            scale = 1.0 / hidden
            out_low = (
                inverse * (scaled - sum_rows(scaled) * scale - normed * (slant * scale))
            ).astype(jnp.bfloat16)
            out_keep[experts_rows(expert), lanes] = out_low
            pre_low = (times(shrink_back_ref[experts_rows(expert), :], out_low) * slope).astype(
                jnp.bfloat16
            )
            pre_keep[experts_rows(expert), lanes] = pre_low
            return pre_low

        pre_lows = []
        for expert in range(6):
            if expert < 4:
                task, place = expert // 2, expert % 2
                prob = probs_two[task][place : place + 1, :]
                upstream = prob * tower_grads[task]
                slant = prob * dq_two[task][place]
            else:
                place = expert - 2
                prob = [probs_two[task][place : place + 1, :] for task in range(2)]
                upstream = prob[0] * tower_grads[0] + prob[1] * tower_grads[1]
                slant = prob[0] * dq_two[0][place] + prob[1] * dq_two[1][place]
            pre_lows.append(
                expert_down(
                    6, expert, kept_two[expert], upstream, slant, shrink_two_back_ref, out_two, pre_two
                )
            )
        carried_grads = []
        for group in range(3):
            grad = 0.0
            for expert in (2 * group, 2 * group + 1):
                grad = grad + times(expand_two_back_ref[experts_rows(expert), :], pre_lows[expert])
            if group < 2:
                score = soft_back(probs_two[group], dq_two[group])
                score = jnp.concatenate([score, jnp.zeros_like(score)], axis=0).astype(jnp.bfloat16)
                score_two[group * 16 : group * 16 + 16, lanes] = score
                grad = grad + times(gate_two_back_ref[experts_rows(group), :], score)
            carried_grads.append(grad)

        dq_one = []
        for group in range(3):
            members = [2 * group, 2 * group + 1, 4, 5] if group < 2 else range(6)
            dq_one.append([sum_rows(kept_one[expert][3] * carried_grads[group]) for expert in members])
        pre_lows = []
        for expert in range(6):
            prob = probs_one[2][expert : expert + 1, :]
            upstream = prob * carried_grads[2]
            slant = prob * dq_one[2][expert]
            for task in range(2):
                if expert // 2 in (task, 2):
                    place = expert % 2 if expert < 4 else expert - 2
                    prob = probs_one[task][place : place + 1, :]
                    upstream = upstream + prob * carried_grads[task]
                    slant = slant + prob * dq_one[task][place]
            pre_lows.append(
                expert_down(
                    0, expert, kept_one[expert], upstream, slant, shrink_one_back_ref, out_one, pre_one
                )
            )
        scores_low = [soft_back(probs_one[group], dq_one[group]) for group in range(3)]
        score = jnp.concatenate(scores_low + [jnp.zeros_like(scores_low[0])], axis=0).astype(
            jnp.bfloat16
        )
        score_one[:, lanes] = score
        grad = times(gate_one_back_ref[...], score)
        for expert in range(6):
            grad = grad + times(
                expand_one_back_ref[expert * width : (expert + 1) * width, :], pre_lows[expert]
            )
        flipped_grad_ref[:, lanes] = grad
        return carry

    lax.fori_loop(0, events // span, span_step, 0)

    half_rows = grads_ref.shape[1]

    def put(row, value):
        while value.shape[0]:
            half, start = row // half_rows, row % half_rows
            count = min(value.shape[0], half_rows - start)
            grads_ref[half, start : start + count, :] = value[:count].astype(jnp.bfloat16)
            row, value = row + count, value[count:]

    rows = 0
    biases = []
    for expert in range(6):
        both = over_events(input_keep[...], pre_one[experts_rows(expert), :])
        put(rows + expert * width, both[:width])
        biases.append(both[width : width + 1])
    rows += 6 * width
    for expert in range(6):
        both = over_events(active_one[expert * tall : (expert + 1) * tall, :], out_one[experts_rows(expert), :])
        put(rows + expert * hidden, both[:hidden])
        biases.append(both[hidden : hidden + 1])
    rows += 6 * hidden
    for expert in range(6):
        group = expert // 2
        both = over_events(carried_keep[group * tall : (group + 1) * tall, :], pre_two[experts_rows(expert), :])
        put(rows + expert * hidden, both[:hidden])
        biases.append(both[hidden : hidden + 1])
    rows += 6 * hidden
    for expert in range(6):
        both = over_events(active_two[expert * tall : (expert + 1) * tall, :], out_two[experts_rows(expert), :])
        put(rows + expert * hidden, both[:hidden])
        biases.append(both[hidden : hidden + 1])
    rows += 6 * hidden
    tower = []
    for task in range(2):
        tower.append(
            over_events(tower_keep[task * tall : (task + 1) * tall, :], first_keep[task * inner : (task + 1) * inner, :])
        )
    tower = jnp.concatenate(tower, axis=1)
    put(rows, tower[:hidden])
    biases.append(tower[hidden : hidden + 1])
    rows += hidden
    put(
        rows,
        jnp.concatenate(
            [
                over_events(
                    top_keep[task * narrow : (task + 1) * narrow, :],
                    tower_act_keep[task * inner : (task + 1) * inner, :],
                )
                for task in range(2)
            ],
            axis=1,
        ),
    )
    rows += narrow
    gates = over_events(score_one[...], flipped_ref[...])
    for start in range(0, width, hidden):
        put(rows, gates[:, start : start + hidden])
        rows += gates.shape[0]
    for task in range(2):
        put(
            rows,
            over_events(
                score_two[task * 16 : task * 16 + 16, :],
                carried_keep[task * tall : task * tall + hidden, :],
            ),
        )
        rows += 16
    tops = over_events(unit, top_keep[...])[:1]
    seen = over_events(unit, tail_keep[...])[:1]
    pieces = []
    for task in range(2):
        pieces.append(tops[:, task * narrow : (task + 1) * narrow])
        pieces.append(
            seen[:, 2 * task * narrow : (2 * task + 1) * narrow]
            + seen[:, (2 * task + 1) * narrow : (2 * task + 2) * narrow]
        )
    biases.append(jnp.concatenate(pieces, axis=1))
    gains = gain_keep[...]
    high = gains.astype(jnp.bfloat16)
    low = (gains - high.astype(jnp.float32)).astype(jnp.bfloat16)
    gains = (over_events(unit[:, :128], high) + over_events(unit[:, :128], low))[:1]
    for expert in range(12):
        biases.append(gains[:, experts_rows(expert)])
    biases = jnp.concatenate(biases, axis=0)
    extra = 2 * half_rows - rows - biases.shape[0]
    put(rows, jnp.concatenate([biases, jnp.zeros((extra, hidden), jnp.float32)], axis=0))
    copies = [
        pltpu.make_async_copy(grads_ref.at[1 - bit], sent_ref, sems.at[0]),
        pltpu.make_async_copy(grads_ref.at[bit], kept_ref, sems.at[1]),
    ]
    for copy in copies:
        copy.start()
    for copy in copies:
        copy.wait()


def dense(bit, flipped, weights, places, thin, cot, grad_rows):
    width, events = flipped.shape
    hidden = thin[0].shape[0]
    inner, narrow = 128, 64
    tall = hidden + ONES
    low = functools.partial(pltpu.VMEM, dtype=jnp.bfloat16)
    kept = (
        width + ONES,
        6 * tall,
        6 * hidden,
        6 * hidden,
        32,
        3 * tall,
        6 * tall,
        6 * hidden,
        6 * hidden,
        32,
        2 * tall,
        2 * inner,
        2 * inner,
        2 * narrow,
        4 * narrow,
    )
    half = (grad_rows // 2, hidden)
    scratch = [pltpu.SemaphoreType.DMA((2,)), low((2,) + half)]
    scratch += [low((rows, events)) for rows in kept]
    scratch.append(pltpu.VMEM((12 * hidden, 128), jnp.float32))
    scratch += [low((6 * hidden, depth)) for depth in (width, hidden, hidden, hidden)]
    vmem = pl.BlockSpec(memory_space=pltpu.VMEM)
    outside = pl.BlockSpec(memory_space=pl.ANY)
    specs = [pl.BlockSpec(memory_space=pltpu.SMEM)] + [vmem] * (len(weights) + len(thin) + 2)
    if places is not None:
        scratch += [low((6 * depth, hidden)) for depth in (width, hidden, hidden, hidden)]
    return pl.pallas_call(
        functools.partial(dense_body, places),
        out_shape=(
            jax.ShapeDtypeStruct((2, events), jnp.float32),
            jax.ShapeDtypeStruct((width, events), jnp.float32),
            jax.ShapeDtypeStruct(half, jnp.bfloat16),
            jax.ShapeDtypeStruct(half, jnp.bfloat16),
        ),
        in_specs=specs,
        out_specs=(vmem, vmem, outside, outside),
        scratch_shapes=scratch,
        compiler_params=pltpu.CompilerParams(vmem_limit_bytes=VMEM_LIMIT),
        cost_estimate=pl.CostEstimate(
            flops=6 * events * hidden * (6 * (width + 3 * hidden) + 2 * inner),
            bytes_accessed=24 * 1024 * 1024,
            transcendentals=12 * events * hidden,
        ),
    )(bit, *weights, flipped, *thin, cot)


def grad_layout(width, hidden):
    sizes = [6 * width, 6 * hidden, 6 * hidden, 6 * hidden]
    starts = [sum(sizes[:index]) for index in range(5)]
    return sizes, starts


def finish_body(
    bit_ref,
    own_a_ref,
    own_b_ref,
    came_a_ref,
    came_b_ref,
    low_expand_ref,
    low_inbias_ref,
    low_shrink_ref,
    low_outbias_ref,
    low_gain_ref,
    low_taskgate_ref,
    low_sharegate_ref,
    up_expand_ref,
    up_inbias_ref,
    up_shrink_ref,
    up_outbias_ref,
    up_gain_ref,
    up_taskgate_ref,
    inner_ref,
    tbias_ref,
    middle_ref,
    tail_ref,
):
    part = own_a_ref.shape[0]
    hidden = up_expand_ref.shape[1]
    width = low_expand_ref.shape[0] // 6
    inner = inner_ref.shape[1]
    narrow = middle_ref.shape[0]
    wide = (low_expand_ref, low_shrink_ref, up_expand_ref, up_shrink_ref)
    sizes, starts = grad_layout(width, hidden)
    block = 128

    def move(source, start, target, place, rows):
        def step(index, carry):
            target[pl.ds(pl.multiple_of(place + index * block, block), block), :] = source[
                pl.ds(pl.multiple_of(start + index * block, block), block), :
            ].astype(jnp.float32)
            return carry

        lax.fori_loop(0, rows // block, step, 0)

    def rest(source, start):
        def take(rows):
            nonlocal start
            start += rows
            return source[start - rows : start, :].astype(jnp.float32)

        both = take(hidden)
        inner_ref[:hidden, :] = both[:, :inner]
        inner_ref[hidden:, :] = both[:, inner:]
        both = take(narrow)
        middle_ref[...] = both
        for index in range(width // hidden):
            gates = take(32)
            span = slice(index * hidden, (index + 1) * hidden)
            low_taskgate_ref[:, span] = gates[0:4]
            low_taskgate_ref[:, width + index * hidden : width + (index + 1) * hidden] = gates[8:12]
            low_sharegate_ref[:, span] = gates[16:22]
        for task in range(2):
            up_taskgate_ref[:, task * hidden : (task + 1) * hidden] = take(16)[0:4]
        rows = take(48)
        flat = (low_inbias_ref, low_outbias_ref, up_inbias_ref, up_outbias_ref, tbias_ref, tail_ref)
        place = 0
        for target in flat + (low_gain_ref, up_gain_ref):
            for index in range(target.shape[0] // hidden):
                target[index * hidden : (index + 1) * hidden] = rows[place]
                place += 1

    def all_parts(pieces):
        for index, source in enumerate(pieces):
            first, last = index * part, (index + 1) * part
            for target, start, size in zip(wide, starts, sizes):
                low, high = max(first, start), min(last, start + size)
                if low < high:
                    move(source, low - first, target, low - start, high - low)
        rest(pieces[-1], starts[4] - (len(pieces) - 1) * part)

    @pl.when(bit_ref[0] == 0)
    def _():
        all_parts((own_a_ref, own_b_ref, came_a_ref, came_b_ref))

    @pl.when(bit_ref[0] != 0)
    def _():
        all_parts((came_a_ref, came_b_ref, own_a_ref, own_b_ref))


def finish(bit, own, came, width, hidden):
    shapes = (
        (6 * width, hidden),
        (6 * hidden,),
        (6 * hidden, hidden),
        (6 * hidden,),
        (6 * hidden,),
        (4, 2 * width),
        (6, width),
        (6 * hidden, hidden),
        (6 * hidden,),
        (6 * hidden, hidden),
        (6 * hidden,),
        (6 * hidden,),
        (4, 2 * hidden),
        (2 * hidden, 128),
        (256,),
        (64, 256),
        (256,),
    )
    done = pl.pallas_call(
        finish_body,
        out_shape=tuple(jax.ShapeDtypeStruct(shape, jnp.float32) for shape in shapes),
        in_specs=[pl.BlockSpec(memory_space=pltpu.SMEM)] + [pl.BlockSpec(memory_space=pltpu.VMEM)] * 4,
        compiler_params=pltpu.CompilerParams(vmem_limit_bytes=VMEM_LIMIT),
        cost_estimate=pl.CostEstimate(
            flops=0, bytes_accessed=12 * width * hidden * 16, transcendentals=0
        ),
    )(bit, *own, *came)
    return tuple(value.T if value.shape[0] in (4, 6, 64) else value for value in done)


def partners(mask, size):
    return [(index, index ^ mask) for index in range(size)]


def swap_with(values, mask, size):
    return lax.ppermute(values, "dp", partners(mask, size))


def cut(values, mask, place):
    rows = values.shape[0] // 2
    bit = jnp.where((place & mask) != 0, 1, 0)
    sent = lax.dynamic_slice_in_dim(values, (1 - bit) * rows, rows, 0)
    return sent, lax.dynamic_slice_in_dim(values, bit * rows, rows, 0)


def add_low(kept, came):
    return (kept.astype(jnp.float32) + came.astype(jnp.float32)).astype(kept.dtype)


def double(values, mask, place, size):
    came = swap_with(values, mask, size)
    upper = (place & mask) != 0
    return jnp.concatenate(
        [jnp.where(upper, came, values), jnp.where(upper, values, came)], axis=0
    )


def swap_groups(values, mask):
    return lax.ppermute(values, "fsdp", partners(mask, lax.axis_size("fsdp")))


def share(values, also=None):
    group = lax.axis_size("fsdp")
    place = lax.axis_index("fsdp")
    pieces = [values] + [swap_groups(values, mask) for mask in range(1, group)]
    if also is not None:
        pieces, _ = lax.optimization_barrier((pieces, also))
    return jnp.stack([pick(place ^ index, pieces) for index in range(group)])


def pick(index, pieces):
    chosen = pieces[0]
    for place in range(1, len(pieces)):
        chosen = jnp.where(index == place, pieces[place], chosen)
    return chosen


def scatter_sum(values):
    group = lax.axis_size("fsdp")
    place = lax.axis_index("fsdp")
    rows = values.shape[0] // group
    pieces = [
        lax.dynamic_slice_in_dim(values, (place ^ mask) * rows, rows, 0) for mask in range(group)
    ]
    pieces = pieces[:1] + [swap_groups(pieces[mask], mask) for mask in range(1, group)]
    total = pieces[0].astype(jnp.float32)
    for piece in pieces[1:]:
        total = total + piece.astype(jnp.float32)
    return total.astype(values.dtype)


def dp_masks(size):
    return [1 << index for index in range(size.bit_length() - 1)]


def dp_orders():
    first, *others = dp_masks(lax.axis_size("dp"))
    return first, [others, others[::-1]]


def spread(parts, late=None, early=None):
    size = lax.axis_size("dp")
    place = lax.axis_index("dp")
    first, orders = dp_orders()
    for step in reversed(range(len(orders[0]))):
        parts = [double(part, order[step], place, size) for part, order in zip(parts, orders)]
        if step == len(orders[0]) - 1 and early is not None:
            parts, early = lax.optimization_barrier((parts, early))
    parts, late = lax.optimization_barrier((parts, late))
    return parts, [swap_with(part, first, size) for part in parts], late, early


def arrival(order, first, group):
    devices = []
    for half in range(2):
        places = []
        for block in range(1 << len(order)):
            dp = half * first
            for index, mask in enumerate(order):
                if block >> (len(order) - 1 - index) & 1:
                    dp |= mask
            places += [dp * group + index for index in range(group)]
        devices.append(places)
    return devices


def in_order(own, came, bit, places, rows):
    whole = jnp.concatenate([jnp.where(bit == 0, own, came), jnp.where(bit == 0, came, own)], axis=0)
    whole = whole.reshape((-1, rows) + own.shape[1:])
    flat = places[0] + places[1]
    return jnp.stack([whole[flat.index(device)] for device in range(len(flat))])


def sum_grads(kept, sent, flipped_grad, prepare, finish_rows, width, hidden):
    size = lax.axis_size("dp")
    group = lax.axis_size("fsdp")
    place = lax.axis_index("dp")
    first, orders = dp_orders()
    mine = add_low(kept, swap_with(sent, first, size))
    rows = mine.shape[0] // 2
    parts = [mine[:rows], mine[rows:]]
    for step in range(len(orders[0])):
        halves = [cut(part, order[step], place) for part, order in zip(parts, orders)]
        if step == 0:
            halves, flipped_grad = lax.optimization_barrier((halves, flipped_grad))
            outgoing = prepare(flipped_grad)
        parts = [
            add_low(kept, swap_with(sent, order[step], size))
            for (sent, kept), order in zip(halves, orders)
        ]
        if step == 0:
            parts, outgoing = lax.optimization_barrier((parts, outgoing))
    incoming = lax.all_to_all(outgoing, ("dp", "fsdp"), split_axis=0, concat_axis=0, tiled=True)
    both = [part.reshape((group, -1) + part.shape[1:]) for part in parts]
    summed = scatter_sum(jnp.concatenate(both, axis=1).reshape((-1,) + kept.shape[1:]))
    summed, incoming = lax.optimization_barrier((summed, incoming))
    shared = share(summed)
    late = (finish_rows(incoming), flipped_grad.T)
    parts = [piece.reshape((-1,) + kept.shape[1:]) for piece in jnp.split(shared, 2, axis=1)]
    own, came, late, _ = spread(parts, late)
    return finish((place & first).reshape(1), own, came, width, hidden), *late


def on_device(
    owner_ids,
    row_ids,
    embed_table,
    expandone,
    expbiasone,
    reduceone,
    redbiasone,
    normgainone,
    taskgateone,
    sharegateone,
    expandtwo,
    expbiastwo,
    reducetwo,
    redbiastwo,
    normgaintwo,
    taskgatetwo,
    towerinner,
    towerbias,
    towermiddle,
    towertail,
    logit_cot,
):
    devices = lax.axis_size(("dp", "fsdp"))
    events, fields = owner_ids.shape
    emb_width = embed_table.shape[1]
    capacity = 2 * events * fields // devices
    hidden = expandone.shape[1]
    width = fields * emb_width
    group = lax.axis_size("fsdp")
    owner_rows = owner_ids.T
    request, rank = assign_slots(owner_rows, row_ids.T, devices, capacity)
    asked_rows = lax.all_to_all(request, ("dp", "fsdp"), split_axis=0, concat_axis=0, tiled=True)
    packed = pack(
        (expbiasone, redbiasone, normgainone, expbiastwo, redbiastwo, normgaintwo),
        (towerbias, towertail, taskgateone.T, sharegateone.T, taskgatetwo.T, towerinner, towermiddle),
        (expandone, reduceone, expandtwo, reducetwo),
    )
    found = find_rows(asked_rows, embed_table.T)
    packed = share(packed, asked_rows)
    split = expandone.shape[0] + THIN_ROWS
    first, orders = dp_orders()
    parts = [packed[:, :split], packed[:, split:]]
    own, came, _, found = spread([part.reshape(-1, hidden) for part in parts], early=found)
    returned = lax.all_to_all(found, ("dp", "fsdp"), split_axis=0, concat_axis=0, tiled=True)
    bit = (lax.axis_index("dp") & first).reshape(1)
    places = [arrival(order, first, group) for order in orders]
    thin = prep_thin(bit, own[0], came[0], places[0], width, hidden)
    sizes = [shard.shape[0] for shard in (expandone, reduceone, expandtwo, reducetwo)]
    if all(size % 16 == 0 for size in sizes):
        weights = (*own, *came)
    else:
        whole = [
            in_order(mine, other, bit[0], place, part.shape[1])
            for mine, other, place, part in zip(own, came, places, parts)
        ]
        starts = [0, 0, sizes[1], sizes[1] + sizes[2]]
        weights = tuple(
            whole[min(index, 1)][:, start : start + size].reshape(-1, hidden)
            for index, (start, size) in enumerate(zip(starts, sizes))
        )
        places = None

    thin, returned = lax.optimization_barrier((thin, returned))
    flipped = place_rows(returned, rank, owner_rows)
    chunk = 16 * devices
    grad_rows = -(-(6 * (width + 3 * hidden) + 2 * hidden) // chunk) * chunk
    logits, flipped_grad, kept, sent = dense(bit, flipped, weights, places, thin, logit_cot, grad_rows)

    def prepare(flipped_grad):
        return send_rows(flipped_grad, rank, owner_rows, capacity)

    def finish_rows(incoming):
        return add_rows(incoming, asked_rows, embed_table.shape[0])

    done, table_grad, x_grad = sum_grads(kept, sent, flipped_grad, prepare, finish_rows, width, hidden)
    return (logits, x_grad, table_grad.T, *done)


def solution(mesh):
    return jax.shard_map(
        on_device,
        mesh=mesh,
        in_specs=(
            P(("dp", "fsdp"), None),
            P(("dp", "fsdp"), None),
            P(("dp", "fsdp"), None),
            P(("dp", "fsdp"), None),
            P(("dp", "fsdp")),
            P(("dp", "fsdp"), None),
            P(("dp", "fsdp")),
            P(("dp", "fsdp")),
            P(("dp", "fsdp"), None),
            P(("dp", "fsdp"), None),
            P(("dp", "fsdp"), None),
            P(("dp", "fsdp")),
            P(("dp", "fsdp"), None),
            P(("dp", "fsdp")),
            P(("dp", "fsdp")),
            P(("dp", "fsdp"), None),
            P(("dp", "fsdp"), None),
            P(("dp", "fsdp")),
            P(("dp", "fsdp"), None),
            P(("dp", "fsdp")),
            P(None, ("dp", "fsdp")),
        ),
        out_specs=(
            P(None, ("dp", "fsdp")),
            P(("dp", "fsdp"), None),
            P(("dp", "fsdp"), None),
            P(),
            P(),
            P(),
            P(),
            P(),
            P(),
            P(),
            P(),
            P(),
            P(),
            P(),
            P(),
            P(),
            P(),
            P(),
            P(),
            P(),
        ),
        check_vma=False,
    )
```

```python
import functools

import jax
import jax.numpy as jnp
from jax import lax
from jax.experimental import pallas as pl
from jax.experimental.pallas import tpu as pltpu
from jax.sharding import PartitionSpec as P

EPS = 1e-05
VMEM_LIMIT = 56 * 1024 * 1024
ROW_BLOCKS = 8


def local_kernel(body, out_shape, flops, moved, scratch=()):
    return pl.pallas_call(
        body,
        out_shape=out_shape,
        scratch_shapes=list(scratch),
        compiler_params=pltpu.CompilerParams(vmem_limit_bytes=VMEM_LIMIT),
        cost_estimate=pl.CostEstimate(flops=flops, bytes_accessed=moved, transcendentals=0),
    )


def one_hot(hit):
    return jnp.where(hit, 1.0, 0.0).astype(jnp.bfloat16)


def iota(shape, axis):
    return lax.broadcasted_iota(jnp.int32, shape, axis)


def slot_body(owner_ref, row_ref, request_ref, rank_ref):
    fields, events = owner_ref.shape
    devices, _, capacity = request_ref.shape
    place = iota((devices, events), 0)
    asked = jnp.zeros((devices, events), jnp.float32)
    for field in range(fields):
        asked = asked + jnp.where(owner_ref[field : field + 1, :] == place, 1.0, 0.0)
    earlier = one_hot(iota((events, events), 0) < iota((events, events), 1))
    rank = jnp.dot(asked.astype(jnp.bfloat16), earlier, preferred_element_type=jnp.float32)
    rank = jnp.where(asked > 0.5, rank.astype(jnp.int32), -1)
    rank_ref[...] = rank
    slots = iota((capacity, events), 0)
    total = jnp.zeros((2 * devices, capacity), jnp.float32)
    for field in range(fields):
        mine = owner_ref[field : field + 1, :] == place
        field_rank = jnp.max(jnp.where(mine, rank, -1).astype(jnp.float32), axis=0, keepdims=True)
        rows = row_ref[field : field + 1, :]
        high = jnp.where(mine, (rows >> 6).astype(jnp.float32), 0.0)
        low = jnp.where(mine, (rows & 63).astype(jnp.float32), 0.0)
        value = jnp.concatenate([high, low], axis=0).astype(jnp.bfloat16)
        total = total + lax.dot_general(
            value,
            one_hot(field_rank.astype(jnp.int32) == slots),
            (((1,), (1,)), ((), ())),
            preferred_element_type=jnp.float32,
        )
    request = (total[:devices] * 64.0 + total[devices:]).astype(jnp.int32)
    for owner in range(devices):
        request_ref[owner] = request[owner : owner + 1]


def assign_slots(owner_rows, row_rows, devices, capacity):
    fields, events = owner_rows.shape
    return local_kernel(
        slot_body,
        (
            jax.ShapeDtypeStruct((devices, 1, capacity), jnp.int32),
            jax.ShapeDtypeStruct((devices, events), jnp.int32),
        ),
        2 * devices * events * (events + 2 * fields * capacity),
        4 * events * (2 * fields + devices),
    )(owner_rows, row_rows)


def find_body(request_ref, table_ref, found_ref, wide_ref):
    devices, _, capacity = request_ref.shape
    width = table_ref.shape[0]
    span = wide_ref.shape[1]
    places = iota((span, capacity), 0)
    for index in range(ROW_BLOCKS):
        wide_ref[index * width : (index + 1) * width, :] = table_ref[
            :, index * span : (index + 1) * span
        ]

    def step(source, carry):
        rows = request_ref[source]
        block = rows // span
        hits = one_hot(rows - block * span == places)
        rows_all = jnp.dot(wide_ref[...], hits, preferred_element_type=jnp.float32)
        picked = jnp.zeros((width, capacity), jnp.float32)
        for index in range(ROW_BLOCKS):
            picked = jnp.where(
                block == index, rows_all[index * width : (index + 1) * width, :], picked
            )
        found_ref[source] = picked.astype(jnp.bfloat16)
        return carry

    lax.fori_loop(0, devices, step, 0, unroll=16)


def find_rows(request, table):
    devices, _, capacity = request.shape
    width, rows = table.shape
    return local_kernel(
        find_body,
        jax.ShapeDtypeStruct((devices, width, capacity), jnp.bfloat16),
        2 * devices * capacity * rows * width,
        2 * (rows * width + devices * capacity * width),
        [pltpu.VMEM((ROW_BLOCKS * width, rows // ROW_BLOCKS), jnp.bfloat16)],
    )(request, table)


def place_body(found_ref, rank_ref, owner_ref, flipped_ref, total_ref):
    devices, width, capacity = found_ref.shape
    fields, events = owner_ref.shape
    slots = iota((capacity, events), 0)
    group = 4
    total_ref[...] = jnp.zeros_like(total_ref)

    def step(start, carry):
        pieces = []
        for index in range(group):
            owner = start * group + index
            hits = one_hot(rank_ref[pl.ds(owner, 1), :] == slots)
            pieces.append(jnp.dot(found_ref[owner], hits, preferred_element_type=jnp.float32))
        for field in range(fields):
            rows = slice(field * width, (field + 1) * width)
            owners = owner_ref[field : field + 1, :]
            value = total_ref[rows, :]
            for index in range(group):
                value = jnp.where(owners == start * group + index, pieces[index], value)
            total_ref[rows, :] = value
        return carry

    lax.fori_loop(0, devices // group, step, 0)
    flipped_ref[...] = total_ref[...].astype(jnp.bfloat16)


def place_rows(found, rank, owner_rows):
    devices, width, capacity = found.shape
    fields, events = owner_rows.shape
    return local_kernel(
        place_body,
        jax.ShapeDtypeStruct((fields * width, events), jnp.bfloat16),
        2 * devices * width * capacity * events,
        2 * (devices * width * capacity + fields * width * events),
        [pltpu.VMEM((fields * width, events), jnp.float32)],
    )(found, rank, owner_rows)


def send_body(grad_ref, rank_ref, owner_ref, sent_ref, low_ref):
    devices, width, capacity = sent_ref.shape
    fields, events = owner_ref.shape
    slots = iota((capacity, events), 0)
    low_ref[...] = grad_ref[...].astype(jnp.bfloat16).astype(jnp.float32)

    def step(owner, carry):
        chosen = jnp.zeros((width, events), jnp.float32)
        for field in range(fields):
            rows = slice(field * width, (field + 1) * width)
            chosen = jnp.where(owner_ref[field : field + 1, :] == owner, low_ref[rows, :], chosen)
        hits = one_hot(rank_ref[pl.ds(owner, 1), :] == slots)
        sent_ref[owner] = lax.dot_general(
            chosen.astype(jnp.bfloat16),
            hits,
            (((1,), (1,)), ((), ())),
            preferred_element_type=jnp.float32,
        ).astype(jnp.bfloat16)
        return carry

    lax.fori_loop(0, devices, step, 0, unroll=16)


def send_rows(grad, rank, owner_rows, capacity):
    devices = rank.shape[0]
    fields, events = owner_rows.shape
    width = grad.shape[0] // fields
    return local_kernel(
        send_body,
        jax.ShapeDtypeStruct((devices, width, capacity), jnp.bfloat16),
        2 * devices * width * capacity * events,
        2 * (devices * width * capacity + 2 * fields * width * events),
        [pltpu.VMEM((fields * width, events), jnp.float32)],
    )(grad, rank, owner_rows)


def add_body(came_ref, request_ref, out_ref, total_ref):
    devices, width, capacity = came_ref.shape
    span = total_ref.shape[1]
    group = 8
    places = iota((span, capacity), 0)
    total_ref[...] = jnp.zeros_like(total_ref)

    def step(start, carry):
        hits = []
        spread = []
        for index in range(group):
            source = start * group + index
            rows = request_ref[source]
            block = rows // span
            hits.append(one_hot(rows - block * span == places))
            came = came_ref[source].astype(jnp.float32)
            spread.append(
                jnp.concatenate(
                    [jnp.where(block == part, came, 0.0) for part in range(ROW_BLOCKS)], axis=0
                ).astype(jnp.bfloat16)
            )
        total_ref[...] += lax.dot_general(
            jnp.concatenate(spread, axis=1),
            jnp.concatenate(hits, axis=1),
            (((1,), (1,)), ((), ())),
            preferred_element_type=jnp.float32,
        )
        return carry

    lax.fori_loop(0, devices // group, step, 0, unroll=4)
    for index in range(ROW_BLOCKS):
        out_ref[:, index * span : (index + 1) * span] = total_ref[
            index * width : (index + 1) * width, :
        ]


def add_rows(came, request, rows):
    devices, width, capacity = came.shape
    span = rows // ROW_BLOCKS
    return local_kernel(
        add_body,
        jax.ShapeDtypeStruct((width, rows), jnp.float32),
        2 * devices * capacity * rows * width,
        2 * devices * width * capacity + 4 * rows * width,
        [pltpu.VMEM((ROW_BLOCKS * width, span), jnp.float32)],
    )(came, request)


THIN_ROWS = 48


def pack_thin_body(*refs):
    *biases, tbias, tail, taskgate, sharegate, upgate, inner, middle = refs[:13]
    *wide, out_ref, hold = refs[13:]
    hold[...] = jnp.zeros_like(hold)
    for row, piece in enumerate(biases + [tbias, tail]):
        hold[row : row + 1, : piece.shape[0]] = piece[...].astype(jnp.float32).reshape(1, -1)
    for row, piece in ((8, taskgate), (16, sharegate), (24, upgate), (32, inner)):
        hold[row : row + piece.shape[0], : piece.shape[1]] = piece[...].astype(jnp.float32)
    hold[32 : 32 + middle.shape[0], 128 : 128 + middle.shape[1]] = middle[...].astype(jnp.float32)
    thin = hold[...].astype(jnp.bfloat16)
    if not wide:
        out_ref[...] = thin
    start = 0
    for index, piece in enumerate(wide):
        out_ref[start : start + piece.shape[0], :] = piece[...]
        start += piece.shape[0]
        if index == 0:
            out_ref[start : start + THIN_ROWS, :] = thin
            start += THIN_ROWS


def pack(biases, others, wide):
    aligned = all(piece.shape[0] % 16 == 0 for piece in wide)
    rows = THIN_ROWS + (sum(piece.shape[0] for piece in wide) if aligned else 0)
    packed = local_kernel(
        pack_thin_body,
        jax.ShapeDtypeStruct((rows, 256), jnp.bfloat16),
        0,
        rows * 1024,
        [pltpu.VMEM((THIN_ROWS, 256), jnp.float32)],
    )(*biases, *others, *(wide if aligned else ()))
    if aligned:
        return packed
    return jnp.concatenate([wide[0], packed, *wide[1:]], axis=0)


def prep_thin_body(
    places,
    bit_ref,
    own_ref,
    came_ref,
    columns_ref,
    gate_one_ref,
    gate_one_back_ref,
    gate_two_ref,
    gate_two_back_ref,
    inner_ref,
    inner_back_ref,
    middle_ref,
    middle_back_ref,
    rows,
    task_rows,
    share_rows,
    up_rows,
    inner_rows,
    middle_rows,
):
    devices = 2 * len(places[0])
    shard = own_ref.shape[0] // len(places[0])
    hidden = columns_ref.shape[0]
    width = gate_one_ref.shape[1]

    def lay(target, source, index, count):
        target[:, index * count : (index + 1) * count] = source[:, :count]

    rows[...] = jnp.zeros_like(rows)
    task_rows[...] = jnp.zeros_like(task_rows)
    share_rows[...] = jnp.zeros_like(share_rows)
    up_rows[...] = jnp.zeros_like(up_rows)
    bias = 6 * hidden // devices
    flat = hidden // devices

    def unpack(pieces):
        for half, source in enumerate(pieces):
            for block, index in enumerate(places[half]):
                end = (block + 1) * shard
                thin = source[end - THIN_ROWS : end, :].astype(jnp.float32)
                rows[0:6, index * bias : (index + 1) * bias] = thin[0:6, :bias]
                rows[6:8, index * flat : (index + 1) * flat] = thin[6:8, :flat]
                lay(task_rows, thin[8:16], index, 2 * width // devices)
                lay(share_rows, thin[16:24], index, width // devices)
                lay(up_rows, thin[24:32], index, 2 * hidden // devices)
                count = 2 * hidden // devices
                inner_rows[index * count : (index + 1) * count, :] = thin[32 : 32 + count, :128]
                count = hidden // devices
                middle_rows[index * count : (index + 1) * count, :] = thin[32 : 32 + count, 128:192]

    @pl.when(bit_ref[0] == 0)
    def _():
        unpack((own_ref, came_ref))

    @pl.when(bit_ref[0] != 0)
    def _():
        unpack((came_ref, own_ref))

    columns_ref[...] = jnp.zeros_like(columns_ref)
    for expert in range(6):
        columns_ref[:, expert * 8 : expert * 8 + 8] = rows[:, expert * hidden : (expert + 1) * hidden].T
    gates = jnp.concatenate(
        [
            task_rows[:, :width],
            task_rows[:, width:],
            share_rows[...],
            jnp.zeros((8, width), jnp.float32),
        ],
        axis=0,
    )
    gate_one_ref[...] = gates.astype(jnp.bfloat16)
    gate_one_back_ref[...] = gates.T.astype(jnp.bfloat16)
    gate_two_ref[...] = jnp.concatenate([up_rows[:, :hidden], up_rows[:, hidden:]], axis=0).astype(
        jnp.bfloat16
    )
    for task in range(2):
        span = slice(task * hidden, (task + 1) * hidden)
        wide = jnp.concatenate([up_rows[:, span], jnp.zeros((8, hidden), jnp.float32)], axis=0)
        gate_two_back_ref[span, :] = wide.T.astype(jnp.bfloat16)
        inner_ref[task * 128 : (task + 1) * 128, :] = inner_rows[span, :].T.astype(jnp.bfloat16)
        span = slice(task * 128, (task + 1) * 128)
        middle_ref[task * 64 : (task + 1) * 64, :] = middle_rows[span, :].T.astype(jnp.bfloat16)
    inner_back_ref[...] = inner_rows[...].astype(jnp.bfloat16)
    middle_back_ref[...] = middle_rows[...].astype(jnp.bfloat16)


def prep_thin(bit, own, came, places, width, hidden):
    low = functools.partial(jax.ShapeDtypeStruct, dtype=jnp.bfloat16)
    return pl.pallas_call(
        functools.partial(prep_thin_body, places),
        out_shape=(
            jax.ShapeDtypeStruct((hidden, 64), jnp.float32),
            low((32, width)),
            low((width, 32)),
            low((16, hidden)),
            low((2 * hidden, 16)),
            low((hidden, hidden)),
            low((2 * hidden, 128)),
            low((128, 128)),
            low((hidden, 64)),
        ),
        in_specs=[pl.BlockSpec(memory_space=pltpu.SMEM)] + [pl.BlockSpec(memory_space=pltpu.VMEM)] * 2,
        scratch_shapes=[
            pltpu.VMEM((8, 6 * hidden), jnp.float32),
            pltpu.VMEM((8, 2 * width), jnp.float32),
            pltpu.VMEM((8, width), jnp.float32),
            pltpu.VMEM((8, 2 * hidden), jnp.float32),
            pltpu.VMEM((2 * hidden, 128), jnp.float32),
            pltpu.VMEM((hidden, 64), jnp.float32),
        ],
        compiler_params=pltpu.CompilerParams(vmem_limit_bytes=VMEM_LIMIT),
        cost_estimate=pl.CostEstimate(flops=0, bytes_accessed=4 * own.size, transcendentals=0),
    )(bit, own, came)


SPAN = 512
ONES = 16


def over_events(left, right):
    return lax.dot_general(left, right, (((1,), (1,)), ((), ())), preferred_element_type=jnp.float32)


def times(left, right):
    return jnp.dot(left, right, preferred_element_type=jnp.float32)


def sum_rows(values):
    return jnp.sum(values, axis=0, keepdims=True)


def sigmoid_of(values):
    return 0.5 * jnp.tanh(0.5 * values) + 0.5


def silu_parts(values):
    sig = sigmoid_of(values)
    active = values * sig
    return active, sig + active * (1.0 - sig)


def expert_up(inputs, expand, expbias, shrink, shrinkbias):
    active, slope = silu_parts(times(expand, inputs) + expbias)
    active = active.astype(jnp.bfloat16)
    output = times(shrink, active) + shrinkbias
    scale = 1.0 / output.shape[0]
    centered = output - sum_rows(output) * scale
    inverse = lax.rsqrt(sum_rows(centered * centered) * scale + EPS)
    return active, slope, centered * inverse, inverse


def soft(scores, count):
    valid = iota(scores.shape, 0) < count
    scores = jnp.where(valid, scores, -1e30)
    shifted = jnp.exp(scores - jnp.max(scores, axis=0, keepdims=True))
    shifted = jnp.where(valid, shifted, 0.0)
    return shifted / sum_rows(shifted)


def soft_back(probs, rows):
    tall = jnp.concatenate(rows + [jnp.zeros_like(rows[0])] * (probs.shape[0] - len(rows)), axis=0)
    return probs * (tall - sum_rows(probs * tall))


def assemble(bit, own_ref, came_ref, homes, places):
    blocks = len(places[0])
    rows = own_ref.shape[0] // blocks
    for half, source in ((bit, own_ref), (1 - bit, came_ref)):
        for block in range(blocks):
            start = block * rows
            for home in homes:
                size = home.shape[0] // (2 * blocks)
                place = places[0][block] * size + half * ((places[1][0] - places[0][0]) * size)
                home[pl.ds(pl.multiple_of(place, 16), size), :] = source[start : start + size, :]
                start += size


def dense_body(places, *refs):
    bit_ref, *refs = refs
    if places is None:
        *naturals, refs = *refs[:4], refs[4:]
    else:
        own_a, own_b, came_a, came_b, *refs = refs
        naturals, refs = refs[-4:], refs[:-4]
    expand_one_back_ref, shrink_one_back_ref, expand_two_back_ref, shrink_two_back_ref = naturals
    (
        flipped_ref,
        columns_ref,
        gate_one_ref,
        gate_one_back_ref,
        gate_two_ref,
        gate_two_back_ref,
        inner_ref,
        inner_back_ref,
        middle_ref,
        middle_back_ref,
        cot_ref,
        logits_ref,
        flipped_grad_ref,
        kept_ref,
        sent_ref,
        sems,
        grads_ref,
        input_keep,
        active_one,
        out_one,
        pre_one,
        score_one,
        carried_keep,
        active_two,
        out_two,
        pre_two,
        score_two,
        tower_keep,
        tower_act_keep,
        first_keep,
        top_keep,
        tail_keep,
        gain_keep,
        expand_one_ref,
        shrink_one_ref,
        expand_two_ref,
        shrink_two_ref,
    ) = refs
    bit = jnp.minimum(bit_ref[0], 1)
    if places is not None:
        assemble(bit, own_a, came_a, [expand_one_back_ref], places[0])
        assemble(
            bit,
            own_b,
            came_b,
            [shrink_one_back_ref, expand_two_back_ref, shrink_two_back_ref],
            places[1],
        )
    for natural, turned in (
        (expand_one_back_ref, expand_one_ref),
        (shrink_one_back_ref, shrink_one_ref),
        (expand_two_back_ref, expand_two_ref),
        (shrink_two_back_ref, shrink_two_ref),
    ):
        depth = natural.shape[0] // 6
        across = natural.shape[1]
        for expert in range(6):
            turned[expert * across : (expert + 1) * across, :] = natural[
                expert * depth : (expert + 1) * depth, :
            ].T

    width, events = flipped_ref.shape
    hidden = shrink_one_back_ref.shape[1]
    inner = inner_ref.shape[0] // 2
    narrow = middle_ref.shape[0] // 2
    tall = hidden + ONES
    span = min(SPAN, events)
    unit = jnp.ones((ONES, events), jnp.bfloat16)

    input_keep[:width, :] = flipped_ref[...]
    input_keep[width:, :] = unit
    for expert in range(6):
        active_one[expert * tall + hidden : (expert + 1) * tall, :] = unit
        active_two[expert * tall + hidden : (expert + 1) * tall, :] = unit
    for group in range(3):
        carried_keep[group * tall + hidden : (group + 1) * tall, :] = unit
    for task in range(2):
        tower_keep[task * tall + hidden : (task + 1) * tall, :] = unit
    gain_keep[...] = jnp.zeros_like(gain_keep)

    def column(index, rows=hidden, start=0):
        return columns_ref[start : start + rows, index : index + 1]

    def experts_rows(expert):
        return slice(expert * hidden, (expert + 1) * hidden)

    def span_step(step, carry):
        lanes = pl.ds(pl.multiple_of(step * span, span), span)
        inputs = flipped_ref[:, lanes]

        def up(level, inputs_of, expand_ref, shrink_ref, active_keep):
            kept = []
            for expert in range(6):
                active, slope, normed, inverse = expert_up(
                    inputs_of(expert),
                    expand_ref[experts_rows(expert), :],
                    column(expert * 8 + level),
                    shrink_ref[experts_rows(expert), :],
                    column(expert * 8 + level + 1),
                )
                active_keep[expert * tall : expert * tall + hidden, lanes] = active
                kept.append((slope, normed, inverse, normed * column(expert * 8 + level + 2)))
            return kept

        kept_one = up(0, lambda expert: inputs, expand_one_ref, shrink_one_ref, active_one)
        scores = times(gate_one_ref[...], inputs)
        probs_one = [soft(scores[0:8], 4), soft(scores[8:16], 4), soft(scores[16:24], 6)]
        carried = []
        for group in range(3):
            members = [2 * group, 2 * group + 1, 4, 5] if group < 2 else range(6)
            mixed = 0.0
            for place, expert in enumerate(members):
                mixed = mixed + probs_one[group][place : place + 1, :] * kept_one[expert][3]
            carried.append(mixed.astype(jnp.bfloat16))
            carried_keep[group * tall : group * tall + hidden, lanes] = carried[group]

        kept_two = up(
            3, lambda expert: carried[expert // 2], expand_two_ref, shrink_two_ref, active_two
        )
        probs_two = []
        tower_grads = []
        dq_two = []
        for task in range(2):
            probs = soft(times(gate_two_ref[task * 8 : task * 8 + 8, :], carried[task]), 4)
            probs_two.append(probs)
            members = [2 * task, 2 * task + 1, 4, 5]
            mixed = 0.0
            for place, expert in enumerate(members):
                mixed = mixed + probs[place : place + 1, :] * kept_two[expert][3]
            mixed = mixed.astype(jnp.bfloat16)
            tower_keep[task * tall : task * tall + hidden, lanes] = mixed
            first, first_slope = silu_parts(
                times(inner_ref[task * inner : (task + 1) * inner, :], mixed)
                + column(6, inner, task * inner)
            )
            first = first.astype(jnp.bfloat16)
            tower_act_keep[task * inner : (task + 1) * inner, lanes] = first
            top, top_slope = silu_parts(
                times(middle_ref[task * narrow : (task + 1) * narrow, :], first)
                + column(7, narrow, 2 * task * narrow)
            )
            weight = column(7, narrow, (2 * task + 1) * narrow)
            logits_ref[task : task + 1, lanes] = sum_rows(top * weight)
            cot = cot_ref[task : task + 1, lanes]
            top_grad = (cot * weight * top_slope).astype(jnp.bfloat16)
            top_keep[task * narrow : (task + 1) * narrow, lanes] = top_grad
            seen = cot * top
            high = seen.astype(jnp.bfloat16)
            tail_keep[2 * task * narrow : (2 * task + 1) * narrow, lanes] = high
            tail_keep[(2 * task + 1) * narrow : (2 * task + 2) * narrow, lanes] = (
                seen - high.astype(jnp.float32)
            ).astype(jnp.bfloat16)
            first_grad = (
                times(middle_back_ref[task * inner : (task + 1) * inner, :], top_grad) * first_slope
            ).astype(jnp.bfloat16)
            first_keep[task * inner : (task + 1) * inner, lanes] = first_grad
            grad = times(inner_back_ref[task * hidden : (task + 1) * hidden, :], first_grad)
            tower_grads.append(grad)
            dq_two.append([sum_rows(kept_two[expert][3] * grad) for expert in members])

        def expert_down(level, expert, kept, upstream, slant, shrink_back_ref, out_keep, pre_keep):
            slope, normed, inverse, _ = kept
            gained = upstream * normed
            part = gained[:, :128]
            for start in range(128, span, 128):
                part = part + gained[:, start : start + 128]
            gain_rows = slice((level + expert) * hidden, (level + expert + 1) * hidden)
            gain_keep[gain_rows, :] += part
            scaled = upstream * column(expert * 8 + level // 2 + 2)
            scale = 1.0 / hidden
            out_low = (
                inverse * (scaled - sum_rows(scaled) * scale - normed * (slant * scale))
            ).astype(jnp.bfloat16)
            out_keep[experts_rows(expert), lanes] = out_low
            pre_low = (times(shrink_back_ref[experts_rows(expert), :], out_low) * slope).astype(
                jnp.bfloat16
            )
            pre_keep[experts_rows(expert), lanes] = pre_low
            return pre_low

        pre_lows = []
        for expert in range(6):
            if expert < 4:
                task, place = expert // 2, expert % 2
                prob = probs_two[task][place : place + 1, :]
                upstream = prob * tower_grads[task]
                slant = prob * dq_two[task][place]
            else:
                place = expert - 2
                prob = [probs_two[task][place : place + 1, :] for task in range(2)]
                upstream = prob[0] * tower_grads[0] + prob[1] * tower_grads[1]
                slant = prob[0] * dq_two[0][place] + prob[1] * dq_two[1][place]
            pre_lows.append(
                expert_down(
                    6, expert, kept_two[expert], upstream, slant, shrink_two_back_ref, out_two, pre_two
                )
            )
        carried_grads = []
        for group in range(3):
            grad = 0.0
            for expert in (2 * group, 2 * group + 1):
                grad = grad + times(expand_two_back_ref[experts_rows(expert), :], pre_lows[expert])
            if group < 2:
                score = soft_back(probs_two[group], dq_two[group])
                score = jnp.concatenate([score, jnp.zeros_like(score)], axis=0).astype(jnp.bfloat16)
                score_two[group * 16 : group * 16 + 16, lanes] = score
                grad = grad + times(gate_two_back_ref[experts_rows(group), :], score)
            carried_grads.append(grad)

        dq_one = []
        for group in range(3):
            members = [2 * group, 2 * group + 1, 4, 5] if group < 2 else range(6)
            dq_one.append([sum_rows(kept_one[expert][3] * carried_grads[group]) for expert in members])
        pre_lows = []
        for expert in range(6):
            prob = probs_one[2][expert : expert + 1, :]
            upstream = prob * carried_grads[2]
            slant = prob * dq_one[2][expert]
            for task in range(2):
                if expert // 2 in (task, 2):
                    place = expert % 2 if expert < 4 else expert - 2
                    prob = probs_one[task][place : place + 1, :]
                    upstream = upstream + prob * carried_grads[task]
                    slant = slant + prob * dq_one[task][place]
            pre_lows.append(
                expert_down(
                    0, expert, kept_one[expert], upstream, slant, shrink_one_back_ref, out_one, pre_one
                )
            )
        scores_low = [soft_back(probs_one[group], dq_one[group]) for group in range(3)]
        score = jnp.concatenate(scores_low + [jnp.zeros_like(scores_low[0])], axis=0).astype(
            jnp.bfloat16
        )
        score_one[:, lanes] = score
        grad = times(gate_one_back_ref[...], score)
        for expert in range(6):
            grad = grad + times(
                expand_one_back_ref[expert * width : (expert + 1) * width, :], pre_lows[expert]
            )
        flipped_grad_ref[:, lanes] = grad
        return carry

    lax.fori_loop(0, events // span, span_step, 0)

    half_rows = grads_ref.shape[1]

    def put(row, value):
        while value.shape[0]:
            half, start = row // half_rows, row % half_rows
            count = min(value.shape[0], half_rows - start)
            grads_ref[half, start : start + count, :] = value[:count].astype(jnp.bfloat16)
            row, value = row + count, value[count:]

    rows = 0
    biases = []
    for expert in range(6):
        both = over_events(input_keep[...], pre_one[experts_rows(expert), :])
        put(rows + expert * width, both[:width])
        biases.append(both[width : width + 1])
    rows += 6 * width
    for expert in range(6):
        both = over_events(active_one[expert * tall : (expert + 1) * tall, :], out_one[experts_rows(expert), :])
        put(rows + expert * hidden, both[:hidden])
        biases.append(both[hidden : hidden + 1])
    rows += 6 * hidden
    for expert in range(6):
        group = expert // 2
        both = over_events(carried_keep[group * tall : (group + 1) * tall, :], pre_two[experts_rows(expert), :])
        put(rows + expert * hidden, both[:hidden])
        biases.append(both[hidden : hidden + 1])
    rows += 6 * hidden
    for expert in range(6):
        both = over_events(active_two[expert * tall : (expert + 1) * tall, :], out_two[experts_rows(expert), :])
        put(rows + expert * hidden, both[:hidden])
        biases.append(both[hidden : hidden + 1])
    rows += 6 * hidden
    tower = []
    for task in range(2):
        tower.append(
            over_events(tower_keep[task * tall : (task + 1) * tall, :], first_keep[task * inner : (task + 1) * inner, :])
        )
    tower = jnp.concatenate(tower, axis=1)
    put(rows, tower[:hidden])
    biases.append(tower[hidden : hidden + 1])
    rows += hidden
    put(
        rows,
        jnp.concatenate(
            [
                over_events(
                    top_keep[task * narrow : (task + 1) * narrow, :],
                    tower_act_keep[task * inner : (task + 1) * inner, :],
                )
                for task in range(2)
            ],
            axis=1,
        ),
    )
    rows += narrow
    gates = over_events(score_one[...], flipped_ref[...])
    for start in range(0, width, hidden):
        put(rows, gates[:, start : start + hidden])
        rows += gates.shape[0]
    for task in range(2):
        put(
            rows,
            over_events(
                score_two[task * 16 : task * 16 + 16, :],
                carried_keep[task * tall : task * tall + hidden, :],
            ),
        )
        rows += 16
    tops = over_events(unit, top_keep[...])[:1]
    seen = over_events(unit, tail_keep[...])[:1]
    pieces = []
    for task in range(2):
        pieces.append(tops[:, task * narrow : (task + 1) * narrow])
        pieces.append(
            seen[:, 2 * task * narrow : (2 * task + 1) * narrow]
            + seen[:, (2 * task + 1) * narrow : (2 * task + 2) * narrow]
        )
    biases.append(jnp.concatenate(pieces, axis=1))
    gains = gain_keep[...]
    high = gains.astype(jnp.bfloat16)
    low = (gains - high.astype(jnp.float32)).astype(jnp.bfloat16)
    gains = (over_events(unit[:, :128], high) + over_events(unit[:, :128], low))[:1]
    for expert in range(12):
        biases.append(gains[:, experts_rows(expert)])
    biases = jnp.concatenate(biases, axis=0)
    extra = 2 * half_rows - rows - biases.shape[0]
    put(rows, jnp.concatenate([biases, jnp.zeros((extra, hidden), jnp.float32)], axis=0))
    copies = [
        pltpu.make_async_copy(grads_ref.at[1 - bit], sent_ref, sems.at[0]),
        pltpu.make_async_copy(grads_ref.at[bit], kept_ref, sems.at[1]),
    ]
    for copy in copies:
        copy.start()
    for copy in copies:
        copy.wait()


def dense(bit, flipped, weights, places, thin, cot, grad_rows):
    width, events = flipped.shape
    hidden = thin[0].shape[0]
    inner, narrow = 128, 64
    tall = hidden + ONES
    low = functools.partial(pltpu.VMEM, dtype=jnp.bfloat16)
    kept = (
        width + ONES,
        6 * tall,
        6 * hidden,
        6 * hidden,
        32,
        3 * tall,
        6 * tall,
        6 * hidden,
        6 * hidden,
        32,
        2 * tall,
        2 * inner,
        2 * inner,
        2 * narrow,
        4 * narrow,
    )
    half = (grad_rows // 2, hidden)
    scratch = [pltpu.SemaphoreType.DMA((2,)), low((2,) + half)]
    scratch += [low((rows, events)) for rows in kept]
    scratch.append(pltpu.VMEM((12 * hidden, 128), jnp.float32))
    scratch += [low((6 * hidden, depth)) for depth in (width, hidden, hidden, hidden)]
    vmem = pl.BlockSpec(memory_space=pltpu.VMEM)
    outside = pl.BlockSpec(memory_space=pl.ANY)
    specs = [pl.BlockSpec(memory_space=pltpu.SMEM)] + [vmem] * (len(weights) + len(thin) + 2)
    if places is not None:
        scratch += [low((6 * depth, hidden)) for depth in (width, hidden, hidden, hidden)]
    return pl.pallas_call(
        functools.partial(dense_body, places),
        out_shape=(
            jax.ShapeDtypeStruct((2, events), jnp.float32),
            jax.ShapeDtypeStruct((width, events), jnp.float32),
            jax.ShapeDtypeStruct(half, jnp.bfloat16),
            jax.ShapeDtypeStruct(half, jnp.bfloat16),
        ),
        in_specs=specs,
        out_specs=(vmem, vmem, outside, outside),
        scratch_shapes=scratch,
        compiler_params=pltpu.CompilerParams(vmem_limit_bytes=VMEM_LIMIT),
        cost_estimate=pl.CostEstimate(
            flops=6 * events * hidden * (6 * (width + 3 * hidden) + 2 * inner),
            bytes_accessed=24 * 1024 * 1024,
            transcendentals=12 * events * hidden,
        ),
    )(bit, *weights, flipped, *thin, cot)


def grad_layout(width, hidden):
    sizes = [6 * width, 6 * hidden, 6 * hidden, 6 * hidden]
    starts = [sum(sizes[:index]) for index in range(5)]
    return sizes, starts


def finish_body(
    bit_ref,
    own_a_ref,
    own_b_ref,
    came_a_ref,
    came_b_ref,
    low_expand_ref,
    low_inbias_ref,
    low_shrink_ref,
    low_outbias_ref,
    low_gain_ref,
    low_taskgate_ref,
    low_sharegate_ref,
    up_expand_ref,
    up_inbias_ref,
    up_shrink_ref,
    up_outbias_ref,
    up_gain_ref,
    up_taskgate_ref,
    inner_ref,
    tbias_ref,
    middle_ref,
    tail_ref,
):
    part = own_a_ref.shape[0]
    hidden = up_expand_ref.shape[1]
    width = low_expand_ref.shape[0] // 6
    inner = inner_ref.shape[1]
    narrow = middle_ref.shape[0]
    wide = (low_expand_ref, low_shrink_ref, up_expand_ref, up_shrink_ref)
    sizes, starts = grad_layout(width, hidden)
    block = 128

    def move(source, start, target, place, rows):
        def step(index, carry):
            target[pl.ds(pl.multiple_of(place + index * block, block), block), :] = source[
                pl.ds(pl.multiple_of(start + index * block, block), block), :
            ].astype(jnp.float32)
            return carry

        lax.fori_loop(0, rows // block, step, 0)

    def rest(source, start):
        def take(rows):
            nonlocal start
            start += rows
            return source[start - rows : start, :].astype(jnp.float32)

        both = take(hidden)
        inner_ref[:hidden, :] = both[:, :inner]
        inner_ref[hidden:, :] = both[:, inner:]
        both = take(narrow)
        middle_ref[...] = both
        for index in range(width // hidden):
            gates = take(32)
            span = slice(index * hidden, (index + 1) * hidden)
            low_taskgate_ref[:, span] = gates[0:4]
            low_taskgate_ref[:, width + index * hidden : width + (index + 1) * hidden] = gates[8:12]
            low_sharegate_ref[:, span] = gates[16:22]
        for task in range(2):
            up_taskgate_ref[:, task * hidden : (task + 1) * hidden] = take(16)[0:4]
        rows = take(48)
        flat = (low_inbias_ref, low_outbias_ref, up_inbias_ref, up_outbias_ref, tbias_ref, tail_ref)
        place = 0
        for target in flat + (low_gain_ref, up_gain_ref):
            for index in range(target.shape[0] // hidden):
                target[index * hidden : (index + 1) * hidden] = rows[place]
                place += 1

    def all_parts(pieces):
        for index, source in enumerate(pieces):
            first, last = index * part, (index + 1) * part
            for target, start, size in zip(wide, starts, sizes):
                low, high = max(first, start), min(last, start + size)
                if low < high:
                    move(source, low - first, target, low - start, high - low)
        rest(pieces[-1], starts[4] - (len(pieces) - 1) * part)

    @pl.when(bit_ref[0] == 0)
    def _():
        all_parts((own_a_ref, own_b_ref, came_a_ref, came_b_ref))

    @pl.when(bit_ref[0] != 0)
    def _():
        all_parts((came_a_ref, came_b_ref, own_a_ref, own_b_ref))


def finish(bit, own, came, width, hidden):
    shapes = (
        (6 * width, hidden),
        (6 * hidden,),
        (6 * hidden, hidden),
        (6 * hidden,),
        (6 * hidden,),
        (4, 2 * width),
        (6, width),
        (6 * hidden, hidden),
        (6 * hidden,),
        (6 * hidden, hidden),
        (6 * hidden,),
        (6 * hidden,),
        (4, 2 * hidden),
        (2 * hidden, 128),
        (256,),
        (64, 256),
        (256,),
    )
    done = pl.pallas_call(
        finish_body,
        out_shape=tuple(jax.ShapeDtypeStruct(shape, jnp.float32) for shape in shapes),
        in_specs=[pl.BlockSpec(memory_space=pltpu.SMEM)] + [pl.BlockSpec(memory_space=pltpu.VMEM)] * 4,
        compiler_params=pltpu.CompilerParams(vmem_limit_bytes=VMEM_LIMIT),
        cost_estimate=pl.CostEstimate(
            flops=0, bytes_accessed=12 * width * hidden * 16, transcendentals=0
        ),
    )(bit, *own, *came)
    return tuple(value.T if value.shape[0] in (4, 6, 64) else value for value in done)


def partners(mask, size):
    return [(index, index ^ mask) for index in range(size)]


def swap_with(values, mask, size):
    return lax.ppermute(values, "dp", partners(mask, size))


def cut(values, mask, place):
    rows = values.shape[0] // 2
    bit = jnp.where((place & mask) != 0, 1, 0)
    sent = lax.dynamic_slice_in_dim(values, (1 - bit) * rows, rows, 0)
    return sent, lax.dynamic_slice_in_dim(values, bit * rows, rows, 0)


def add_low(kept, came):
    return (kept.astype(jnp.float32) + came.astype(jnp.float32)).astype(kept.dtype)


def double(values, mask, place, size):
    came = swap_with(values, mask, size)
    upper = (place & mask) != 0
    return jnp.concatenate(
        [jnp.where(upper, came, values), jnp.where(upper, values, came)], axis=0
    )


def swap_groups(values, mask):
    return lax.ppermute(values, "fsdp", partners(mask, lax.axis_size("fsdp")))


def share(values, also=None):
    group = lax.axis_size("fsdp")
    place = lax.axis_index("fsdp")
    pieces = [values] + [swap_groups(values, mask) for mask in range(1, group)]
    if also is not None:
        pieces, _ = lax.optimization_barrier((pieces, also))
    return jnp.stack([pick(place ^ index, pieces) for index in range(group)])


def pick(index, pieces):
    chosen = pieces[0]
    for place in range(1, len(pieces)):
        chosen = jnp.where(index == place, pieces[place], chosen)
    return chosen


def scatter_sum(values):
    group = lax.axis_size("fsdp")
    place = lax.axis_index("fsdp")
    rows = values.shape[0] // group
    pieces = [
        lax.dynamic_slice_in_dim(values, (place ^ mask) * rows, rows, 0) for mask in range(group)
    ]
    pieces = pieces[:1] + [swap_groups(pieces[mask], mask) for mask in range(1, group)]
    total = pieces[0].astype(jnp.float32)
    for piece in pieces[1:]:
        total = total + piece.astype(jnp.float32)
    return total.astype(values.dtype)


def dp_masks(size):
    return [1 << index for index in range(size.bit_length() - 1)]


def dp_orders():
    first, *others = dp_masks(lax.axis_size("dp"))
    return first, [others, others[::-1]]


def spread(parts, late=None, early=None):
    size = lax.axis_size("dp")
    place = lax.axis_index("dp")
    first, orders = dp_orders()
    for step in reversed(range(len(orders[0]))):
        parts = [double(part, order[step], place, size) for part, order in zip(parts, orders)]
        if step == len(orders[0]) - 1 and early is not None:
            parts, early = lax.optimization_barrier((parts, early))
    parts, late = lax.optimization_barrier((parts, late))
    return parts, [swap_with(part, first, size) for part in parts], late, early


def arrival(order, first, group):
    devices = []
    for half in range(2):
        places = []
        for block in range(1 << len(order)):
            dp = half * first
            for index, mask in enumerate(order):
                if block >> (len(order) - 1 - index) & 1:
                    dp |= mask
            places += [dp * group + index for index in range(group)]
        devices.append(places)
    return devices


def in_order(own, came, bit, places, rows):
    whole = jnp.concatenate([jnp.where(bit == 0, own, came), jnp.where(bit == 0, came, own)], axis=0)
    whole = whole.reshape((-1, rows) + own.shape[1:])
    flat = places[0] + places[1]
    return jnp.stack([whole[flat.index(device)] for device in range(len(flat))])


def sum_grads(kept, sent, flipped_grad, prepare, finish_rows, width, hidden):
    size = lax.axis_size("dp")
    group = lax.axis_size("fsdp")
    place = lax.axis_index("dp")
    first, orders = dp_orders()
    mine = add_low(kept, swap_with(sent, first, size))
    rows = mine.shape[0] // 2
    parts = [mine[:rows], mine[rows:]]
    for step in range(len(orders[0])):
        halves = [cut(part, order[step], place) for part, order in zip(parts, orders)]
        if step == 0:
            halves, flipped_grad = lax.optimization_barrier((halves, flipped_grad))
            outgoing = prepare(flipped_grad)
        parts = [
            add_low(kept, swap_with(sent, order[step], size))
            for (sent, kept), order in zip(halves, orders)
        ]
        if step == 0:
            parts, outgoing = lax.optimization_barrier((parts, outgoing))
    incoming = lax.all_to_all(outgoing, ("dp", "fsdp"), split_axis=0, concat_axis=0, tiled=True)
    both = [part.reshape((group, -1) + part.shape[1:]) for part in parts]
    summed = scatter_sum(jnp.concatenate(both, axis=1).reshape((-1,) + kept.shape[1:]))
    summed, incoming = lax.optimization_barrier((summed, incoming))
    shared = share(summed)
    late = (finish_rows(incoming), flipped_grad.T)
    parts = [piece.reshape((-1,) + kept.shape[1:]) for piece in jnp.split(shared, 2, axis=1)]
    own, came, late, _ = spread(parts, late)
    return finish((place & first).reshape(1), own, came, width, hidden), *late


def on_device(
    owner_ids,
    row_ids,
    embed_table,
    expandone,
    expbiasone,
    reduceone,
    redbiasone,
    normgainone,
    taskgateone,
    sharegateone,
    expandtwo,
    expbiastwo,
    reducetwo,
    redbiastwo,
    normgaintwo,
    taskgatetwo,
    towerinner,
    towerbias,
    towermiddle,
    towertail,
    logit_cot,
):
    devices = lax.axis_size(("dp", "fsdp"))
    events, fields = owner_ids.shape
    emb_width = embed_table.shape[1]
    capacity = 2 * events * fields // devices
    hidden = expandone.shape[1]
    width = fields * emb_width
    group = lax.axis_size("fsdp")
    owner_rows = owner_ids.T
    request, rank = assign_slots(owner_rows, row_ids.T, devices, capacity)
    asked_rows = lax.all_to_all(request, ("dp", "fsdp"), split_axis=0, concat_axis=0, tiled=True)
    packed = pack(
        (expbiasone, redbiasone, normgainone, expbiastwo, redbiastwo, normgaintwo),
        (towerbias, towertail, taskgateone.T, sharegateone.T, taskgatetwo.T, towerinner, towermiddle),
        (expandone, reduceone, expandtwo, reducetwo),
    )
    found = find_rows(asked_rows, embed_table.T)
    packed = share(packed, asked_rows)
    split = expandone.shape[0] + THIN_ROWS
    first, orders = dp_orders()
    parts = [packed[:, :split], packed[:, split:]]
    own, came, _, found = spread([part.reshape(-1, hidden) for part in parts], early=found)
    returned = lax.all_to_all(found, ("dp", "fsdp"), split_axis=0, concat_axis=0, tiled=True)
    bit = (lax.axis_index("dp") & first).reshape(1)
    places = [arrival(order, first, group) for order in orders]
    flipped = place_rows(returned, rank, owner_rows)
    came, flipped = lax.optimization_barrier((came, flipped))
    thin = prep_thin(bit, own[0], came[0], places[0], width, hidden)
    sizes = [shard.shape[0] for shard in (expandone, reduceone, expandtwo, reducetwo)]
    if all(size % 16 == 0 for size in sizes):
        weights = (*own, *came)
    else:
        whole = [
            in_order(mine, other, bit[0], place, part.shape[1])
            for mine, other, place, part in zip(own, came, places, parts)
        ]
        starts = [0, 0, sizes[1], sizes[1] + sizes[2]]
        weights = tuple(
            whole[min(index, 1)][:, start : start + size].reshape(-1, hidden)
            for index, (start, size) in enumerate(zip(starts, sizes))
        )
        places = None

    chunk = 16 * devices
    grad_rows = -(-(6 * (width + 3 * hidden) + 2 * hidden) // chunk) * chunk
    logits, flipped_grad, kept, sent = dense(bit, flipped, weights, places, thin, logit_cot, grad_rows)

    def prepare(flipped_grad):
        return send_rows(flipped_grad, rank, owner_rows, capacity)

    def finish_rows(incoming):
        return add_rows(incoming, asked_rows, embed_table.shape[0])

    done, table_grad, x_grad = sum_grads(kept, sent, flipped_grad, prepare, finish_rows, width, hidden)
    return (logits, x_grad, table_grad.T, *done)


def solution(mesh):
    return jax.shard_map(
        on_device,
        mesh=mesh,
        in_specs=(
            P(("dp", "fsdp"), None),
            P(("dp", "fsdp"), None),
            P(("dp", "fsdp"), None),
            P(("dp", "fsdp"), None),
            P(("dp", "fsdp")),
            P(("dp", "fsdp"), None),
            P(("dp", "fsdp")),
            P(("dp", "fsdp")),
            P(("dp", "fsdp"), None),
            P(("dp", "fsdp"), None),
            P(("dp", "fsdp"), None),
            P(("dp", "fsdp")),
            P(("dp", "fsdp"), None),
            P(("dp", "fsdp")),
            P(("dp", "fsdp")),
            P(("dp", "fsdp"), None),
            P(("dp", "fsdp"), None),
            P(("dp", "fsdp")),
            P(("dp", "fsdp"), None),
            P(("dp", "fsdp")),
            P(None, ("dp", "fsdp")),
        ),
        out_specs=(
            P(None, ("dp", "fsdp")),
            P(("dp", "fsdp"), None),
            P(("dp", "fsdp"), None),
            P(),
            P(),
            P(),
            P(),
            P(),
            P(),
            P(),
            P(),
            P(),
            P(),
            P(),
            P(),
            P(),
            P(),
            P(),
            P(),
            P(),
        ),
        check_vma=False,
    )
```

```python
import functools

import jax
import jax.numpy as jnp
from jax import lax
from jax.experimental import pallas as pl
from jax.experimental.pallas import tpu as pltpu
from jax.sharding import PartitionSpec as P

EPS = 1e-05
VMEM_LIMIT = 56 * 1024 * 1024
ROW_BLOCKS = 8


def local_kernel(body, out_shape, flops, moved, scratch=()):
    return pl.pallas_call(
        body,
        out_shape=out_shape,
        scratch_shapes=list(scratch),
        compiler_params=pltpu.CompilerParams(vmem_limit_bytes=VMEM_LIMIT),
        cost_estimate=pl.CostEstimate(flops=flops, bytes_accessed=moved, transcendentals=0),
    )


def one_hot(hit):
    return jnp.where(hit, 1.0, 0.0).astype(jnp.bfloat16)


def low(value):
    return value.astype(jnp.float32).astype(jnp.bfloat16)


def iota(shape, axis):
    return lax.broadcasted_iota(jnp.int32, shape, axis)


def slot_body(owner_ref, row_ref, request_ref, rank_ref):
    fields, events = owner_ref.shape
    devices, _, capacity = request_ref.shape
    place = iota((devices, events), 0)
    asked = jnp.zeros((devices, events), jnp.float32)
    for field in range(fields):
        asked = asked + jnp.where(owner_ref[field : field + 1, :] == place, 1.0, 0.0)
    earlier = one_hot(iota((events, events), 0) < iota((events, events), 1))
    rank = jnp.dot(asked.astype(jnp.bfloat16), earlier, preferred_element_type=jnp.float32)
    rank = jnp.where(asked > 0.5, rank.astype(jnp.int32), -1)
    rank_ref[...] = rank
    slots = iota((capacity, events), 0)
    total = jnp.zeros((2 * devices, capacity), jnp.float32)
    for field in range(fields):
        mine = owner_ref[field : field + 1, :] == place
        field_rank = jnp.max(jnp.where(mine, rank, -1).astype(jnp.float32), axis=0, keepdims=True)
        rows = row_ref[field : field + 1, :]
        high = jnp.where(mine, (rows >> 6).astype(jnp.float32), 0.0)
        low = jnp.where(mine, (rows & 63).astype(jnp.float32), 0.0)
        value = jnp.concatenate([high, low], axis=0).astype(jnp.bfloat16)
        total = total + lax.dot_general(
            value,
            one_hot(field_rank.astype(jnp.int32) == slots),
            (((1,), (1,)), ((), ())),
            preferred_element_type=jnp.float32,
        )
    request = (total[:devices] * 64.0 + total[devices:]).astype(jnp.int32)
    for owner in range(devices):
        request_ref[owner] = request[owner : owner + 1]


def assign_slots(owner_rows, row_rows, devices, capacity):
    fields, events = owner_rows.shape
    return local_kernel(
        slot_body,
        (
            jax.ShapeDtypeStruct((devices, 1, capacity), jnp.int32),
            jax.ShapeDtypeStruct((devices, events), jnp.int32),
        ),
        2 * devices * events * (events + 2 * fields * capacity),
        4 * events * (2 * fields + devices),
    )(owner_rows, row_rows)


def find_body(request_ref, table_ref, found_ref, wide_ref):
    devices, _, capacity = request_ref.shape
    width = table_ref.shape[0]
    span = wide_ref.shape[1]
    places = iota((span, capacity), 0)
    for index in range(ROW_BLOCKS):
        wide_ref[index * width : (index + 1) * width, :] = table_ref[
            :, index * span : (index + 1) * span
        ]

    def step(source, carry):
        rows = request_ref[source]
        block = rows // span
        hits = one_hot(rows - block * span == places)
        rows_all = jnp.dot(wide_ref[...], hits, preferred_element_type=jnp.float32)
        picked = jnp.zeros((width, capacity), jnp.float32)
        for index in range(ROW_BLOCKS):
            picked = jnp.where(
                block == index, rows_all[index * width : (index + 1) * width, :], picked
            )
        found_ref[source] = picked.astype(jnp.bfloat16)
        return carry

    lax.fori_loop(0, devices, step, 0, unroll=16)


def find_rows(request, table):
    devices, _, capacity = request.shape
    width, rows = table.shape
    return local_kernel(
        find_body,
        jax.ShapeDtypeStruct((devices, width, capacity), jnp.bfloat16),
        2 * devices * capacity * rows * width,
        2 * (rows * width + devices * capacity * width),
        [pltpu.VMEM((ROW_BLOCKS * width, rows // ROW_BLOCKS), jnp.bfloat16)],
    )(request, table)


def place_body(found_ref, rank_ref, owner_ref, flipped_ref, total_ref):
    devices, width, capacity = found_ref.shape
    fields, events = owner_ref.shape
    slots = iota((capacity, events), 0)
    group = 4
    owners_low = low(owner_ref[...])
    total_ref[...] = jnp.zeros_like(total_ref)

    def step(start, carry):
        pieces = []
        for index in range(group):
            owner = start * group + index
            hits = one_hot(rank_ref[pl.ds(owner, 1), :] == slots)
            pieces.append(
                jnp.dot(found_ref[owner], hits, preferred_element_type=jnp.float32).astype(
                    jnp.bfloat16
                )
            )
        for field in range(fields):
            rows = slice(field * width, (field + 1) * width)
            owners = owners_low[field : field + 1, :]
            value = total_ref[rows, :]
            for index in range(group):
                value = jnp.where(owners == low(start * group + index), pieces[index], value)
            total_ref[rows, :] = value
        return carry

    lax.fori_loop(0, devices // group, step, 0)
    flipped_ref[...] = total_ref[...]


def place_rows(found, rank, owner_rows):
    devices, width, capacity = found.shape
    fields, events = owner_rows.shape
    return local_kernel(
        place_body,
        jax.ShapeDtypeStruct((fields * width, events), jnp.bfloat16),
        2 * devices * width * capacity * events,
        2 * (devices * width * capacity + fields * width * events),
        [pltpu.VMEM((fields * width, events), jnp.bfloat16)],
    )(found, rank, owner_rows)


def send_body(group, grad_ref, rank_ref, owner_ref, sent_ref, turned_ref, low_ref):
    devices, width, capacity = sent_ref.shape
    fields, events = owner_ref.shape
    slots = iota((capacity, events), 0)
    owners_low = low(owner_ref[...])
    low_ref[...] = grad_ref[...].astype(jnp.bfloat16)
    turned_ref[...] = grad_ref[...].T

    def step(owner, carry):
        chosen = jnp.zeros((width, events), jnp.bfloat16)
        for field in range(fields):
            rows = slice(field * width, (field + 1) * width)
            chosen = jnp.where(
                owners_low[field : field + 1, :] == low(owner), low_ref[rows, :], chosen
            )
        hits = one_hot(rank_ref[pl.ds(owner, 1), :] == slots)
        place = lax.rem(owner, group) * (devices // group) + lax.div(owner, group)
        sent_ref[place] = lax.dot_general(
            chosen,
            hits,
            (((1,), (1,)), ((), ())),
            preferred_element_type=jnp.float32,
        ).astype(jnp.bfloat16)
        return carry

    lax.fori_loop(0, devices, step, 0, unroll=16)


def send_rows(grad, rank, owner_rows, capacity, group):
    devices = rank.shape[0]
    fields, events = owner_rows.shape
    width = grad.shape[0] // fields
    return local_kernel(
        functools.partial(send_body, group),
        (
            jax.ShapeDtypeStruct((devices, width, capacity), jnp.bfloat16),
            jax.ShapeDtypeStruct((events, fields * width), jnp.float32),
        ),
        2 * devices * width * capacity * events,
        2 * (devices * width * capacity + 2 * fields * width * events),
        [pltpu.VMEM((fields * width, events), jnp.bfloat16)],
    )(grad, rank, owner_rows)


def add_body(came_ref, request_ref, out_ref, total_ref):
    devices, width, capacity = came_ref.shape
    span = total_ref.shape[1]
    group = 8
    places = iota((span, capacity), 0)
    total_ref[...] = jnp.zeros_like(total_ref)

    def step(start, carry):
        hits = []
        spread = []
        for index in range(group):
            source = start * group + index
            rows = request_ref[source]
            block = rows // span
            hits.append(one_hot(rows - block * span == places))
            came = came_ref[source].astype(jnp.float32)
            spread.append(
                jnp.concatenate(
                    [jnp.where(block == part, came, 0.0) for part in range(ROW_BLOCKS)], axis=0
                ).astype(jnp.bfloat16)
            )
        total_ref[...] += lax.dot_general(
            jnp.concatenate(spread, axis=1),
            jnp.concatenate(hits, axis=1),
            (((1,), (1,)), ((), ())),
            preferred_element_type=jnp.float32,
        )
        return carry

    lax.fori_loop(0, devices // group, step, 0, unroll=4)
    for index in range(ROW_BLOCKS):
        out_ref[:, index * span : (index + 1) * span] = total_ref[
            index * width : (index + 1) * width, :
        ]


def add_rows(came, request, rows):
    devices, width, capacity = came.shape
    span = rows // ROW_BLOCKS
    return local_kernel(
        add_body,
        jax.ShapeDtypeStruct((width, rows), jnp.float32),
        2 * devices * capacity * rows * width,
        2 * devices * width * capacity + 4 * rows * width,
        [pltpu.VMEM((ROW_BLOCKS * width, span), jnp.float32)],
    )(came, request)


THIN_ROWS = 48


def pack_thin_body(*refs):
    *biases, tbias, tail, taskgate, sharegate, upgate, inner, middle = refs[:13]
    *wide, out_ref, hold = refs[13:]
    hold[...] = jnp.zeros_like(hold)
    for row, piece in enumerate(biases + [tbias, tail]):
        hold[row : row + 1, : piece.shape[0]] = piece[...].astype(jnp.float32).reshape(1, -1)
    for row, piece in ((8, taskgate), (16, sharegate), (24, upgate), (32, inner)):
        hold[row : row + piece.shape[0], : piece.shape[1]] = piece[...].astype(jnp.float32)
    hold[32 : 32 + middle.shape[0], 128 : 128 + middle.shape[1]] = middle[...].astype(jnp.float32)
    thin = hold[...].astype(jnp.bfloat16)
    if not wide:
        out_ref[...] = thin
    start = 0
    for index, piece in enumerate(wide):
        out_ref[start : start + piece.shape[0], :] = piece[...]
        start += piece.shape[0]
        if index == 0:
            out_ref[start : start + THIN_ROWS, :] = thin
            start += THIN_ROWS


def pack(biases, others, wide):
    aligned = all(piece.shape[0] % 16 == 0 for piece in wide)
    rows = THIN_ROWS + (sum(piece.shape[0] for piece in wide) if aligned else 0)
    packed = local_kernel(
        pack_thin_body,
        jax.ShapeDtypeStruct((rows, 256), jnp.bfloat16),
        0,
        rows * 1024,
        [pltpu.VMEM((THIN_ROWS, 256), jnp.float32)],
    )(*biases, *others, *(wide if aligned else ()))
    if aligned:
        return packed
    return jnp.concatenate([wide[0], packed, *wide[1:]], axis=0)


def prep_thin_body(
    places,
    bit_ref,
    own_ref,
    came_ref,
    columns_ref,
    gate_one_ref,
    gate_one_back_ref,
    gate_two_ref,
    gate_two_back_ref,
    inner_ref,
    inner_back_ref,
    middle_ref,
    middle_back_ref,
    rows,
    task_rows,
    share_rows,
    up_rows,
    inner_rows,
    middle_rows,
    thin_own,
    thin_came,
    sems,
):
    devices = 2 * len(places[0])
    start = own_ref.shape[1] - THIN_ROWS
    copies = [
        pltpu.make_async_copy(ref.at[:, pl.ds(start, THIN_ROWS), :], held, sems.at[index])
        for index, (ref, held) in enumerate(((own_ref, thin_own), (came_ref, thin_came)))
    ]
    for copy in copies:
        copy.start()
    hidden = columns_ref.shape[0]
    width = gate_one_ref.shape[1]

    def lay(target, source, index, count):
        target[:, index * count : (index + 1) * count] = source[:, :count]

    rows[...] = jnp.zeros_like(rows)
    task_rows[...] = jnp.zeros_like(task_rows)
    share_rows[...] = jnp.zeros_like(share_rows)
    up_rows[...] = jnp.zeros_like(up_rows)
    bias = 6 * hidden // devices
    flat = hidden // devices

    def unpack(pieces):
        for half, source in enumerate(pieces):
            for block, index in enumerate(places[half]):
                thin = source[block].astype(jnp.float32)
                rows[0:6, index * bias : (index + 1) * bias] = thin[0:6, :bias]
                rows[6:8, index * flat : (index + 1) * flat] = thin[6:8, :flat]
                lay(task_rows, thin[8:16], index, 2 * width // devices)
                lay(share_rows, thin[16:24], index, width // devices)
                lay(up_rows, thin[24:32], index, 2 * hidden // devices)
                count = 2 * hidden // devices
                inner_rows[index * count : (index + 1) * count, :] = thin[32 : 32 + count, :128]
                count = hidden // devices
                middle_rows[index * count : (index + 1) * count, :] = thin[32 : 32 + count, 128:192]

    for copy in copies:
        copy.wait()

    @pl.when(bit_ref[0] == 0)
    def _():
        unpack((thin_own, thin_came))

    @pl.when(bit_ref[0] != 0)
    def _():
        unpack((thin_came, thin_own))

    columns_ref[...] = jnp.zeros_like(columns_ref)
    for expert in range(6):
        columns_ref[:, expert * 8 : expert * 8 + 8] = rows[:, expert * hidden : (expert + 1) * hidden].T
    gates = jnp.concatenate(
        [
            task_rows[:, :width],
            task_rows[:, width:],
            share_rows[...],
            jnp.zeros((8, width), jnp.float32),
        ],
        axis=0,
    )
    gate_one_ref[...] = gates.astype(jnp.bfloat16)
    gate_one_back_ref[...] = gates.T.astype(jnp.bfloat16)
    gate_two_ref[...] = jnp.concatenate([up_rows[:, :hidden], up_rows[:, hidden:]], axis=0).astype(
        jnp.bfloat16
    )
    for task in range(2):
        span = slice(task * hidden, (task + 1) * hidden)
        wide = jnp.concatenate([up_rows[:, span], jnp.zeros((8, hidden), jnp.float32)], axis=0)
        gate_two_back_ref[span, :] = wide.T.astype(jnp.bfloat16)
        inner_ref[task * 128 : (task + 1) * 128, :] = inner_rows[span, :].T.astype(jnp.bfloat16)
        span = slice(task * 128, (task + 1) * 128)
        middle_ref[task * 64 : (task + 1) * 64, :] = middle_rows[span, :].T.astype(jnp.bfloat16)
    inner_back_ref[...] = inner_rows[...].astype(jnp.bfloat16)
    middle_back_ref[...] = middle_rows[...].astype(jnp.bfloat16)


def prep_thin(bit, own, came, places, width, hidden):
    blocks = len(places[0])
    low = functools.partial(jax.ShapeDtypeStruct, dtype=jnp.bfloat16)
    return pl.pallas_call(
        functools.partial(prep_thin_body, places),
        out_shape=(
            jax.ShapeDtypeStruct((hidden, 64), jnp.float32),
            low((32, width)),
            low((width, 32)),
            low((16, hidden)),
            low((2 * hidden, 16)),
            low((hidden, hidden)),
            low((2 * hidden, 128)),
            low((128, 128)),
            low((hidden, 64)),
        ),
        in_specs=[pl.BlockSpec(memory_space=pltpu.SMEM)] + [pl.BlockSpec(memory_space=pl.ANY)] * 2,
        scratch_shapes=[
            pltpu.VMEM((8, 6 * hidden), jnp.float32),
            pltpu.VMEM((8, 2 * width), jnp.float32),
            pltpu.VMEM((8, width), jnp.float32),
            pltpu.VMEM((8, 2 * hidden), jnp.float32),
            pltpu.VMEM((2 * hidden, 128), jnp.float32),
            pltpu.VMEM((hidden, 64), jnp.float32),
            pltpu.VMEM((blocks, THIN_ROWS, hidden), jnp.bfloat16),
            pltpu.VMEM((blocks, THIN_ROWS, hidden), jnp.bfloat16),
            pltpu.SemaphoreType.DMA((2,)),
        ],
        compiler_params=pltpu.CompilerParams(vmem_limit_bytes=VMEM_LIMIT),
        cost_estimate=pl.CostEstimate(flops=0, bytes_accessed=4 * own.size, transcendentals=0),
    )(bit, own.reshape(blocks, -1, hidden), came.reshape(blocks, -1, hidden))


SPAN = 512
ONES = 16


def over_events(left, right):
    return lax.dot_general(left, right, (((1,), (1,)), ((), ())), preferred_element_type=jnp.float32)


def times(left, right):
    return jnp.dot(left, right, preferred_element_type=jnp.float32)


def sum_rows(values):
    return jnp.sum(values, axis=0, keepdims=True)


def sigmoid_of(values):
    return 0.5 * jnp.tanh(0.5 * values) + 0.5


def silu_parts(values):
    sig = sigmoid_of(values)
    active = values * sig
    return active, sig + active * (1.0 - sig)


def expert_up(inputs, expand, expbias, shrink, shrinkbias):
    active, slope = silu_parts(times(expand, inputs) + expbias)
    active = active.astype(jnp.bfloat16)
    output = times(shrink, active) + shrinkbias
    scale = 1.0 / output.shape[0]
    centered = output - sum_rows(output) * scale
    inverse = lax.rsqrt(sum_rows(centered * centered) * scale + EPS)
    return active, slope, centered * inverse, inverse


def soft(scores, count):
    valid = iota(scores.shape, 0) < count
    scores = jnp.where(valid, scores, -1e30)
    shifted = jnp.exp(scores - jnp.max(scores, axis=0, keepdims=True))
    shifted = jnp.where(valid, shifted, 0.0)
    return shifted / sum_rows(shifted)


def soft_back(probs, rows):
    tall = jnp.concatenate(rows + [jnp.zeros_like(rows[0])] * (probs.shape[0] - len(rows)), axis=0)
    return probs * (tall - sum_rows(probs * tall))


def assemble(bit, own_ref, came_ref, homes, places):
    blocks = len(places[0])
    rows = own_ref.shape[0] // blocks
    for half, source in ((bit, own_ref), (1 - bit, came_ref)):
        for block in range(blocks):
            start = block * rows
            for home in homes:
                size = home.shape[0] // (2 * blocks)
                place = places[0][block] * size + half * ((places[1][0] - places[0][0]) * size)
                home[pl.ds(pl.multiple_of(place, 16), size), :] = source[start : start + size, :]
                start += size


def dense_body(places, *refs):
    bit_ref, *refs = refs
    if places is None:
        *naturals, refs = *refs[:4], refs[4:]
    else:
        own_a, own_b, came_a, came_b, *refs = refs
        naturals, refs = refs[-4:], refs[:-4]
    expand_one_back_ref, shrink_one_back_ref, expand_two_back_ref, shrink_two_back_ref = naturals
    (
        flipped_ref,
        columns_ref,
        gate_one_ref,
        gate_one_back_ref,
        gate_two_ref,
        gate_two_back_ref,
        inner_ref,
        inner_back_ref,
        middle_ref,
        middle_back_ref,
        cot_ref,
        logits_ref,
        flipped_grad_ref,
        kept_ref,
        sent_ref,
        sems,
        grads_ref,
        input_keep,
        active_one,
        out_one,
        pre_one,
        score_one,
        carried_keep,
        active_two,
        out_two,
        pre_two,
        score_two,
        tower_keep,
        tower_act_keep,
        first_keep,
        top_keep,
        tail_keep,
        gain_keep,
        expand_one_ref,
        shrink_one_ref,
        expand_two_ref,
        shrink_two_ref,
    ) = refs
    bit = jnp.minimum(bit_ref[0], 1)
    if places is not None:
        assemble(bit, own_a, came_a, [expand_one_back_ref], places[0])
        assemble(
            bit,
            own_b,
            came_b,
            [shrink_one_back_ref, expand_two_back_ref, shrink_two_back_ref],
            places[1],
        )
    for natural, turned in (
        (expand_one_back_ref, expand_one_ref),
        (shrink_one_back_ref, shrink_one_ref),
        (expand_two_back_ref, expand_two_ref),
        (shrink_two_back_ref, shrink_two_ref),
    ):
        depth = natural.shape[0] // 6
        across = natural.shape[1]
        for expert in range(6):
            turned[expert * across : (expert + 1) * across, :] = natural[
                expert * depth : (expert + 1) * depth, :
            ].T

    width, events = flipped_ref.shape
    hidden = shrink_one_back_ref.shape[1]
    inner = inner_ref.shape[0] // 2
    narrow = middle_ref.shape[0] // 2
    tall = hidden + ONES
    span = min(SPAN, events)
    unit = jnp.ones((ONES, events), jnp.bfloat16)

    input_keep[:width, :] = flipped_ref[...]
    input_keep[width:, :] = unit
    for expert in range(6):
        active_one[expert * tall + hidden : (expert + 1) * tall, :] = unit
        active_two[expert * tall + hidden : (expert + 1) * tall, :] = unit
    for group in range(3):
        carried_keep[group * tall + hidden : (group + 1) * tall, :] = unit
    for task in range(2):
        tower_keep[task * tall + hidden : (task + 1) * tall, :] = unit
    gain_keep[...] = jnp.zeros_like(gain_keep)

    def column(index, rows=hidden, start=0):
        return columns_ref[start : start + rows, index : index + 1]

    def experts_rows(expert):
        return slice(expert * hidden, (expert + 1) * hidden)

    def span_step(step, carry):
        lanes = pl.ds(pl.multiple_of(step * span, span), span)
        inputs = flipped_ref[:, lanes]

        def up(level, inputs_of, expand_ref, shrink_ref, active_keep):
            kept = []
            for expert in range(6):
                active, slope, normed, inverse = expert_up(
                    inputs_of(expert),
                    expand_ref[experts_rows(expert), :],
                    column(expert * 8 + level),
                    shrink_ref[experts_rows(expert), :],
                    column(expert * 8 + level + 1),
                )
                active_keep[expert * tall : expert * tall + hidden, lanes] = active
                kept.append((slope, normed, inverse, normed * column(expert * 8 + level + 2)))
            return kept

        kept_one = up(0, lambda expert: inputs, expand_one_ref, shrink_one_ref, active_one)
        scores = times(gate_one_ref[...], inputs)
        probs_one = [soft(scores[0:8], 4), soft(scores[8:16], 4), soft(scores[16:24], 6)]
        carried = []
        for group in range(3):
            members = [2 * group, 2 * group + 1, 4, 5] if group < 2 else range(6)
            mixed = 0.0
            for place, expert in enumerate(members):
                mixed = mixed + probs_one[group][place : place + 1, :] * kept_one[expert][3]
            carried.append(mixed.astype(jnp.bfloat16))
            carried_keep[group * tall : group * tall + hidden, lanes] = carried[group]

        kept_two = up(
            3, lambda expert: carried[expert // 2], expand_two_ref, shrink_two_ref, active_two
        )
        probs_two = []
        tower_grads = []
        dq_two = []
        for task in range(2):
            probs = soft(times(gate_two_ref[task * 8 : task * 8 + 8, :], carried[task]), 4)
            probs_two.append(probs)
            members = [2 * task, 2 * task + 1, 4, 5]
            mixed = 0.0
            for place, expert in enumerate(members):
                mixed = mixed + probs[place : place + 1, :] * kept_two[expert][3]
            mixed = mixed.astype(jnp.bfloat16)
            tower_keep[task * tall : task * tall + hidden, lanes] = mixed
            first, first_slope = silu_parts(
                times(inner_ref[task * inner : (task + 1) * inner, :], mixed)
                + column(6, inner, task * inner)
            )
            first = first.astype(jnp.bfloat16)
            tower_act_keep[task * inner : (task + 1) * inner, lanes] = first
            top, top_slope = silu_parts(
                times(middle_ref[task * narrow : (task + 1) * narrow, :], first)
                + column(7, narrow, 2 * task * narrow)
            )
            weight = column(7, narrow, (2 * task + 1) * narrow)
            logits_ref[task : task + 1, lanes] = sum_rows(top * weight)
            cot = cot_ref[task : task + 1, lanes]
            top_grad = (cot * weight * top_slope).astype(jnp.bfloat16)
            top_keep[task * narrow : (task + 1) * narrow, lanes] = top_grad
            seen = cot * top
            high = seen.astype(jnp.bfloat16)
            tail_keep[2 * task * narrow : (2 * task + 1) * narrow, lanes] = high
            tail_keep[(2 * task + 1) * narrow : (2 * task + 2) * narrow, lanes] = (
                seen - high.astype(jnp.float32)
            ).astype(jnp.bfloat16)
            first_grad = (
                times(middle_back_ref[task * inner : (task + 1) * inner, :], top_grad) * first_slope
            ).astype(jnp.bfloat16)
            first_keep[task * inner : (task + 1) * inner, lanes] = first_grad
            grad = times(inner_back_ref[task * hidden : (task + 1) * hidden, :], first_grad)
            tower_grads.append(grad)
            dq_two.append([sum_rows(kept_two[expert][3] * grad) for expert in members])

        def expert_down(level, expert, kept, upstream, slant, shrink_back_ref, out_keep, pre_keep):
            slope, normed, inverse, _ = kept
            gained = upstream * normed
            part = gained[:, :128]
            for start in range(128, span, 128):
                part = part + gained[:, start : start + 128]
            gain_rows = slice((level + expert) * hidden, (level + expert + 1) * hidden)
            gain_keep[gain_rows, :] += part
            scaled = upstream * column(expert * 8 + level // 2 + 2)
            scale = 1.0 / hidden
            out_low = (
                inverse * (scaled - sum_rows(scaled) * scale - normed * (slant * scale))
            ).astype(jnp.bfloat16)
            out_keep[experts_rows(expert), lanes] = out_low
            pre_low = (times(shrink_back_ref[experts_rows(expert), :], out_low) * slope).astype(
                jnp.bfloat16
            )
            pre_keep[experts_rows(expert), lanes] = pre_low
            return pre_low

        pre_lows = []
        for expert in range(6):
            if expert < 4:
                task, place = expert // 2, expert % 2
                prob = probs_two[task][place : place + 1, :]
                upstream = prob * tower_grads[task]
                slant = prob * dq_two[task][place]
            else:
                place = expert - 2
                prob = [probs_two[task][place : place + 1, :] for task in range(2)]
                upstream = prob[0] * tower_grads[0] + prob[1] * tower_grads[1]
                slant = prob[0] * dq_two[0][place] + prob[1] * dq_two[1][place]
            pre_lows.append(
                expert_down(
                    6, expert, kept_two[expert], upstream, slant, shrink_two_back_ref, out_two, pre_two
                )
            )
        carried_grads = []
        for group in range(3):
            grad = 0.0
            for expert in (2 * group, 2 * group + 1):
                grad = grad + times(expand_two_back_ref[experts_rows(expert), :], pre_lows[expert])
            if group < 2:
                score = soft_back(probs_two[group], dq_two[group])
                score = jnp.concatenate([score, jnp.zeros_like(score)], axis=0).astype(jnp.bfloat16)
                score_two[group * 16 : group * 16 + 16, lanes] = score
                grad = grad + times(gate_two_back_ref[experts_rows(group), :], score)
            carried_grads.append(grad)

        dq_one = []
        for group in range(3):
            members = [2 * group, 2 * group + 1, 4, 5] if group < 2 else range(6)
            dq_one.append([sum_rows(kept_one[expert][3] * carried_grads[group]) for expert in members])
        pre_lows = []
        for expert in range(6):
            prob = probs_one[2][expert : expert + 1, :]
            upstream = prob * carried_grads[2]
            slant = prob * dq_one[2][expert]
            for task in range(2):
                if expert // 2 in (task, 2):
                    place = expert % 2 if expert < 4 else expert - 2
                    prob = probs_one[task][place : place + 1, :]
                    upstream = upstream + prob * carried_grads[task]
                    slant = slant + prob * dq_one[task][place]
            pre_lows.append(
                expert_down(
                    0, expert, kept_one[expert], upstream, slant, shrink_one_back_ref, out_one, pre_one
                )
            )
        scores_low = [soft_back(probs_one[group], dq_one[group]) for group in range(3)]
        score = jnp.concatenate(scores_low + [jnp.zeros_like(scores_low[0])], axis=0).astype(
            jnp.bfloat16
        )
        score_one[:, lanes] = score
        grad = times(gate_one_back_ref[...], score)
        for expert in range(6):
            grad = grad + times(
                expand_one_back_ref[expert * width : (expert + 1) * width, :], pre_lows[expert]
            )
        flipped_grad_ref[:, lanes] = grad
        return carry

    lax.fori_loop(0, events // span, span_step, 0)

    half_rows = grads_ref.shape[1]

    def leave(half):
        for target, sem, when in ((kept_ref, 0, half), (sent_ref, 1, 1 - half)):

            @pl.when(bit == when)
            def _():
                pltpu.make_async_copy(grads_ref.at[half], target, sems.at[sem]).start()

    def put(row, value):
        while value.shape[0]:
            half, start = row // half_rows, row % half_rows
            count = min(value.shape[0], half_rows - start)
            grads_ref[half, start : start + count, :] = value[:count].astype(jnp.bfloat16)
            row, value = row + count, value[count:]
            if row % half_rows == 0:
                leave(half)

    rows = 0
    biases = []
    for expert in range(6):
        both = over_events(input_keep[...], pre_one[experts_rows(expert), :])
        put(rows + expert * width, both[:width])
        biases.append(both[width : width + 1])
    rows += 6 * width
    for expert in range(6):
        both = over_events(active_one[expert * tall : (expert + 1) * tall, :], out_one[experts_rows(expert), :])
        put(rows + expert * hidden, both[:hidden])
        biases.append(both[hidden : hidden + 1])
    rows += 6 * hidden
    for expert in range(6):
        group = expert // 2
        both = over_events(carried_keep[group * tall : (group + 1) * tall, :], pre_two[experts_rows(expert), :])
        put(rows + expert * hidden, both[:hidden])
        biases.append(both[hidden : hidden + 1])
    rows += 6 * hidden
    for expert in range(6):
        both = over_events(active_two[expert * tall : (expert + 1) * tall, :], out_two[experts_rows(expert), :])
        put(rows + expert * hidden, both[:hidden])
        biases.append(both[hidden : hidden + 1])
    rows += 6 * hidden
    tower = []
    for task in range(2):
        tower.append(
            over_events(tower_keep[task * tall : (task + 1) * tall, :], first_keep[task * inner : (task + 1) * inner, :])
        )
    tower = jnp.concatenate(tower, axis=1)
    put(rows, tower[:hidden])
    biases.append(tower[hidden : hidden + 1])
    rows += hidden
    put(
        rows,
        jnp.concatenate(
            [
                over_events(
                    top_keep[task * narrow : (task + 1) * narrow, :],
                    tower_act_keep[task * inner : (task + 1) * inner, :],
                )
                for task in range(2)
            ],
            axis=1,
        ),
    )
    rows += narrow
    gates = over_events(score_one[...], flipped_ref[...])
    for start in range(0, width, hidden):
        put(rows, gates[:, start : start + hidden])
        rows += gates.shape[0]
    for task in range(2):
        put(
            rows,
            over_events(
                score_two[task * 16 : task * 16 + 16, :],
                carried_keep[task * tall : task * tall + hidden, :],
            ),
        )
        rows += 16
    tops = over_events(unit, top_keep[...])[:1]
    seen = over_events(unit, tail_keep[...])[:1]
    pieces = []
    for task in range(2):
        pieces.append(tops[:, task * narrow : (task + 1) * narrow])
        pieces.append(
            seen[:, 2 * task * narrow : (2 * task + 1) * narrow]
            + seen[:, (2 * task + 1) * narrow : (2 * task + 2) * narrow]
        )
    biases.append(jnp.concatenate(pieces, axis=1))
    gains = gain_keep[...]
    high = gains.astype(jnp.bfloat16)
    low = (gains - high.astype(jnp.float32)).astype(jnp.bfloat16)
    gains = (over_events(unit[:, :128], high) + over_events(unit[:, :128], low))[:1]
    for expert in range(12):
        biases.append(gains[:, experts_rows(expert)])
    biases = jnp.concatenate(biases, axis=0)
    extra = 2 * half_rows - rows - biases.shape[0]
    put(rows, jnp.concatenate([biases, jnp.zeros((extra, hidden), jnp.float32)], axis=0))
    pltpu.make_async_copy(grads_ref.at[bit], kept_ref, sems.at[0]).wait()
    pltpu.make_async_copy(grads_ref.at[1 - bit], sent_ref, sems.at[1]).wait()


def dense(bit, flipped, weights, places, thin, cot, grad_rows):
    width, events = flipped.shape
    hidden = thin[0].shape[0]
    inner, narrow = 128, 64
    tall = hidden + ONES
    low = functools.partial(pltpu.VMEM, dtype=jnp.bfloat16)
    kept = (
        width + ONES,
        6 * tall,
        6 * hidden,
        6 * hidden,
        32,
        3 * tall,
        6 * tall,
        6 * hidden,
        6 * hidden,
        32,
        2 * tall,
        2 * inner,
        2 * inner,
        2 * narrow,
        4 * narrow,
    )
    half = (grad_rows // 2, hidden)
    scratch = [pltpu.SemaphoreType.DMA((2,)), low((2,) + half)]
    scratch += [low((rows, events)) for rows in kept]
    scratch.append(pltpu.VMEM((12 * hidden, 128), jnp.float32))
    scratch += [low((6 * hidden, depth)) for depth in (width, hidden, hidden, hidden)]
    vmem = pl.BlockSpec(memory_space=pltpu.VMEM)
    outside = pl.BlockSpec(memory_space=pl.ANY)
    specs = [pl.BlockSpec(memory_space=pltpu.SMEM)] + [vmem] * (len(weights) + len(thin) + 2)
    if places is not None:
        scratch += [low((6 * depth, hidden)) for depth in (width, hidden, hidden, hidden)]
    return pl.pallas_call(
        functools.partial(dense_body, places),
        out_shape=(
            jax.ShapeDtypeStruct((2, events), jnp.float32),
            jax.ShapeDtypeStruct((width, events), jnp.float32),
            jax.ShapeDtypeStruct(half, jnp.bfloat16),
            jax.ShapeDtypeStruct(half, jnp.bfloat16),
        ),
        in_specs=specs,
        out_specs=(vmem, vmem, outside, outside),
        scratch_shapes=scratch,
        compiler_params=pltpu.CompilerParams(vmem_limit_bytes=VMEM_LIMIT),
        cost_estimate=pl.CostEstimate(
            flops=6 * events * hidden * (6 * (width + 3 * hidden) + 2 * inner),
            bytes_accessed=24 * 1024 * 1024,
            transcendentals=12 * events * hidden,
        ),
    )(bit, *weights, flipped, *thin, cot)


def grad_layout(width, hidden):
    sizes = [6 * width, 6 * hidden, 6 * hidden, 6 * hidden]
    starts = [sum(sizes[:index]) for index in range(5)]
    return sizes, starts


def grad_moves(part, wide, half, hidden, width):
    sizes, starts = grad_layout(width, hidden)
    moves = []
    for index in range(2):
        first = (2 * half + index) * part
        for target, (start, size) in enumerate(zip(starts, sizes)):
            low_row, high_row = max(first, start), min(first + part, start + size)
            if low_row < high_row:
                moves.append((index, low_row - first, target, low_row - start, high_row - low_row))
    return moves


def write_wide(half, pieces, wide, hold, sems, width, hidden):
    part = pieces[0].shape[0]
    block = 128
    copies = []
    for number, (index, start, target, place, rows) in enumerate(
        grad_moves(part, wide, half, hidden, width)
    ):
        source = pieces[index]
        base = index * part + start

        def step(count, carry):
            hold[pl.ds(pl.multiple_of(base + count * block, block), block), :] = source[
                pl.ds(pl.multiple_of(start + count * block, block), block), :
            ].astype(jnp.float32)
            return carry

        lax.fori_loop(0, rows // block, step, 0, unroll=4)
        copy = pltpu.make_async_copy(
            hold.at[pl.ds(base, rows), :], wide[target].at[pl.ds(place, rows), :], sems.at[number]
        )
        copy.start()
        copies.append(copy)
    return copies


def own_body(bit_ref, own_a_ref, own_b_ref, *refs):
    *wide, hold, sems = refs
    hidden = wide[0].shape[1]
    width = wide[0].shape[0] // 6

    for half in range(2):

        @pl.when(jnp.minimum(bit_ref[0], 1) == half)
        def _():
            for copy in write_wide(half, (own_a_ref, own_b_ref), wide, hold, sems, width, hidden):
                copy.wait()


def came_body(bit_ref, own_b_ref, came_a_ref, came_b_ref, *refs):
    wide, outs, (hold, sems) = refs[4:8], refs[8:21], refs[21:]
    hidden = wide[0].shape[1]
    width = wide[0].shape[0] // 6
    part = came_a_ref.shape[0]
    start = grad_layout(width, hidden)[1][4] - 3 * part

    for half in range(2):

        @pl.when(jnp.minimum(bit_ref[0], 1) != half)
        def _():
            copies = write_wide(half, (came_a_ref, came_b_ref), wide, hold, sems, width, hidden)
            write_rest(came_b_ref if half else own_b_ref, start, outs, width, hidden)
            for copy in copies:
                copy.wait()


def write_rest(source, start, outs, width, hidden):
    (
        low_inbias_ref,
        low_outbias_ref,
        low_gain_ref,
        low_taskgate_ref,
        low_sharegate_ref,
        up_inbias_ref,
        up_outbias_ref,
        up_gain_ref,
        up_taskgate_ref,
        inner_ref,
        tbias_ref,
        middle_ref,
        tail_ref,
    ) = outs
    inner = inner_ref.shape[1]

    def take(rows):
        nonlocal start
        start += rows
        return source[start - rows : start, :].astype(jnp.float32)

    both = take(hidden)
    inner_ref[:hidden, :] = both[:, :inner]
    inner_ref[hidden:, :] = both[:, inner:]
    middle_ref[...] = take(middle_ref.shape[0])
    for index in range(width // hidden):
        gates = take(32)
        span = slice(index * hidden, (index + 1) * hidden)
        low_taskgate_ref[:, span] = gates[0:4]
        low_taskgate_ref[:, width + index * hidden : width + (index + 1) * hidden] = gates[8:12]
        low_sharegate_ref[:, span] = gates[16:22]
    for task in range(2):
        up_taskgate_ref[:, task * hidden : (task + 1) * hidden] = take(16)[0:4]
    rows = take(48)
    flat = (low_inbias_ref, low_outbias_ref, up_inbias_ref, up_outbias_ref, tbias_ref, tail_ref)
    place = 0
    for target in flat + (low_gain_ref, up_gain_ref):
        for index in range(target.shape[0] // hidden):
            target[index * hidden : (index + 1) * hidden] = rows[place]
            place += 1


def finish(bit, own, came, width, hidden):
    wide_shapes = tuple(
        jax.ShapeDtypeStruct((size, hidden), jnp.float32) for size in grad_layout(width, hidden)[0]
    )
    rest_shapes = (
        (6 * hidden,),
        (6 * hidden,),
        (6 * hidden,),
        (4, 2 * width),
        (6, width),
        (6 * hidden,),
        (6 * hidden,),
        (6 * hidden,),
        (4, 2 * hidden),
        (2 * hidden, 128),
        (256,),
        (64, 256),
        (256,),
    )
    outside, inside = pl.BlockSpec(memory_space=pl.ANY), pl.BlockSpec(memory_space=pltpu.VMEM)
    small = pl.BlockSpec(memory_space=pltpu.SMEM)
    params = pltpu.CompilerParams(vmem_limit_bytes=VMEM_LIMIT)
    moved = 6 * 2 * own[0].size
    scratch = [pltpu.VMEM((2 * own[0].shape[0], hidden), jnp.float32), pltpu.SemaphoreType.DMA((4,))]
    wide = pl.pallas_call(
        own_body,
        out_shape=wide_shapes,
        in_specs=[small, inside, inside],
        out_specs=(outside,) * 4,
        scratch_shapes=scratch,
        compiler_params=params,
        cost_estimate=pl.CostEstimate(flops=0, bytes_accessed=moved, transcendentals=0),
    )(bit, *own)
    done = pl.pallas_call(
        came_body,
        out_shape=wide_shapes
        + tuple(jax.ShapeDtypeStruct(shape, jnp.float32) for shape in rest_shapes),
        in_specs=[small] + [inside] * 3 + [outside] * 4,
        out_specs=(outside,) * 4 + (inside,) * 13,
        scratch_shapes=scratch,
        input_output_aliases={4 + index: index for index in range(4)},
        compiler_params=params,
        cost_estimate=pl.CostEstimate(flops=0, bytes_accessed=moved, transcendentals=0),
    )(bit, own[1], *came, *wide)
    done = [value.T if value.shape[0] in (4, 6, 64) else value for value in done]
    wide, rest = done[:4], done[4:]
    return (wide[0], rest[0], wide[1], *rest[1:5], wide[2], rest[5], wide[3], *rest[6:])


def partners(mask, size):
    return [(index, index ^ mask) for index in range(size)]


def swap_with(values, mask, size):
    return lax.ppermute(values, "dp", partners(mask, size))


def cut(values, mask, place):
    rows = values.shape[0] // 2
    bit = jnp.where((place & mask) != 0, 1, 0)
    sent = lax.dynamic_slice_in_dim(values, (1 - bit) * rows, rows, 0)
    return sent, lax.dynamic_slice_in_dim(values, bit * rows, rows, 0)


def add_low(kept, came):
    return (kept.astype(jnp.float32) + came.astype(jnp.float32)).astype(kept.dtype)


def double(values, mask, place, size):
    came = swap_with(values, mask, size)
    upper = (place & mask) != 0
    return jnp.concatenate(
        [jnp.where(upper, came, values), jnp.where(upper, values, came)], axis=0
    )


def swap_groups(values, mask):
    return lax.ppermute(values, "fsdp", partners(mask, lax.axis_size("fsdp")))


def share(values, also=None):
    group = lax.axis_size("fsdp")
    place = lax.axis_index("fsdp")
    pieces = [values] + [swap_groups(values, mask) for mask in range(1, group)]
    if also is not None:
        pieces, _ = lax.optimization_barrier((pieces, also))
    return jnp.stack([pick(place ^ index, pieces) for index in range(group)])


def pick(index, pieces):
    chosen = pieces[0]
    for place in range(1, len(pieces)):
        chosen = jnp.where(index == place, pieces[place], chosen)
    return chosen


def z_pieces(values):
    group = lax.axis_size("fsdp")
    place = lax.axis_index("fsdp")
    rows = values.shape[0] // group
    return [
        lax.dynamic_slice_in_dim(values, (place ^ mask) * rows, rows, 0) for mask in range(group)
    ]


def scatter_sum(pieces):
    came = [swap_groups(piece, mask) for mask, piece in enumerate(pieces) if mask]
    total = pieces[0].astype(jnp.float32)
    for piece in came:
        total = total + piece.astype(jnp.float32)
    return total.astype(pieces[0].dtype)


def dp_masks(size):
    return [1 << index for index in range(size.bit_length() - 1)]


def dp_orders():
    first, *others = dp_masks(lax.axis_size("dp"))
    return first, [others, others[::-1]]


def spread(parts, late=None, early=None):
    size = lax.axis_size("dp")
    place = lax.axis_index("dp")
    first, orders = dp_orders()
    for step in reversed(range(len(orders[0]))):
        parts = [double(part, order[step], place, size) for part, order in zip(parts, orders)]
        if step == len(orders[0]) - 1 and early is not None:
            parts, early = lax.optimization_barrier((parts, early))
    parts, late = lax.optimization_barrier((parts, late))
    return parts, [swap_with(part, first, size) for part in parts], late, early


def arrival(order, first, group):
    devices = []
    for half in range(2):
        places = []
        for block in range(1 << len(order)):
            dp = half * first
            for index, mask in enumerate(order):
                if block >> (len(order) - 1 - index) & 1:
                    dp |= mask
            places += [dp * group + index for index in range(group)]
        devices.append(places)
    return devices


def in_order(own, came, bit, places, rows):
    whole = jnp.concatenate([jnp.where(bit == 0, own, came), jnp.where(bit == 0, came, own)], axis=0)
    whole = whole.reshape((-1, rows) + own.shape[1:])
    flat = places[0] + places[1]
    return jnp.stack([whole[flat.index(device)] for device in range(len(flat))])


def sum_grads(kept, sent, flipped_grad, prepare, finish_rows, width, hidden):
    size = lax.axis_size("dp")
    group = lax.axis_size("fsdp")
    place = lax.axis_index("dp")
    first, orders = dp_orders()
    came = swap_with(sent, first, size)
    outgoing, x_grad = prepare(flipped_grad)
    came, outgoing = lax.optimization_barrier((came, outgoing))
    mine = add_low(kept, came)
    rows = mine.shape[0] // 2
    parts = [mine[:rows], mine[rows:]]
    for step in range(len(orders[0])):
        halves = [cut(part, order[step], place) for part, order in zip(parts, orders)]
        if step == 0:
            halves, outgoing = lax.optimization_barrier((halves, outgoing))
            incoming = lax.all_to_all(
                outgoing, ("dp", "fsdp"), split_axis=0, concat_axis=0, tiled=True
            )
        parts = [
            add_low(kept, swap_with(sent, order[step], size))
            for (sent, kept), order in zip(halves, orders)
        ]
    both = [part.reshape((group, -1) + part.shape[1:]) for part in parts]
    both = jnp.concatenate(both, axis=1).reshape((-1,) + kept.shape[1:])
    pieces = z_pieces(both)
    pieces, incoming = lax.optimization_barrier((pieces, incoming))
    shared = share(scatter_sum(pieces))
    late = (finish_rows(incoming), x_grad)
    parts = [piece.reshape((-1,) + kept.shape[1:]) for piece in jnp.split(shared, 2, axis=1)]
    own, came, late, _ = spread(parts, late)
    return finish((place & first).reshape(1), own, came, width, hidden), *late


def on_device(
    owner_ids,
    row_ids,
    embed_table,
    expandone,
    expbiasone,
    reduceone,
    redbiasone,
    normgainone,
    taskgateone,
    sharegateone,
    expandtwo,
    expbiastwo,
    reducetwo,
    redbiastwo,
    normgaintwo,
    taskgatetwo,
    towerinner,
    towerbias,
    towermiddle,
    towertail,
    logit_cot,
):
    devices = lax.axis_size(("dp", "fsdp"))
    events, fields = owner_ids.shape
    emb_width = embed_table.shape[1]
    capacity = 2 * events * fields // devices
    hidden = expandone.shape[1]
    width = fields * emb_width
    group = lax.axis_size("fsdp")
    owner_rows = owner_ids.T
    request, rank = assign_slots(owner_rows, row_ids.T, devices, capacity)
    asked_rows = lax.all_to_all(request, ("dp", "fsdp"), split_axis=0, concat_axis=0, tiled=True)
    packed = pack(
        (expbiasone, redbiasone, normgainone, expbiastwo, redbiastwo, normgaintwo),
        (towerbias, towertail, taskgateone.T, sharegateone.T, taskgatetwo.T, towerinner, towermiddle),
        (expandone, reduceone, expandtwo, reducetwo),
    )
    found = find_rows(asked_rows, embed_table.T)
    packed = share(packed, asked_rows)
    split = expandone.shape[0] + THIN_ROWS
    first, orders = dp_orders()
    parts = [packed[:, :split], packed[:, split:]]
    own, came, _, found = spread([part.reshape(-1, hidden) for part in parts], early=found)
    returned = lax.all_to_all(found, ("dp", "fsdp"), split_axis=0, concat_axis=0, tiled=True)
    bit = (lax.axis_index("dp") & first).reshape(1)
    places = [arrival(order, first, group) for order in orders]
    flipped = place_rows(returned, rank, owner_rows)
    came, flipped = lax.optimization_barrier((came, flipped))
    thin = prep_thin(bit, own[0], came[0], places[0], width, hidden)
    sizes = [shard.shape[0] for shard in (expandone, reduceone, expandtwo, reducetwo)]
    if all(size % 16 == 0 for size in sizes):
        weights = (*own, *came)
    else:
        whole = [
            in_order(mine, other, bit[0], place, part.shape[1])
            for mine, other, place, part in zip(own, came, places, parts)
        ]
        starts = [0, 0, sizes[1], sizes[1] + sizes[2]]
        weights = tuple(
            whole[min(index, 1)][:, start : start + size].reshape(-1, hidden)
            for index, (start, size) in enumerate(zip(starts, sizes))
        )
        places = None

    chunk = 16 * devices
    grad_rows = -(-(6 * (width + 3 * hidden) + 2 * hidden) // chunk) * chunk
    logits, flipped_grad, kept, sent = dense(bit, flipped, weights, places, thin, logit_cot, grad_rows)

    def prepare(flipped_grad):
        return send_rows(flipped_grad, rank, owner_rows, capacity, 1)

    def finish_rows(incoming):
        return add_rows(incoming, asked_rows, embed_table.shape[0])

    done, table_grad, x_grad = sum_grads(kept, sent, flipped_grad, prepare, finish_rows, width, hidden)
    return (logits, x_grad, table_grad.T, *done)


def solution(mesh):
    return jax.shard_map(
        on_device,
        mesh=mesh,
        in_specs=(
            P(("dp", "fsdp"), None),
            P(("dp", "fsdp"), None),
            P(("dp", "fsdp"), None),
            P(("dp", "fsdp"), None),
            P(("dp", "fsdp")),
            P(("dp", "fsdp"), None),
            P(("dp", "fsdp")),
            P(("dp", "fsdp")),
            P(("dp", "fsdp"), None),
            P(("dp", "fsdp"), None),
            P(("dp", "fsdp"), None),
            P(("dp", "fsdp")),
            P(("dp", "fsdp"), None),
            P(("dp", "fsdp")),
            P(("dp", "fsdp")),
            P(("dp", "fsdp"), None),
            P(("dp", "fsdp"), None),
            P(("dp", "fsdp")),
            P(("dp", "fsdp"), None),
            P(("dp", "fsdp")),
            P(None, ("dp", "fsdp")),
        ),
        out_specs=(
            P(None, ("dp", "fsdp")),
            P(("dp", "fsdp"), None),
            P(("dp", "fsdp"), None),
            P(),
            P(),
            P(),
            P(),
            P(),
            P(),
            P(),
            P(),
            P(),
            P(),
            P(),
            P(),
            P(),
            P(),
            P(),
            P(),
            P(),
        ),
        check_vma=False,
    )
```

```python
import functools

import jax
import jax.numpy as jnp
from jax import lax
from jax.experimental import pallas as pl
from jax.experimental.pallas import tpu as pltpu
from jax.sharding import PartitionSpec as P

EPS = 1e-05
VMEM_LIMIT = 56 * 1024 * 1024
SMALL_LIMIT = 16 * 1024 * 1024
ROW_BLOCKS = 8


def local_kernel(body, out_shape, flops, moved, scratch=(), limit=SMALL_LIMIT):
    return pl.pallas_call(
        body,
        out_shape=out_shape,
        scratch_shapes=list(scratch),
        compiler_params=pltpu.CompilerParams(vmem_limit_bytes=limit),
        cost_estimate=pl.CostEstimate(flops=flops, bytes_accessed=moved, transcendentals=0),
    )


def one_hot(hit):
    return jnp.where(hit, 1.0, 0.0).astype(jnp.bfloat16)


def low(value):
    return value.astype(jnp.float32).astype(jnp.bfloat16)


def iota(shape, axis):
    return lax.broadcasted_iota(jnp.int32, shape, axis)


def slot_body(owner_ref, row_ref, request_ref, rank_ref):
    fields, events = owner_ref.shape
    devices, _, capacity = request_ref.shape
    place = iota((devices, events), 0)
    asked = jnp.zeros((devices, events), jnp.float32)
    for field in range(fields):
        asked = asked + jnp.where(owner_ref[field : field + 1, :] == place, 1.0, 0.0)
    earlier = one_hot(iota((events, events), 0) < iota((events, events), 1))
    rank = jnp.dot(asked.astype(jnp.bfloat16), earlier, preferred_element_type=jnp.float32)
    rank = jnp.where(asked > 0.5, rank.astype(jnp.int32), -1)
    rank_ref[...] = rank
    slots = iota((capacity, events), 0)
    total = jnp.zeros((2 * devices, capacity), jnp.float32)
    for field in range(fields):
        mine = owner_ref[field : field + 1, :] == place
        field_rank = jnp.max(jnp.where(mine, rank, -1).astype(jnp.float32), axis=0, keepdims=True)
        rows = row_ref[field : field + 1, :]
        high = jnp.where(mine, (rows >> 6).astype(jnp.float32), 0.0)
        low = jnp.where(mine, (rows & 63).astype(jnp.float32), 0.0)
        value = jnp.concatenate([high, low], axis=0).astype(jnp.bfloat16)
        total = total + lax.dot_general(
            value,
            one_hot(field_rank.astype(jnp.int32) == slots),
            (((1,), (1,)), ((), ())),
            preferred_element_type=jnp.float32,
        )
    request = (total[:devices] * 64.0 + total[devices:]).astype(jnp.int32)
    for owner in range(devices):
        request_ref[owner] = request[owner : owner + 1]


def assign_slots(owner_rows, row_rows, devices, capacity):
    fields, events = owner_rows.shape
    return local_kernel(
        slot_body,
        (
            jax.ShapeDtypeStruct((devices, 1, capacity), jnp.int32),
            jax.ShapeDtypeStruct((devices, events), jnp.int32),
        ),
        2 * devices * events * (events + 2 * fields * capacity),
        4 * events * (2 * fields + devices),
        limit=VMEM_LIMIT,
    )(owner_rows, row_rows)


def find_body(request_ref, table_ref, found_ref, wide_ref):
    devices, _, capacity = request_ref.shape
    width = table_ref.shape[0]
    span = wide_ref.shape[1]
    places = iota((span, capacity), 0)
    for index in range(ROW_BLOCKS):
        wide_ref[index * width : (index + 1) * width, :] = table_ref[
            :, index * span : (index + 1) * span
        ]

    def step(source, carry):
        rows = request_ref[source]
        block = rows // span
        hits = one_hot(rows - block * span == places)
        rows_all = jnp.dot(wide_ref[...], hits, preferred_element_type=jnp.float32)
        picked = jnp.zeros((width, capacity), jnp.float32)
        for index in range(ROW_BLOCKS):
            picked = jnp.where(
                block == index, rows_all[index * width : (index + 1) * width, :], picked
            )
        found_ref[source] = picked.astype(jnp.bfloat16)
        return carry

    lax.fori_loop(0, devices, step, 0, unroll=16)


def find_rows(request, table):
    devices, _, capacity = request.shape
    width, rows = table.shape
    return local_kernel(
        find_body,
        jax.ShapeDtypeStruct((devices, width, capacity), jnp.bfloat16),
        16 * devices * capacity * rows * width,
        2 * (rows * width + devices * capacity * width),
        [pltpu.VMEM((ROW_BLOCKS * width, rows // ROW_BLOCKS), jnp.bfloat16)],
    )(request, table)


def place_body(found_ref, rank_ref, owner_ref, flipped_ref, total_ref):
    devices, width, capacity = found_ref.shape
    fields, events = owner_ref.shape
    slots = iota((capacity, events), 0)
    group = 4
    owners_low = low(owner_ref[...])
    total_ref[...] = jnp.zeros_like(total_ref)

    def step(start, carry):
        pieces = []
        for index in range(group):
            owner = start * group + index
            hits = one_hot(rank_ref[pl.ds(owner, 1), :] == slots)
            pieces.append(
                jnp.dot(found_ref[owner], hits, preferred_element_type=jnp.float32).astype(
                    jnp.bfloat16
                )
            )
        for field in range(fields):
            rows = slice(field * width, (field + 1) * width)
            owners = owners_low[field : field + 1, :]
            value = total_ref[rows, :]
            for index in range(group):
                value = jnp.where(owners == low(start * group + index), pieces[index], value)
            total_ref[rows, :] = value
        return carry

    lax.fori_loop(0, devices // group, step, 0)
    flipped_ref[...] = total_ref[...]


def place_rows(found, rank, owner_rows):
    devices, width, capacity = found.shape
    fields, events = owner_rows.shape
    return local_kernel(
        place_body,
        jax.ShapeDtypeStruct((fields * width, events), jnp.bfloat16),
        2 * devices * width * capacity * events,
        2 * (devices * width * capacity + fields * width * events),
        [pltpu.VMEM((fields * width, events), jnp.bfloat16)],
    )(found, rank, owner_rows)


def send_body(group, grad_ref, rank_ref, owner_ref, sent_ref, turned_ref, low_ref):
    devices, width, capacity = sent_ref.shape
    fields, events = owner_ref.shape
    slots = iota((capacity, events), 0)
    owners_low = low(owner_ref[...])
    low_ref[...] = grad_ref[...].astype(jnp.bfloat16)
    turned_ref[...] = grad_ref[...].T

    def step(owner, carry):
        chosen = jnp.zeros((width, events), jnp.bfloat16)
        for field in range(fields):
            rows = slice(field * width, (field + 1) * width)
            chosen = jnp.where(
                owners_low[field : field + 1, :] == low(owner), low_ref[rows, :], chosen
            )
        hits = one_hot(rank_ref[pl.ds(owner, 1), :] == slots)
        place = lax.rem(owner, group) * (devices // group) + lax.div(owner, group)
        sent_ref[place] = lax.dot_general(
            chosen,
            hits,
            (((1,), (1,)), ((), ())),
            preferred_element_type=jnp.float32,
        ).astype(jnp.bfloat16)
        return carry

    lax.fori_loop(0, devices, step, 0, unroll=16)


def send_rows(grad, rank, owner_rows, capacity, group):
    devices = rank.shape[0]
    fields, events = owner_rows.shape
    width = grad.shape[0] // fields
    return local_kernel(
        functools.partial(send_body, group),
        (
            jax.ShapeDtypeStruct((devices, width, capacity), jnp.bfloat16),
            jax.ShapeDtypeStruct((events, fields * width), jnp.float32),
        ),
        2 * devices * width * capacity * events,
        2 * (devices * width * capacity + 2 * fields * width * events),
        [pltpu.VMEM((fields * width, events), jnp.bfloat16)],
    )(grad, rank, owner_rows)


def add_body(came_ref, request_ref, out_ref, total_ref):
    devices, width, capacity = came_ref.shape
    span = total_ref.shape[1]
    group = 8
    places = iota((span, capacity), 0)
    total_ref[...] = jnp.zeros_like(total_ref)

    def step(start, carry):
        hits = []
        spread = []
        for index in range(group):
            source = start * group + index
            rows = request_ref[source]
            block = rows // span
            hits.append(one_hot(rows - block * span == places))
            came = came_ref[source].astype(jnp.float32)
            spread.append(
                jnp.concatenate(
                    [jnp.where(block == part, came, 0.0) for part in range(ROW_BLOCKS)], axis=0
                ).astype(jnp.bfloat16)
            )
        total_ref[...] += lax.dot_general(
            jnp.concatenate(spread, axis=1),
            jnp.concatenate(hits, axis=1),
            (((1,), (1,)), ((), ())),
            preferred_element_type=jnp.float32,
        )
        return carry

    lax.fori_loop(0, devices // group, step, 0, unroll=4)
    for index in range(ROW_BLOCKS):
        out_ref[:, index * span : (index + 1) * span] = total_ref[
            index * width : (index + 1) * width, :
        ]


def add_rows(came, request, rows):
    devices, width, capacity = came.shape
    span = rows // ROW_BLOCKS
    return local_kernel(
        add_body,
        jax.ShapeDtypeStruct((width, rows), jnp.float32),
        2 * devices * capacity * rows * width,
        2 * devices * width * capacity + 4 * rows * width,
        [pltpu.VMEM((ROW_BLOCKS * width, span), jnp.float32)],
    )(came, request)


THIN_ROWS = 48


def pack_thin_body(*refs):
    *biases, tbias, tail, taskgate, sharegate, upgate, inner, middle = refs[:13]
    *wide, out_ref, hold = refs[13:]
    hold[...] = jnp.zeros_like(hold)
    for row, piece in enumerate(biases + [tbias, tail]):
        hold[row : row + 1, : piece.shape[0]] = piece[...].astype(jnp.float32).reshape(1, -1)
    for row, piece in ((8, taskgate), (16, sharegate), (24, upgate), (32, inner)):
        hold[row : row + piece.shape[0], : piece.shape[1]] = piece[...].astype(jnp.float32)
    hold[32 : 32 + middle.shape[0], 128 : 128 + middle.shape[1]] = middle[...].astype(jnp.float32)
    thin = hold[...].astype(jnp.bfloat16)
    if not wide:
        out_ref[...] = thin
    start = 0
    for index, piece in enumerate(wide):
        out_ref[start : start + piece.shape[0], :] = piece[...]
        start += piece.shape[0]
        if index == 0:
            out_ref[start : start + THIN_ROWS, :] = thin
            start += THIN_ROWS


def pack(biases, others, wide):
    aligned = all(piece.shape[0] % 16 == 0 for piece in wide)
    rows = THIN_ROWS + (sum(piece.shape[0] for piece in wide) if aligned else 0)
    packed = local_kernel(
        pack_thin_body,
        jax.ShapeDtypeStruct((rows, 256), jnp.bfloat16),
        0,
        rows * 1024,
        [pltpu.VMEM((THIN_ROWS, 256), jnp.float32)],
        limit=VMEM_LIMIT,
    )(*biases, *others, *(wide if aligned else ()))
    if aligned:
        return packed
    return jnp.concatenate([wide[0], packed, *wide[1:]], axis=0)


def lay_thin(bit, sources, places, outs, holds):
    (
        columns_ref,
        gate_one_ref,
        gate_one_back_ref,
        gate_two_ref,
        gate_two_back_ref,
        inner_ref,
        inner_back_ref,
        middle_ref,
        middle_back_ref,
    ) = outs
    rows, task_rows, share_rows, up_rows, inner_rows, middle_rows = holds
    devices = 2 * len(places[0])
    hidden = columns_ref.shape[0]
    width = gate_one_ref.shape[1]

    def lay(target, source, index, count):
        target[:, index * count : (index + 1) * count] = source[:, :count]

    for held in (rows, task_rows, share_rows, up_rows):
        held[...] = jnp.zeros_like(held)
    bias = 6 * hidden // devices
    flat = hidden // devices

    def unpack(pieces):
        for half, source in enumerate(pieces):
            for block, index in enumerate(places[half]):
                thin = source(block).astype(jnp.float32)
                rows[0:6, index * bias : (index + 1) * bias] = thin[0:6, :bias]
                rows[6:8, index * flat : (index + 1) * flat] = thin[6:8, :flat]
                lay(task_rows, thin[8:16], index, 2 * width // devices)
                lay(share_rows, thin[16:24], index, width // devices)
                lay(up_rows, thin[24:32], index, 2 * hidden // devices)
                count = 2 * hidden // devices
                inner_rows[index * count : (index + 1) * count, :] = thin[32 : 32 + count, :128]
                count = hidden // devices
                middle_rows[index * count : (index + 1) * count, :] = thin[32 : 32 + count, 128:192]

    @pl.when(bit == 0)
    def _():
        unpack(sources)

    @pl.when(bit != 0)
    def _():
        unpack(sources[::-1])

    columns_ref[...] = jnp.zeros_like(columns_ref)
    for expert in range(6):
        columns_ref[:, expert * 8 : expert * 8 + 8] = rows[:, expert * hidden : (expert + 1) * hidden].T
    gates = jnp.concatenate(
        [
            task_rows[:, :width],
            task_rows[:, width:],
            share_rows[...],
            jnp.zeros((8, width), jnp.float32),
        ],
        axis=0,
    )
    gate_one_ref[...] = gates.astype(jnp.bfloat16)
    gate_one_back_ref[...] = gates.T.astype(jnp.bfloat16)
    gate_two_ref[...] = jnp.concatenate([up_rows[:, :hidden], up_rows[:, hidden:]], axis=0).astype(
        jnp.bfloat16
    )
    for task in range(2):
        span = slice(task * hidden, (task + 1) * hidden)
        wide = jnp.concatenate([up_rows[:, span], jnp.zeros((8, hidden), jnp.float32)], axis=0)
        gate_two_back_ref[span, :] = wide.T.astype(jnp.bfloat16)
        inner_ref[task * 128 : (task + 1) * 128, :] = inner_rows[span, :].T.astype(jnp.bfloat16)
        span = slice(task * 128, (task + 1) * 128)
        middle_ref[task * 64 : (task + 1) * 64, :] = middle_rows[span, :].T.astype(jnp.bfloat16)
    inner_back_ref[...] = inner_rows[...].astype(jnp.bfloat16)
    middle_back_ref[...] = middle_rows[...].astype(jnp.bfloat16)


def prep_thin_body(places, bit_ref, own_ref, came_ref, *refs):
    outs, holds, (thin_own, thin_came, sems) = refs[:9], refs[9:15], refs[15:]
    start = own_ref.shape[1] - THIN_ROWS
    copies = [
        pltpu.make_async_copy(ref.at[:, pl.ds(start, THIN_ROWS), :], held, sems.at[index])
        for index, (ref, held) in enumerate(((own_ref, thin_own), (came_ref, thin_came)))
    ]
    for copy in copies:
        copy.start()
    for copy in copies:
        copy.wait()
    sources = (lambda block: thin_own[block], lambda block: thin_came[block])
    lay_thin(bit_ref[0], sources, places, outs, holds)


def thin_shapes(width, hidden):
    outs = (
        ((hidden, 64), jnp.float32),
        ((32, width), jnp.bfloat16),
        ((width, 32), jnp.bfloat16),
        ((16, hidden), jnp.bfloat16),
        ((2 * hidden, 16), jnp.bfloat16),
        ((hidden, hidden), jnp.bfloat16),
        ((2 * hidden, 128), jnp.bfloat16),
        ((128, 128), jnp.bfloat16),
        ((hidden, 64), jnp.bfloat16),
    )
    holds = (
        (8, 6 * hidden),
        (8, 2 * width),
        (8, width),
        (8, 2 * hidden),
        (2 * hidden, 128),
        (hidden, 64),
    )
    return outs, [pltpu.VMEM(shape, jnp.float32) for shape in holds]


def prep_thin(bit, own, came, places, width, hidden):
    blocks = len(places[0])
    outs, holds = thin_shapes(width, hidden)
    thin_held = pltpu.VMEM((blocks, THIN_ROWS, hidden), jnp.bfloat16)
    return pl.pallas_call(
        functools.partial(prep_thin_body, places),
        out_shape=tuple(jax.ShapeDtypeStruct(*out) for out in outs),
        in_specs=[pl.BlockSpec(memory_space=pltpu.SMEM)] + [pl.BlockSpec(memory_space=pl.ANY)] * 2,
        scratch_shapes=holds + [thin_held, thin_held, pltpu.SemaphoreType.DMA((2,))],
        compiler_params=pltpu.CompilerParams(vmem_limit_bytes=VMEM_LIMIT),
        cost_estimate=pl.CostEstimate(flops=0, bytes_accessed=4 * own.size, transcendentals=0),
    )(bit, own.reshape(blocks, -1, hidden), came.reshape(blocks, -1, hidden))


SPAN = 512
ONES = 16


def over_events(left, right):
    return lax.dot_general(left, right, (((1,), (1,)), ((), ())), preferred_element_type=jnp.float32)


def times(left, right):
    return jnp.dot(left, right, preferred_element_type=jnp.float32)


def sum_rows(values):
    return jnp.sum(values, axis=0, keepdims=True)


def sigmoid_of(values):
    return 0.5 * jnp.tanh(0.5 * values) + 0.5


def silu_parts(values):
    sig = sigmoid_of(values)
    active = values * sig
    return active, sig + active * (1.0 - sig)


def expert_up(inputs, expand, expbias, shrink, shrinkbias):
    active, slope = silu_parts(times(expand, inputs) + expbias)
    active = active.astype(jnp.bfloat16)
    output = times(shrink, active) + shrinkbias
    scale = 1.0 / output.shape[0]
    centered = output - sum_rows(output) * scale
    inverse = lax.rsqrt(sum_rows(centered * centered) * scale + EPS)
    return active, slope, centered * inverse, inverse


def soft(scores, count):
    valid = iota(scores.shape, 0) < count
    scores = jnp.where(valid, scores, -1e30)
    shifted = jnp.exp(scores - jnp.max(scores, axis=0, keepdims=True))
    shifted = jnp.where(valid, shifted, 0.0)
    return shifted / sum_rows(shifted)


def soft_back(probs, rows):
    tall = jnp.concatenate(rows + [jnp.zeros_like(rows[0])] * (probs.shape[0] - len(rows)), axis=0)
    return probs * (tall - sum_rows(probs * tall))


def assemble(bit, own_ref, came_ref, homes, places):
    blocks = len(places[0])
    rows = own_ref.shape[0] // blocks
    for half, source in ((bit, own_ref), (1 - bit, came_ref)):
        for block in range(blocks):
            start = block * rows
            for home in homes:
                size = home.shape[0] // (2 * blocks)
                place = places[0][block] * size + half * ((places[1][0] - places[0][0]) * size)
                home[pl.ds(pl.multiple_of(place, 16), size), :] = source[start : start + size, :]
                start += size


def dense_body(places, *refs):
    bit_ref, *refs = refs
    if places is None:
        *naturals, refs = *refs[:4], refs[4:]
    else:
        arrived, refs = refs[:4], refs[4:]
        refs, naturals, holds, held, loads = refs[:-15], refs[-15:-11], refs[-11:-5], refs[-5:-1], refs[-1]
        thin, refs = refs[-9:], refs[:-9]
        refs = [refs[0], *thin, *refs[1:]]
    expand_one_back_ref, shrink_one_back_ref, expand_two_back_ref, shrink_two_back_ref = naturals
    (
        flipped_ref,
        columns_ref,
        gate_one_ref,
        gate_one_back_ref,
        gate_two_ref,
        gate_two_back_ref,
        inner_ref,
        inner_back_ref,
        middle_ref,
        middle_back_ref,
        cot_ref,
        logits_ref,
        flipped_grad_ref,
        kept_ref,
        sent_ref,
        sems,
        grads_ref,
        input_keep,
        active_one,
        out_one,
        pre_one,
        score_one,
        carried_keep,
        active_two,
        out_two,
        pre_two,
        score_two,
        tower_keep,
        tower_act_keep,
        first_keep,
        top_keep,
        tail_keep,
        gain_keep,
        expand_one_ref,
        shrink_one_ref,
        expand_two_ref,
        shrink_two_ref,
    ) = refs
    bit = jnp.minimum(bit_ref[0], 1)
    if places is not None:
        copies = [
            pltpu.make_async_copy(arrived[index], held[index], loads.at[index]) for index in (0, 2, 1, 3)
        ]
        for copy in copies:
            copy.start()
        own_a, own_b, came_a, came_b = held
        for copy in copies[:2]:
            copy.wait()
        shard = own_a.shape[0] // len(places[0][0])

        def thin_of(ref):
            return lambda block: ref[(block + 1) * shard - THIN_ROWS : (block + 1) * shard, :]

        lay_thin(bit, (thin_of(own_a), thin_of(came_a)), places[0], thin, holds)
        for copy in copies[2:]:
            copy.wait()
        assemble(bit, own_a, came_a, [expand_one_back_ref], places[0])
        assemble(
            bit,
            own_b,
            came_b,
            [shrink_one_back_ref, expand_two_back_ref, shrink_two_back_ref],
            places[1],
        )
    for natural, turned in (
        (expand_one_back_ref, expand_one_ref),
        (shrink_one_back_ref, shrink_one_ref),
        (expand_two_back_ref, expand_two_ref),
        (shrink_two_back_ref, shrink_two_ref),
    ):
        depth = natural.shape[0] // 6
        across = natural.shape[1]
        for expert in range(6):
            turned[expert * across : (expert + 1) * across, :] = natural[
                expert * depth : (expert + 1) * depth, :
            ].T

    width, events = flipped_ref.shape
    hidden = shrink_one_back_ref.shape[1]
    inner = inner_ref.shape[0] // 2
    narrow = middle_ref.shape[0] // 2
    tall = hidden + ONES
    span = min(SPAN, events)
    unit = jnp.ones((ONES, events), jnp.bfloat16)

    input_keep[:width, :] = flipped_ref[...]
    input_keep[width:, :] = unit
    for expert in range(6):
        active_one[expert * tall + hidden : (expert + 1) * tall, :] = unit
        active_two[expert * tall + hidden : (expert + 1) * tall, :] = unit
    for group in range(3):
        carried_keep[group * tall + hidden : (group + 1) * tall, :] = unit
    for task in range(2):
        tower_keep[task * tall + hidden : (task + 1) * tall, :] = unit
    gain_keep[...] = jnp.zeros_like(gain_keep)

    def column(index, rows=hidden, start=0):
        return columns_ref[start : start + rows, index : index + 1]

    def experts_rows(expert):
        return slice(expert * hidden, (expert + 1) * hidden)

    def span_step(step, carry):
        lanes = pl.ds(pl.multiple_of(step * span, span), span)
        inputs = flipped_ref[:, lanes]

        def up(level, inputs_of, expand_ref, shrink_ref, active_keep):
            kept = []
            for expert in range(6):
                active, slope, normed, inverse = expert_up(
                    inputs_of(expert),
                    expand_ref[experts_rows(expert), :],
                    column(expert * 8 + level),
                    shrink_ref[experts_rows(expert), :],
                    column(expert * 8 + level + 1),
                )
                active_keep[expert * tall : expert * tall + hidden, lanes] = active
                kept.append((slope, normed, inverse, normed * column(expert * 8 + level + 2)))
            return kept

        kept_one = up(0, lambda expert: inputs, expand_one_ref, shrink_one_ref, active_one)
        scores = times(gate_one_ref[...], inputs)
        probs_one = [soft(scores[0:8], 4), soft(scores[8:16], 4), soft(scores[16:24], 6)]
        carried = []
        for group in range(3):
            members = [2 * group, 2 * group + 1, 4, 5] if group < 2 else range(6)
            mixed = 0.0
            for place, expert in enumerate(members):
                mixed = mixed + probs_one[group][place : place + 1, :] * kept_one[expert][3]
            carried.append(mixed.astype(jnp.bfloat16))
            carried_keep[group * tall : group * tall + hidden, lanes] = carried[group]

        kept_two = up(
            3, lambda expert: carried[expert // 2], expand_two_ref, shrink_two_ref, active_two
        )
        probs_two = []
        tower_grads = []
        dq_two = []
        for task in range(2):
            probs = soft(times(gate_two_ref[task * 8 : task * 8 + 8, :], carried[task]), 4)
            probs_two.append(probs)
            members = [2 * task, 2 * task + 1, 4, 5]
            mixed = 0.0
            for place, expert in enumerate(members):
                mixed = mixed + probs[place : place + 1, :] * kept_two[expert][3]
            mixed = mixed.astype(jnp.bfloat16)
            tower_keep[task * tall : task * tall + hidden, lanes] = mixed
            first, first_slope = silu_parts(
                times(inner_ref[task * inner : (task + 1) * inner, :], mixed)
                + column(6, inner, task * inner)
            )
            first = first.astype(jnp.bfloat16)
            tower_act_keep[task * inner : (task + 1) * inner, lanes] = first
            top, top_slope = silu_parts(
                times(middle_ref[task * narrow : (task + 1) * narrow, :], first)
                + column(7, narrow, 2 * task * narrow)
            )
            weight = column(7, narrow, (2 * task + 1) * narrow)
            logits_ref[task : task + 1, lanes] = sum_rows(top * weight)
            cot = cot_ref[task : task + 1, lanes]
            top_grad = (cot * weight * top_slope).astype(jnp.bfloat16)
            top_keep[task * narrow : (task + 1) * narrow, lanes] = top_grad
            seen = cot * top
            high = seen.astype(jnp.bfloat16)
            tail_keep[2 * task * narrow : (2 * task + 1) * narrow, lanes] = high
            tail_keep[(2 * task + 1) * narrow : (2 * task + 2) * narrow, lanes] = (
                seen - high.astype(jnp.float32)
            ).astype(jnp.bfloat16)
            first_grad = (
                times(middle_back_ref[task * inner : (task + 1) * inner, :], top_grad) * first_slope
            ).astype(jnp.bfloat16)
            first_keep[task * inner : (task + 1) * inner, lanes] = first_grad
            grad = times(inner_back_ref[task * hidden : (task + 1) * hidden, :], first_grad)
            tower_grads.append(grad)
            dq_two.append([sum_rows(kept_two[expert][3] * grad) for expert in members])

        def expert_down(level, expert, kept, upstream, slant, shrink_back_ref, out_keep, pre_keep):
            slope, normed, inverse, _ = kept
            gained = upstream * normed
            part = gained[:, :128]
            for start in range(128, span, 128):
                part = part + gained[:, start : start + 128]
            gain_rows = slice((level + expert) * hidden, (level + expert + 1) * hidden)
            gain_keep[gain_rows, :] += part
            scaled = upstream * column(expert * 8 + level // 2 + 2)
            scale = 1.0 / hidden
            out_low = (
                inverse * (scaled - sum_rows(scaled) * scale - normed * (slant * scale))
            ).astype(jnp.bfloat16)
            out_keep[experts_rows(expert), lanes] = out_low
            pre_low = (times(shrink_back_ref[experts_rows(expert), :], out_low) * slope).astype(
                jnp.bfloat16
            )
            pre_keep[experts_rows(expert), lanes] = pre_low
            return pre_low

        pre_lows = []
        for expert in range(6):
            if expert < 4:
                task, place = expert // 2, expert % 2
                prob = probs_two[task][place : place + 1, :]
                upstream = prob * tower_grads[task]
                slant = prob * dq_two[task][place]
            else:
                place = expert - 2
                prob = [probs_two[task][place : place + 1, :] for task in range(2)]
                upstream = prob[0] * tower_grads[0] + prob[1] * tower_grads[1]
                slant = prob[0] * dq_two[0][place] + prob[1] * dq_two[1][place]
            pre_lows.append(
                expert_down(
                    6, expert, kept_two[expert], upstream, slant, shrink_two_back_ref, out_two, pre_two
                )
            )
        carried_grads = []
        for group in range(3):
            grad = 0.0
            for expert in (2 * group, 2 * group + 1):
                grad = grad + times(expand_two_back_ref[experts_rows(expert), :], pre_lows[expert])
            if group < 2:
                score = soft_back(probs_two[group], dq_two[group])
                score = jnp.concatenate([score, jnp.zeros_like(score)], axis=0).astype(jnp.bfloat16)
                score_two[group * 16 : group * 16 + 16, lanes] = score
                grad = grad + times(gate_two_back_ref[experts_rows(group), :], score)
            carried_grads.append(grad)

        dq_one = []
        for group in range(3):
            members = [2 * group, 2 * group + 1, 4, 5] if group < 2 else range(6)
            dq_one.append([sum_rows(kept_one[expert][3] * carried_grads[group]) for expert in members])
        pre_lows = []
        for expert in range(6):
            prob = probs_one[2][expert : expert + 1, :]
            upstream = prob * carried_grads[2]
            slant = prob * dq_one[2][expert]
            for task in range(2):
                if expert // 2 in (task, 2):
                    place = expert % 2 if expert < 4 else expert - 2
                    prob = probs_one[task][place : place + 1, :]
                    upstream = upstream + prob * carried_grads[task]
                    slant = slant + prob * dq_one[task][place]
            pre_lows.append(
                expert_down(
                    0, expert, kept_one[expert], upstream, slant, shrink_one_back_ref, out_one, pre_one
                )
            )
        scores_low = [soft_back(probs_one[group], dq_one[group]) for group in range(3)]
        score = jnp.concatenate(scores_low + [jnp.zeros_like(scores_low[0])], axis=0).astype(
            jnp.bfloat16
        )
        score_one[:, lanes] = score
        grad = times(gate_one_back_ref[...], score)
        for expert in range(6):
            grad = grad + times(
                expand_one_back_ref[expert * width : (expert + 1) * width, :], pre_lows[expert]
            )
        flipped_grad_ref[:, lanes] = grad
        return carry

    lax.fori_loop(0, events // span, span_step, 0)

    half_rows = grads_ref.shape[1]

    def leave(half):
        for target, sem, when in ((kept_ref, 0, half), (sent_ref, 1, 1 - half)):

            @pl.when(bit == when)
            def _():
                pltpu.make_async_copy(grads_ref.at[half], target, sems.at[sem]).start()

    def put(row, value):
        while value.shape[0]:
            half, start = row // half_rows, row % half_rows
            count = min(value.shape[0], half_rows - start)
            grads_ref[half, start : start + count, :] = value[:count].astype(jnp.bfloat16)
            row, value = row + count, value[count:]
            if row % half_rows == 0:
                leave(half)

    rows = 0
    biases = []
    for expert in range(6):
        both = over_events(input_keep[...], pre_one[experts_rows(expert), :])
        put(rows + expert * width, both[:width])
        biases.append(both[width : width + 1])
    rows += 6 * width
    for expert in range(6):
        both = over_events(active_one[expert * tall : (expert + 1) * tall, :], out_one[experts_rows(expert), :])
        put(rows + expert * hidden, both[:hidden])
        biases.append(both[hidden : hidden + 1])
    rows += 6 * hidden
    for expert in range(6):
        group = expert // 2
        both = over_events(carried_keep[group * tall : (group + 1) * tall, :], pre_two[experts_rows(expert), :])
        put(rows + expert * hidden, both[:hidden])
        biases.append(both[hidden : hidden + 1])
    rows += 6 * hidden
    for expert in range(6):
        both = over_events(active_two[expert * tall : (expert + 1) * tall, :], out_two[experts_rows(expert), :])
        put(rows + expert * hidden, both[:hidden])
        biases.append(both[hidden : hidden + 1])
    rows += 6 * hidden
    tower = []
    for task in range(2):
        tower.append(
            over_events(tower_keep[task * tall : (task + 1) * tall, :], first_keep[task * inner : (task + 1) * inner, :])
        )
    tower = jnp.concatenate(tower, axis=1)
    put(rows, tower[:hidden])
    biases.append(tower[hidden : hidden + 1])
    rows += hidden
    put(
        rows,
        jnp.concatenate(
            [
                over_events(
                    top_keep[task * narrow : (task + 1) * narrow, :],
                    tower_act_keep[task * inner : (task + 1) * inner, :],
                )
                for task in range(2)
            ],
            axis=1,
        ),
    )
    rows += narrow
    gates = over_events(score_one[...], flipped_ref[...])
    for start in range(0, width, hidden):
        put(rows, gates[:, start : start + hidden])
        rows += gates.shape[0]
    for task in range(2):
        put(
            rows,
            over_events(
                score_two[task * 16 : task * 16 + 16, :],
                carried_keep[task * tall : task * tall + hidden, :],
            ),
        )
        rows += 16
    tops = over_events(unit, top_keep[...])[:1]
    seen = over_events(unit, tail_keep[...])[:1]
    pieces = []
    for task in range(2):
        pieces.append(tops[:, task * narrow : (task + 1) * narrow])
        pieces.append(
            seen[:, 2 * task * narrow : (2 * task + 1) * narrow]
            + seen[:, (2 * task + 1) * narrow : (2 * task + 2) * narrow]
        )
    biases.append(jnp.concatenate(pieces, axis=1))
    gains = gain_keep[...]
    high = gains.astype(jnp.bfloat16)
    low = (gains - high.astype(jnp.float32)).astype(jnp.bfloat16)
    gains = (over_events(unit[:, :128], high) + over_events(unit[:, :128], low))[:1]
    for expert in range(12):
        biases.append(gains[:, experts_rows(expert)])
    biases = jnp.concatenate(biases, axis=0)
    extra = 2 * half_rows - rows - biases.shape[0]
    put(rows, jnp.concatenate([biases, jnp.zeros((extra, hidden), jnp.float32)], axis=0))
    pltpu.make_async_copy(grads_ref.at[bit], kept_ref, sems.at[0]).wait()
    pltpu.make_async_copy(grads_ref.at[1 - bit], sent_ref, sems.at[1]).wait()


def dense(bit, flipped, weights, places, thin, cot, grad_rows):
    width, events = flipped.shape
    hidden = weights[0].shape[1]
    inner, narrow = 128, 64
    tall = hidden + ONES
    low = functools.partial(pltpu.VMEM, dtype=jnp.bfloat16)
    kept = (
        width + ONES,
        6 * tall,
        6 * hidden,
        6 * hidden,
        32,
        3 * tall,
        6 * tall,
        6 * hidden,
        6 * hidden,
        32,
        2 * tall,
        2 * inner,
        2 * inner,
        2 * narrow,
        4 * narrow,
    )
    half = (grad_rows // 2, hidden)
    scratch = [pltpu.SemaphoreType.DMA((2,)), low((2,) + half)]
    scratch += [low((rows, events)) for rows in kept]
    scratch.append(pltpu.VMEM((12 * hidden, 128), jnp.float32))
    scratch += [low((6 * hidden, depth)) for depth in (width, hidden, hidden, hidden)]
    vmem = pl.BlockSpec(memory_space=pltpu.VMEM)
    outside = pl.BlockSpec(memory_space=pl.ANY)
    specs = [pl.BlockSpec(memory_space=pltpu.SMEM)]
    specs += [vmem if places is None else outside] * 4 + [vmem] * (len(thin) + 2)
    if places is not None:
        outs, holds = thin_shapes(width, hidden)
        scratch += [pltpu.VMEM(*out) for out in outs]
        scratch += [low((6 * depth, hidden)) for depth in (width, hidden, hidden, hidden)]
        scratch += holds + [low(weight.shape) for weight in weights]
        scratch.append(pltpu.SemaphoreType.DMA((4,)))
    return pl.pallas_call(
        functools.partial(dense_body, places),
        out_shape=(
            jax.ShapeDtypeStruct((2, events), jnp.float32),
            jax.ShapeDtypeStruct((width, events), jnp.float32),
            jax.ShapeDtypeStruct(half, jnp.bfloat16),
            jax.ShapeDtypeStruct(half, jnp.bfloat16),
        ),
        in_specs=specs,
        out_specs=(vmem, vmem, outside, outside),
        scratch_shapes=scratch,
        compiler_params=pltpu.CompilerParams(vmem_limit_bytes=VMEM_LIMIT),
        cost_estimate=pl.CostEstimate(
            flops=6 * events * hidden * (6 * (width + 3 * hidden) + 2 * inner),
            bytes_accessed=24 * 1024 * 1024,
            transcendentals=12 * events * hidden,
        ),
    )(bit, *weights, flipped, *thin, cot)


def grad_layout(width, hidden):
    sizes = [6 * width, 6 * hidden, 6 * hidden, 6 * hidden]
    starts = [sum(sizes[:index]) for index in range(5)]
    return sizes, starts


def grad_moves(part, half, hidden, width):
    sizes, starts = grad_layout(width, hidden)
    most = 512
    moves = []
    for index in range(2):
        first = (2 * half + index) * part
        for target, (start, size) in enumerate(zip(starts, sizes)):
            low_row, high_row = max(first, start), min(first + part, start + size)
            for row in range(low_row, high_row, most):
                moves.append((index, row - first, target, row - start, min(most, high_row - row)))
    return moves


def write_wide(half, pieces, ready, wide, hold, sems, width, hidden):
    part = pieces[0].shape[0]
    block = 128
    copies = []
    for number, (index, start, target, place, rows) in enumerate(grad_moves(part, half, hidden, width)):
        if ready and start == 0:
            ready[index].wait()
        source = pieces[index]
        base = index * part + start

        def step(count, carry):
            hold[pl.ds(pl.multiple_of(base + count * block, block), block), :] = source[
                pl.ds(pl.multiple_of(start + count * block, block), block), :
            ].astype(jnp.float32)
            return carry

        lax.fori_loop(0, rows // block, step, 0, unroll=4)
        copy = pltpu.make_async_copy(
            hold.at[pl.ds(base, rows), :], wide[target].at[pl.ds(place, rows), :], sems.at[number]
        )
        copy.start()
        copies.append(copy)
    return copies


def own_body(bit_ref, own_a_ref, own_b_ref, *refs):
    *wide, hold, sems = refs
    hidden = wide[0].shape[1]
    width = wide[0].shape[0] // 6

    for half in range(2):

        @pl.when(jnp.minimum(bit_ref[0], 1) == half)
        def _():
            for copy in write_wide(half, (own_a_ref, own_b_ref), (), wide, hold, sems, width, hidden):
                copy.wait()


def came_body(bit_ref, own_b_ref, came_a_ref, came_b_ref, *refs):
    wide, outs, (hold, sems) = refs[4:8], refs[8:21], refs[21:]
    hidden = wide[0].shape[1]
    width = wide[0].shape[0] // 6
    part = came_a_ref.shape[0]
    start = grad_layout(width, hidden)[1][4] - 3 * part
    bit = jnp.minimum(bit_ref[0], 1)
    for half in range(2):

        @pl.when(bit != half)
        def _():
            copies = write_wide(half, (came_a_ref, came_b_ref), (), wide, hold, sems, width, hidden)
            write_rest(came_b_ref if half else own_b_ref, start, outs, width, hidden)
            for copy in copies:
                copy.wait()


def write_rest(source, start, outs, width, hidden):
    (
        low_inbias_ref,
        low_outbias_ref,
        low_gain_ref,
        low_taskgate_ref,
        low_sharegate_ref,
        up_inbias_ref,
        up_outbias_ref,
        up_gain_ref,
        up_taskgate_ref,
        inner_ref,
        tbias_ref,
        middle_ref,
        tail_ref,
    ) = outs
    inner = inner_ref.shape[1]

    def take(rows):
        nonlocal start
        start += rows
        return source[start - rows : start, :].astype(jnp.float32)

    both = take(hidden)
    inner_ref[:hidden, :] = both[:, :inner]
    inner_ref[hidden:, :] = both[:, inner:]
    middle_ref[...] = take(middle_ref.shape[0])
    for index in range(width // hidden):
        gates = take(32)
        span = slice(index * hidden, (index + 1) * hidden)
        low_taskgate_ref[:, span] = gates[0:4]
        low_taskgate_ref[:, width + index * hidden : width + (index + 1) * hidden] = gates[8:12]
        low_sharegate_ref[:, span] = gates[16:22]
    for task in range(2):
        up_taskgate_ref[:, task * hidden : (task + 1) * hidden] = take(16)[0:4]
    rows = take(48)
    flat = (low_inbias_ref, low_outbias_ref, up_inbias_ref, up_outbias_ref, tbias_ref, tail_ref)
    place = 0
    for target in flat + (low_gain_ref, up_gain_ref):
        for index in range(target.shape[0] // hidden):
            target[index * hidden : (index + 1) * hidden] = rows[place]
            place += 1


def finish(bit, own, came, width, hidden):
    wide_shapes = tuple(
        jax.ShapeDtypeStruct((size, hidden), jnp.float32) for size in grad_layout(width, hidden)[0]
    )
    rest_shapes = (
        (6 * hidden,),
        (6 * hidden,),
        (6 * hidden,),
        (4, 2 * width),
        (6, width),
        (6 * hidden,),
        (6 * hidden,),
        (6 * hidden,),
        (4, 2 * hidden),
        (2 * hidden, 128),
        (256,),
        (64, 256),
        (256,),
    )
    outside, inside = pl.BlockSpec(memory_space=pl.ANY), pl.BlockSpec(memory_space=pltpu.VMEM)
    small = pl.BlockSpec(memory_space=pltpu.SMEM)
    params = pltpu.CompilerParams(vmem_limit_bytes=SMALL_LIMIT)
    moved = 6 * 2 * own[0].size
    part = own[0].shape[0]
    scratch = [pltpu.VMEM((2 * part, hidden), jnp.float32), pltpu.SemaphoreType.DMA((16,))]
    wide = pl.pallas_call(
        own_body,
        out_shape=wide_shapes,
        in_specs=[small, inside, inside],
        out_specs=(outside,) * 4,
        scratch_shapes=scratch,
        compiler_params=params,
        cost_estimate=pl.CostEstimate(flops=0, bytes_accessed=moved, transcendentals=0),
    )(bit, *own)
    done = pl.pallas_call(
        came_body,
        out_shape=wide_shapes
        + tuple(jax.ShapeDtypeStruct(shape, jnp.float32) for shape in rest_shapes),
        in_specs=[small] + [inside] * 3 + [outside] * 4,
        out_specs=(outside,) * 4 + (inside,) * 13,
        scratch_shapes=scratch,
        input_output_aliases={4 + index: index for index in range(4)},
        compiler_params=params,
        cost_estimate=pl.CostEstimate(flops=0, bytes_accessed=moved, transcendentals=0),
    )(bit, own[1], *came, *wide)
    done = [value.T if value.shape[0] in (4, 6, 64) else value for value in done]
    wide, rest = done[:4], done[4:]
    return (wide[0], rest[0], wide[1], *rest[1:5], wide[2], rest[5], wide[3], *rest[6:])


def partners(mask, size):
    return [(index, index ^ mask) for index in range(size)]


def swap_with(values, mask, size):
    return lax.ppermute(values, "dp", partners(mask, size))


def cut(values, mask, place):
    rows = values.shape[0] // 2
    bit = jnp.where((place & mask) != 0, 1, 0)
    sent = lax.dynamic_slice_in_dim(values, (1 - bit) * rows, rows, 0)
    return sent, lax.dynamic_slice_in_dim(values, bit * rows, rows, 0)


def add_low(kept, came):
    return (kept.astype(jnp.float32) + came.astype(jnp.float32)).astype(kept.dtype)


def double(values, mask, place, size):
    came = swap_with(values, mask, size)
    upper = (place & mask) != 0
    return jnp.concatenate(
        [jnp.where(upper, came, values), jnp.where(upper, values, came)], axis=0
    )


def swap_groups(values, mask):
    return lax.ppermute(values, "fsdp", partners(mask, lax.axis_size("fsdp")))


def share(values, also=None):
    group = lax.axis_size("fsdp")
    place = lax.axis_index("fsdp")
    pieces = [values] + [swap_groups(values, mask) for mask in range(1, group)]
    if also is not None:
        pieces, _ = lax.optimization_barrier((pieces, also))
    return jnp.stack([pick(place ^ index, pieces) for index in range(group)])


def pick(index, pieces):
    chosen = pieces[0]
    for place in range(1, len(pieces)):
        chosen = jnp.where(index == place, pieces[place], chosen)
    return chosen


def z_pieces(values):
    group = lax.axis_size("fsdp")
    place = lax.axis_index("fsdp")
    rows = values.shape[0] // group
    return [
        lax.dynamic_slice_in_dim(values, (place ^ mask) * rows, rows, 0) for mask in range(group)
    ]


def scatter_sum(pieces):
    came = [swap_groups(piece, mask) for mask, piece in enumerate(pieces) if mask]
    total = pieces[0].astype(jnp.float32)
    for piece in came:
        total = total + piece.astype(jnp.float32)
    return total.astype(pieces[0].dtype)


def dp_masks(size):
    return [1 << index for index in range(size.bit_length() - 1)]


def dp_orders():
    first, *others = dp_masks(lax.axis_size("dp"))
    return first, [others, others[::-1]]


def spread(parts, late=None, early=None):
    size = lax.axis_size("dp")
    place = lax.axis_index("dp")
    first, orders = dp_orders()
    for step in reversed(range(len(orders[0]))):
        parts = [double(part, order[step], place, size) for part, order in zip(parts, orders)]
        if step == len(orders[0]) - 1 and early is not None:
            parts, early = lax.optimization_barrier((parts, early))
    parts, late = lax.optimization_barrier((parts, late))
    return parts, [swap_with(part, first, size) for part in parts], late, early


def arrival(order, first, group):
    devices = []
    for half in range(2):
        places = []
        for block in range(1 << len(order)):
            dp = half * first
            for index, mask in enumerate(order):
                if block >> (len(order) - 1 - index) & 1:
                    dp |= mask
            places += [dp * group + index for index in range(group)]
        devices.append(places)
    return devices


def in_order(own, came, bit, places, rows):
    whole = jnp.concatenate([jnp.where(bit == 0, own, came), jnp.where(bit == 0, came, own)], axis=0)
    whole = whole.reshape((-1, rows) + own.shape[1:])
    flat = places[0] + places[1]
    return jnp.stack([whole[flat.index(device)] for device in range(len(flat))])


def sum_grads(kept, sent, flipped_grad, prepare, finish_rows, width, hidden):
    size = lax.axis_size("dp")
    group = lax.axis_size("fsdp")
    place = lax.axis_index("dp")
    first, orders = dp_orders()
    came = swap_with(sent, first, size)
    outgoing, x_grad = prepare(flipped_grad)
    came, outgoing = lax.optimization_barrier((came, outgoing))
    mine = add_low(kept, came)
    rows = mine.shape[0] // 2
    parts = [mine[:rows], mine[rows:]]
    for step in range(len(orders[0])):
        halves = [cut(part, order[step], place) for part, order in zip(parts, orders)]
        if step == 0:
            halves, outgoing = lax.optimization_barrier((halves, outgoing))
            incoming = lax.all_to_all(
                outgoing, ("dp", "fsdp"), split_axis=0, concat_axis=0, tiled=True
            )
        parts = [
            add_low(kept, swap_with(sent, order[step], size))
            for (sent, kept), order in zip(halves, orders)
        ]
    both = [part.reshape((group, -1) + part.shape[1:]) for part in parts]
    both = jnp.concatenate(both, axis=1).reshape((-1,) + kept.shape[1:])
    pieces = z_pieces(both)
    pieces, incoming = lax.optimization_barrier((pieces, incoming))
    shared = share(scatter_sum(pieces))
    late = (finish_rows(incoming), x_grad)
    parts = [piece.reshape((-1,) + kept.shape[1:]) for piece in jnp.split(shared, 2, axis=1)]
    own, came, late, _ = spread(parts, late)
    return finish((place & first).reshape(1), own, came, width, hidden), *late


def on_device(
    owner_ids,
    row_ids,
    embed_table,
    expandone,
    expbiasone,
    reduceone,
    redbiasone,
    normgainone,
    taskgateone,
    sharegateone,
    expandtwo,
    expbiastwo,
    reducetwo,
    redbiastwo,
    normgaintwo,
    taskgatetwo,
    towerinner,
    towerbias,
    towermiddle,
    towertail,
    logit_cot,
):
    devices = lax.axis_size(("dp", "fsdp"))
    events, fields = owner_ids.shape
    emb_width = embed_table.shape[1]
    capacity = 2 * events * fields // devices
    hidden = expandone.shape[1]
    width = fields * emb_width
    group = lax.axis_size("fsdp")
    owner_rows = owner_ids.T
    request, rank = assign_slots(owner_rows, row_ids.T, devices, capacity)
    asked_rows = lax.all_to_all(request, ("dp", "fsdp"), split_axis=0, concat_axis=0, tiled=True)
    packed = pack(
        (expbiasone, redbiasone, normgainone, expbiastwo, redbiastwo, normgaintwo),
        (towerbias, towertail, taskgateone.T, sharegateone.T, taskgatetwo.T, towerinner, towermiddle),
        (expandone, reduceone, expandtwo, reducetwo),
    )
    found = find_rows(asked_rows, embed_table.T)
    packed = share(packed, request)
    split = expandone.shape[0] + THIN_ROWS
    first, orders = dp_orders()
    parts = [packed[:, :split], packed[:, split:]]
    own, came, _, found = spread([part.reshape(-1, hidden) for part in parts], early=found)
    returned = lax.all_to_all(found, ("dp", "fsdp"), split_axis=0, concat_axis=0, tiled=True)
    bit = (lax.axis_index("dp") & first).reshape(1)
    places = [arrival(order, first, group) for order in orders]
    flipped = place_rows(returned, rank, owner_rows)
    sizes = [shard.shape[0] for shard in (expandone, reduceone, expandtwo, reducetwo)]
    if all(size % 16 == 0 for size in sizes):
        weights, thin = (*own, *came), ()
    else:
        thin = prep_thin(bit, own[0], came[0], places[0], width, hidden)
        whole = [
            in_order(mine, other, bit[0], place, part.shape[1])
            for mine, other, place, part in zip(own, came, places, parts)
        ]
        starts = [0, 0, sizes[1], sizes[1] + sizes[2]]
        weights = tuple(
            whole[min(index, 1)][:, start : start + size].reshape(-1, hidden)
            for index, (start, size) in enumerate(zip(starts, sizes))
        )
        places = None

    chunk = 16 * devices
    grad_rows = -(-(6 * (width + 3 * hidden) + 2 * hidden) // chunk) * chunk
    logits, flipped_grad, kept, sent = dense(bit, flipped, weights, places, thin, logit_cot, grad_rows)

    def prepare(flipped_grad):
        return send_rows(flipped_grad, rank, owner_rows, capacity, 1)

    def finish_rows(incoming):
        return add_rows(incoming, asked_rows, embed_table.shape[0])

    done, table_grad, x_grad = sum_grads(kept, sent, flipped_grad, prepare, finish_rows, width, hidden)
    return (logits, x_grad, table_grad.T, *done)


def solution(mesh):
    return jax.shard_map(
        on_device,
        mesh=mesh,
        in_specs=(
            P(("dp", "fsdp"), None),
            P(("dp", "fsdp"), None),
            P(("dp", "fsdp"), None),
            P(("dp", "fsdp"), None),
            P(("dp", "fsdp")),
            P(("dp", "fsdp"), None),
            P(("dp", "fsdp")),
            P(("dp", "fsdp")),
            P(("dp", "fsdp"), None),
            P(("dp", "fsdp"), None),
            P(("dp", "fsdp"), None),
            P(("dp", "fsdp")),
            P(("dp", "fsdp"), None),
            P(("dp", "fsdp")),
            P(("dp", "fsdp")),
            P(("dp", "fsdp"), None),
            P(("dp", "fsdp"), None),
            P(("dp", "fsdp")),
            P(("dp", "fsdp"), None),
            P(("dp", "fsdp")),
            P(None, ("dp", "fsdp")),
        ),
        out_specs=(
            P(None, ("dp", "fsdp")),
            P(("dp", "fsdp"), None),
            P(("dp", "fsdp"), None),
            P(),
            P(),
            P(),
            P(),
            P(),
            P(),
            P(),
            P(),
            P(),
            P(),
            P(),
            P(),
            P(),
            P(),
            P(),
            P(),
            P(),
        ),
        check_vma=False,
    )
```

```python
import functools

import jax
import jax.numpy as jnp
from jax import lax
from jax.experimental import pallas as pl
from jax.experimental.pallas import tpu as pltpu
from jax.sharding import PartitionSpec as P

EPS = 1e-05
VMEM_LIMIT = 56 * 1024 * 1024
SMALL_LIMIT = 16 * 1024 * 1024
ROW_BLOCKS = 8


def local_kernel(body, out_shape, flops, moved, scratch=(), limit=SMALL_LIMIT):
    return pl.pallas_call(
        body,
        out_shape=out_shape,
        scratch_shapes=list(scratch),
        compiler_params=pltpu.CompilerParams(vmem_limit_bytes=limit),
        cost_estimate=pl.CostEstimate(flops=flops, bytes_accessed=moved, transcendentals=0),
    )


def one_hot(hit):
    return jnp.where(hit, 1.0, 0.0).astype(jnp.bfloat16)


def low(value):
    return value.astype(jnp.float32).astype(jnp.bfloat16)


def iota(shape, axis):
    return lax.broadcasted_iota(jnp.int32, shape, axis)


def slot_body(owner_ref, row_ref, request_ref, rank_ref):
    fields, events = owner_ref.shape
    devices, _, capacity = request_ref.shape
    place = iota((devices, events), 0)
    asked = jnp.zeros((devices, events), jnp.float32)
    for field in range(fields):
        asked = asked + jnp.where(owner_ref[field : field + 1, :] == place, 1.0, 0.0)
    earlier = one_hot(iota((events, events), 0) < iota((events, events), 1))
    rank = jnp.dot(asked.astype(jnp.bfloat16), earlier, preferred_element_type=jnp.float32)
    rank = jnp.where(asked > 0.5, rank.astype(jnp.int32), -1)
    rank_ref[...] = rank
    slots = iota((capacity, events), 0)
    total = jnp.zeros((2 * devices, capacity), jnp.float32)
    for field in range(fields):
        mine = owner_ref[field : field + 1, :] == place
        field_rank = jnp.max(jnp.where(mine, rank, -1).astype(jnp.float32), axis=0, keepdims=True)
        rows = row_ref[field : field + 1, :]
        high = jnp.where(mine, (rows >> 6).astype(jnp.float32), 0.0)
        low = jnp.where(mine, (rows & 63).astype(jnp.float32), 0.0)
        value = jnp.concatenate([high, low], axis=0).astype(jnp.bfloat16)
        total = total + lax.dot_general(
            value,
            one_hot(field_rank.astype(jnp.int32) == slots),
            (((1,), (1,)), ((), ())),
            preferred_element_type=jnp.float32,
        )
    request = (total[:devices] * 64.0 + total[devices:]).astype(jnp.int32)
    for owner in range(devices):
        request_ref[owner] = request[owner : owner + 1]


def assign_slots(owner_rows, row_rows, devices, capacity):
    fields, events = owner_rows.shape
    return local_kernel(
        slot_body,
        (
            jax.ShapeDtypeStruct((devices, 1, capacity), jnp.int32),
            jax.ShapeDtypeStruct((devices, events), jnp.int32),
        ),
        2 * devices * events * (events + 2 * fields * capacity),
        4 * events * (2 * fields + devices),
        limit=VMEM_LIMIT,
    )(owner_rows, row_rows)


def find_body(request_ref, table_ref, found_ref, wide_ref):
    devices, _, capacity = request_ref.shape
    width = table_ref.shape[0]
    span = wide_ref.shape[1]
    places = iota((span, capacity), 0)
    for index in range(ROW_BLOCKS):
        wide_ref[index * width : (index + 1) * width, :] = table_ref[
            :, index * span : (index + 1) * span
        ]

    def step(source, carry):
        rows = request_ref[source]
        block = rows // span
        hits = one_hot(rows - block * span == places)
        rows_all = jnp.dot(wide_ref[...], hits, preferred_element_type=jnp.float32)
        picked = jnp.zeros((width, capacity), jnp.float32)
        for index in range(ROW_BLOCKS):
            picked = jnp.where(
                block == index, rows_all[index * width : (index + 1) * width, :], picked
            )
        found_ref[source] = picked.astype(jnp.bfloat16)
        return carry

    lax.fori_loop(0, devices, step, 0, unroll=16)


def find_rows(request, table):
    devices, _, capacity = request.shape
    width, rows = table.shape
    return local_kernel(
        find_body,
        jax.ShapeDtypeStruct((devices, width, capacity), jnp.bfloat16),
        16 * devices * capacity * rows * width,
        2 * (rows * width + devices * capacity * width),
        [pltpu.VMEM((ROW_BLOCKS * width, rows // ROW_BLOCKS), jnp.bfloat16)],
    )(request, table)


def place_body(found_ref, rank_ref, owner_ref, flipped_ref, total_ref):
    devices, width, capacity = found_ref.shape
    fields, events = owner_ref.shape
    slots = iota((capacity, events), 0)
    group = 4
    owners_low = low(owner_ref[...])
    total_ref[...] = jnp.zeros_like(total_ref)

    def step(start, carry):
        pieces = []
        for index in range(group):
            owner = start * group + index
            hits = one_hot(rank_ref[pl.ds(owner, 1), :] == slots)
            pieces.append(
                jnp.dot(found_ref[owner], hits, preferred_element_type=jnp.float32).astype(
                    jnp.bfloat16
                )
            )
        for field in range(fields):
            rows = slice(field * width, (field + 1) * width)
            owners = owners_low[field : field + 1, :]
            value = total_ref[rows, :]
            for index in range(group):
                value = jnp.where(owners == low(start * group + index), pieces[index], value)
            total_ref[rows, :] = value
        return carry

    lax.fori_loop(0, devices // group, step, 0)
    flipped_ref[...] = total_ref[...]


def place_rows(found, rank, owner_rows):
    devices, width, capacity = found.shape
    fields, events = owner_rows.shape
    return local_kernel(
        place_body,
        jax.ShapeDtypeStruct((fields * width, events), jnp.bfloat16),
        2 * devices * width * capacity * events,
        2 * (devices * width * capacity + fields * width * events),
        [pltpu.VMEM((fields * width, events), jnp.bfloat16)],
    )(found, rank, owner_rows)


def send_body(group, grad_ref, rank_ref, owner_ref, sent_ref, turned_ref, low_ref):
    devices, width, capacity = sent_ref.shape
    fields, events = owner_ref.shape
    slots = iota((capacity, events), 0)
    owners_low = low(owner_ref[...])
    low_ref[...] = grad_ref[...].astype(jnp.bfloat16)
    turned_ref[...] = grad_ref[...].T

    def step(owner, carry):
        chosen = jnp.zeros((width, events), jnp.bfloat16)
        for field in range(fields):
            rows = slice(field * width, (field + 1) * width)
            chosen = jnp.where(
                owners_low[field : field + 1, :] == low(owner), low_ref[rows, :], chosen
            )
        hits = one_hot(rank_ref[pl.ds(owner, 1), :] == slots)
        place = lax.rem(owner, group) * (devices // group) + lax.div(owner, group)
        sent_ref[place] = lax.dot_general(
            chosen,
            hits,
            (((1,), (1,)), ((), ())),
            preferred_element_type=jnp.float32,
        ).astype(jnp.bfloat16)
        return carry

    lax.fori_loop(0, devices, step, 0, unroll=16)


def send_rows(grad, rank, owner_rows, capacity, group):
    devices = rank.shape[0]
    fields, events = owner_rows.shape
    width = grad.shape[0] // fields
    return local_kernel(
        functools.partial(send_body, group),
        (
            jax.ShapeDtypeStruct((devices, width, capacity), jnp.bfloat16),
            jax.ShapeDtypeStruct((events, fields * width), jnp.float32),
        ),
        2 * devices * width * capacity * events,
        2 * (devices * width * capacity + 2 * fields * width * events),
        [pltpu.VMEM((fields * width, events), jnp.bfloat16)],
    )(grad, rank, owner_rows)


def add_body(came_ref, request_ref, out_ref, total_ref):
    devices, width, capacity = came_ref.shape
    span = total_ref.shape[1]
    group = 8
    places = iota((span, capacity), 0)
    total_ref[...] = jnp.zeros_like(total_ref)

    def step(start, carry):
        hits = []
        spread = []
        for index in range(group):
            source = start * group + index
            rows = request_ref[source]
            block = rows // span
            hits.append(one_hot(rows - block * span == places))
            came = came_ref[source].astype(jnp.float32)
            spread.append(
                jnp.concatenate(
                    [jnp.where(block == part, came, 0.0) for part in range(ROW_BLOCKS)], axis=0
                ).astype(jnp.bfloat16)
            )
        total_ref[...] += lax.dot_general(
            jnp.concatenate(spread, axis=1),
            jnp.concatenate(hits, axis=1),
            (((1,), (1,)), ((), ())),
            preferred_element_type=jnp.float32,
        )
        return carry

    lax.fori_loop(0, devices // group, step, 0, unroll=4)
    for index in range(ROW_BLOCKS):
        out_ref[:, index * span : (index + 1) * span] = total_ref[
            index * width : (index + 1) * width, :
        ]


def add_rows(came, request, rows):
    devices, width, capacity = came.shape
    span = rows // ROW_BLOCKS
    return local_kernel(
        add_body,
        jax.ShapeDtypeStruct((width, rows), jnp.float32),
        2 * devices * capacity * rows * width,
        2 * devices * width * capacity + 4 * rows * width,
        [pltpu.VMEM((ROW_BLOCKS * width, span), jnp.float32)],
    )(came, request)


THIN_ROWS = 48


def pack_thin_body(*refs):
    *biases, tbias, tail, taskgate, sharegate, upgate, inner, middle = refs[:13]
    *wide, out_ref, hold = refs[13:]
    hold[...] = jnp.zeros_like(hold)
    for row, piece in enumerate(biases + [tbias, tail]):
        hold[row : row + 1, : piece.shape[0]] = piece[...].astype(jnp.float32).reshape(1, -1)
    for row, piece in ((8, taskgate), (16, sharegate), (24, upgate), (32, inner)):
        hold[row : row + piece.shape[0], : piece.shape[1]] = piece[...].astype(jnp.float32)
    hold[32 : 32 + middle.shape[0], 128 : 128 + middle.shape[1]] = middle[...].astype(jnp.float32)
    thin = hold[...].astype(jnp.bfloat16)
    if not wide:
        out_ref[...] = thin
    start = 0
    for index, piece in enumerate(wide):
        out_ref[start : start + piece.shape[0], :] = piece[...]
        start += piece.shape[0]
        if index == 0:
            out_ref[start : start + THIN_ROWS, :] = thin
            start += THIN_ROWS


def pack(biases, others, wide):
    aligned = all(piece.shape[0] % 16 == 0 for piece in wide)
    rows = THIN_ROWS + (sum(piece.shape[0] for piece in wide) if aligned else 0)
    packed = local_kernel(
        pack_thin_body,
        jax.ShapeDtypeStruct((rows, 256), jnp.bfloat16),
        0,
        rows * 1024,
        [pltpu.VMEM((THIN_ROWS, 256), jnp.float32)],
        limit=VMEM_LIMIT,
    )(*biases, *others, *(wide if aligned else ()))
    if aligned:
        return packed
    return jnp.concatenate([wide[0], packed, *wide[1:]], axis=0)


def lay_thin(bit, sources, places, outs, holds):
    (
        columns_ref,
        gate_one_ref,
        gate_one_back_ref,
        gate_two_ref,
        gate_two_back_ref,
        inner_ref,
        inner_back_ref,
        middle_ref,
        middle_back_ref,
    ) = outs
    rows, task_rows, share_rows, up_rows, inner_rows, middle_rows = holds
    devices = 2 * len(places[0])
    hidden = columns_ref.shape[0]
    width = gate_one_ref.shape[1]

    def lay(target, source, index, count):
        target[:, index * count : (index + 1) * count] = source[:, :count]

    for held in (rows, task_rows, share_rows, up_rows):
        held[...] = jnp.zeros_like(held)
    bias = 6 * hidden // devices
    flat = hidden // devices

    def unpack(pieces):
        for half, source in enumerate(pieces):
            for block, index in enumerate(places[half]):
                thin = source(block).astype(jnp.float32)
                rows[0:6, index * bias : (index + 1) * bias] = thin[0:6, :bias]
                rows[6:8, index * flat : (index + 1) * flat] = thin[6:8, :flat]
                lay(task_rows, thin[8:16], index, 2 * width // devices)
                lay(share_rows, thin[16:24], index, width // devices)
                lay(up_rows, thin[24:32], index, 2 * hidden // devices)
                count = 2 * hidden // devices
                inner_rows[index * count : (index + 1) * count, :] = thin[32 : 32 + count, :128]
                count = hidden // devices
                middle_rows[index * count : (index + 1) * count, :] = thin[32 : 32 + count, 128:192]

    @pl.when(bit == 0)
    def _():
        unpack(sources)

    @pl.when(bit != 0)
    def _():
        unpack(sources[::-1])

    columns_ref[...] = jnp.zeros_like(columns_ref)
    for expert in range(6):
        columns_ref[:, expert * 8 : expert * 8 + 8] = rows[:, expert * hidden : (expert + 1) * hidden].T
    gates = jnp.concatenate(
        [
            task_rows[:, :width],
            task_rows[:, width:],
            share_rows[...],
            jnp.zeros((8, width), jnp.float32),
        ],
        axis=0,
    )
    gate_one_ref[...] = gates.astype(jnp.bfloat16)
    gate_one_back_ref[...] = gates.T.astype(jnp.bfloat16)
    gate_two_ref[...] = jnp.concatenate([up_rows[:, :hidden], up_rows[:, hidden:]], axis=0).astype(
        jnp.bfloat16
    )
    for task in range(2):
        span = slice(task * hidden, (task + 1) * hidden)
        wide = jnp.concatenate([up_rows[:, span], jnp.zeros((8, hidden), jnp.float32)], axis=0)
        gate_two_back_ref[span, :] = wide.T.astype(jnp.bfloat16)
        inner_ref[task * 128 : (task + 1) * 128, :] = inner_rows[span, :].T.astype(jnp.bfloat16)
        span = slice(task * 128, (task + 1) * 128)
        middle_ref[task * 64 : (task + 1) * 64, :] = middle_rows[span, :].T.astype(jnp.bfloat16)
    inner_back_ref[...] = inner_rows[...].astype(jnp.bfloat16)
    middle_back_ref[...] = middle_rows[...].astype(jnp.bfloat16)


def prep_thin_body(places, bit_ref, own_ref, came_ref, *refs):
    outs, holds, (thin_own, thin_came, sems) = refs[:9], refs[9:15], refs[15:]
    start = own_ref.shape[1] - THIN_ROWS
    copies = [
        pltpu.make_async_copy(ref.at[:, pl.ds(start, THIN_ROWS), :], held, sems.at[index])
        for index, (ref, held) in enumerate(((own_ref, thin_own), (came_ref, thin_came)))
    ]
    for copy in copies:
        copy.start()
    for copy in copies:
        copy.wait()
    sources = (lambda block: thin_own[block], lambda block: thin_came[block])
    lay_thin(bit_ref[0], sources, places, outs, holds)


def thin_shapes(width, hidden):
    outs = (
        ((hidden, 64), jnp.float32),
        ((32, width), jnp.bfloat16),
        ((width, 32), jnp.bfloat16),
        ((16, hidden), jnp.bfloat16),
        ((2 * hidden, 16), jnp.bfloat16),
        ((hidden, hidden), jnp.bfloat16),
        ((2 * hidden, 128), jnp.bfloat16),
        ((128, 128), jnp.bfloat16),
        ((hidden, 64), jnp.bfloat16),
    )
    holds = (
        (8, 6 * hidden),
        (8, 2 * width),
        (8, width),
        (8, 2 * hidden),
        (2 * hidden, 128),
        (hidden, 64),
    )
    return outs, [pltpu.VMEM(shape, jnp.float32) for shape in holds]


def prep_thin(bit, own, came, places, width, hidden):
    blocks = len(places[0])
    outs, holds = thin_shapes(width, hidden)
    thin_held = pltpu.VMEM((blocks, THIN_ROWS, hidden), jnp.bfloat16)
    return pl.pallas_call(
        functools.partial(prep_thin_body, places),
        out_shape=tuple(jax.ShapeDtypeStruct(*out) for out in outs),
        in_specs=[pl.BlockSpec(memory_space=pltpu.SMEM)] + [pl.BlockSpec(memory_space=pl.ANY)] * 2,
        scratch_shapes=holds + [thin_held, thin_held, pltpu.SemaphoreType.DMA((2,))],
        compiler_params=pltpu.CompilerParams(vmem_limit_bytes=VMEM_LIMIT),
        cost_estimate=pl.CostEstimate(flops=0, bytes_accessed=4 * own.size, transcendentals=0),
    )(bit, own.reshape(blocks, -1, hidden), came.reshape(blocks, -1, hidden))


SPAN = 512
ONES = 16


def over_events(left, right):
    return lax.dot_general(left, right, (((1,), (1,)), ((), ())), preferred_element_type=jnp.float32)


def times(left, right):
    return jnp.dot(left, right, preferred_element_type=jnp.float32)


def sum_rows(values):
    return jnp.sum(values, axis=0, keepdims=True)


def sigmoid_of(values):
    return 0.5 * jnp.tanh(0.5 * values) + 0.5


def silu_parts(values):
    sig = sigmoid_of(values)
    active = values * sig
    return active, sig + active * (1.0 - sig)


def expert_up(inputs, expand, expbias, shrink, shrinkbias):
    active, slope = silu_parts(times(expand, inputs) + expbias)
    active = active.astype(jnp.bfloat16)
    output = times(shrink, active) + shrinkbias
    scale = 1.0 / output.shape[0]
    centered = output - sum_rows(output) * scale
    inverse = lax.rsqrt(sum_rows(centered * centered) * scale + EPS)
    return active, slope, centered * inverse, inverse


def soft(scores, count):
    valid = iota(scores.shape, 0) < count
    scores = jnp.where(valid, scores, -1e30)
    shifted = jnp.exp(scores - jnp.max(scores, axis=0, keepdims=True))
    shifted = jnp.where(valid, shifted, 0.0)
    return shifted / sum_rows(shifted)


def soft_back(probs, rows):
    tall = jnp.concatenate(rows + [jnp.zeros_like(rows[0])] * (probs.shape[0] - len(rows)), axis=0)
    return probs * (tall - sum_rows(probs * tall))


def assemble(bit, own_ref, came_ref, homes, places):
    blocks = len(places[0])
    rows = own_ref.shape[0] // blocks
    for half, source in ((bit, own_ref), (1 - bit, came_ref)):
        for block in range(blocks):
            start = block * rows
            for home in homes:
                size = home.shape[0] // (2 * blocks)
                place = places[0][block] * size + half * ((places[1][0] - places[0][0]) * size)
                home[pl.ds(pl.multiple_of(place, 16), size), :] = source[start : start + size, :]
                start += size


def dense_body(places, *refs):
    bit_ref, *refs = refs
    if places is None:
        *naturals, refs = *refs[:4], refs[4:]
    else:
        arrived, refs = refs[:4], refs[4:]
        refs, naturals, holds, held, loads = refs[:-15], refs[-15:-11], refs[-11:-5], refs[-5:-1], refs[-1]
        thin, refs = refs[-9:], refs[:-9]
        refs = [refs[0], *thin, *refs[1:]]
    expand_one_back_ref, shrink_one_back_ref, expand_two_back_ref, shrink_two_back_ref = naturals
    (
        flipped_ref,
        columns_ref,
        gate_one_ref,
        gate_one_back_ref,
        gate_two_ref,
        gate_two_back_ref,
        inner_ref,
        inner_back_ref,
        middle_ref,
        middle_back_ref,
        cot_ref,
        logits_ref,
        flipped_grad_ref,
        kept_ref,
        sent_ref,
        sems,
        grads_ref,
        input_keep,
        active_one,
        out_one,
        pre_one,
        score_one,
        carried_keep,
        active_two,
        out_two,
        pre_two,
        score_two,
        tower_keep,
        tower_act_keep,
        first_keep,
        top_keep,
        tail_keep,
        gain_keep,
        expand_one_ref,
        shrink_one_ref,
        expand_two_ref,
        shrink_two_ref,
    ) = refs
    bit = jnp.minimum(bit_ref[0], 1)
    if places is not None:
        copies = [
            pltpu.make_async_copy(arrived[index], held[index], loads.at[index]) for index in (0, 2, 1, 3)
        ]
        for copy in copies:
            copy.start()
        own_a, own_b, came_a, came_b = held
        for copy in copies[:2]:
            copy.wait()
        shard = own_a.shape[0] // len(places[0][0])

        def thin_of(ref):
            return lambda block: ref[(block + 1) * shard - THIN_ROWS : (block + 1) * shard, :]

        lay_thin(bit, (thin_of(own_a), thin_of(came_a)), places[0], thin, holds)
        for copy in copies[2:]:
            copy.wait()
        assemble(bit, own_a, came_a, [expand_one_back_ref], places[0])
        assemble(
            bit,
            own_b,
            came_b,
            [shrink_one_back_ref, expand_two_back_ref, shrink_two_back_ref],
            places[1],
        )
    for natural, turned in (
        (expand_one_back_ref, expand_one_ref),
        (shrink_one_back_ref, shrink_one_ref),
        (expand_two_back_ref, expand_two_ref),
        (shrink_two_back_ref, shrink_two_ref),
    ):
        depth = natural.shape[0] // 6
        across = natural.shape[1]
        for expert in range(6):
            turned[expert * across : (expert + 1) * across, :] = natural[
                expert * depth : (expert + 1) * depth, :
            ].T

    width, events = flipped_ref.shape
    hidden = shrink_one_back_ref.shape[1]
    inner = inner_ref.shape[0] // 2
    narrow = middle_ref.shape[0] // 2
    tall = hidden + ONES
    span = min(SPAN, events)
    unit = jnp.ones((ONES, events), jnp.bfloat16)

    input_keep[:width, :] = flipped_ref[...]
    input_keep[width:, :] = unit
    for expert in range(6):
        active_one[expert * tall + hidden : (expert + 1) * tall, :] = unit
        active_two[expert * tall + hidden : (expert + 1) * tall, :] = unit
    for group in range(3):
        carried_keep[group * tall + hidden : (group + 1) * tall, :] = unit
    for task in range(2):
        tower_keep[task * tall + hidden : (task + 1) * tall, :] = unit
    gain_keep[...] = jnp.zeros_like(gain_keep)

    def column(index, rows=hidden, start=0):
        return columns_ref[start : start + rows, index : index + 1]

    def experts_rows(expert):
        return slice(expert * hidden, (expert + 1) * hidden)

    def span_step(step, carry):
        lanes = pl.ds(pl.multiple_of(step * span, span), span)
        inputs = flipped_ref[:, lanes]

        def up(level, inputs_of, expand_ref, shrink_ref, active_keep):
            kept = []
            for expert in range(6):
                active, slope, normed, inverse = expert_up(
                    inputs_of(expert),
                    expand_ref[experts_rows(expert), :],
                    column(expert * 8 + level),
                    shrink_ref[experts_rows(expert), :],
                    column(expert * 8 + level + 1),
                )
                active_keep[expert * tall : expert * tall + hidden, lanes] = active
                kept.append((slope, normed, inverse, normed * column(expert * 8 + level + 2)))
            return kept

        kept_one = up(0, lambda expert: inputs, expand_one_ref, shrink_one_ref, active_one)
        scores = times(gate_one_ref[...], inputs)
        probs_one = [soft(scores[0:8], 4), soft(scores[8:16], 4), soft(scores[16:24], 6)]
        carried = []
        for group in range(3):
            members = [2 * group, 2 * group + 1, 4, 5] if group < 2 else range(6)
            mixed = 0.0
            for place, expert in enumerate(members):
                mixed = mixed + probs_one[group][place : place + 1, :] * kept_one[expert][3]
            carried.append(mixed.astype(jnp.bfloat16))
            carried_keep[group * tall : group * tall + hidden, lanes] = carried[group]

        kept_two = up(
            3, lambda expert: carried[expert // 2], expand_two_ref, shrink_two_ref, active_two
        )
        probs_two = []
        tower_grads = []
        dq_two = []
        for task in range(2):
            probs = soft(times(gate_two_ref[task * 8 : task * 8 + 8, :], carried[task]), 4)
            probs_two.append(probs)
            members = [2 * task, 2 * task + 1, 4, 5]
            mixed = 0.0
            for place, expert in enumerate(members):
                mixed = mixed + probs[place : place + 1, :] * kept_two[expert][3]
            mixed = mixed.astype(jnp.bfloat16)
            tower_keep[task * tall : task * tall + hidden, lanes] = mixed
            first, first_slope = silu_parts(
                times(inner_ref[task * inner : (task + 1) * inner, :], mixed)
                + column(6, inner, task * inner)
            )
            first = first.astype(jnp.bfloat16)
            tower_act_keep[task * inner : (task + 1) * inner, lanes] = first
            top, top_slope = silu_parts(
                times(middle_ref[task * narrow : (task + 1) * narrow, :], first)
                + column(7, narrow, 2 * task * narrow)
            )
            weight = column(7, narrow, (2 * task + 1) * narrow)
            logits_ref[task : task + 1, lanes] = sum_rows(top * weight)
            cot = cot_ref[task : task + 1, lanes]
            top_grad = (cot * weight * top_slope).astype(jnp.bfloat16)
            top_keep[task * narrow : (task + 1) * narrow, lanes] = top_grad
            seen = cot * top
            high = seen.astype(jnp.bfloat16)
            tail_keep[2 * task * narrow : (2 * task + 1) * narrow, lanes] = high
            tail_keep[(2 * task + 1) * narrow : (2 * task + 2) * narrow, lanes] = (
                seen - high.astype(jnp.float32)
            ).astype(jnp.bfloat16)
            first_grad = (
                times(middle_back_ref[task * inner : (task + 1) * inner, :], top_grad) * first_slope
            ).astype(jnp.bfloat16)
            first_keep[task * inner : (task + 1) * inner, lanes] = first_grad
            grad = times(inner_back_ref[task * hidden : (task + 1) * hidden, :], first_grad)
            tower_grads.append(grad)
            dq_two.append([sum_rows(kept_two[expert][3] * grad) for expert in members])

        def expert_down(level, expert, kept, upstream, slant, shrink_back_ref, out_keep, pre_keep):
            slope, normed, inverse, _ = kept
            gained = upstream * normed
            part = gained[:, :128]
            for start in range(128, span, 128):
                part = part + gained[:, start : start + 128]
            gain_rows = slice((level + expert) * hidden, (level + expert + 1) * hidden)
            gain_keep[gain_rows, :] += part
            scaled = upstream * column(expert * 8 + level // 2 + 2)
            scale = 1.0 / hidden
            out_low = (
                inverse * (scaled - sum_rows(scaled) * scale - normed * (slant * scale))
            ).astype(jnp.bfloat16)
            out_keep[experts_rows(expert), lanes] = out_low
            pre_low = (times(shrink_back_ref[experts_rows(expert), :], out_low) * slope).astype(
                jnp.bfloat16
            )
            pre_keep[experts_rows(expert), lanes] = pre_low
            return pre_low

        pre_lows = []
        for expert in range(6):
            if expert < 4:
                task, place = expert // 2, expert % 2
                prob = probs_two[task][place : place + 1, :]
                upstream = prob * tower_grads[task]
                slant = prob * dq_two[task][place]
            else:
                place = expert - 2
                prob = [probs_two[task][place : place + 1, :] for task in range(2)]
                upstream = prob[0] * tower_grads[0] + prob[1] * tower_grads[1]
                slant = prob[0] * dq_two[0][place] + prob[1] * dq_two[1][place]
            pre_lows.append(
                expert_down(
                    6, expert, kept_two[expert], upstream, slant, shrink_two_back_ref, out_two, pre_two
                )
            )
        carried_grads = []
        for group in range(3):
            grad = 0.0
            for expert in (2 * group, 2 * group + 1):
                grad = grad + times(expand_two_back_ref[experts_rows(expert), :], pre_lows[expert])
            if group < 2:
                score = soft_back(probs_two[group], dq_two[group])
                score = jnp.concatenate([score, jnp.zeros_like(score)], axis=0).astype(jnp.bfloat16)
                score_two[group * 16 : group * 16 + 16, lanes] = score
                grad = grad + times(gate_two_back_ref[experts_rows(group), :], score)
            carried_grads.append(grad)

        dq_one = []
        for group in range(3):
            members = [2 * group, 2 * group + 1, 4, 5] if group < 2 else range(6)
            dq_one.append([sum_rows(kept_one[expert][3] * carried_grads[group]) for expert in members])
        pre_lows = []
        for expert in range(6):
            prob = probs_one[2][expert : expert + 1, :]
            upstream = prob * carried_grads[2]
            slant = prob * dq_one[2][expert]
            for task in range(2):
                if expert // 2 in (task, 2):
                    place = expert % 2 if expert < 4 else expert - 2
                    prob = probs_one[task][place : place + 1, :]
                    upstream = upstream + prob * carried_grads[task]
                    slant = slant + prob * dq_one[task][place]
            pre_lows.append(
                expert_down(
                    0, expert, kept_one[expert], upstream, slant, shrink_one_back_ref, out_one, pre_one
                )
            )
        scores_low = [soft_back(probs_one[group], dq_one[group]) for group in range(3)]
        score = jnp.concatenate(scores_low + [jnp.zeros_like(scores_low[0])], axis=0).astype(
            jnp.bfloat16
        )
        score_one[:, lanes] = score
        grad = times(gate_one_back_ref[...], score)
        for expert in range(6):
            grad = grad + times(
                expand_one_back_ref[expert * width : (expert + 1) * width, :], pre_lows[expert]
            )
        flipped_grad_ref[:, lanes] = grad
        return carry

    lax.fori_loop(0, events // span, span_step, 0)

    half_rows = grads_ref.shape[1]

    def leave(half):
        for target, sem, when in ((kept_ref, 0, half), (sent_ref, 1, 1 - half)):

            @pl.when(bit == when)
            def _():
                pltpu.make_async_copy(grads_ref.at[half], target, sems.at[sem]).start()

    def put(row, value):
        while value.shape[0]:
            half, start = row // half_rows, row % half_rows
            count = min(value.shape[0], half_rows - start)
            grads_ref[half, start : start + count, :] = value[:count].astype(jnp.bfloat16)
            row, value = row + count, value[count:]
            if row % half_rows == 0:
                leave(half)

    rows = 0
    biases = []
    for expert in range(6):
        both = over_events(input_keep[...], pre_one[experts_rows(expert), :])
        put(rows + expert * width, both[:width])
        biases.append(both[width : width + 1])
    rows += 6 * width
    for expert in range(6):
        both = over_events(active_one[expert * tall : (expert + 1) * tall, :], out_one[experts_rows(expert), :])
        put(rows + expert * hidden, both[:hidden])
        biases.append(both[hidden : hidden + 1])
    rows += 6 * hidden
    for expert in range(6):
        group = expert // 2
        both = over_events(carried_keep[group * tall : (group + 1) * tall, :], pre_two[experts_rows(expert), :])
        put(rows + expert * hidden, both[:hidden])
        biases.append(both[hidden : hidden + 1])
    rows += 6 * hidden
    for expert in range(6):
        both = over_events(active_two[expert * tall : (expert + 1) * tall, :], out_two[experts_rows(expert), :])
        put(rows + expert * hidden, both[:hidden])
        biases.append(both[hidden : hidden + 1])
    rows += 6 * hidden
    tower = []
    for task in range(2):
        tower.append(
            over_events(tower_keep[task * tall : (task + 1) * tall, :], first_keep[task * inner : (task + 1) * inner, :])
        )
    tower = jnp.concatenate(tower, axis=1)
    put(rows, tower[:hidden])
    biases.append(tower[hidden : hidden + 1])
    rows += hidden
    put(
        rows,
        jnp.concatenate(
            [
                over_events(
                    top_keep[task * narrow : (task + 1) * narrow, :],
                    tower_act_keep[task * inner : (task + 1) * inner, :],
                )
                for task in range(2)
            ],
            axis=1,
        ),
    )
    rows += narrow
    gates = over_events(score_one[...], flipped_ref[...])
    for start in range(0, width, hidden):
        put(rows, gates[:, start : start + hidden])
        rows += gates.shape[0]
    for task in range(2):
        put(
            rows,
            over_events(
                score_two[task * 16 : task * 16 + 16, :],
                carried_keep[task * tall : task * tall + hidden, :],
            ),
        )
        rows += 16
    tops = over_events(unit, top_keep[...])[:1]
    seen = over_events(unit, tail_keep[...])[:1]
    pieces = []
    for task in range(2):
        pieces.append(tops[:, task * narrow : (task + 1) * narrow])
        pieces.append(
            seen[:, 2 * task * narrow : (2 * task + 1) * narrow]
            + seen[:, (2 * task + 1) * narrow : (2 * task + 2) * narrow]
        )
    biases.append(jnp.concatenate(pieces, axis=1))
    gains = gain_keep[...]
    high = gains.astype(jnp.bfloat16)
    low = (gains - high.astype(jnp.float32)).astype(jnp.bfloat16)
    gains = (over_events(unit[:, :128], high) + over_events(unit[:, :128], low))[:1]
    for expert in range(12):
        biases.append(gains[:, experts_rows(expert)])
    biases = jnp.concatenate(biases, axis=0)
    extra = 2 * half_rows - rows - biases.shape[0]
    put(rows, jnp.concatenate([biases, jnp.zeros((extra, hidden), jnp.float32)], axis=0))
    pltpu.make_async_copy(grads_ref.at[bit], kept_ref, sems.at[0]).wait()
    pltpu.make_async_copy(grads_ref.at[1 - bit], sent_ref, sems.at[1]).wait()


def dense(bit, flipped, weights, places, thin, cot, grad_rows):
    width, events = flipped.shape
    hidden = weights[0].shape[1]
    inner, narrow = 128, 64
    tall = hidden + ONES
    low = functools.partial(pltpu.VMEM, dtype=jnp.bfloat16)
    kept = (
        width + ONES,
        6 * tall,
        6 * hidden,
        6 * hidden,
        32,
        3 * tall,
        6 * tall,
        6 * hidden,
        6 * hidden,
        32,
        2 * tall,
        2 * inner,
        2 * inner,
        2 * narrow,
        4 * narrow,
    )
    half = (grad_rows // 2, hidden)
    scratch = [pltpu.SemaphoreType.DMA((2,)), low((2,) + half)]
    scratch += [low((rows, events)) for rows in kept]
    scratch.append(pltpu.VMEM((12 * hidden, 128), jnp.float32))
    scratch += [low((6 * hidden, depth)) for depth in (width, hidden, hidden, hidden)]
    vmem = pl.BlockSpec(memory_space=pltpu.VMEM)
    outside = pl.BlockSpec(memory_space=pl.ANY)
    specs = [pl.BlockSpec(memory_space=pltpu.SMEM)]
    specs += [vmem if places is None else outside] * 4 + [vmem] * (len(thin) + 2)
    if places is not None:
        outs, holds = thin_shapes(width, hidden)
        scratch += [pltpu.VMEM(*out) for out in outs]
        scratch += [low((6 * depth, hidden)) for depth in (width, hidden, hidden, hidden)]
        scratch += holds + [low(weight.shape) for weight in weights]
        scratch.append(pltpu.SemaphoreType.DMA((4,)))
    return pl.pallas_call(
        functools.partial(dense_body, places),
        out_shape=(
            jax.ShapeDtypeStruct((2, events), jnp.float32),
            jax.ShapeDtypeStruct((width, events), jnp.float32),
            jax.ShapeDtypeStruct(half, jnp.bfloat16),
            jax.ShapeDtypeStruct(half, jnp.bfloat16),
        ),
        in_specs=specs,
        out_specs=(vmem, vmem, outside, outside),
        scratch_shapes=scratch,
        compiler_params=pltpu.CompilerParams(vmem_limit_bytes=51 * 1024 * 1024),
        cost_estimate=pl.CostEstimate(
            flops=6 * events * hidden * (6 * (width + 3 * hidden) + 2 * inner),
            bytes_accessed=24 * 1024 * 1024,
            transcendentals=12 * events * hidden,
        ),
    )(bit, *weights, flipped, *thin, cot)


def grad_layout(width, hidden):
    sizes = [6 * width, 6 * hidden, 6 * hidden, 6 * hidden]
    starts = [sum(sizes[:index]) for index in range(5)]
    return sizes, starts


def grad_moves(part, half, hidden, width):
    sizes, starts = grad_layout(width, hidden)
    most = 512
    moves = []
    for index in range(2):
        first = (2 * half + index) * part
        for target, (start, size) in enumerate(zip(starts, sizes)):
            low_row, high_row = max(first, start), min(first + part, start + size)
            for row in range(low_row, high_row, most):
                moves.append((index, row - first, target, row - start, min(most, high_row - row)))
    return moves


def write_wide(half, pieces, ready, wide, hold, sems, width, hidden):
    part = pieces[0].shape[0]
    block = 128
    copies = []
    for number, (index, start, target, place, rows) in enumerate(grad_moves(part, half, hidden, width)):
        if ready and start == 0:
            ready[index].wait()
        source = pieces[index]
        base = index * part + start

        def step(count, carry):
            hold[pl.ds(pl.multiple_of(base + count * block, block), block), :] = source[
                pl.ds(pl.multiple_of(start + count * block, block), block), :
            ].astype(jnp.float32)
            return carry

        lax.fori_loop(0, rows // block, step, 0, unroll=4)
        copy = pltpu.make_async_copy(
            hold.at[pl.ds(base, rows), :], wide[target].at[pl.ds(place, rows), :], sems.at[number]
        )
        copy.start()
        copies.append(copy)
    return copies


def own_body(bit_ref, own_a_ref, own_b_ref, *refs):
    *wide, hold, sems = refs
    hidden = wide[0].shape[1]
    width = wide[0].shape[0] // 6

    for half in range(2):

        @pl.when(jnp.minimum(bit_ref[0], 1) == half)
        def _():
            for copy in write_wide(half, (own_a_ref, own_b_ref), (), wide, hold, sems, width, hidden):
                copy.wait()


def came_body(bit_ref, own_b_ref, came_a_ref, came_b_ref, *refs):
    wide, outs, (hold, sems) = refs[4:8], refs[8:21], refs[21:]
    hidden = wide[0].shape[1]
    width = wide[0].shape[0] // 6
    part = came_a_ref.shape[0]
    start = grad_layout(width, hidden)[1][4] - 3 * part
    bit = jnp.minimum(bit_ref[0], 1)
    for half in range(2):

        @pl.when(bit != half)
        def _():
            copies = write_wide(half, (came_a_ref, came_b_ref), (), wide, hold, sems, width, hidden)
            write_rest(came_b_ref if half else own_b_ref, start, outs, width, hidden)
            for copy in copies:
                copy.wait()


def write_rest(source, start, outs, width, hidden):
    (
        low_inbias_ref,
        low_outbias_ref,
        low_gain_ref,
        low_taskgate_ref,
        low_sharegate_ref,
        up_inbias_ref,
        up_outbias_ref,
        up_gain_ref,
        up_taskgate_ref,
        inner_ref,
        tbias_ref,
        middle_ref,
        tail_ref,
    ) = outs
    inner = inner_ref.shape[1]

    def take(rows):
        nonlocal start
        start += rows
        return source[start - rows : start, :].astype(jnp.float32)

    both = take(hidden)
    inner_ref[:hidden, :] = both[:, :inner]
    inner_ref[hidden:, :] = both[:, inner:]
    middle_ref[...] = take(middle_ref.shape[0])
    for index in range(width // hidden):
        gates = take(32)
        span = slice(index * hidden, (index + 1) * hidden)
        low_taskgate_ref[:, span] = gates[0:4]
        low_taskgate_ref[:, width + index * hidden : width + (index + 1) * hidden] = gates[8:12]
        low_sharegate_ref[:, span] = gates[16:22]
    for task in range(2):
        up_taskgate_ref[:, task * hidden : (task + 1) * hidden] = take(16)[0:4]
    rows = take(48)
    flat = (low_inbias_ref, low_outbias_ref, up_inbias_ref, up_outbias_ref, tbias_ref, tail_ref)
    place = 0
    for target in flat + (low_gain_ref, up_gain_ref):
        for index in range(target.shape[0] // hidden):
            target[index * hidden : (index + 1) * hidden] = rows[place]
            place += 1


def finish(bit, own, came, width, hidden):
    wide_shapes = tuple(
        jax.ShapeDtypeStruct((size, hidden), jnp.float32) for size in grad_layout(width, hidden)[0]
    )
    rest_shapes = (
        (6 * hidden,),
        (6 * hidden,),
        (6 * hidden,),
        (4, 2 * width),
        (6, width),
        (6 * hidden,),
        (6 * hidden,),
        (6 * hidden,),
        (4, 2 * hidden),
        (2 * hidden, 128),
        (256,),
        (64, 256),
        (256,),
    )
    outside, inside = pl.BlockSpec(memory_space=pl.ANY), pl.BlockSpec(memory_space=pltpu.VMEM)
    small = pl.BlockSpec(memory_space=pltpu.SMEM)
    params = pltpu.CompilerParams(vmem_limit_bytes=SMALL_LIMIT)
    moved = 6 * 2 * own[0].size
    part = own[0].shape[0]
    scratch = [pltpu.VMEM((2 * part, hidden), jnp.float32), pltpu.SemaphoreType.DMA((16,))]
    wide = pl.pallas_call(
        own_body,
        out_shape=wide_shapes,
        in_specs=[small, inside, inside],
        out_specs=(outside,) * 4,
        scratch_shapes=scratch,
        compiler_params=params,
        cost_estimate=pl.CostEstimate(flops=0, bytes_accessed=moved, transcendentals=0),
    )(bit, *own)
    done = pl.pallas_call(
        came_body,
        out_shape=wide_shapes
        + tuple(jax.ShapeDtypeStruct(shape, jnp.float32) for shape in rest_shapes),
        in_specs=[small] + [inside] * 3 + [outside] * 4,
        out_specs=(outside,) * 4 + (inside,) * 13,
        scratch_shapes=scratch,
        input_output_aliases={4 + index: index for index in range(4)},
        compiler_params=params,
        cost_estimate=pl.CostEstimate(flops=0, bytes_accessed=moved, transcendentals=0),
    )(bit, own[1], *came, *wide)
    done = [value.T if value.shape[0] in (4, 6, 64) else value for value in done]
    wide, rest = done[:4], done[4:]
    return (wide[0], rest[0], wide[1], *rest[1:5], wide[2], rest[5], wide[3], *rest[6:])


def partners(mask, size):
    return [(index, index ^ mask) for index in range(size)]


def swap_with(values, mask, size):
    return lax.ppermute(values, "dp", partners(mask, size))


def cut(values, mask, place):
    rows = values.shape[0] // 2
    bit = jnp.where((place & mask) != 0, 1, 0)
    sent = lax.dynamic_slice_in_dim(values, (1 - bit) * rows, rows, 0)
    return sent, lax.dynamic_slice_in_dim(values, bit * rows, rows, 0)


def add_low(kept, came):
    return (kept.astype(jnp.float32) + came.astype(jnp.float32)).astype(kept.dtype)


def double(values, mask, place, size):
    came = swap_with(values, mask, size)
    upper = (place & mask) != 0
    return jnp.concatenate(
        [jnp.where(upper, came, values), jnp.where(upper, values, came)], axis=0
    )


def swap_groups(values, mask):
    return lax.ppermute(values, "fsdp", partners(mask, lax.axis_size("fsdp")))


def share(values, also=None):
    group = lax.axis_size("fsdp")
    place = lax.axis_index("fsdp")
    pieces = [values] + [swap_groups(values, mask) for mask in range(1, group)]
    if also is not None:
        pieces, _ = lax.optimization_barrier((pieces, also))
    return jnp.stack([pick(place ^ index, pieces) for index in range(group)])


def pick(index, pieces):
    chosen = pieces[0]
    for place in range(1, len(pieces)):
        chosen = jnp.where(index == place, pieces[place], chosen)
    return chosen


def z_pieces(values):
    group = lax.axis_size("fsdp")
    place = lax.axis_index("fsdp")
    rows = values.shape[0] // group
    return [
        lax.dynamic_slice_in_dim(values, (place ^ mask) * rows, rows, 0) for mask in range(group)
    ]


def scatter_sum(pieces):
    came = [swap_groups(piece, mask) for mask, piece in enumerate(pieces) if mask]
    total = pieces[0].astype(jnp.float32)
    for piece in came:
        total = total + piece.astype(jnp.float32)
    return total.astype(pieces[0].dtype)


def dp_masks(size):
    return [1 << index for index in range(size.bit_length() - 1)]


def dp_orders():
    first, *others = dp_masks(lax.axis_size("dp"))
    return first, [others, others[::-1]]


def spread(parts, late=None, early=None):
    size = lax.axis_size("dp")
    place = lax.axis_index("dp")
    first, orders = dp_orders()
    for step in reversed(range(len(orders[0]))):
        parts = [double(part, order[step], place, size) for part, order in zip(parts, orders)]
        if step == len(orders[0]) - 1 and early is not None:
            parts, early = lax.optimization_barrier((parts, early))
    parts, late = lax.optimization_barrier((parts, late))
    return parts, [swap_with(part, first, size) for part in parts], late, early


def arrival(order, first, group):
    devices = []
    for half in range(2):
        places = []
        for block in range(1 << len(order)):
            dp = half * first
            for index, mask in enumerate(order):
                if block >> (len(order) - 1 - index) & 1:
                    dp |= mask
            places += [dp * group + index for index in range(group)]
        devices.append(places)
    return devices


def in_order(own, came, bit, places, rows):
    whole = jnp.concatenate([jnp.where(bit == 0, own, came), jnp.where(bit == 0, came, own)], axis=0)
    whole = whole.reshape((-1, rows) + own.shape[1:])
    flat = places[0] + places[1]
    return jnp.stack([whole[flat.index(device)] for device in range(len(flat))])


def sum_grads(kept, sent, flipped_grad, prepare, finish_rows, width, hidden):
    size = lax.axis_size("dp")
    group = lax.axis_size("fsdp")
    place = lax.axis_index("dp")
    first, orders = dp_orders()
    came = swap_with(sent, first, size)
    outgoing, x_grad = prepare(flipped_grad)
    came, outgoing = lax.optimization_barrier((came, outgoing))
    mine = add_low(kept, came)
    rows = mine.shape[0] // 2
    parts = [mine[:rows], mine[rows:]]
    for step in range(len(orders[0])):
        halves = [cut(part, order[step], place) for part, order in zip(parts, orders)]
        if step == 0:
            halves, outgoing = lax.optimization_barrier((halves, outgoing))
            incoming = lax.all_to_all(
                outgoing, ("dp", "fsdp"), split_axis=0, concat_axis=0, tiled=True
            )
        parts = [
            add_low(kept, swap_with(sent, order[step], size))
            for (sent, kept), order in zip(halves, orders)
        ]
    both = [part.reshape((group, -1) + part.shape[1:]) for part in parts]
    both = jnp.concatenate(both, axis=1).reshape((-1,) + kept.shape[1:])
    pieces = z_pieces(both)
    pieces, incoming = lax.optimization_barrier((pieces, incoming))
    shared = share(scatter_sum(pieces))
    late = (finish_rows(incoming), x_grad)
    parts = [piece.reshape((-1,) + kept.shape[1:]) for piece in jnp.split(shared, 2, axis=1)]
    own, came, late, _ = spread(parts, late)
    return finish((place & first).reshape(1), own, came, width, hidden), *late


def on_device(
    owner_ids,
    row_ids,
    embed_table,
    expandone,
    expbiasone,
    reduceone,
    redbiasone,
    normgainone,
    taskgateone,
    sharegateone,
    expandtwo,
    expbiastwo,
    reducetwo,
    redbiastwo,
    normgaintwo,
    taskgatetwo,
    towerinner,
    towerbias,
    towermiddle,
    towertail,
    logit_cot,
):
    devices = lax.axis_size(("dp", "fsdp"))
    events, fields = owner_ids.shape
    emb_width = embed_table.shape[1]
    capacity = 2 * events * fields // devices
    hidden = expandone.shape[1]
    width = fields * emb_width
    group = lax.axis_size("fsdp")
    owner_rows = owner_ids.T
    request, rank = assign_slots(owner_rows, row_ids.T, devices, capacity)
    asked_rows = lax.all_to_all(request, ("dp", "fsdp"), split_axis=0, concat_axis=0, tiled=True)
    packed = pack(
        (expbiasone, redbiasone, normgainone, expbiastwo, redbiastwo, normgaintwo),
        (towerbias, towertail, taskgateone.T, sharegateone.T, taskgatetwo.T, towerinner, towermiddle),
        (expandone, reduceone, expandtwo, reducetwo),
    )
    found = find_rows(asked_rows, embed_table.T)
    packed = share(packed, request)
    split = expandone.shape[0] + THIN_ROWS
    first, orders = dp_orders()
    parts = [packed[:, :split], packed[:, split:]]
    own, came, _, found = spread([part.reshape(-1, hidden) for part in parts], early=found)
    returned = lax.all_to_all(found, ("dp", "fsdp"), split_axis=0, concat_axis=0, tiled=True)
    bit = (lax.axis_index("dp") & first).reshape(1)
    places = [arrival(order, first, group) for order in orders]
    flipped = place_rows(returned, rank, owner_rows)
    sizes = [shard.shape[0] for shard in (expandone, reduceone, expandtwo, reducetwo)]
    if all(size % 16 == 0 for size in sizes):
        weights, thin = (*own, *came), ()
    else:
        thin = prep_thin(bit, own[0], came[0], places[0], width, hidden)
        whole = [
            in_order(mine, other, bit[0], place, part.shape[1])
            for mine, other, place, part in zip(own, came, places, parts)
        ]
        starts = [0, 0, sizes[1], sizes[1] + sizes[2]]
        weights = tuple(
            whole[min(index, 1)][:, start : start + size].reshape(-1, hidden)
            for index, (start, size) in enumerate(zip(starts, sizes))
        )
        places = None

    chunk = 16 * devices
    grad_rows = -(-(6 * (width + 3 * hidden) + 2 * hidden) // chunk) * chunk
    logits, flipped_grad, kept, sent = dense(bit, flipped, weights, places, thin, logit_cot, grad_rows)

    def prepare(flipped_grad):
        return send_rows(flipped_grad, rank, owner_rows, capacity, 1)

    def finish_rows(incoming):
        return add_rows(incoming, asked_rows, embed_table.shape[0])

    done, table_grad, x_grad = sum_grads(kept, sent, flipped_grad, prepare, finish_rows, width, hidden)
    return (logits, x_grad, table_grad.T, *done)


def solution(mesh):
    return jax.shard_map(
        on_device,
        mesh=mesh,
        in_specs=(
            P(("dp", "fsdp"), None),
            P(("dp", "fsdp"), None),
            P(("dp", "fsdp"), None),
            P(("dp", "fsdp"), None),
            P(("dp", "fsdp")),
            P(("dp", "fsdp"), None),
            P(("dp", "fsdp")),
            P(("dp", "fsdp")),
            P(("dp", "fsdp"), None),
            P(("dp", "fsdp"), None),
            P(("dp", "fsdp"), None),
            P(("dp", "fsdp")),
            P(("dp", "fsdp"), None),
            P(("dp", "fsdp")),
            P(("dp", "fsdp")),
            P(("dp", "fsdp"), None),
            P(("dp", "fsdp"), None),
            P(("dp", "fsdp")),
            P(("dp", "fsdp"), None),
            P(("dp", "fsdp")),
            P(None, ("dp", "fsdp")),
        ),
        out_specs=(
            P(None, ("dp", "fsdp")),
            P(("dp", "fsdp"), None),
            P(("dp", "fsdp"), None),
            P(),
            P(),
            P(),
            P(),
            P(),
            P(),
            P(),
            P(),
            P(),
            P(),
            P(),
            P(),
            P(),
            P(),
            P(),
            P(),
            P(),
        ),
        check_vma=False,
    )
```

```python
import functools

import jax
import jax.numpy as jnp
from jax import lax
from jax.experimental import pallas as pl
from jax.experimental.pallas import tpu as pltpu
from jax.sharding import PartitionSpec as P

EPS = 1e-05
VMEM_LIMIT = 56 * 1024 * 1024
SMALL_LIMIT = 24 * 1024 * 1024
ROW_BLOCKS = 8


def local_kernel(body, out_shape, flops, moved, scratch=(), limit=SMALL_LIMIT):
    return pl.pallas_call(
        body,
        out_shape=out_shape,
        scratch_shapes=list(scratch),
        compiler_params=pltpu.CompilerParams(vmem_limit_bytes=limit),
        cost_estimate=pl.CostEstimate(flops=flops, bytes_accessed=moved, transcendentals=0),
    )


def one_hot(hit):
    return jnp.where(hit, 1.0, 0.0).astype(jnp.bfloat16)


def low(value):
    return value.astype(jnp.float32).astype(jnp.bfloat16)


def iota(shape, axis):
    return lax.broadcasted_iota(jnp.int32, shape, axis)


def slot_body(owner_ref, row_ref, request_ref, rank_ref):
    fields, events = owner_ref.shape
    devices, _, capacity = request_ref.shape
    place = iota((devices, events), 0)
    asked = jnp.zeros((devices, events), jnp.float32)
    for field in range(fields):
        asked = asked + jnp.where(owner_ref[field : field + 1, :] == place, 1.0, 0.0)
    earlier = one_hot(iota((events, events), 0) < iota((events, events), 1))
    rank = jnp.dot(asked.astype(jnp.bfloat16), earlier, preferred_element_type=jnp.float32)
    rank = jnp.where(asked > 0.5, rank.astype(jnp.int32), -1)
    rank_ref[...] = rank
    slots = iota((capacity, events), 0)
    total = jnp.zeros((2 * devices, capacity), jnp.float32)
    for field in range(fields):
        mine = owner_ref[field : field + 1, :] == place
        field_rank = jnp.max(jnp.where(mine, rank, -1).astype(jnp.float32), axis=0, keepdims=True)
        rows = row_ref[field : field + 1, :]
        high = jnp.where(mine, (rows >> 6).astype(jnp.float32), 0.0)
        low = jnp.where(mine, (rows & 63).astype(jnp.float32), 0.0)
        value = jnp.concatenate([high, low], axis=0).astype(jnp.bfloat16)
        total = total + lax.dot_general(
            value,
            one_hot(field_rank.astype(jnp.int32) == slots),
            (((1,), (1,)), ((), ())),
            preferred_element_type=jnp.float32,
        )
    request = (total[:devices] * 64.0 + total[devices:]).astype(jnp.int32)
    for owner in range(devices):
        request_ref[owner] = request[owner : owner + 1]


def assign_slots(owner_rows, row_rows, devices, capacity):
    fields, events = owner_rows.shape
    return local_kernel(
        slot_body,
        (
            jax.ShapeDtypeStruct((devices, 1, capacity), jnp.int32),
            jax.ShapeDtypeStruct((devices, events), jnp.int32),
        ),
        2 * devices * events * (events + 2 * fields * capacity),
        4 * events * (2 * fields + devices),
        limit=VMEM_LIMIT,
    )(owner_rows, row_rows)


def find_body(request_ref, table_ref, found_ref, wide_ref):
    devices, _, capacity = request_ref.shape
    width = table_ref.shape[0]
    span = wide_ref.shape[1]
    places = iota((span, capacity), 0)
    for index in range(ROW_BLOCKS):
        wide_ref[index * width : (index + 1) * width, :] = table_ref[
            :, index * span : (index + 1) * span
        ]

    def step(source, carry):
        rows = request_ref[source]
        block = rows // span
        hits = one_hot(rows - block * span == places)
        rows_all = jnp.dot(wide_ref[...], hits, preferred_element_type=jnp.float32)
        picked = jnp.zeros((width, capacity), jnp.float32)
        for index in range(ROW_BLOCKS):
            picked = jnp.where(
                block == index, rows_all[index * width : (index + 1) * width, :], picked
            )
        found_ref[source] = picked.astype(jnp.bfloat16)
        return carry

    lax.fori_loop(0, devices, step, 0, unroll=16)


def find_rows(request, table):
    devices, _, capacity = request.shape
    width, rows = table.shape
    return local_kernel(
        find_body,
        jax.ShapeDtypeStruct((devices, width, capacity), jnp.bfloat16),
        16 * devices * capacity * rows * width,
        2 * (rows * width + devices * capacity * width),
        [pltpu.VMEM((ROW_BLOCKS * width, rows // ROW_BLOCKS), jnp.bfloat16)],
    )(request, table)


def place_body(found_ref, rank_ref, owner_ref, flipped_ref, total_ref):
    devices, width, capacity = found_ref.shape
    fields, events = owner_ref.shape
    slots = iota((capacity, events), 0)
    group = 4
    owners_low = low(owner_ref[...])
    total_ref[...] = jnp.zeros_like(total_ref)

    def step(start, carry):
        pieces = []
        for index in range(group):
            owner = start * group + index
            hits = one_hot(rank_ref[pl.ds(owner, 1), :] == slots)
            pieces.append(
                jnp.dot(found_ref[owner], hits, preferred_element_type=jnp.float32).astype(
                    jnp.bfloat16
                )
            )
        for field in range(fields):
            rows = slice(field * width, (field + 1) * width)
            owners = owners_low[field : field + 1, :]
            value = total_ref[rows, :]
            for index in range(group):
                value = jnp.where(owners == low(start * group + index), pieces[index], value)
            total_ref[rows, :] = value
        return carry

    lax.fori_loop(0, devices // group, step, 0)
    flipped_ref[...] = total_ref[...]


def place_rows(found, rank, owner_rows):
    devices, width, capacity = found.shape
    fields, events = owner_rows.shape
    return local_kernel(
        place_body,
        jax.ShapeDtypeStruct((fields * width, events), jnp.bfloat16),
        2 * devices * width * capacity * events,
        2 * (devices * width * capacity + fields * width * events),
        [pltpu.VMEM((fields * width, events), jnp.bfloat16)],
    )(found, rank, owner_rows)


def send_body(group, grad_ref, rank_ref, owner_ref, sent_ref, turned_ref, low_ref):
    devices, width, capacity = sent_ref.shape
    fields, events = owner_ref.shape
    slots = iota((capacity, events), 0)
    owners_low = low(owner_ref[...])
    low_ref[...] = grad_ref[...].astype(jnp.bfloat16)
    turned_ref[...] = grad_ref[...].T

    def step(owner, carry):
        chosen = jnp.zeros((width, events), jnp.bfloat16)
        for field in range(fields):
            rows = slice(field * width, (field + 1) * width)
            chosen = jnp.where(
                owners_low[field : field + 1, :] == low(owner), low_ref[rows, :], chosen
            )
        hits = one_hot(rank_ref[pl.ds(owner, 1), :] == slots)
        place = lax.rem(owner, group) * (devices // group) + lax.div(owner, group)
        sent_ref[place] = lax.dot_general(
            chosen,
            hits,
            (((1,), (1,)), ((), ())),
            preferred_element_type=jnp.float32,
        ).astype(jnp.bfloat16)
        return carry

    lax.fori_loop(0, devices, step, 0, unroll=16)


def send_rows(grad, rank, owner_rows, capacity, group):
    devices = rank.shape[0]
    fields, events = owner_rows.shape
    width = grad.shape[0] // fields
    return local_kernel(
        functools.partial(send_body, group),
        (
            jax.ShapeDtypeStruct((devices, width, capacity), jnp.bfloat16),
            jax.ShapeDtypeStruct((events, fields * width), jnp.float32),
        ),
        32 * devices * width * capacity * events,
        2 * (devices * width * capacity + 2 * fields * width * events),
        [pltpu.VMEM((fields * width, events), jnp.bfloat16)],
    )(grad, rank, owner_rows)


def add_body(came_ref, request_ref, out_ref, total_ref):
    devices, width, capacity = came_ref.shape
    span = total_ref.shape[1]
    group = 8
    places = iota((span, capacity), 0)
    total_ref[...] = jnp.zeros_like(total_ref)

    def step(start, carry):
        hits = []
        spread = []
        for index in range(group):
            source = start * group + index
            rows = request_ref[source]
            block = rows // span
            hits.append(one_hot(rows - block * span == places))
            came = came_ref[source].astype(jnp.float32)
            spread.append(
                jnp.concatenate(
                    [jnp.where(block == part, came, 0.0) for part in range(ROW_BLOCKS)], axis=0
                ).astype(jnp.bfloat16)
            )
        total_ref[...] += lax.dot_general(
            jnp.concatenate(spread, axis=1),
            jnp.concatenate(hits, axis=1),
            (((1,), (1,)), ((), ())),
            preferred_element_type=jnp.float32,
        )
        return carry

    lax.fori_loop(0, devices // group, step, 0, unroll=4)
    for index in range(ROW_BLOCKS):
        out_ref[:, index * span : (index + 1) * span] = total_ref[
            index * width : (index + 1) * width, :
        ]


def add_rows(came, request, rows):
    devices, width, capacity = came.shape
    span = rows // ROW_BLOCKS
    return local_kernel(
        add_body,
        jax.ShapeDtypeStruct((width, rows), jnp.float32),
        2 * devices * capacity * rows * width,
        2 * devices * width * capacity + 4 * rows * width,
        [pltpu.VMEM((ROW_BLOCKS * width, span), jnp.float32)],
    )(came, request)


THIN_ROWS = 48


def pack_thin_body(*refs):
    *biases, tbias, tail, taskgate, sharegate, upgate, inner, middle = refs[:13]
    *wide, out_ref, hold = refs[13:]
    hold[...] = jnp.zeros_like(hold)
    for row, piece in enumerate(biases + [tbias, tail]):
        hold[row : row + 1, : piece.shape[0]] = piece[...].astype(jnp.float32).reshape(1, -1)
    for row, piece in ((8, taskgate), (16, sharegate), (24, upgate), (32, inner)):
        hold[row : row + piece.shape[0], : piece.shape[1]] = piece[...].astype(jnp.float32)
    hold[32 : 32 + middle.shape[0], 128 : 128 + middle.shape[1]] = middle[...].astype(jnp.float32)
    thin = hold[...].astype(jnp.bfloat16)
    if not wide:
        out_ref[...] = thin
    start = 0
    for index, piece in enumerate(wide):
        out_ref[start : start + piece.shape[0], :] = piece[...]
        start += piece.shape[0]
        if index == 0:
            out_ref[start : start + THIN_ROWS, :] = thin
            start += THIN_ROWS


def pack(biases, others, wide):
    aligned = all(piece.shape[0] % 16 == 0 for piece in wide)
    rows = THIN_ROWS + (sum(piece.shape[0] for piece in wide) if aligned else 0)
    packed = local_kernel(
        pack_thin_body,
        jax.ShapeDtypeStruct((rows, 256), jnp.bfloat16),
        0,
        rows * 1024,
        [pltpu.VMEM((THIN_ROWS, 256), jnp.float32)],
        limit=VMEM_LIMIT,
    )(*biases, *others, *(wide if aligned else ()))
    if aligned:
        return packed
    return jnp.concatenate([wide[0], packed, *wide[1:]], axis=0)


def lay_thin(bit, sources, places, outs, holds):
    (
        columns_ref,
        gate_one_ref,
        gate_one_back_ref,
        gate_two_ref,
        gate_two_back_ref,
        inner_ref,
        inner_back_ref,
        middle_ref,
        middle_back_ref,
    ) = outs
    rows, task_rows, share_rows, up_rows, inner_rows, middle_rows = holds
    devices = 2 * len(places[0])
    hidden = columns_ref.shape[0]
    width = gate_one_ref.shape[1]

    def lay(target, source, index, count):
        target[:, index * count : (index + 1) * count] = source[:, :count]

    for held in (rows, task_rows, share_rows, up_rows):
        held[...] = jnp.zeros_like(held)
    bias = 6 * hidden // devices
    flat = hidden // devices

    def unpack(pieces):
        for half, source in enumerate(pieces):
            for block, index in enumerate(places[half]):
                thin = source(block).astype(jnp.float32)
                rows[0:6, index * bias : (index + 1) * bias] = thin[0:6, :bias]
                rows[6:8, index * flat : (index + 1) * flat] = thin[6:8, :flat]
                lay(task_rows, thin[8:16], index, 2 * width // devices)
                lay(share_rows, thin[16:24], index, width // devices)
                lay(up_rows, thin[24:32], index, 2 * hidden // devices)
                count = 2 * hidden // devices
                inner_rows[index * count : (index + 1) * count, :] = thin[32 : 32 + count, :128]
                count = hidden // devices
                middle_rows[index * count : (index + 1) * count, :] = thin[32 : 32 + count, 128:192]

    @pl.when(bit == 0)
    def _():
        unpack(sources)

    @pl.when(bit != 0)
    def _():
        unpack(sources[::-1])

    columns_ref[...] = jnp.zeros_like(columns_ref)
    for expert in range(6):
        columns_ref[:, expert * 8 : expert * 8 + 8] = rows[:, expert * hidden : (expert + 1) * hidden].T
    gates = jnp.concatenate(
        [
            task_rows[:, :width],
            task_rows[:, width:],
            share_rows[...],
            jnp.zeros((8, width), jnp.float32),
        ],
        axis=0,
    )
    gate_one_ref[...] = gates.astype(jnp.bfloat16)
    gate_one_back_ref[...] = gates.T.astype(jnp.bfloat16)
    gate_two_ref[...] = jnp.concatenate([up_rows[:, :hidden], up_rows[:, hidden:]], axis=0).astype(
        jnp.bfloat16
    )
    for task in range(2):
        span = slice(task * hidden, (task + 1) * hidden)
        wide = jnp.concatenate([up_rows[:, span], jnp.zeros((8, hidden), jnp.float32)], axis=0)
        gate_two_back_ref[span, :] = wide.T.astype(jnp.bfloat16)
        inner_ref[task * 128 : (task + 1) * 128, :] = inner_rows[span, :].T.astype(jnp.bfloat16)
        span = slice(task * 128, (task + 1) * 128)
        middle_ref[task * 64 : (task + 1) * 64, :] = middle_rows[span, :].T.astype(jnp.bfloat16)
    inner_back_ref[...] = inner_rows[...].astype(jnp.bfloat16)
    middle_back_ref[...] = middle_rows[...].astype(jnp.bfloat16)


def prep_thin_body(places, bit_ref, own_ref, came_ref, *refs):
    outs, holds, (thin_own, thin_came, sems) = refs[:9], refs[9:15], refs[15:]
    start = own_ref.shape[1] - THIN_ROWS
    copies = [
        pltpu.make_async_copy(ref.at[:, pl.ds(start, THIN_ROWS), :], held, sems.at[index])
        for index, (ref, held) in enumerate(((own_ref, thin_own), (came_ref, thin_came)))
    ]
    for copy in copies:
        copy.start()
    for copy in copies:
        copy.wait()
    sources = (lambda block: thin_own[block], lambda block: thin_came[block])
    lay_thin(bit_ref[0], sources, places, outs, holds)


def thin_shapes(width, hidden):
    outs = (
        ((hidden, 64), jnp.float32),
        ((32, width), jnp.bfloat16),
        ((width, 32), jnp.bfloat16),
        ((16, hidden), jnp.bfloat16),
        ((2 * hidden, 16), jnp.bfloat16),
        ((hidden, hidden), jnp.bfloat16),
        ((2 * hidden, 128), jnp.bfloat16),
        ((128, 128), jnp.bfloat16),
        ((hidden, 64), jnp.bfloat16),
    )
    holds = (
        (8, 6 * hidden),
        (8, 2 * width),
        (8, width),
        (8, 2 * hidden),
        (2 * hidden, 128),
        (hidden, 64),
    )
    return outs, [pltpu.VMEM(shape, jnp.float32) for shape in holds]


def prep_thin(bit, own, came, places, width, hidden):
    blocks = len(places[0])
    outs, holds = thin_shapes(width, hidden)
    thin_held = pltpu.VMEM((blocks, THIN_ROWS, hidden), jnp.bfloat16)
    return pl.pallas_call(
        functools.partial(prep_thin_body, places),
        out_shape=tuple(jax.ShapeDtypeStruct(*out) for out in outs),
        in_specs=[pl.BlockSpec(memory_space=pltpu.SMEM)] + [pl.BlockSpec(memory_space=pl.ANY)] * 2,
        scratch_shapes=holds + [thin_held, thin_held, pltpu.SemaphoreType.DMA((2,))],
        compiler_params=pltpu.CompilerParams(vmem_limit_bytes=VMEM_LIMIT),
        cost_estimate=pl.CostEstimate(flops=0, bytes_accessed=4 * own.size, transcendentals=0),
    )(bit, own.reshape(blocks, -1, hidden), came.reshape(blocks, -1, hidden))


SPAN = 512
ONES = 16


def over_events(left, right):
    return lax.dot_general(left, right, (((1,), (1,)), ((), ())), preferred_element_type=jnp.float32)


def times(left, right):
    return jnp.dot(left, right, preferred_element_type=jnp.float32)


def sum_rows(values):
    return jnp.sum(values, axis=0, keepdims=True)


def sigmoid_of(values):
    return 0.5 * jnp.tanh(0.5 * values) + 0.5


def silu_parts(values):
    sig = sigmoid_of(values)
    active = values * sig
    return active, sig + active * (1.0 - sig)


def expert_up(inputs, expand, expbias, shrink, shrinkbias):
    active, slope = silu_parts(times(expand, inputs) + expbias)
    active = active.astype(jnp.bfloat16)
    output = times(shrink, active) + shrinkbias
    scale = 1.0 / output.shape[0]
    centered = output - sum_rows(output) * scale
    inverse = lax.rsqrt(sum_rows(centered * centered) * scale + EPS)
    return active, slope, centered * inverse, inverse


def soft(scores, count):
    valid = iota(scores.shape, 0) < count
    scores = jnp.where(valid, scores, -1e30)
    shifted = jnp.exp(scores - jnp.max(scores, axis=0, keepdims=True))
    shifted = jnp.where(valid, shifted, 0.0)
    return shifted / sum_rows(shifted)


def soft_back(probs, rows):
    tall = jnp.concatenate(rows + [jnp.zeros_like(rows[0])] * (probs.shape[0] - len(rows)), axis=0)
    return probs * (tall - sum_rows(probs * tall))


def assemble(bit, own_ref, came_ref, homes, places):
    blocks = len(places[0])
    rows = own_ref.shape[0] // blocks
    for half, source in ((bit, own_ref), (1 - bit, came_ref)):
        for block in range(blocks):
            start = block * rows
            for home in homes:
                size = home.shape[0] // (2 * blocks)
                place = places[0][block] * size + half * ((places[1][0] - places[0][0]) * size)
                home[pl.ds(pl.multiple_of(place, 16), size), :] = source[start : start + size, :]
                start += size


def dense_body(places, *refs):
    bit_ref, *refs = refs
    if places is None:
        *naturals, refs = *refs[:4], refs[4:]
    else:
        arrived, refs = refs[:4], refs[4:]
        refs, naturals, holds, held, loads = refs[:-15], refs[-15:-11], refs[-11:-5], refs[-5:-1], refs[-1]
        thin, refs = refs[-9:], refs[:-9]
        refs = [refs[0], *thin, *refs[1:]]
    expand_one_back_ref, shrink_one_back_ref, expand_two_back_ref, shrink_two_back_ref = naturals
    (
        flipped_ref,
        columns_ref,
        gate_one_ref,
        gate_one_back_ref,
        gate_two_ref,
        gate_two_back_ref,
        inner_ref,
        inner_back_ref,
        middle_ref,
        middle_back_ref,
        cot_ref,
        logits_ref,
        flipped_grad_ref,
        kept_ref,
        sent_ref,
        sems,
        grads_ref,
        input_keep,
        active_one,
        out_one,
        pre_one,
        score_one,
        carried_keep,
        active_two,
        out_two,
        pre_two,
        score_two,
        tower_keep,
        tower_act_keep,
        first_keep,
        top_keep,
        tail_keep,
        gain_keep,
        expand_one_ref,
        shrink_one_ref,
        expand_two_ref,
        shrink_two_ref,
    ) = refs
    bit = jnp.minimum(bit_ref[0], 1)
    if places is not None:
        copies = [
            pltpu.make_async_copy(arrived[index], held[index], loads.at[index]) for index in (0, 2, 1, 3)
        ]
        for copy in copies:
            copy.start()
        own_a, own_b, came_a, came_b = held
        for copy in copies[:2]:
            copy.wait()
        shard = own_a.shape[0] // len(places[0][0])

        def thin_of(ref):
            return lambda block: ref[(block + 1) * shard - THIN_ROWS : (block + 1) * shard, :]

        lay_thin(bit, (thin_of(own_a), thin_of(came_a)), places[0], thin, holds)
        for copy in copies[2:]:
            copy.wait()
        assemble(bit, own_a, came_a, [expand_one_back_ref], places[0])
        assemble(
            bit,
            own_b,
            came_b,
            [shrink_one_back_ref, expand_two_back_ref, shrink_two_back_ref],
            places[1],
        )
    for natural, turned in (
        (expand_one_back_ref, expand_one_ref),
        (shrink_one_back_ref, shrink_one_ref),
        (expand_two_back_ref, expand_two_ref),
        (shrink_two_back_ref, shrink_two_ref),
    ):
        depth = natural.shape[0] // 6
        across = natural.shape[1]
        for expert in range(6):
            turned[expert * across : (expert + 1) * across, :] = natural[
                expert * depth : (expert + 1) * depth, :
            ].T

    width, events = flipped_ref.shape
    hidden = shrink_one_back_ref.shape[1]
    inner = inner_ref.shape[0] // 2
    narrow = middle_ref.shape[0] // 2
    tall = hidden + ONES
    span = min(SPAN, events)
    unit = jnp.ones((ONES, events), jnp.bfloat16)

    input_keep[:width, :] = flipped_ref[...]
    input_keep[width:, :] = unit
    for expert in range(6):
        active_one[expert * tall + hidden : (expert + 1) * tall, :] = unit
        active_two[expert * tall + hidden : (expert + 1) * tall, :] = unit
    for group in range(3):
        carried_keep[group * tall + hidden : (group + 1) * tall, :] = unit
    for task in range(2):
        tower_keep[task * tall + hidden : (task + 1) * tall, :] = unit
    gain_keep[...] = jnp.zeros_like(gain_keep)

    def column(index, rows=hidden, start=0):
        return columns_ref[start : start + rows, index : index + 1]

    def experts_rows(expert):
        return slice(expert * hidden, (expert + 1) * hidden)

    def span_step(step, carry):
        lanes = pl.ds(pl.multiple_of(step * span, span), span)
        inputs = flipped_ref[:, lanes]

        def up(level, inputs_of, expand_ref, shrink_ref, active_keep):
            kept = []
            for expert in range(6):
                active, slope, normed, inverse = expert_up(
                    inputs_of(expert),
                    expand_ref[experts_rows(expert), :],
                    column(expert * 8 + level),
                    shrink_ref[experts_rows(expert), :],
                    column(expert * 8 + level + 1),
                )
                active_keep[expert * tall : expert * tall + hidden, lanes] = active
                kept.append((slope, normed, inverse, normed * column(expert * 8 + level + 2)))
            return kept

        kept_one = up(0, lambda expert: inputs, expand_one_ref, shrink_one_ref, active_one)
        scores = times(gate_one_ref[...], inputs)
        probs_one = [soft(scores[0:8], 4), soft(scores[8:16], 4), soft(scores[16:24], 6)]
        carried = []
        for group in range(3):
            members = [2 * group, 2 * group + 1, 4, 5] if group < 2 else range(6)
            mixed = 0.0
            for place, expert in enumerate(members):
                mixed = mixed + probs_one[group][place : place + 1, :] * kept_one[expert][3]
            carried.append(mixed.astype(jnp.bfloat16))
            carried_keep[group * tall : group * tall + hidden, lanes] = carried[group]

        kept_two = up(
            3, lambda expert: carried[expert // 2], expand_two_ref, shrink_two_ref, active_two
        )
        probs_two = []
        tower_grads = []
        dq_two = []
        for task in range(2):
            probs = soft(times(gate_two_ref[task * 8 : task * 8 + 8, :], carried[task]), 4)
            probs_two.append(probs)
            members = [2 * task, 2 * task + 1, 4, 5]
            mixed = 0.0
            for place, expert in enumerate(members):
                mixed = mixed + probs[place : place + 1, :] * kept_two[expert][3]
            mixed = mixed.astype(jnp.bfloat16)
            tower_keep[task * tall : task * tall + hidden, lanes] = mixed
            first, first_slope = silu_parts(
                times(inner_ref[task * inner : (task + 1) * inner, :], mixed)
                + column(6, inner, task * inner)
            )
            first = first.astype(jnp.bfloat16)
            tower_act_keep[task * inner : (task + 1) * inner, lanes] = first
            top, top_slope = silu_parts(
                times(middle_ref[task * narrow : (task + 1) * narrow, :], first)
                + column(7, narrow, 2 * task * narrow)
            )
            weight = column(7, narrow, (2 * task + 1) * narrow)
            logits_ref[task : task + 1, lanes] = sum_rows(top * weight)
            cot = cot_ref[task : task + 1, lanes]
            top_grad = (cot * weight * top_slope).astype(jnp.bfloat16)
            top_keep[task * narrow : (task + 1) * narrow, lanes] = top_grad
            seen = cot * top
            high = seen.astype(jnp.bfloat16)
            tail_keep[2 * task * narrow : (2 * task + 1) * narrow, lanes] = high
            tail_keep[(2 * task + 1) * narrow : (2 * task + 2) * narrow, lanes] = (
                seen - high.astype(jnp.float32)
            ).astype(jnp.bfloat16)
            first_grad = (
                times(middle_back_ref[task * inner : (task + 1) * inner, :], top_grad) * first_slope
            ).astype(jnp.bfloat16)
            first_keep[task * inner : (task + 1) * inner, lanes] = first_grad
            grad = times(inner_back_ref[task * hidden : (task + 1) * hidden, :], first_grad)
            tower_grads.append(grad)
            dq_two.append([sum_rows(kept_two[expert][3] * grad) for expert in members])

        def expert_down(level, expert, kept, upstream, slant, shrink_back_ref, out_keep, pre_keep):
            slope, normed, inverse, _ = kept
            gained = upstream * normed
            part = gained[:, :128]
            for start in range(128, span, 128):
                part = part + gained[:, start : start + 128]
            gain_rows = slice((level + expert) * hidden, (level + expert + 1) * hidden)
            gain_keep[gain_rows, :] += part
            scaled = upstream * column(expert * 8 + level // 2 + 2)
            scale = 1.0 / hidden
            out_low = (
                inverse * (scaled - sum_rows(scaled) * scale - normed * (slant * scale))
            ).astype(jnp.bfloat16)
            out_keep[experts_rows(expert), lanes] = out_low
            pre_low = (times(shrink_back_ref[experts_rows(expert), :], out_low) * slope).astype(
                jnp.bfloat16
            )
            pre_keep[experts_rows(expert), lanes] = pre_low
            return pre_low

        pre_lows = []
        for expert in range(6):
            if expert < 4:
                task, place = expert // 2, expert % 2
                prob = probs_two[task][place : place + 1, :]
                upstream = prob * tower_grads[task]
                slant = prob * dq_two[task][place]
            else:
                place = expert - 2
                prob = [probs_two[task][place : place + 1, :] for task in range(2)]
                upstream = prob[0] * tower_grads[0] + prob[1] * tower_grads[1]
                slant = prob[0] * dq_two[0][place] + prob[1] * dq_two[1][place]
            pre_lows.append(
                expert_down(
                    6, expert, kept_two[expert], upstream, slant, shrink_two_back_ref, out_two, pre_two
                )
            )
        carried_grads = []
        for group in range(3):
            grad = 0.0
            for expert in (2 * group, 2 * group + 1):
                grad = grad + times(expand_two_back_ref[experts_rows(expert), :], pre_lows[expert])
            if group < 2:
                score = soft_back(probs_two[group], dq_two[group])
                score = jnp.concatenate([score, jnp.zeros_like(score)], axis=0).astype(jnp.bfloat16)
                score_two[group * 16 : group * 16 + 16, lanes] = score
                grad = grad + times(gate_two_back_ref[experts_rows(group), :], score)
            carried_grads.append(grad)

        dq_one = []
        for group in range(3):
            members = [2 * group, 2 * group + 1, 4, 5] if group < 2 else range(6)
            dq_one.append([sum_rows(kept_one[expert][3] * carried_grads[group]) for expert in members])
        pre_lows = []
        for expert in range(6):
            prob = probs_one[2][expert : expert + 1, :]
            upstream = prob * carried_grads[2]
            slant = prob * dq_one[2][expert]
            for task in range(2):
                if expert // 2 in (task, 2):
                    place = expert % 2 if expert < 4 else expert - 2
                    prob = probs_one[task][place : place + 1, :]
                    upstream = upstream + prob * carried_grads[task]
                    slant = slant + prob * dq_one[task][place]
            pre_lows.append(
                expert_down(
                    0, expert, kept_one[expert], upstream, slant, shrink_one_back_ref, out_one, pre_one
                )
            )
        scores_low = [soft_back(probs_one[group], dq_one[group]) for group in range(3)]
        score = jnp.concatenate(scores_low + [jnp.zeros_like(scores_low[0])], axis=0).astype(
            jnp.bfloat16
        )
        score_one[:, lanes] = score
        grad = times(gate_one_back_ref[...], score)
        for expert in range(6):
            grad = grad + times(
                expand_one_back_ref[expert * width : (expert + 1) * width, :], pre_lows[expert]
            )
        flipped_grad_ref[:, lanes] = grad
        return carry

    lax.fori_loop(0, events // span, span_step, 0)

    half_rows = grads_ref.shape[1]

    def leave(half):
        for target, sem, when in ((kept_ref, 0, half), (sent_ref, 1, 1 - half)):

            @pl.when(bit == when)
            def _():
                pltpu.make_async_copy(grads_ref.at[half], target, sems.at[sem]).start()

    def put(row, value):
        while value.shape[0]:
            half, start = row // half_rows, row % half_rows
            count = min(value.shape[0], half_rows - start)
            grads_ref[half, start : start + count, :] = value[:count].astype(jnp.bfloat16)
            row, value = row + count, value[count:]
            if row % half_rows == 0:
                leave(half)

    rows = 0
    biases = []
    for expert in range(6):
        both = over_events(input_keep[...], pre_one[experts_rows(expert), :])
        put(rows + expert * width, both[:width])
        biases.append(both[width : width + 1])
    rows += 6 * width
    for expert in range(6):
        both = over_events(active_one[expert * tall : (expert + 1) * tall, :], out_one[experts_rows(expert), :])
        put(rows + expert * hidden, both[:hidden])
        biases.append(both[hidden : hidden + 1])
    rows += 6 * hidden
    for expert in range(6):
        group = expert // 2
        both = over_events(carried_keep[group * tall : (group + 1) * tall, :], pre_two[experts_rows(expert), :])
        put(rows + expert * hidden, both[:hidden])
        biases.append(both[hidden : hidden + 1])
    rows += 6 * hidden
    for expert in range(6):
        both = over_events(active_two[expert * tall : (expert + 1) * tall, :], out_two[experts_rows(expert), :])
        put(rows + expert * hidden, both[:hidden])
        biases.append(both[hidden : hidden + 1])
    rows += 6 * hidden
    tower = []
    for task in range(2):
        tower.append(
            over_events(tower_keep[task * tall : (task + 1) * tall, :], first_keep[task * inner : (task + 1) * inner, :])
        )
    tower = jnp.concatenate(tower, axis=1)
    put(rows, tower[:hidden])
    biases.append(tower[hidden : hidden + 1])
    rows += hidden
    put(
        rows,
        jnp.concatenate(
            [
                over_events(
                    top_keep[task * narrow : (task + 1) * narrow, :],
                    tower_act_keep[task * inner : (task + 1) * inner, :],
                )
                for task in range(2)
            ],
            axis=1,
        ),
    )
    rows += narrow
    gates = over_events(score_one[...], flipped_ref[...])
    for start in range(0, width, hidden):
        put(rows, gates[:, start : start + hidden])
        rows += gates.shape[0]
    for task in range(2):
        put(
            rows,
            over_events(
                score_two[task * 16 : task * 16 + 16, :],
                carried_keep[task * tall : task * tall + hidden, :],
            ),
        )
        rows += 16
    tops = over_events(unit, top_keep[...])[:1]
    seen = over_events(unit, tail_keep[...])[:1]
    pieces = []
    for task in range(2):
        pieces.append(tops[:, task * narrow : (task + 1) * narrow])
        pieces.append(
            seen[:, 2 * task * narrow : (2 * task + 1) * narrow]
            + seen[:, (2 * task + 1) * narrow : (2 * task + 2) * narrow]
        )
    biases.append(jnp.concatenate(pieces, axis=1))
    gains = gain_keep[...]
    high = gains.astype(jnp.bfloat16)
    low = (gains - high.astype(jnp.float32)).astype(jnp.bfloat16)
    gains = (over_events(unit[:, :128], high) + over_events(unit[:, :128], low))[:1]
    for expert in range(12):
        biases.append(gains[:, experts_rows(expert)])
    biases = jnp.concatenate(biases, axis=0)
    extra = 2 * half_rows - rows - biases.shape[0]
    put(rows, jnp.concatenate([biases, jnp.zeros((extra, hidden), jnp.float32)], axis=0))
    pltpu.make_async_copy(grads_ref.at[bit], kept_ref, sems.at[0]).wait()
    pltpu.make_async_copy(grads_ref.at[1 - bit], sent_ref, sems.at[1]).wait()


def dense(bit, flipped, weights, places, thin, cot, grad_rows):
    width, events = flipped.shape
    hidden = weights[0].shape[1]
    inner, narrow = 128, 64
    tall = hidden + ONES
    low = functools.partial(pltpu.VMEM, dtype=jnp.bfloat16)
    kept = (
        width + ONES,
        6 * tall,
        6 * hidden,
        6 * hidden,
        32,
        3 * tall,
        6 * tall,
        6 * hidden,
        6 * hidden,
        32,
        2 * tall,
        2 * inner,
        2 * inner,
        2 * narrow,
        4 * narrow,
    )
    half = (grad_rows // 2, hidden)
    scratch = [pltpu.SemaphoreType.DMA((2,)), low((2,) + half)]
    scratch += [low((rows, events)) for rows in kept]
    scratch.append(pltpu.VMEM((12 * hidden, 128), jnp.float32))
    scratch += [low((6 * hidden, depth)) for depth in (width, hidden, hidden, hidden)]
    vmem = pl.BlockSpec(memory_space=pltpu.VMEM)
    outside = pl.BlockSpec(memory_space=pl.ANY)
    specs = [pl.BlockSpec(memory_space=pltpu.SMEM)]
    specs += [vmem if places is None else outside] * 4 + [vmem] * (len(thin) + 2)
    if places is not None:
        outs, holds = thin_shapes(width, hidden)
        scratch += [pltpu.VMEM(*out) for out in outs]
        scratch += [low((6 * depth, hidden)) for depth in (width, hidden, hidden, hidden)]
        scratch += holds + [low(weight.shape) for weight in weights]
        scratch.append(pltpu.SemaphoreType.DMA((4,)))
    return pl.pallas_call(
        functools.partial(dense_body, places),
        out_shape=(
            jax.ShapeDtypeStruct((2, events), jnp.float32),
            jax.ShapeDtypeStruct((width, events), jnp.float32),
            jax.ShapeDtypeStruct(half, jnp.bfloat16),
            jax.ShapeDtypeStruct(half, jnp.bfloat16),
        ),
        in_specs=specs,
        out_specs=(vmem, vmem, outside, outside),
        scratch_shapes=scratch,
        compiler_params=pltpu.CompilerParams(vmem_limit_bytes=51 * 1024 * 1024),
        cost_estimate=pl.CostEstimate(
            flops=6 * events * hidden * (6 * (width + 3 * hidden) + 2 * inner),
            bytes_accessed=24 * 1024 * 1024,
            transcendentals=12 * events * hidden,
        ),
    )(bit, *weights, flipped, *thin, cot)


def grad_layout(width, hidden):
    sizes = [6 * width, 6 * hidden, 6 * hidden, 6 * hidden]
    starts = [sum(sizes[:index]) for index in range(5)]
    return sizes, starts


def grad_moves(part, half, hidden, width):
    sizes, starts = grad_layout(width, hidden)
    most = 512
    moves = []
    for index in range(2):
        first = (2 * half + index) * part
        for target, (start, size) in enumerate(zip(starts, sizes)):
            low_row, high_row = max(first, start), min(first + part, start + size)
            for row in range(low_row, high_row, most):
                moves.append((index, row - first, target, row - start, min(most, high_row - row)))
    return moves


def write_wide(half, pieces, ready, wide, hold, sems, width, hidden):
    part = pieces[0].shape[0]
    block = 128
    copies = []
    for number, (index, start, target, place, rows) in enumerate(grad_moves(part, half, hidden, width)):
        if ready and start == 0:
            ready[index].wait()
        source = pieces[index]
        base = index * part + start

        def step(count, carry):
            hold[pl.ds(pl.multiple_of(base + count * block, block), block), :] = source[
                pl.ds(pl.multiple_of(start + count * block, block), block), :
            ].astype(jnp.float32)
            return carry

        lax.fori_loop(0, rows // block, step, 0, unroll=4)
        copy = pltpu.make_async_copy(
            hold.at[pl.ds(base, rows), :], wide[target].at[pl.ds(place, rows), :], sems.at[number]
        )
        copy.start()
        copies.append(copy)
    return copies


def own_body(bit_ref, own_a_ref, own_b_ref, *refs):
    *wide, hold, sems = refs
    hidden = wide[0].shape[1]
    width = wide[0].shape[0] // 6

    for half in range(2):

        @pl.when(jnp.minimum(bit_ref[0], 1) == half)
        def _():
            for copy in write_wide(half, (own_a_ref, own_b_ref), (), wide, hold, sems, width, hidden):
                copy.wait()


def came_body(bit_ref, own_b_ref, came_a_ref, came_b_ref, *refs):
    wide, outs, (hold, sems) = refs[4:8], refs[8:21], refs[21:]
    hidden = wide[0].shape[1]
    width = wide[0].shape[0] // 6
    part = came_a_ref.shape[0]
    start = grad_layout(width, hidden)[1][4] - 3 * part
    bit = jnp.minimum(bit_ref[0], 1)
    for half in range(2):

        @pl.when(bit != half)
        def _():
            copies = write_wide(half, (came_a_ref, came_b_ref), (), wide, hold, sems, width, hidden)
            write_rest(came_b_ref if half else own_b_ref, start, outs, width, hidden)
            for copy in copies:
                copy.wait()


def write_rest(source, start, outs, width, hidden):
    (
        low_inbias_ref,
        low_outbias_ref,
        low_gain_ref,
        low_taskgate_ref,
        low_sharegate_ref,
        up_inbias_ref,
        up_outbias_ref,
        up_gain_ref,
        up_taskgate_ref,
        inner_ref,
        tbias_ref,
        middle_ref,
        tail_ref,
    ) = outs
    inner = inner_ref.shape[1]

    def take(rows):
        nonlocal start
        start += rows
        return source[start - rows : start, :].astype(jnp.float32)

    both = take(hidden)
    inner_ref[:hidden, :] = both[:, :inner]
    inner_ref[hidden:, :] = both[:, inner:]
    middle_ref[...] = take(middle_ref.shape[0])
    for index in range(width // hidden):
        gates = take(32)
        span = slice(index * hidden, (index + 1) * hidden)
        low_taskgate_ref[:, span] = gates[0:4]
        low_taskgate_ref[:, width + index * hidden : width + (index + 1) * hidden] = gates[8:12]
        low_sharegate_ref[:, span] = gates[16:22]
    for task in range(2):
        up_taskgate_ref[:, task * hidden : (task + 1) * hidden] = take(16)[0:4]
    rows = take(48)
    flat = (low_inbias_ref, low_outbias_ref, up_inbias_ref, up_outbias_ref, tbias_ref, tail_ref)
    place = 0
    for target in flat + (low_gain_ref, up_gain_ref):
        for index in range(target.shape[0] // hidden):
            target[index * hidden : (index + 1) * hidden] = rows[place]
            place += 1


def finish(bit, own, came, width, hidden):
    wide_shapes = tuple(
        jax.ShapeDtypeStruct((size, hidden), jnp.float32) for size in grad_layout(width, hidden)[0]
    )
    rest_shapes = (
        (6 * hidden,),
        (6 * hidden,),
        (6 * hidden,),
        (4, 2 * width),
        (6, width),
        (6 * hidden,),
        (6 * hidden,),
        (6 * hidden,),
        (4, 2 * hidden),
        (2 * hidden, 128),
        (256,),
        (64, 256),
        (256,),
    )
    outside, inside = pl.BlockSpec(memory_space=pl.ANY), pl.BlockSpec(memory_space=pltpu.VMEM)
    small = pl.BlockSpec(memory_space=pltpu.SMEM)
    params = pltpu.CompilerParams(vmem_limit_bytes=SMALL_LIMIT)
    moved = 6 * 2 * own[0].size
    part = own[0].shape[0]
    scratch = [pltpu.VMEM((2 * part, hidden), jnp.float32), pltpu.SemaphoreType.DMA((16,))]
    wide = pl.pallas_call(
        own_body,
        out_shape=wide_shapes,
        in_specs=[small, inside, inside],
        out_specs=(outside,) * 4,
        scratch_shapes=scratch,
        compiler_params=params,
        cost_estimate=pl.CostEstimate(flops=0, bytes_accessed=moved, transcendentals=0),
    )(bit, *own)
    done = pl.pallas_call(
        came_body,
        out_shape=wide_shapes
        + tuple(jax.ShapeDtypeStruct(shape, jnp.float32) for shape in rest_shapes),
        in_specs=[small] + [inside] * 3 + [outside] * 4,
        out_specs=(outside,) * 4 + (inside,) * 13,
        scratch_shapes=scratch,
        input_output_aliases={4 + index: index for index in range(4)},
        compiler_params=params,
        cost_estimate=pl.CostEstimate(flops=0, bytes_accessed=moved, transcendentals=0),
    )(bit, own[1], *came, *wide)
    done = [value.T if value.shape[0] in (4, 6, 64) else value for value in done]
    wide, rest = done[:4], done[4:]
    return (wide[0], rest[0], wide[1], *rest[1:5], wide[2], rest[5], wide[3], *rest[6:])


def partners(mask, size):
    return [(index, index ^ mask) for index in range(size)]


def swap_with(values, mask, size):
    return lax.ppermute(values, "dp", partners(mask, size))


def cut(values, mask, place):
    rows = values.shape[0] // 2
    bit = jnp.where((place & mask) != 0, 1, 0)
    sent = lax.dynamic_slice_in_dim(values, (1 - bit) * rows, rows, 0)
    return sent, lax.dynamic_slice_in_dim(values, bit * rows, rows, 0)


def add_low(kept, came):
    return (kept.astype(jnp.float32) + came.astype(jnp.float32)).astype(kept.dtype)


def double(values, mask, place, size):
    came = swap_with(values, mask, size)
    upper = (place & mask) != 0
    return jnp.concatenate(
        [jnp.where(upper, came, values), jnp.where(upper, values, came)], axis=0
    )


def swap_groups(values, mask):
    return lax.ppermute(values, "fsdp", partners(mask, lax.axis_size("fsdp")))


def share(values, also=None):
    group = lax.axis_size("fsdp")
    place = lax.axis_index("fsdp")
    pieces = [values] + [swap_groups(values, mask) for mask in range(1, group)]
    if also is not None:
        pieces, _ = lax.optimization_barrier((pieces, also))
    return jnp.stack([pick(place ^ index, pieces) for index in range(group)])


def pick(index, pieces):
    chosen = pieces[0]
    for place in range(1, len(pieces)):
        chosen = jnp.where(index == place, pieces[place], chosen)
    return chosen


def z_pieces(values):
    group = lax.axis_size("fsdp")
    place = lax.axis_index("fsdp")
    rows = values.shape[0] // group
    return [
        lax.dynamic_slice_in_dim(values, (place ^ mask) * rows, rows, 0) for mask in range(group)
    ]


def scatter_sum(pieces):
    came = [swap_groups(piece, mask) for mask, piece in enumerate(pieces) if mask]
    total = pieces[0].astype(jnp.float32)
    for piece in came:
        total = total + piece.astype(jnp.float32)
    return total.astype(pieces[0].dtype)


def dp_masks(size):
    return [1 << index for index in range(size.bit_length() - 1)]


def dp_orders():
    first, *others = dp_masks(lax.axis_size("dp"))
    return first, [others, others[::-1]]


def spread(parts, late=None, early=None):
    size = lax.axis_size("dp")
    place = lax.axis_index("dp")
    first, orders = dp_orders()
    for step in reversed(range(len(orders[0]))):
        parts = [double(part, order[step], place, size) for part, order in zip(parts, orders)]
        if step == len(orders[0]) - 1 and early is not None:
            parts, early = lax.optimization_barrier((parts, early))
    parts, late = lax.optimization_barrier((parts, late))
    return parts, [swap_with(part, first, size) for part in parts], late, early


def arrival(order, first, group):
    devices = []
    for half in range(2):
        places = []
        for block in range(1 << len(order)):
            dp = half * first
            for index, mask in enumerate(order):
                if block >> (len(order) - 1 - index) & 1:
                    dp |= mask
            places += [dp * group + index for index in range(group)]
        devices.append(places)
    return devices


def in_order(own, came, bit, places, rows):
    whole = jnp.concatenate([jnp.where(bit == 0, own, came), jnp.where(bit == 0, came, own)], axis=0)
    whole = whole.reshape((-1, rows) + own.shape[1:])
    flat = places[0] + places[1]
    return jnp.stack([whole[flat.index(device)] for device in range(len(flat))])


def sum_grads(kept, sent, flipped_grad, prepare, finish_rows, width, hidden):
    size = lax.axis_size("dp")
    group = lax.axis_size("fsdp")
    place = lax.axis_index("dp")
    first, orders = dp_orders()
    came = swap_with(sent, first, size)
    outgoing, x_grad = prepare(flipped_grad)
    came, outgoing = lax.optimization_barrier((came, outgoing))
    mine = add_low(kept, came)
    rows = mine.shape[0] // 2
    parts = [mine[:rows], mine[rows:]]
    for step in range(len(orders[0])):
        halves = [cut(part, order[step], place) for part, order in zip(parts, orders)]
        if step == 0:
            halves, outgoing = lax.optimization_barrier((halves, outgoing))
            incoming = lax.all_to_all(
                outgoing, ("dp", "fsdp"), split_axis=0, concat_axis=0, tiled=True
            )
        parts = [
            add_low(kept, swap_with(sent, order[step], size))
            for (sent, kept), order in zip(halves, orders)
        ]
    both = [part.reshape((group, -1) + part.shape[1:]) for part in parts]
    both = jnp.concatenate(both, axis=1).reshape((-1,) + kept.shape[1:])
    pieces = z_pieces(both)
    pieces, incoming = lax.optimization_barrier((pieces, incoming))
    shared = share(scatter_sum(pieces))
    late = (finish_rows(incoming), x_grad)
    parts = [piece.reshape((-1,) + kept.shape[1:]) for piece in jnp.split(shared, 2, axis=1)]
    own, came, late, _ = spread(parts, late)
    return finish((place & first).reshape(1), own, came, width, hidden), *late


def on_device(
    owner_ids,
    row_ids,
    embed_table,
    expandone,
    expbiasone,
    reduceone,
    redbiasone,
    normgainone,
    taskgateone,
    sharegateone,
    expandtwo,
    expbiastwo,
    reducetwo,
    redbiastwo,
    normgaintwo,
    taskgatetwo,
    towerinner,
    towerbias,
    towermiddle,
    towertail,
    logit_cot,
):
    devices = lax.axis_size(("dp", "fsdp"))
    events, fields = owner_ids.shape
    emb_width = embed_table.shape[1]
    capacity = 2 * events * fields // devices
    hidden = expandone.shape[1]
    width = fields * emb_width
    group = lax.axis_size("fsdp")
    owner_rows = owner_ids.T
    request, rank = assign_slots(owner_rows, row_ids.T, devices, capacity)
    asked_rows = lax.all_to_all(request, ("dp", "fsdp"), split_axis=0, concat_axis=0, tiled=True)
    packed = pack(
        (expbiasone, redbiasone, normgainone, expbiastwo, redbiastwo, normgaintwo),
        (towerbias, towertail, taskgateone.T, sharegateone.T, taskgatetwo.T, towerinner, towermiddle),
        (expandone, reduceone, expandtwo, reducetwo),
    )
    found = find_rows(asked_rows, embed_table.T)
    packed = share(packed, request)
    split = expandone.shape[0] + THIN_ROWS
    first, orders = dp_orders()
    parts = [packed[:, :split], packed[:, split:]]
    own, came, _, found = spread([part.reshape(-1, hidden) for part in parts], early=found)
    returned = lax.all_to_all(found, ("dp", "fsdp"), split_axis=0, concat_axis=0, tiled=True)
    bit = (lax.axis_index("dp") & first).reshape(1)
    places = [arrival(order, first, group) for order in orders]
    flipped = place_rows(returned, rank, owner_rows)
    sizes = [shard.shape[0] for shard in (expandone, reduceone, expandtwo, reducetwo)]
    if all(size % 16 == 0 for size in sizes):
        weights, thin = (*own, *came), ()
    else:
        thin = prep_thin(bit, own[0], came[0], places[0], width, hidden)
        whole = [
            in_order(mine, other, bit[0], place, part.shape[1])
            for mine, other, place, part in zip(own, came, places, parts)
        ]
        starts = [0, 0, sizes[1], sizes[1] + sizes[2]]
        weights = tuple(
            whole[min(index, 1)][:, start : start + size].reshape(-1, hidden)
            for index, (start, size) in enumerate(zip(starts, sizes))
        )
        places = None

    chunk = 16 * devices
    grad_rows = -(-(6 * (width + 3 * hidden) + 2 * hidden) // chunk) * chunk
    logits, flipped_grad, kept, sent = dense(bit, flipped, weights, places, thin, logit_cot, grad_rows)

    def prepare(flipped_grad):
        return send_rows(flipped_grad, rank, owner_rows, capacity, 1)

    def finish_rows(incoming):
        return add_rows(incoming, asked_rows, embed_table.shape[0])

    done, table_grad, x_grad = sum_grads(kept, sent, flipped_grad, prepare, finish_rows, width, hidden)
    return (logits, x_grad, table_grad.T, *done)


def solution(mesh):
    return jax.shard_map(
        on_device,
        mesh=mesh,
        in_specs=(
            P(("dp", "fsdp"), None),
            P(("dp", "fsdp"), None),
            P(("dp", "fsdp"), None),
            P(("dp", "fsdp"), None),
            P(("dp", "fsdp")),
            P(("dp", "fsdp"), None),
            P(("dp", "fsdp")),
            P(("dp", "fsdp")),
            P(("dp", "fsdp"), None),
            P(("dp", "fsdp"), None),
            P(("dp", "fsdp"), None),
            P(("dp", "fsdp")),
            P(("dp", "fsdp"), None),
            P(("dp", "fsdp")),
            P(("dp", "fsdp")),
            P(("dp", "fsdp"), None),
            P(("dp", "fsdp"), None),
            P(("dp", "fsdp")),
            P(("dp", "fsdp"), None),
            P(("dp", "fsdp")),
            P(None, ("dp", "fsdp")),
        ),
        out_specs=(
            P(None, ("dp", "fsdp")),
            P(("dp", "fsdp"), None),
            P(("dp", "fsdp"), None),
            P(),
            P(),
            P(),
            P(),
            P(),
            P(),
            P(),
            P(),
            P(),
            P(),
            P(),
            P(),
            P(),
            P(),
            P(),
            P(),
            P(),
        ),
        check_vma=False,
    )
```
